256 devices in a mesh: ctx: 8 (over x, core), exp: 16 (over y_hi, z), dp: 2 (over y_lo).
Axes of the slice: x: 4, y: 4 (y_hi: 2, y_lo: 2; y = y_hi * 2 + y_lo), z: 8, core: 2. Of those that a mesh axis runs over, the one named last changes fastest.
Arguments:
- hidden_in: bfloat16 [32768, 3584], P(('dp', 'ctx', 'exp')), parts along dimension 0, may hold values from -6 to 6
- queries: bfloat16 [32768, 3584], P(('dp', 'ctx', 'exp')), parts along dimension 0, may hold values from -6 to 6
- keys_values: bfloat16 [32768, 1024], P(('dp', 'ctx', 'exp')), parts along dimension 0, may hold values from -6 to 6
- doc_ids: int32 [32768], P(('dp', 'ctx', 'exp')), parts along dimension 0, may hold values from 0 to 15, never falling along the last dimension, each value on 1 to 2048 neighbouring positions
- route_ids: int32 [32768, 8], P(('dp', 'ctx', 'exp')), parts along dimension 0, may hold values from 0 to 63, as said below
- route_weights: float32 [32768, 8], P(('dp', 'ctx', 'exp')), parts along dimension 0, may hold values from 0.1 to 0.6
- norm_gain: bfloat16 [3584], replicated, may hold values from 0.5 to 1.5
- gate_up: bfloat16 [2, 2, 3584, 2560], P(None, None, None, 'exp'), may hold values from -0.09375 to 0.09375
- down: bfloat16 [2, 2560, 3584], P(None, 'exp'), may hold values from -0.125 to 0.125
Outputs:
- output: bfloat16 [32768, 3584], P(('dp', 'ctx', 'exp')), parts along dimension 0
The draws below stay inside these ranges and needn't reach their ends.
There are 2 independent parts, one for each index of `dp`. The reference program is written for one: setup_inputs(seed, part) draws one part's arguments, and reference() takes and returns one part's arrays. A program takes and returns all parts, laid end to end along the dimension named above; an argument that names none is the same for every part. Nothing has to cross between parts.
Inputs may be any that keep to these rules, and one draw needn't show every extreme that they name: `doc_ids`: each document is a run of consecutive tokens of at most 2048 tokens; ids never fall along the sequence. `route_ids`: the ids in a row are distinct; within the 128 rows of one device (aligned blocks), each expert below 2 is named by at most 32 rows, and by exactly 32 rows in some block.
All inputs are finite; a program needn't handle non-finite values.
Results may differ from the reference program's by a relative error of at most 0.009.
Values may be sent and summed in bfloat16 or wider, within the bound.
No kernel may reach another device: no remote copies, remote signals or barrier semaphores. Data moves between devices by JAX's collectives and lax.ppermute only.
A program may use at most 128 MiB of HBM per device.

```python
import math
import jax
import jax.numpy as jnp
import numpy as np
from jax import lax

D = 3584
HEADS = 28
KV_HEADS = 4
HEAD_DIM = 128
EXPERTS = 64
FF = 2560
TOP = 8
EXP_FLIGHT = 2
TOK_DEV = 128
CAP = 32
SLAB = 2048
SEQ = 16384
DOCS = 16


def draw_queries(key, part):
    key = jax.random.fold_in(key, 3)
    first_key = jax.random.fold_in(key, 0)
    noise = jax.random.normal(first_key, (SEQ, HEADS, HEAD_DIM), jnp.float32)
    values = noise
    return jnp.clip(values, -6.0, 6.0).reshape(SEQ, HEADS * HEAD_DIM).astype(jnp.bfloat16)


def draw_keys_values(key, part):
    key = jax.random.fold_in(key, 5)
    first_key = jax.random.fold_in(key, 0)
    third_key = jax.random.fold_in(key, 2)
    noise = jax.random.normal(first_key, (SEQ, KV_HEADS, HEAD_DIM), jnp.float32)
    key_part = noise
    value_part = jax.random.normal(third_key, (SEQ, KV_HEADS, HEAD_DIM), jnp.float32)
    joined = jnp.concatenate([key_part.reshape(SEQ, KV_HEADS * HEAD_DIM), value_part.reshape(SEQ, KV_HEADS * HEAD_DIM)], 1)
    return jnp.clip(joined, -6.0, 6.0).astype(jnp.bfloat16)


def draw_route_ids(key, part):
    key = jax.random.fold_in(key, 7)
    blocks = SEQ // TOK_DEV
    spare_ids = EXPERTS - EXP_FLIGHT
    subkeys = jax.random.split(key, 2 + 3 * EXP_FLIGHT)
    row_keys = jax.random.split(subkeys[0], SEQ)
    chooser = jax.vmap(lambda k: jax.random.permutation(k, spare_ids)[:TOP])
    choose = chooser(row_keys) + EXP_FLIGHT
    columns = jnp.arange(TOP)
    ranker = jax.vmap(lambda k: jax.random.permutation(k, TOK_DEV))
    for flight in range(EXP_FLIGHT):
        counts = jax.random.randint(subkeys[1 + 3 * flight], (blocks,), CAP // 3, CAP + 1)
        fullest = jax.random.randint(subkeys[2 + 3 * flight], (), 0, blocks)
        counts = jnp.where(jnp.arange(blocks) == fullest, CAP, counts)
        ranking = ranker(jax.random.split(subkeys[3 + 3 * flight], blocks))
        member = (ranking < counts[:, None]).reshape(SEQ)
        choose = jnp.where(member[:, None] & (columns[None, :] == flight), flight, choose)
    column_keys = jax.random.split(subkeys[1 + 3 * EXP_FLIGHT], SEQ)
    shuffler = jax.vmap(lambda k: jax.random.permutation(k, TOP))
    column_order = shuffler(column_keys)
    return jnp.take_along_axis(choose, column_order, axis=1).astype(jnp.int32)


def shard_levels(key, shape, cuts, least, largest):
    level = 1.0
    for position, shards_of in cuts:
        heights = jax.random.uniform(jax.random.fold_in(jax.random.fold_in(key, 6), position), (shards_of,), jnp.float32, least / len(cuts), largest / len(cuts))
        level = level * jnp.repeat(jnp.exp(heights), shape[position] // shards_of).reshape((-1,) + (1,) * (len(shape) - 1 - position))
    return level


def length_profile(number_of, total, limit, slope):
    portions = [(1 << 20) // math.isqrt(standing ** slope) + 1 for standing in range(2, number_of + 1)]
    surplus, given = total - limit - (number_of - 1), [1] * (number_of - 1)
    while surplus > 0:
        candidates = [i for i in range(number_of - 1) if given[i] < limit]
        whole, remaining = sum([portions[i] for i in candidates]), surplus
        for i in candidates:
            more = min(limit - given[i], max(1, remaining * portions[i] // whole), surplus)
            given[i] = given[i] + more
            surplus = surplus - more
    return np.array([limit] + given)


def uneven_parts(rng, number_of, total, bound, skew):
    if number_of == 2:
        one = jax.random.randint(rng, (), max(1, total - bound), min(bound, total - 1) + 1)
        return jnp.stack([one, total - one])
    tallies = jnp.asarray(length_profile(number_of, total, bound, skew), jnp.int32)
    couples = (number_of - 1) // 2
    donor, receiver = tallies[1:1 + 2 * couples:2], tallies[2:2 + 2 * couples:2]
    room = jnp.minimum(donor - 1, bound - receiver)
    passed = jax.random.randint(jax.random.fold_in(rng, 1), (couples,), 0, 1 << 20) % (room + 1)
    tallies = tallies.at[1:1 + 2 * couples:2].set(donor - passed).at[2:2 + 2 * couples:2].set(receiver + passed)
    return tallies[jax.random.permutation(jax.random.fold_in(rng, 2), number_of)]


def normal_values(key, shape, width, limit, shards=(), kind=jnp.bfloat16):
    entries = jax.random.normal(key, shape, jnp.float32) * width
    if len(shards) > 0:
        entries = shard_levels(key, shape, shards, -0.22, 0.18) * entries
    return jnp.clip(entries, min=-limit, max=limit).astype(kind)


def setup_inputs(seed: int = 0, part: int = 0) -> dict:
    key_list = jax.random.split(jax.random.key(seed), 10)
    part_splits = jax.random.split(jax.random.fold_in(key_list[9], part), 10)
    return {
        "hidden_in": normal_values(part_splits[0], (SEQ, D), 1.0, 6.0, ((0, 128),)),
        "queries": draw_queries(jax.random.fold_in(jax.random.fold_in(key_list[9], part), 71), part),
        "keys_values": draw_keys_values(jax.random.fold_in(jax.random.fold_in(key_list[9], part), 71), part),
        "doc_ids": jnp.searchsorted(jnp.cumsum(uneven_parts(part_splits[3], DOCS, SEQ, SLAB, 1)), jnp.arange(SEQ), side="right").astype(jnp.int32),
        "route_ids": draw_route_ids(jax.random.fold_in(jax.random.fold_in(key_list[9], part), 71), part),
        "route_weights": jnp.clip(0.1 + 0.5 * jax.random.uniform(part_splits[5], (SEQ, TOP), jnp.float32) ** shard_levels(part_splits[5], (SEQ, TOP), ((0, 128),), -0.2, 0.2), 0.1, 0.6),
        "norm_gain": jnp.clip(1.0 + 0.1 * jax.random.normal(key_list[6], (D,), jnp.float32), 0.5, 1.5).astype(jnp.bfloat16),
        "gate_up": normal_values(key_list[7], (EXP_FLIGHT, 2, D, FF), D ** -0.5, 0.09375, ((3, 16),)),
        "down": normal_values(key_list[8], (EXP_FLIGHT, FF, D), FF ** -0.5, 0.125, ((1, 16),)),
    }


def attend(queries, keys_values, doc_ids):
    q_group = HEADS // KV_HEADS
    kv_width = KV_HEADS * HEAD_DIM
    score_scale = HEAD_DIM ** (-0.5)
    key_count = SLAB + TOK_DEV
    padded_kv = jnp.concatenate([jnp.zeros((SLAB, 2 * kv_width), keys_values.dtype), keys_values], 0)
    padded_doc = jnp.concatenate([jnp.full((SLAB,), -1, jnp.int32), doc_ids.astype(jnp.int32)], 0)

    def one_block(block_index):
        offset = (block_index * TOK_DEV).astype(jnp.int32)
        query_rows = lax.dynamic_slice_in_dim(queries, offset, TOK_DEV, 0).astype(jnp.float32)
        query_rows = query_rows.reshape(TOK_DEV, KV_HEADS, q_group, HEAD_DIM)
        query_doc = lax.dynamic_slice_in_dim(doc_ids.astype(jnp.int32), offset, TOK_DEV, 0)
        window = lax.dynamic_slice_in_dim(padded_kv, offset, key_count, 0).astype(jnp.float32)
        window_doc = lax.dynamic_slice_in_dim(padded_doc, offset, key_count, 0)
        key_rows = window[:, :kv_width].reshape(key_count, KV_HEADS, HEAD_DIM)
        value_rows = window[:, kv_width:].reshape(key_count, KV_HEADS, HEAD_DIM)
        query_pos = offset + jnp.arange(TOK_DEV, dtype=jnp.int32)
        key_pos = offset - SLAB + jnp.arange(key_count, dtype=jnp.int32)
        allowed = (query_doc[:, None] == window_doc[None, :]) & (key_pos[None, :] <= query_pos[:, None])
        scores = jnp.einsum('tkgd,skd->kgts', query_rows, key_rows) * score_scale
        scores = jnp.where(allowed, scores, -1e+30)
        highest = lax.optimization_barrier(jnp.max(scores, axis=-1, keepdims=True))
        powers = jnp.where(allowed, jnp.exp(scores - highest), 0.0)
        totals = lax.optimization_barrier(jnp.sum(powers, axis=-1))
        rounded = lax.optimization_barrier(powers.astype(jnp.bfloat16)).astype(jnp.float32)
        mixture = jnp.einsum('kgts,skd->kgtd', rounded, value_rows) / totals[..., None]
        return jnp.transpose(mixture, (2, 0, 1, 3)).reshape(TOK_DEV, HEADS * HEAD_DIM)
    blocks = lax.map(one_block, jnp.arange(SEQ // TOK_DEV, dtype=jnp.int32))
    return blocks.reshape(SEQ, HEADS * HEAD_DIM).astype(jnp.bfloat16)

def experts(normed, route_ids, route_weights, gate_up, down):
    slot_rows = SEQ // TOK_DEV * CAP
    combined = jnp.zeros((SEQ, D), jnp.float32)
    for flight in range(EXP_FLIGHT):
        chosen = route_ids == flight
        weight = lax.optimization_barrier(jnp.sum(jnp.where(chosen, route_weights.astype(jnp.float32), 0.0), axis=1))
        routed = jnp.any(chosen, axis=1)
        picked_ids = jnp.nonzero(routed, size=slot_rows, fill_value=0)[0].astype(jnp.int32)
        is_valid = jnp.arange(slot_rows) < jnp.sum(routed.astype(jnp.int32))
        picked = normed[picked_ids]
        gate_part = jnp.dot(picked, gate_up[flight, 0], preferred_element_type=jnp.float32)
        up_part = jnp.dot(picked, gate_up[flight, 1], preferred_element_type=jnp.float32)
        hidden_act = (jax.nn.silu(gate_part) * up_part).astype(jnp.bfloat16)
        result = jnp.dot(hidden_act, down[flight], preferred_element_type=jnp.float32)
        factor = jnp.where(is_valid, weight[picked_ids], 0.0)
        combined = combined.at[picked_ids].add(result * factor[:, None])
    return combined

def reference(hidden_in, queries, keys_values, doc_ids, route_ids, route_weights, norm_gain, gate_up, down):
    attended = attend(queries, keys_values, doc_ids)
    stream = (hidden_in.astype(jnp.float32) + attended.astype(jnp.float32)).astype(jnp.bfloat16)
    stream_f = lax.optimization_barrier(stream).astype(jnp.float32)
    inverse = lax.rsqrt(lax.optimization_barrier(jnp.mean(stream_f * stream_f, axis=-1, keepdims=True)) + 1e-06)
    normed = (stream_f * inverse * norm_gain.astype(jnp.float32)).astype(jnp.bfloat16)
    combined = experts(normed, route_ids, route_weights, gate_up, down)
    return (stream_f + combined).astype(jnp.bfloat16)
```

```python
import functools
import math

import jax
import jax.numpy as jnp
from jax import lax
from jax.experimental import pallas as pl
from jax.experimental.pallas import tpu as pltpu
from jax.sharding import Mesh
from jax.sharding import PartitionSpec as P

EXP_FLIGHT = 2
HEADS=28; KV_HEADS=4; HD=128; GROUP=7
EXP2_SCALE = math.log2(math.e) / math.sqrt(HD)

def attend_kernel(info_ref, q_ref, hid_ref, start_ref, gain_ref, place_ref, pa_ref, pb_ref, oa_ref, ob_ref,
                  stream_ref, panel_ref, kscr, vscr, m_scr, l_scr, acc_scr, s_all, ssq, sem, *, tok, span):
    c = pl.program_id(0)
    nc = pl.num_programs(0)
    half = oa_ref.shape[0]
    wide = GROUP * HD
    first = info_ref[0]
    off_a = pl.multiple_of(info_ref[1], half)
    off_b = pl.multiple_of(half - info_ref[1], half)
    start_min = info_ref[2]
    start_max = info_ref[3]

    def copies(head, slot):
        out = []
        for n, (src, off) in enumerate(((pa_ref, off_a), (pb_ref, off_b), (oa_ref, off_a + 2 * half), (ob_ref, off_b + 2 * half))):
            for which, dst in ((0, kscr), (1, vscr)):
                col = pl.multiple_of(which * KV_HEADS * HD + head * HD, HD)
                out.append(pltpu.make_async_copy(src.at[:, pl.ds(col, HD)], dst.at[slot, pl.ds(off, half), :], sem.at[slot, n, which]))
        return out

    slot = lax.rem(c, 2)

    @pl.when(c == 0)
    def _():
        for cp in copies(0, 0):
            cp.start()
        ssq[...] = jnp.zeros_like(ssq)

    @pl.when(c + 1 < nc)
    def _():
        for cp in copies(c + 1, 1 - slot):
            cp.start()
    for cp in copies(c, slot):
        cp.wait()

    q = jnp.concatenate([q_ref[:, g * HD:(g + 1) * HD] for g in range(GROUP)], 0)
    start = start_ref[...]
    row = lax.broadcasted_iota(jnp.int32, (tok, 1), 0) + first + 2 * half

    def scores(offset, width):
        k = kscr[slot, pl.ds(offset, width), :]
        return lax.dot_general(q, k, (((1,), (1,)), ((), ())), preferred_element_type=jnp.float32)

    def rowmax(s, width):
        t = s[:, :128]
        for j in range(1, width // 128):
            t = jnp.maximum(t, s[:, j * 128:(j + 1) * 128])
        return jnp.max(t, axis=1, keepdims=True)

    def lanesum(p, width):
        t = p[:, :128]
        for j in range(1, width // 128):
            t = t + p[:, j * 128:(j + 1) * 128]
        return t

    def masked(s, offset, width, causal):
        key = lax.broadcasted_iota(jnp.int32, (tok, width), 1) + offset
        ok = key >= start
        if causal:
            ok = ok & (key <= row)
        return jnp.where(ok[None], s.reshape(GROUP, tok, width), -1e30).reshape(GROUP * tok, width)

    own = pl.multiple_of(first + 2 * half, tok)
    s = masked(scores(own, tok), own, tok, True)
    m = rowmax(s, tok)
    p = jnp.exp2((s - m) * EXP2_SCALE)
    m_scr[...] = jnp.broadcast_to(m, m_scr.shape)
    l_scr[...] = lanesum(p, tok)
    acc_scr[...] = jnp.dot(p.astype(jnp.bfloat16), vscr[slot, pl.ds(own, tok), :], preferred_element_type=jnp.float32)

    def step(i, mask):
        offset = pl.multiple_of(first + i * span, tok)
        s = scores(offset, span)
        if mask:
            s = masked(s, offset, span, False)
        old = m_scr[...]
        new = jnp.maximum(old, rowmax(s, span))
        m_scr[...] = new
        shrink = jnp.exp2((old - new) * EXP2_SCALE)
        p = jnp.exp2((s - jnp.concatenate([new] * (span // 128), 1)) * EXP2_SCALE)
        l_scr[...] = l_scr[...] * shrink + lanesum(p, span)
        acc_scr[...] = acc_scr[...] * shrink + jnp.dot(p.astype(jnp.bfloat16), vscr[slot, pl.ds(offset, span), :], preferred_element_type=jnp.float32)

    count = 2 * half // span
    begin = jnp.clip(lax.div(start_min - first, span), 0, count)

    def loop(i, carry):
        whole = start_max <= first + i * span
        @pl.when(whole)
        def _():
            step(i, False)
        @pl.when(jnp.logical_not(whole))
        def _():
            step(i, True)
        return carry
    lax.fori_loop(begin, count, loop, 0)

    total = jnp.sum(l_scr[...], axis=1, keepdims=True)
    att = (acc_scr[...] / total).astype(jnp.bfloat16).astype(jnp.float32)
    att = jnp.concatenate([att[g * tok:(g + 1) * tok] for g in range(GROUP)], 1)
    stream = (hid_ref[...].astype(jnp.float32) + att).astype(jnp.bfloat16)
    stream_ref[...] = stream
    sf = stream.astype(jnp.float32)
    ssq[...] += lanesum(sf * sf, wide)
    for h in range(KV_HEADS):
        @pl.when(c == h)
        def _(h=h):
            s_all[:, h * wide:(h + 1) * wide] = stream

    @pl.when(c == nc - 1)
    def _():
        inv = lax.rsqrt(jnp.sum(ssq[...], axis=1, keepdims=True) / (KV_HEADS * wide) + 1e-6)
        normed = (s_all[...].astype(jnp.float32) * inv * gain_ref[...].astype(jnp.float32)).astype(jnp.bfloat16)
        panel_ref[...] = jnp.dot(place_ref[...], normed, preferred_element_type=jnp.float32).astype(jnp.bfloat16)

def attend(info, queries, hidden, start, gain, place, pa, pb, oa, ob, span=512):
    tok, d = queries.shape
    wide = GROUP * HD
    half = oa.shape[0]
    rows = place.shape[0]
    blk = pl.BlockSpec((tok, wide), lambda c, s: (0, c))
    whole = lambda shape: pl.BlockSpec(shape, lambda c, s: (0, 0))
    hbm = pl.BlockSpec(memory_space=pl.ANY)
    return pl.pallas_call(
        functools.partial(attend_kernel, tok=tok, span=span),
        grid_spec=pltpu.PrefetchScalarGridSpec(
            num_scalar_prefetch=1, grid=(KV_HEADS,),
            in_specs=[blk, blk, whole((tok, 1)), whole((1, d)), whole((rows, tok)), hbm, hbm, hbm, hbm],
            out_specs=[blk, whole((rows, d))],
            scratch_shapes=[pltpu.VMEM((2, 4 * half, HD), jnp.bfloat16), pltpu.VMEM((2, 4 * half, HD), jnp.bfloat16),
                            pltpu.VMEM((GROUP * tok, 128), jnp.float32), pltpu.VMEM((GROUP * tok, 128), jnp.float32),
                            pltpu.VMEM((GROUP * tok, 128), jnp.float32), pltpu.VMEM((tok, d), jnp.bfloat16),
                            pltpu.VMEM((tok, 128), jnp.float32), pltpu.SemaphoreType.DMA((2, 4, 2))]),
        out_shape=[jax.ShapeDtypeStruct((tok, d), jnp.bfloat16), jax.ShapeDtypeStruct((rows, d), jnp.bfloat16)],
        compiler_params=pltpu.CompilerParams(vmem_limit_bytes=48 << 20),
        cost_estimate=pl.CostEstimate(flops=4 * 10**9, bytes_accessed=12 << 20, transcendentals=8 * 10**6),
        name="attend",
    )(info, queries, hidden, start, gain, place, pa, pb, oa, ob)

def expert_kernel(x_ref, wo_ref, do_ref, r1_ref, r2_ref, y_ref, wg, wu, wd, sem):
    n = wo_ref.shape[1]
    h = r1_ref.shape[1]
    cps = []
    def cp(src, dst):
        c = pltpu.make_async_copy(src, dst, sem.at[len(cps)]); c.start(); cps.append(c)
    cp(wo_ref.at[0], wg.at[pl.ds(0, n)])
    cp(r1_ref.at[0], wg.at[pl.ds(n, h)])
    cp(r2_ref.at[0], wg.at[pl.ds(n + h, h)])
    cp(wo_ref.at[1], wu.at[pl.ds(0, n)])
    cp(r1_ref.at[1], wu.at[pl.ds(n, h)])
    cp(r2_ref.at[1], wu.at[pl.ds(n + h, h)])
    cp(do_ref, wd.at[pl.ds(0, n)])
    cp(r1_ref.at[2], wd.at[pl.ds(n, h)])
    cp(r2_ref.at[2], wd.at[pl.ds(n + h, h)])
    nt = (((1,), (1,)), ((), ()))
    for c in cps[:3]: c.wait()
    x = x_ref[...]
    gate = lax.dot_general(x, wg[...], nt, preferred_element_type=jnp.float32)
    for c in cps[3:6]: c.wait()
    up = lax.dot_general(x, wu[...], nt, preferred_element_type=jnp.float32)
    inner = (gate / (1 + jnp.exp(-gate)) * up).astype(jnp.bfloat16)
    for c in cps[6:]: c.wait()
    y_ref[...] = jnp.dot(inner, wd[...], preferred_element_type=jnp.float32).astype(jnp.bfloat16)

def experts(x, wo, do, r1, r2):
    rows, d = x.shape
    n = wo.shape[1] + r1.shape[1] + r2.shape[1]
    hbm = pl.BlockSpec(memory_space=pl.ANY)
    vm = pl.BlockSpec(memory_space=pltpu.VMEM)
    return pl.pallas_call(
        expert_kernel,
        in_specs=[vm, hbm, hbm, hbm, hbm], out_specs=vm,
        scratch_shapes=[pltpu.VMEM((n, d), jnp.bfloat16)] * 3 + [pltpu.SemaphoreType.DMA((9,))],
        out_shape=jax.ShapeDtypeStruct((rows, d), jnp.bfloat16),
        compiler_params=pltpu.CompilerParams(vmem_limit_bytes=48 << 20),
        cost_estimate=pl.CostEstimate(flops=6 * rows * n * d, bytes_accessed=2 * (3 * n * d + 2 * rows * d), transcendentals=rows * n),
        name="experts",
    )(x, wo, do, r1, r2)


def combine_kernel(stream_ref, keep_ref, back_ref, hot1_ref, hot2_ref, w1_ref, w2_ref, out_ref):
    one = jnp.dot(hot1_ref[...], keep_ref[...], preferred_element_type=jnp.float32)
    two = jnp.dot(hot2_ref[...], back_ref[...], preferred_element_type=jnp.float32)
    total = stream_ref[...].astype(jnp.float32) + one * w1_ref[...] + two * w2_ref[...]
    out_ref[...] = total.astype(out_ref.dtype)


def combine(stream, keep, back, hot1, hot2, w1, w2):
    tok, d = stream.shape
    cap = keep.shape[0]
    wide = d // 4
    cols = lambda rows: pl.BlockSpec((rows, wide), lambda c: (0, c))
    whole = lambda shape: pl.BlockSpec(shape, lambda c: (0, 0))
    return pl.pallas_call(
        combine_kernel,
        grid=(4,),
        in_specs=[cols(tok), cols(cap), cols(cap), whole((tok, cap)), whole((tok, cap)), whole((tok, 1)), whole((tok, 1))],
        out_specs=cols(tok),
        out_shape=jax.ShapeDtypeStruct((tok, d), stream.dtype),
        name="combine",
    )(stream, keep, back, hot1, hot2, w1, w2)


def shift(value, axis, size, steps):
    return lax.ppermute(value, axis, [(i, (i + steps) % size) for i in range(size)])


def swap(value, axis):
    return shift(value, axis, 2, 1)


def doc_starts(doc_ids, sizes):
    ids = jnp.arange(128, dtype=jnp.int32)
    counts = jnp.sum((doc_ids[:, None] < ids[None, :]).astype(jnp.float32), axis=0)
    counts = jnp.broadcast_to(counts[None], (8, 128))
    for axis, size in sizes:
        hop = 1
        while hop < size:
            counts = counts + lax.ppermute(counts, axis, [(i, i ^ hop) for i in range(size)])
            hop *= 2
    hot = doc_ids[:, None] == ids[None, :]
    return jnp.sum(jnp.where(hot, counts[:1], 0.0), axis=1).astype(jnp.int32)


def routing(route_ids, route_weights, flight, capacity):
    chosen = route_ids == flight
    routed = jnp.any(chosen, axis=1)
    weight = jnp.sum(jnp.where(chosen, route_weights, 0.0), axis=1)
    slot_of = jnp.cumsum(routed.astype(jnp.int32)) - 1
    slots = jnp.arange(capacity, dtype=jnp.int32)
    hot = (slot_of[:, None] == slots[None, :]) & routed[:, None]
    return hot.astype(jnp.bfloat16), jnp.where(routed, weight, 0.0)[:, None]


def body(sizes, hidden_in, queries, keys_values, doc_ids, route_ids, route_weights, norm_gain, gate_up, down):
    tok = queries.shape[0]
    capacity = tok // 4
    n_z, n_core, n_cx = sizes["z"], sizes["core"], sizes["cx"]
    yhi, z = lax.axis_index("yhi"), lax.axis_index("z")
    core = lax.axis_index("core")
    ctx = lax.axis_index("cx") * n_core + core
    half = n_z * tok
    n_ctx = n_cx * n_core

    other_kv = swap(keys_values, "yhi")
    own_a = lax.all_gather(keys_values, "z", axis=0, tiled=True)
    own_b = lax.all_gather(other_kv, "z", axis=0, tiled=True)
    ahead = [(i, i + 1) for i in range(n_ctx - 1)]
    prior_a = lax.ppermute(own_a, ("cx", "core"), ahead)
    prior_b = lax.ppermute(own_b, ("cx", "core"), ahead)

    wide_t = jnp.swapaxes(gate_up, 2, 3)
    units = wide_t.shape[2] // n_core
    theirs = jnp.concatenate(
        [
            lax.dynamic_slice(wide_t, (1 - yhi, 0, core * units, 0), (1, 2, units, wide_t.shape[3]))[0],
            lax.dynamic_slice(down, (1 - yhi, core * units, 0), (1, units, down.shape[2])),
        ],
        0,
    )
    theirs, _ = lax.optimization_barrier((theirs, other_kv))
    got_1 = swap(theirs, "yhi")
    got_2 = swap(got_1, "core")
    mine_gu = lax.dynamic_index_in_dim(wide_t, yhi, 0, False)
    mine_d = lax.dynamic_index_in_dim(down, yhi, 0, False)

    axes = [("z", n_z), ("yhi", 2), ("core", n_core), ("cx", n_cx)]
    start = doc_starts(doc_ids, axes) - (ctx - 1) * (2 * half)
    first = yhi * half + z * tok
    info = jnp.stack([first, yhi * half, start[0], start[tok - 1]]).astype(jnp.int32)

    hot_1, w_1 = routing(route_ids, route_weights, yhi, capacity)
    hot_2, w_2 = routing(route_ids, route_weights, 1 - yhi, capacity)
    place = jnp.concatenate([hot_1, hot_2], 1).T

    stream, panels = attend(
        info, queries, hidden_in, start[:, None], norm_gain[None], place, prior_a, prior_b, own_a, own_b
    )
    keep, send = panels[:capacity], panels[capacity:]
    other = swap(send, "yhi")
    rows_a = lax.all_gather(keep, "z", axis=0, tiled=True)
    rows_b = lax.all_gather(other, "z", axis=0, tiled=True)
    out_a = experts(rows_a, mine_gu, mine_d, got_1, got_2)
    out_b = experts(rows_b, mine_gu, mine_d, got_1, got_2)
    sum_a = lax.psum_scatter(out_a, "z", scatter_dimension=0, tiled=True)
    sum_b = lax.psum_scatter(out_b, "z", scatter_dimension=0, tiled=True)
    back = swap(sum_b, "yhi")
    return combine(stream, sum_a, back, hot_1, hot_2, w_1, w_2)


def solution(mesh):
    sizes = {"cx": mesh.shape["ctx"] // 2, "core": 2, "yhi": 2, "z": mesh.shape["exp"] // 2, "dp": mesh.shape["dp"]}
    fine = Mesh(mesh.devices.reshape(tuple(sizes.values())), tuple(sizes))
    tokens = ("dp", "cx", "core", "yhi", "z")
    rows = P(tokens, None)
    hidden = ("yhi", "z")
    in_specs = (rows, rows, rows, P(tokens), rows, rows, P(), P(None, None, None, hidden), P(None, hidden, None))
    return jax.shard_map(
        functools.partial(body, sizes), mesh=fine, in_specs=in_specs, out_specs=rows, check_vma=False
    )
```

```python
import functools
import math

import jax
import jax.numpy as jnp
from jax import lax
from jax.experimental import pallas as pl
from jax.experimental.pallas import tpu as pltpu
from jax.sharding import Mesh
from jax.sharding import PartitionSpec as P

EXP_FLIGHT = 2
HD = 128
GROUP = 7
EXP2_SCALE = math.log2(math.e) / math.sqrt(HD)

def attend_kernel(info_ref, q_ref, doc_ref, *refs, tok, span, moves, heads):
    count = 2 * len(moves)
    pieces, out_ref = refs[:count], refs[count]
    kv, ids, start_scr, m_scr, l_scr, acc_scr, bounds, sem = refs[count + 1:]
    c = pl.program_id(0)
    z = info_ref[0]
    half = len(moves) * tok
    near = pl.multiple_of(info_ref[1], half)
    far = pl.multiple_of(half - info_ref[1], half)
    first = pl.multiple_of(info_ref[2], tok)

    @pl.when(c == 0)
    def _():
        copies = []
        for n, piece in enumerate(pieces):
            place = lax.rem(z + moves[n % len(moves)] + len(moves), len(moves)) * tok
            slab = n // len(moves) * 2 * half
            for part, base in ((0, near), (1, far)):
                at = pl.multiple_of(slab + base + place, tok)
                copies.append(pltpu.make_async_copy(piece.at[pl.ds(part * tok, tok)], kv.at[pl.ds(at, tok)], sem.at[n, part]))
            copies.append(pltpu.make_async_copy(piece.at[pl.ds(2 * tok, 16)], ids.at[n], sem.at[n, 2]))
        for cp in copies:
            cp.start()
        for cp in copies:
            cp.wait()
        own = doc_ref[...]
        less = jnp.zeros((tok, 2 * tok), jnp.float32)
        for n in range(count):
            row = ids[n, 0:1, :2 * tok].astype(jnp.float32)
            less = less + jnp.where(row < own, 1.0, 0.0)
        begin = jnp.sum(less, axis=1, keepdims=True)
        start_scr[...] = begin.astype(jnp.int32)
        bounds[0] = jnp.min(begin).astype(jnp.int32)
        bounds[1] = jnp.max(begin).astype(jnp.int32)

    start_min, start_max = bounds[0], bounds[1]
    q = jnp.concatenate([q_ref[:, g * HD:(g + 1) * HD] for g in range(GROUP)], 0)
    start = start_scr[...]
    row = lax.broadcasted_iota(jnp.int32, (tok, 1), 0) + first + 2 * half
    key_col = pl.multiple_of(c * HD, HD)
    value_col = pl.multiple_of((heads + c) * HD, HD)

    def keys(offset, width):
        return kv[pl.ds(offset, width), pl.ds(key_col, HD)]

    def values(offset, width):
        return kv[pl.ds(offset, width), pl.ds(value_col, HD)]

    def scores(offset, width):
        return lax.dot_general(q, keys(offset, width), (((1,), (1,)), ((), ())), preferred_element_type=jnp.float32)

    def rowmax(s, width):
        t = s[:, :128]
        for j in range(1, width // 128):
            t = jnp.maximum(t, s[:, j * 128:(j + 1) * 128])
        return jnp.max(t, axis=1, keepdims=True)

    def lanesum(p, width):
        t = p[:, :128]
        for j in range(1, width // 128):
            t = t + p[:, j * 128:(j + 1) * 128]
        return t

    def masked(s, offset, width, causal):
        key = lax.broadcasted_iota(jnp.int32, (tok, width), 1) + offset
        ok = key >= start
        if causal:
            ok = ok & (key <= row)
        return jnp.where(ok[None], s.reshape(GROUP, tok, width), -1e30).reshape(GROUP * tok, width)

    own = pl.multiple_of(first + 2 * half, tok)
    s = masked(scores(own, tok), own, tok, True)
    m = rowmax(s, tok)
    p = jnp.exp2((s - m) * EXP2_SCALE)
    m_scr[...] = jnp.broadcast_to(m, m_scr.shape)
    l_scr[...] = lanesum(p, tok)
    acc_scr[...] = jnp.dot(p.astype(jnp.bfloat16), values(own, tok), preferred_element_type=jnp.float32)

    def step(i, mask):
        offset = pl.multiple_of(first + i * span, tok)
        s = scores(offset, span)
        if mask:
            s = masked(s, offset, span, False)
        old = m_scr[...]
        new = jnp.maximum(old, rowmax(s, span))
        m_scr[...] = new
        shrink = jnp.exp2((old - new) * EXP2_SCALE)
        p = jnp.exp2((s - jnp.concatenate([new] * (span // 128), 1)) * EXP2_SCALE)
        l_scr[...] = l_scr[...] * shrink + lanesum(p, span)
        acc_scr[...] = acc_scr[...] * shrink + jnp.dot(p.astype(jnp.bfloat16), values(offset, span), preferred_element_type=jnp.float32)

    steps = 2 * half // span

    def loop(i, carry):
        whole = start_max <= first + i * span

        @pl.when(whole)
        def _():
            step(i, False)

        @pl.when(jnp.logical_not(whole))
        def _():
            step(i, True)

        return carry

    lax.fori_loop(jnp.clip(lax.div(start_min - first, span), 0, steps), steps, loop, 0)

    total = jnp.sum(l_scr[...], axis=1, keepdims=True)
    att = (acc_scr[...] / total).astype(jnp.bfloat16)
    for g in range(GROUP):
        out_ref[:, g * HD:(g + 1) * HD] = att[g * tok:(g + 1) * tok]


def attend(info, queries, doc, pieces, moves, span=512):
    tok, d = queries.shape
    wide = GROUP * HD
    heads = d // wide
    n = len(moves)
    blk = pl.BlockSpec((tok, wide), lambda c, s: (0, c))
    hbm = pl.BlockSpec(memory_space=pl.ANY)
    scratch = pltpu.VMEM((GROUP * tok, 128), jnp.float32)
    return pl.pallas_call(
        functools.partial(attend_kernel, tok=tok, span=span, moves=moves, heads=heads),
        grid_spec=pltpu.PrefetchScalarGridSpec(
            num_scalar_prefetch=1,
            grid=(heads,),
            in_specs=[blk, pl.BlockSpec((tok, 1), lambda c, s: (0, 0))] + [hbm] * (2 * n),
            out_specs=blk,
            scratch_shapes=[
                pltpu.VMEM((4 * n * tok, 2 * heads * HD), jnp.bfloat16),
                pltpu.VMEM((2 * n, 16, 2 * heads * HD), jnp.bfloat16),
                pltpu.VMEM((tok, 1), jnp.int32),
                scratch, scratch, scratch,
                pltpu.SMEM((2,), jnp.int32),
                pltpu.SemaphoreType.DMA((2 * n, 3)),
            ],
        ),
        out_shape=jax.ShapeDtypeStruct((tok, d), jnp.bfloat16),
        compiler_params=pltpu.CompilerParams(vmem_limit_bytes=56 << 20),
        cost_estimate=pl.CostEstimate(flops=2 * 10**9, bytes_accessed=5 << 20, transcendentals=4 * 10**6),
        name="attend",
    )(info, queries, doc, *pieces)


def norm_kernel(info_ref, hid_ref, mine_ref, other_ref, gain_ref, place_ref, stream_ref, panel_ref, att):
    wide = mine_ref.shape[1]
    near = info_ref[1]

    @pl.when(near == 0)
    def _():
        att[:, :wide] = mine_ref[...]
        att[:, wide:] = other_ref[...]

    @pl.when(near != 0)
    def _():
        att[:, :wide] = other_ref[...]
        att[:, wide:] = mine_ref[...]

    stream = (hid_ref[...].astype(jnp.float32) + att[...].astype(jnp.float32)).astype(jnp.bfloat16)
    stream_ref[...] = stream
    sf = stream.astype(jnp.float32)
    inv = lax.rsqrt(jnp.mean(sf * sf, axis=1, keepdims=True) + 1e-6)
    normed = (sf * inv * gain_ref[...].astype(jnp.float32)).astype(jnp.bfloat16)
    rows = panel_ref.shape[1]
    for n in range(panel_ref.shape[0]):
        panel_ref[n] = jnp.dot(place_ref[n * rows:(n + 1) * rows], normed, preferred_element_type=jnp.float32).astype(jnp.bfloat16)


def norm_panels(info, hidden, mine, other, gain, place):
    tok, d = hidden.shape
    rows = place.shape[0] // EXP_FLIGHT
    vm = pl.BlockSpec(memory_space=pltpu.VMEM)
    return pl.pallas_call(
        norm_kernel,
        in_specs=[pl.BlockSpec(memory_space=pltpu.SMEM)] + [vm] * 5,
        out_specs=[vm, vm],
        out_shape=[jax.ShapeDtypeStruct((tok, d), jnp.bfloat16), jax.ShapeDtypeStruct((EXP_FLIGHT, rows, d), jnp.bfloat16)],
        scratch_shapes=[pltpu.VMEM((tok, d), jnp.bfloat16)],
        compiler_params=pltpu.CompilerParams(vmem_limit_bytes=32 << 20),
        name="norm_panels",
    )(info, hidden, mine, other, gain, place)


def expert_kernel(*refs, count, rows):
    xs = refs[:count]
    wo_ref, do_ref, r1_ref, r2_ref = refs[count:count + 4]
    ys = refs[count + 4:2 * count + 4]
    x, wg, wu, wd, sem = refs[2 * count + 4:]
    n = wo_ref.shape[1]
    h = r1_ref.shape[1]
    cps = []

    def cp(src, dst):
        c = pltpu.make_async_copy(src, dst, sem.at[len(cps)])
        c.start()
        cps.append(c)

    for i in range(count):
        cp(xs[i], x.at[pl.ds(i * rows, rows)])
    for i, w in enumerate((wg, wu, wd)):
        cp(do_ref if i == 2 else wo_ref.at[i], w.at[pl.ds(0, n)])
        cp(r1_ref.at[i], w.at[pl.ds(n, h)])
        cp(r2_ref.at[i], w.at[pl.ds(n + h, h)])
    nt = (((1,), (1,)), ((), ()))
    for c in cps[:count + 3]:
        c.wait()
    xv = x[...]
    gate = lax.dot_general(xv, wg[...], nt, preferred_element_type=jnp.float32)
    for c in cps[count + 3:count + 6]:
        c.wait()
    up = lax.dot_general(xv, wu[...], nt, preferred_element_type=jnp.float32)
    inner = (gate / (1 + jnp.exp(-gate)) * up).astype(jnp.bfloat16)
    for c in cps[count + 6:]:
        c.wait()
    y = jnp.dot(inner, wd[...], preferred_element_type=jnp.float32).astype(jnp.bfloat16)
    for i in range(count):
        ys[i][...] = y[i * rows:(i + 1) * rows]


def experts(xs, wo, do, r1, r2):
    count = len(xs)
    rows, d = xs[0].shape
    n = wo.shape[1] + r1.shape[1] + r2.shape[1]
    hbm = pl.BlockSpec(memory_space=pl.ANY)
    vm = pl.BlockSpec(memory_space=pltpu.VMEM)
    weight = pltpu.VMEM((n, d), jnp.bfloat16)
    return pl.pallas_call(
        functools.partial(expert_kernel, count=count, rows=rows),
        in_specs=[hbm] * (count + 4),
        out_specs=[vm] * count,
        scratch_shapes=[pltpu.VMEM((count * rows, d), jnp.bfloat16), weight, weight, weight, pltpu.SemaphoreType.DMA((count + 9,))],
        out_shape=[jax.ShapeDtypeStruct((rows, d), jnp.bfloat16)] * count,
        compiler_params=pltpu.CompilerParams(vmem_limit_bytes=56 << 20),
        cost_estimate=pl.CostEstimate(flops=6 * count * rows * n * d, bytes_accessed=2 * (3 * n * d + 2 * count * rows * d), transcendentals=count * rows * n),
        name="experts",
    )(*xs, wo, do, r1, r2)


def combine_kernel(stream_ref, a1_ref, a2_ref, a3_ref, back_ref, hot1_ref, hot2_ref, w1_ref, w2_ref, out_ref):
    keep = a1_ref[...].astype(jnp.float32) + a2_ref[...].astype(jnp.float32) + a3_ref[...].astype(jnp.float32)
    one = jnp.dot(hot1_ref[...], keep.astype(jnp.bfloat16), preferred_element_type=jnp.float32)
    two = jnp.dot(hot2_ref[...], back_ref[...], preferred_element_type=jnp.float32)
    total = stream_ref[...].astype(jnp.float32) + one * w1_ref[...] + two * w2_ref[...]
    out_ref[...] = total.astype(out_ref.dtype)


def combine(stream, parts, back, hot1, hot2, w1, w2):
    tok, d = stream.shape
    cap = back.shape[0]
    wide = d // 4
    cols = lambda rows: pl.BlockSpec((rows, wide), lambda c: (0, c))
    whole = lambda shape: pl.BlockSpec(shape, lambda c: (0, 0))
    return pl.pallas_call(
        combine_kernel,
        grid=(4,),
        in_specs=[cols(tok)] + [cols(cap)] * 4 + [whole((tok, cap))] * 2 + [whole((tok, 1))] * 2,
        out_specs=cols(tok),
        out_shape=jax.ShapeDtypeStruct((tok, d), stream.dtype),
        name="combine",
    )(stream, *parts, back, hot1, hot2, w1, w2)


def shift(value, axis, size, steps):
    return lax.ppermute(value, axis, [(i, (i + steps) % size) for i in range(size)])


def swap(value, axis):
    return shift(value, axis, 2, 1)


def routing(route_ids, route_weights, flight, capacity):
    chosen = route_ids == flight
    routed = jnp.any(chosen, axis=1)
    weight = jnp.sum(jnp.where(chosen, route_weights, 0.0), axis=1)
    slot_of = jnp.cumsum(routed.astype(jnp.int32)) - 1
    slots = jnp.arange(capacity, dtype=jnp.int32)
    hot = (slot_of[:, None] == slots[None, :]) & routed[:, None]
    return hot.astype(jnp.bfloat16), jnp.where(routed, weight, 0.0)[:, None]


def ring_moves(size):
    out = [0]
    for s in range(1, size // 2 + 1):
        out.append(-s)
        if 2 * s < size:
            out.append(s)
    return out


def ring_gather(parts, size):
    got = [{0: x} for x in parts]
    for s in range(1, size // 2 + 1):
        for g in got:
            g[-s] = shift(g[1 - s], "z", size, 1)
            if 2 * s < size:
                g[s] = shift(g[s - 1], "z", size, -1)
    return got


def ring_scatter(parts, size):
    reach = size // 2
    ups = [p[-reach] for p in parts]
    downs = [p[1 - reach] for p in parts]
    for s in range(1, reach + 1):
        for i, p in enumerate(parts):
            ups[i] = shift(ups[i], "z", size, 1)
            if s < reach:
                ups[i] = ups[i] + p[reach - s]
        for i, p in enumerate(parts):
            if s < reach:
                downs[i] = shift(downs[i], "z", size, -1)
            if s < reach - 1:
                downs[i] = downs[i] + p[1 - reach + s]
    return [(ups[i], downs[i], p[0]) for i, p in enumerate(parts)]


def body(sizes, hidden_in, queries, keys_values, doc_ids, route_ids, route_weights, norm_gain, gate_up, down):
    tok, d = queries.shape
    capacity = tok // 4
    n_z, n_core, n_cx = sizes["z"], sizes["core"], sizes["cx"]
    yhi, z, core = lax.axis_index("yhi"), lax.axis_index("z"), lax.axis_index("core")
    half = n_z * tok
    n_ctx = n_cx * n_core
    moves = ring_moves(n_z)

    kv_width = keys_values.shape[1] // 4
    low = jnp.concatenate([keys_values[:, :kv_width], keys_values[:, 2 * kv_width:3 * kv_width]], 1)
    high = jnp.concatenate([keys_values[:, kv_width:2 * kv_width], keys_values[:, 3 * kv_width:]], 1)
    is_low = yhi == 0
    docs = (doc_ids + 1).astype(jnp.bfloat16)
    doc_row = jnp.pad(docs[None], ((0, 15), (0, 2 * kv_width - tok)))
    other = swap(jnp.concatenate([jnp.where(is_low, high, low), doc_row], 0), "yhi")
    other_docs = other[tok, :tok]
    ids = doc_row + jnp.pad(other[tok:, :tok], ((0, 0), (tok, 2 * kv_width - 2 * tok)))
    unit = jnp.concatenate([jnp.where(is_low, low, high), other[:tok], ids], 0)

    my_q = lax.dynamic_slice_in_dim(queries, yhi * (d // 2), d // 2, 1)
    q_out = lax.dynamic_slice_in_dim(queries, (1 - yhi) * (d // 2), d // 2, 1)
    q_out, unit = lax.optimization_barrier((q_out, unit))
    other_q = swap(q_out, "yhi")
    wide_t = jnp.swapaxes(gate_up, 2, 3)
    units = wide_t.shape[2] // n_core
    theirs = jnp.concatenate(
        [
            lax.dynamic_slice(wide_t, (1 - yhi, 0, core * units, 0), (1, 2, units, d))[0],
            lax.dynamic_slice(down, (1 - yhi, core * units, 0), (1, units, d)),
        ],
        0,
    )
    theirs, other_q = lax.optimization_barrier((theirs, other_q))
    got_1 = swap(theirs, "yhi")
    got_2 = swap(got_1, "core")
    mine_gu = lax.dynamic_index_in_dim(wide_t, yhi, 0, False)
    mine_d = lax.dynamic_index_in_dim(down, yhi, 0, False)

    own = ring_gather([unit], n_z)[0]
    own = [own[m] for m in moves]
    ahead = [(i, i + 1) for i in range(n_ctx - 1)]
    prior = [lax.ppermute(x, ("cx", "core"), ahead) for x in own]

    hot_1, w_1 = routing(route_ids, route_weights, yhi, capacity)
    hot_2, w_2 = routing(route_ids, route_weights, 1 - yhi, capacity)
    place = jnp.concatenate([hot_1, hot_2], 1).T

    info_own = jnp.stack([z, yhi * half, yhi * half + z * tok]).astype(jnp.int32)
    info_other = jnp.stack([z, yhi * half, (1 - yhi) * half + z * tok]).astype(jnp.int32)
    column = lambda x: x.astype(jnp.float32)[:, None]
    pieces = prior + own
    theirs_att = attend(info_other, other_q, column(other_docs), pieces, moves)
    other_att = swap(theirs_att, "yhi")
    my_q, got_1, _ = lax.optimization_barrier((my_q, got_1, theirs_att))
    mine_att = attend(info_own, my_q, column(docs), pieces, moves)
    stream, panels = norm_panels(info_own, hidden_in, mine_att, other_att, norm_gain[None], place)

    keep, send = panels[0], panels[1]
    rows = ring_gather([keep, swap(send, "yhi")], n_z)
    last = -(n_z // 2)
    early = [m for m in moves if m != last]
    args = (mine_gu, mine_d, got_1, got_2)
    first_out = experts([r[m] for r in rows for m in early], *args)
    last_out = experts([r[last] for r in rows], *args)
    outs = [{m: first_out[i * len(early) + j] for j, m in enumerate(early)} | {last: last_out[i]} for i in range(2)]
    sum_b, sum_a = ring_scatter([outs[1], outs[0]], n_z)
    back = swap(sum_b[0] + sum_b[1] + sum_b[2], "yhi")
    return combine(stream, sum_a, back, hot_1, hot_2, w_1, w_2)


def solution(mesh):
    sizes = {"cx": mesh.shape["ctx"] // 2, "core": 2, "yhi": 2, "z": mesh.shape["exp"] // 2, "dp": mesh.shape["dp"]}
    fine = Mesh(mesh.devices.reshape(tuple(sizes.values())), tuple(sizes))
    tokens = ("dp", "cx", "core", "yhi", "z")
    rows = P(tokens, None)
    hidden = ("yhi", "z")
    in_specs = (rows, rows, rows, P(tokens), rows, rows, P(), P(None, None, None, hidden), P(None, hidden, None))
    return jax.shard_map(
        functools.partial(body, sizes), mesh=fine, in_specs=in_specs, out_specs=rows, check_vma=False
    )
```

```python
import functools
import math

import jax
import jax.numpy as jnp
from jax import lax
from jax.experimental import pallas as pl
from jax.experimental.pallas import tpu as pltpu
from jax.sharding import Mesh
from jax.sharding import PartitionSpec as P

EXP_FLIGHT = 2
HD = 128
GROUP = 7
EXP2_SCALE = math.log2(math.e) / math.sqrt(HD)

def attend_kernel(info_ref, q_ref, *refs, tok, span, moves, heads, layout, part):
    arrays, out_ref = refs[:-9], refs[-9]
    kv, ids, start_scr, m_scr, l_scr, acc_scr, bounds, sem = refs[-8:]
    c = pl.program_id(0)
    z = info_ref[0]
    half = len(moves) * tok
    near = pl.multiple_of(info_ref[1], half)
    far = pl.multiple_of(half - info_ref[1], half)
    first = pl.multiple_of((far if part else near) + z * tok, tok)

    @pl.when(c == 0)
    def _():
        blocks = []
        copies = []
        for n, (which, row) in enumerate(layout):
            piece = arrays[which]
            place = lax.rem(z + moves[n % len(moves)] + len(moves), len(moves)) * tok
            slab = n // len(moves) * 2 * half
            for side, base in ((0, near), (1, far)):
                at = pl.multiple_of(slab + base + place, tok)
                cp = pltpu.make_async_copy(piece.at[pl.ds(row + side * tok, tok)], kv.at[pl.ds(at, tok)], sem.at[n, side])
                blocks.append((cp, (at >= first) & (at <= first + 2 * half)))
            copies.append(pltpu.make_async_copy(piece.at[pl.ds(row + 2 * tok, 16)], ids.at[n], sem.at[n, 2]))
        for cp in copies:
            cp.start()
        for cp, needed in blocks:
            pl.when(needed)(cp.start)
        for cp in copies:
            cp.wait()
        own = ids[len(moves), 0:1, part * tok:(part + 1) * tok].astype(jnp.float32)
        own = jnp.broadcast_to(own, (tok, tok)).T
        less = jnp.zeros((tok, tok), jnp.float32)
        for n in range(len(layout)):
            for side in range(2):
                row = ids[n, 0:1, side * tok:(side + 1) * tok].astype(jnp.float32)
                less = less + jnp.where(row < own, 1.0, 0.0)
        begin = jnp.sum(less, axis=1, keepdims=True)
        start_scr[...] = begin.astype(jnp.int32)
        bounds[0] = jnp.min(begin).astype(jnp.int32)
        bounds[1] = jnp.max(begin).astype(jnp.int32)
        for cp, needed in blocks:
            pl.when(needed)(cp.wait)

    start_min, start_max = bounds[0], bounds[1]
    q = jnp.concatenate([q_ref[:, g * HD:(g + 1) * HD] for g in range(GROUP)], 0)
    start = start_scr[...]
    row = lax.broadcasted_iota(jnp.int32, (tok, 1), 0) + first + 2 * half
    key_col = pl.multiple_of(c * HD, HD)
    value_col = pl.multiple_of((heads + c) * HD, HD)

    def keys(offset, width):
        return kv[pl.ds(offset, width), pl.ds(key_col, HD)]

    def values(offset, width):
        return kv[pl.ds(offset, width), pl.ds(value_col, HD)]

    def scores(offset, width):
        return lax.dot_general(q, keys(offset, width), (((1,), (1,)), ((), ())), preferred_element_type=jnp.float32)

    def rowmax(s, width):
        t = s[:, :128]
        for j in range(1, width // 128):
            t = jnp.maximum(t, s[:, j * 128:(j + 1) * 128])
        return jnp.max(t, axis=1, keepdims=True)

    def lanesum(p, width):
        t = p[:, :128]
        for j in range(1, width // 128):
            t = t + p[:, j * 128:(j + 1) * 128]
        return t

    def masked(s, offset, width, causal):
        key = lax.broadcasted_iota(jnp.int32, (tok, width), 1) + offset
        ok = key >= start
        if causal:
            ok = ok & (key <= row)
        return jnp.where(ok[None], s.reshape(GROUP, tok, width), -1e30).reshape(GROUP * tok, width)

    own = pl.multiple_of(first + 2 * half, tok)
    s = masked(scores(own, tok), own, tok, True)
    m = rowmax(s, tok)
    p = jnp.exp2((s - m) * EXP2_SCALE)
    m_scr[...] = jnp.broadcast_to(m, m_scr.shape)
    l_scr[...] = lanesum(p, tok)
    acc_scr[...] = jnp.dot(p.astype(jnp.bfloat16), values(own, tok), preferred_element_type=jnp.float32)

    def step(i, mask):
        offset = pl.multiple_of(first + i * span, tok)
        s = scores(offset, span)
        if mask:
            s = masked(s, offset, span, False)
        old = m_scr[...]
        new = jnp.maximum(old, rowmax(s, span))
        m_scr[...] = new
        shrink = jnp.exp2((old - new) * EXP2_SCALE)
        p = jnp.exp2((s - jnp.concatenate([new] * (span // 128), 1)) * EXP2_SCALE)
        l_scr[...] = l_scr[...] * shrink + lanesum(p, span)
        acc_scr[...] = acc_scr[...] * shrink + jnp.dot(p.astype(jnp.bfloat16), values(offset, span), preferred_element_type=jnp.float32)

    steps = 2 * half // span

    def loop(i, carry):
        whole = start_max <= first + i * span

        @pl.when(whole)
        def _():
            step(i, False)

        @pl.when(jnp.logical_not(whole))
        def _():
            step(i, True)

        return carry

    lax.fori_loop(jnp.clip(lax.div(start_min - first, span), 0, steps), steps, loop, 0)

    total = jnp.sum(l_scr[...], axis=1, keepdims=True)
    att = (acc_scr[...] / total).astype(jnp.bfloat16)
    for g in range(GROUP):
        out_ref[:, g * HD:(g + 1) * HD] = att[g * tok:(g + 1) * tok]


def attend(info, queries, pieces, layout, moves, part, heads, offset, span=512):
    tok = queries.shape[0]
    wide = GROUP * HD
    n = len(moves)
    hbm = pl.BlockSpec(memory_space=pl.ANY)
    scratch = pltpu.VMEM((GROUP * tok, 128), jnp.float32)
    return pl.pallas_call(
        functools.partial(attend_kernel, tok=tok, span=span, moves=moves, heads=heads, layout=layout, part=part),
        grid_spec=pltpu.PrefetchScalarGridSpec(
            num_scalar_prefetch=1,
            grid=(heads,),
            in_specs=[pl.BlockSpec((tok, wide), lambda c, s: (0, c + (s[2] * heads if offset else 0)))] + [hbm] * len(pieces),
            out_specs=pl.BlockSpec((tok, wide), lambda c, s: (0, c)),
            scratch_shapes=[
                pltpu.VMEM((4 * n * tok, 2 * heads * HD), jnp.bfloat16),
                pltpu.VMEM((2 * n, 16, 2 * heads * HD), jnp.bfloat16),
                pltpu.VMEM((tok, 1), jnp.int32),
                scratch, scratch, scratch,
                pltpu.SMEM((2,), jnp.int32),
                pltpu.SemaphoreType.DMA((2 * n, 3)),
            ],
        ),
        out_shape=jax.ShapeDtypeStruct((tok, heads * wide), jnp.bfloat16),
        compiler_params=pltpu.CompilerParams(vmem_limit_bytes=60 << 20),
        cost_estimate=pl.CostEstimate(flops=8 * 10**9, bytes_accessed=5 << 20, transcendentals=4 * 10**6),
        name="attend",
    )(info, queries, *pieces)


def prepare_kernel(info_ref, kv_ref, doc_ref, q_ref, send_ref, mine_ref, qout_ref):
    tok = kv_ref.shape[0]
    w = kv_ref.shape[1] // 4
    q = q_ref.shape[1] // 2
    send_ref[tok:, :] = jnp.zeros((16, 2 * w), send_ref.dtype)
    send_ref[tok:tok + 16, :tok] = jnp.broadcast_to((doc_ref[...] + 1).astype(jnp.float32), (16, tok)).astype(send_ref.dtype)
    for yhi in range(2):
        @pl.when(info_ref[2] == yhi)
        def _(yhi=yhi):
            away = 1 - yhi
            mine_ref[:, :w] = kv_ref[:, yhi * w:(yhi + 1) * w]
            mine_ref[:, w:] = kv_ref[:, (2 + yhi) * w:(3 + yhi) * w]
            send_ref[:tok, :w] = kv_ref[:, away * w:(away + 1) * w]
            send_ref[:tok, w:] = kv_ref[:, (2 + away) * w:(3 + away) * w]
            qout_ref[...] = q_ref[:, away * q:(away + 1) * q]


def prepare(info, keys_values, doc_ids, queries):
    tok, width = keys_values.shape
    vm = pl.BlockSpec(memory_space=pltpu.VMEM)
    shape = lambda r, c: jax.ShapeDtypeStruct((r, c), jnp.bfloat16)
    return pl.pallas_call(
        prepare_kernel,
        in_specs=[pl.BlockSpec(memory_space=pltpu.SMEM)] + [vm] * 3,
        out_specs=[vm] * 3,
        out_shape=[shape(tok + 16, width // 2), shape(tok, width // 2), shape(tok, queries.shape[1] // 2)],
        compiler_params=pltpu.CompilerParams(vmem_limit_bytes=60 << 20),
        name="prepare",
    )(info, keys_values, doc_ids[None], queries)


def join_kernel(send_ref, mine_ref, other_ref, unit_ref):
    tok = mine_ref.shape[0]
    unit_ref[:tok] = mine_ref[...]
    unit_ref[tok:2 * tok] = other_ref[:tok]
    unit_ref[2 * tok:] = send_ref[tok:]
    unit_ref[2 * tok:, tok:2 * tok] = other_ref[tok:, :tok]


def join(send, mine, other):
    tok, width = mine.shape
    vm = pl.BlockSpec(memory_space=pltpu.VMEM)
    return pl.pallas_call(
        join_kernel,
        in_specs=[vm] * 3,
        out_specs=vm,
        out_shape=jax.ShapeDtypeStruct((2 * tok + 16, width), mine.dtype),
        compiler_params=pltpu.CompilerParams(vmem_limit_bytes=60 << 20),
        name="join",
    )(send, mine, other)


def pack_kernel(info_ref, gu_ref, down_ref, out_ref, sem):
    away = 1 - info_ref[2]
    units = out_ref.shape[1]
    at = pl.ds(pl.multiple_of(info_ref[3] * units, units), units)
    one = pltpu.make_async_copy(gu_ref.at[away, :, at], out_ref.at[pl.ds(0, 2)], sem.at[0])
    two = pltpu.make_async_copy(down_ref.at[away, at], out_ref.at[2], sem.at[1])
    one.start()
    two.start()
    one.wait()
    two.wait()


def pack(info, wide_t, down, cores):
    hbm = pl.BlockSpec(memory_space=pl.ANY)
    return pl.pallas_call(
        pack_kernel,
        in_specs=[pl.BlockSpec(memory_space=pltpu.SMEM), hbm, hbm],
        out_specs=hbm,
        out_shape=jax.ShapeDtypeStruct((3, down.shape[1] // cores, down.shape[2]), down.dtype),
        scratch_shapes=[pltpu.SemaphoreType.DMA((2,))],
        name="pack",
    )(info, wide_t, down)


def norm_kernel(info_ref, hid_ref, mine_ref, other_ref, gain_ref, place_ref, stream_ref, panel_ref, att):
    wide = mine_ref.shape[1]
    near = info_ref[2]

    @pl.when(near == 0)
    def _():
        att[:, :wide] = mine_ref[...]
        att[:, wide:] = other_ref[...]

    @pl.when(near != 0)
    def _():
        att[:, :wide] = other_ref[...]
        att[:, wide:] = mine_ref[...]

    stream = (hid_ref[...].astype(jnp.float32) + att[...].astype(jnp.float32)).astype(jnp.bfloat16)
    stream_ref[...] = stream
    sf = stream.astype(jnp.float32)
    inv = lax.rsqrt(jnp.mean(sf * sf, axis=1, keepdims=True) + 1e-6)
    normed = (sf * inv * gain_ref[...].astype(jnp.float32)).astype(jnp.bfloat16)
    rows = panel_ref.shape[1]
    for n in range(panel_ref.shape[0]):
        panel_ref[n] = jnp.dot(place_ref[n * rows:(n + 1) * rows], normed, preferred_element_type=jnp.float32).astype(jnp.bfloat16)


def norm_panels(info, hidden, mine, other, gain, place):
    tok, d = hidden.shape
    rows = place.shape[0] // EXP_FLIGHT
    vm = pl.BlockSpec(memory_space=pltpu.VMEM)
    return pl.pallas_call(
        norm_kernel,
        in_specs=[pl.BlockSpec(memory_space=pltpu.SMEM)] + [vm] * 5,
        out_specs=[vm, vm],
        out_shape=[jax.ShapeDtypeStruct((tok, d), jnp.bfloat16), jax.ShapeDtypeStruct((EXP_FLIGHT, rows, d), jnp.bfloat16)],
        scratch_shapes=[pltpu.VMEM((tok, d), jnp.bfloat16)],
        compiler_params=pltpu.CompilerParams(vmem_limit_bytes=60 << 20),
        name="norm_panels",
    )(info, hidden, mine, other, gain, place)


def expert_kernel(info_ref, *refs, count, rows, after):
    xs = refs[:count]
    wo_ref, do_ref, r1_ref, r2_ref = refs[count:count + 4]
    refs = refs[count + 4 + after:]
    ys = refs[:count]
    x, wg, wu, wd, sem = refs[count:]
    yhi = info_ref[2]
    n = wo_ref.shape[2]
    h = r1_ref.shape[1]
    cps = []

    def cp(src, dst):
        c = pltpu.make_async_copy(src, dst, sem.at[len(cps)])
        c.start()
        cps.append(c)

    for i in range(count):
        cp(xs[i], x.at[pl.ds(i * rows, rows)])
    for i, w in enumerate((wg, wu, wd)):
        cp(do_ref.at[yhi] if i == 2 else wo_ref.at[yhi, i], w.at[pl.ds(0, n)])
        cp(r1_ref.at[i], w.at[pl.ds(n, h)])
        cp(r2_ref.at[i], w.at[pl.ds(n + h, h)])
    nt = (((1,), (1,)), ((), ()))
    for c in cps[:count + 3]:
        c.wait()
    xv = x[...]
    gate = lax.dot_general(xv, wg[...], nt, preferred_element_type=jnp.float32)
    for c in cps[count + 3:count + 6]:
        c.wait()
    up = lax.dot_general(xv, wu[...], nt, preferred_element_type=jnp.float32)
    inner = (gate / (1 + jnp.exp(-gate)) * up).astype(jnp.bfloat16)
    for c in cps[count + 6:]:
        c.wait()
    y = jnp.dot(inner, wd[...], preferred_element_type=jnp.float32).astype(jnp.bfloat16)
    for i in range(count):
        ys[i][...] = y[i * rows:(i + 1) * rows]


def experts(info, xs, wo, do, r1, r2, after=()):
    count = len(xs)
    rows, d = xs[0].shape
    n = wo.shape[2] + r1.shape[1] + r2.shape[1]
    hbm = pl.BlockSpec(memory_space=pl.ANY)
    vm = pl.BlockSpec(memory_space=pltpu.VMEM)
    weight = pltpu.VMEM((n, d), jnp.bfloat16)
    return pl.pallas_call(
        functools.partial(expert_kernel, count=count, rows=rows, after=len(after)),
        in_specs=[pl.BlockSpec(memory_space=pltpu.SMEM)] + [hbm] * (count + 4 + len(after)),
        out_specs=[vm] * count,
        scratch_shapes=[pltpu.VMEM((count * rows, d), jnp.bfloat16), weight, weight, weight, pltpu.SemaphoreType.DMA((count + 9,))],
        out_shape=[jax.ShapeDtypeStruct((rows, d), jnp.bfloat16)] * count,
        compiler_params=pltpu.CompilerParams(vmem_limit_bytes=60 << 20),
        cost_estimate=pl.CostEstimate(flops=20 * count * rows * n * d, bytes_accessed=2 * (3 * n * d + 2 * count * rows * d), transcendentals=count * rows * n),
        name="experts",
    )(info, *xs, wo, do, r1, r2, *after)


def combine_kernel(stream_ref, a1_ref, a2_ref, a3_ref, back_ref, hot1_ref, hot2_ref, w1_ref, w2_ref, out_ref):
    keep = a1_ref[...].astype(jnp.float32) + a2_ref[...].astype(jnp.float32) + a3_ref[...].astype(jnp.float32)
    one = jnp.dot(hot1_ref[...], keep.astype(jnp.bfloat16), preferred_element_type=jnp.float32)
    two = jnp.dot(hot2_ref[...], back_ref[...], preferred_element_type=jnp.float32)
    total = stream_ref[...].astype(jnp.float32) + one * w1_ref[...] + two * w2_ref[...]
    out_ref[...] = total.astype(out_ref.dtype)


def combine(stream, parts, back, hot1, hot2, w1, w2):
    tok, d = stream.shape
    cap = back.shape[0]
    wide = d // 4
    cols = lambda rows: pl.BlockSpec((rows, wide), lambda c: (0, c))
    whole = lambda shape: pl.BlockSpec(shape, lambda c: (0, 0))
    return pl.pallas_call(
        combine_kernel,
        grid=(4,),
        in_specs=[cols(tok)] + [cols(cap)] * 4 + [whole((tok, cap))] * 2 + [whole((tok, 1))] * 2,
        out_specs=cols(tok),
        out_shape=jax.ShapeDtypeStruct((tok, d), stream.dtype),
        compiler_params=pltpu.CompilerParams(vmem_limit_bytes=60 << 20),
        name="combine",
    )(stream, *parts, back, hot1, hot2, w1, w2)


def shift(value, axis, size, steps):
    return lax.ppermute(value, axis, [(i, (i + steps) % size) for i in range(size)])


def swap(value, axis):
    return shift(value, axis, 2, 1)


def routing(route_ids, route_weights, flight, capacity):
    chosen = route_ids == flight
    routed = jnp.any(chosen, axis=1)
    weight = jnp.sum(jnp.where(chosen, route_weights, 0.0), axis=1)
    slot_of = jnp.cumsum(routed.astype(jnp.int32)) - 1
    slots = jnp.arange(capacity, dtype=jnp.int32)
    hot = (slot_of[:, None] == slots[None, :]) & routed[:, None]
    return hot.astype(jnp.bfloat16), jnp.where(routed, weight, 0.0)[:, None]


def ring_moves(size):
    out = [0]
    for s in range(1, size // 2 + 1):
        out.append(-s)
        if 2 * s < size:
            out.append(s)
    return out


def ring_gather(parts, signs, size):
    got = [{0: x} for x in parts]
    for s in range(1, size // 2 + 1):
        for g, sign in zip(got, signs):
            g[-s * sign] = shift(g[(1 - s) * sign], "z", size, sign)
            if 2 * s < size:
                g[s * sign] = shift(g[(s - 1) * sign], "z", size, -sign)
    return got


def ring_scatter(parts, signs, size):
    reach = size // 2
    ups = [p[-reach * sign] for p, sign in zip(parts, signs)]
    downs = [p[(1 - reach) * sign] for p, sign in zip(parts, signs)]
    for s in range(1, reach + 1):
        for i, (p, sign) in enumerate(zip(parts, signs)):
            ups[i] = shift(ups[i], "z", size, sign)
            if s < reach:
                ups[i] = ups[i] + p[(reach - s) * sign]
                downs[i] = shift(downs[i], "z", size, -sign)
            if s < reach - 1:
                downs[i] = downs[i] + p[(1 - reach + s) * sign]
    return [(ups[i], downs[i], p[0]) for i, p in enumerate(parts)]


def body(sizes, hidden_in, queries, keys_values, doc_ids, route_ids, route_weights, norm_gain, gate_up, down):
    tok, d = queries.shape
    capacity = tok // 4
    n_z, n_core, n_cx = sizes["z"], sizes["core"], sizes["cx"]
    yhi, z, core = lax.axis_index("yhi"), lax.axis_index("z"), lax.axis_index("core")
    half = n_z * tok
    n_ctx = n_cx * n_core
    moves = ring_moves(n_z)
    heads = keys_values.shape[1] // (4 * HD)
    info = jnp.stack([z, yhi * half, yhi, core]).astype(jnp.int32)

    send, mine, q_out = prepare(info, keys_values, doc_ids, queries)
    other = swap(send, "yhi")
    unit = join(send, mine, other)

    q_out, unit = lax.optimization_barrier((q_out, unit))
    other_q = swap(q_out, "yhi")
    wide_t = jnp.swapaxes(gate_up, 2, 3)
    theirs, other_q = lax.optimization_barrier((pack(info, wide_t, down, n_core), other_q))
    got_1 = swap(theirs, "yhi")
    got_2 = swap(got_1, "core")

    own = ring_gather([unit], [1], n_z)[0]
    own = [own[m] for m in moves]
    ahead = [(i, i + 1) for i in range(n_ctx - 1)]
    groups = [range(0, 1), range(1, n_z // 2 + 1), range(n_z // 2 + 1, n_z - 1), range(n_z - 1, n_z)]
    prior, layout = [], []
    for n, group in enumerate(groups):
        block = jnp.concatenate([own[i] for i in group], 0) if len(group) > 1 else own[group[0]]
        prior.append(lax.ppermute(block, ("cx", "core"), ahead))
        layout += [(n, k * unit.shape[0]) for k in range(len(group))]
    layout += [(len(groups) + i, 0) for i in range(n_z)]
    pieces = prior + own

    hot_1, w_1 = routing(route_ids, route_weights, yhi, capacity)
    hot_2, w_2 = routing(route_ids, route_weights, 1 - yhi, capacity)
    place = jnp.concatenate([hot_1, hot_2], 1).T

    theirs_att = attend(info, other_q, pieces, layout, moves, 1, heads, False)
    other_att = swap(theirs_att, "yhi")
    queries, got_1, _ = lax.optimization_barrier((queries, got_1, theirs_att))
    mine_att = attend(info, queries, pieces, layout, moves, 0, heads, True)
    stream, panels = norm_panels(info, hidden_in, mine_att, other_att, norm_gain[None], place)

    keep, back_way = panels[0], panels[1]
    signs = [1, -1]
    rows = ring_gather([keep, swap(back_way, "yhi")], signs, n_z)
    last = [-n_z // 2 * sign for sign in signs]
    early = [[m for m in r if m != l] for r, l in zip(rows, last)]
    args = (wide_t, down, got_1, got_2)
    keys = [(i, m) for i in range(2) for m in early[i]]
    first_out = experts(info, [rows[i][m] for i, m in keys], *args)
    last_out = experts(info, [rows[i][last[i]] for i in range(2)], *args, after=first_out[:1])
    outs = [{last[i]: last_out[i]} for i in range(2)]
    for (i, m), y in zip(keys, first_out):
        outs[i][m] = y
    sum_b, sum_a = ring_scatter([outs[1], outs[0]], signs[::-1], n_z)
    back = swap(sum_b[0] + sum_b[1] + sum_b[2], "yhi")
    return combine(stream, sum_a, back, hot_1, hot_2, w_1, w_2)


def solution(mesh):
    sizes = {"cx": mesh.shape["ctx"] // 2, "core": 2, "yhi": 2, "z": mesh.shape["exp"] // 2, "dp": mesh.shape["dp"]}
    fine = Mesh(mesh.devices.reshape(tuple(sizes.values())), tuple(sizes))
    tokens = ("dp", "cx", "core", "yhi", "z")
    rows = P(tokens, None)
    hidden = ("yhi", "z")
    in_specs = (rows, rows, rows, P(tokens), rows, rows, P(), P(None, None, None, hidden), P(None, hidden, None))
    return jax.shard_map(
        functools.partial(body, sizes), mesh=fine, in_specs=in_specs, out_specs=rows, check_vma=False
    )
```

```python
import functools
import math

import jax
import jax.numpy as jnp
from jax import lax
from jax.experimental import pallas as pl
from jax.experimental.pallas import tpu as pltpu
from jax.sharding import Mesh
from jax.sharding import PartitionSpec as P

EXP_FLIGHT = 2
HD = 128
GROUP = 7
EXP2_SCALE = math.log2(math.e) / math.sqrt(HD)

def attend_kernel(info_ref, q_ref, place_ref, *refs, tok, span, moves, heads, layout, part):
    arrays, out_ref, low_ref, high_ref = refs[:-11], refs[-11], refs[-10], refs[-9]
    kv, ids, start_scr, m_scr, l_scr, acc_scr, bounds, sem = refs[-8:]
    c = pl.program_id(0)
    z = info_ref[0]
    half = len(moves) * tok
    near = pl.multiple_of(info_ref[1], half)
    far = pl.multiple_of(half - info_ref[1], half)
    first = pl.multiple_of((far if part else near) + z * tok, tok)

    @pl.when(c == 0)
    def _():
        blocks = []
        copies = []
        for n, (which, row) in enumerate(layout):
            piece = arrays[which]
            place = lax.rem(z + moves[n % len(moves)] + len(moves), len(moves)) * tok
            slab = n // len(moves) * 2 * half
            for side, base in ((0, near), (1, far)):
                at = pl.multiple_of(slab + base + place, tok)
                cp = pltpu.make_async_copy(piece.at[pl.ds(row + side * tok, tok)], kv.at[pl.ds(at, tok)], sem.at[n, side])
                blocks.append((cp, (at >= first) & (at <= first + 2 * half)))
            copies.append(pltpu.make_async_copy(piece.at[pl.ds(row + 2 * tok, 16)], ids.at[n], sem.at[n, 2]))
        for cp in copies:
            cp.start()
        for cp, needed in blocks:
            pl.when(needed)(cp.start)
        for cp in copies:
            cp.wait()
        own = ids[len(moves), 0:1, part * tok:(part + 1) * tok].astype(jnp.float32)
        own = jnp.broadcast_to(own, (tok, tok)).T
        less = jnp.zeros((tok, tok), jnp.float32)
        for n in range(len(layout)):
            for side in range(2):
                row = ids[n, 0:1, side * tok:(side + 1) * tok].astype(jnp.float32)
                less = less + jnp.where(row < own, 1.0, 0.0)
        begin = jnp.sum(less, axis=1, keepdims=True)
        start_scr[...] = begin.astype(jnp.int32)
        bounds[0] = jnp.min(begin).astype(jnp.int32)
        bounds[1] = jnp.max(begin).astype(jnp.int32)
        for cp, needed in blocks:
            pl.when(needed)(cp.wait)

    start_min, start_max = bounds[0], bounds[1]
    q = jnp.concatenate([q_ref[:, g * HD:(g + 1) * HD] for g in range(GROUP)], 0)
    start = start_scr[...]
    row = lax.broadcasted_iota(jnp.int32, (tok, 1), 0) + first + 2 * half
    key_col = pl.multiple_of(c * HD, HD)
    value_col = pl.multiple_of((heads + c) * HD, HD)

    def keys(offset, width):
        return kv[pl.ds(offset, width), pl.ds(key_col, HD)]

    def values(offset, width):
        return kv[pl.ds(offset, width), pl.ds(value_col, HD)]

    def scores(offset, width):
        return lax.dot_general(q, keys(offset, width), (((1,), (1,)), ((), ())), preferred_element_type=jnp.float32)

    def rowmax(s, width):
        t = s[:, :128]
        for j in range(1, width // 128):
            t = jnp.maximum(t, s[:, j * 128:(j + 1) * 128])
        return jnp.max(t, axis=1, keepdims=True)

    def lanesum(p, width):
        t = p[:, :128]
        for j in range(1, width // 128):
            t = t + p[:, j * 128:(j + 1) * 128]
        return t

    def masked(s, offset, width, causal):
        key = lax.broadcasted_iota(jnp.int32, (tok, width), 1) + offset
        ok = key >= start
        if causal:
            ok = ok & (key <= row)
        return jnp.where(ok[None], s.reshape(GROUP, tok, width), -1e30).reshape(GROUP * tok, width)

    own = pl.multiple_of(first + 2 * half, tok)
    s = masked(scores(own, tok), own, tok, True)
    m = rowmax(s, tok)
    p = jnp.exp2((s - m) * EXP2_SCALE)
    m_scr[...] = jnp.broadcast_to(m, m_scr.shape)
    l_scr[...] = lanesum(p, tok)
    acc_scr[...] = jnp.dot(p.astype(jnp.bfloat16), values(own, tok), preferred_element_type=jnp.float32)

    def step(i, mask):
        offset = pl.multiple_of(first + i * span, tok)
        s = scores(offset, span)
        if mask:
            s = masked(s, offset, span, False)
        old = m_scr[...]
        new = jnp.maximum(old, rowmax(s, span))
        m_scr[...] = new
        shrink = jnp.exp2((old - new) * EXP2_SCALE)
        p = jnp.exp2((s - jnp.concatenate([new] * (span // 128), 1)) * EXP2_SCALE)
        l_scr[...] = l_scr[...] * shrink + lanesum(p, span)
        acc_scr[...] = acc_scr[...] * shrink + jnp.dot(p.astype(jnp.bfloat16), values(offset, span), preferred_element_type=jnp.float32)

    steps = 2 * half // span

    def loop(i, carry):
        whole = start_max <= first + i * span

        @pl.when(whole)
        def _():
            step(i, False)

        @pl.when(jnp.logical_not(whole))
        def _():
            step(i, True)

        return carry

    lax.fori_loop(jnp.clip(lax.div(start_min - first, span), 0, steps), steps, loop, 0)

    total = jnp.sum(l_scr[...], axis=1, keepdims=True)
    att = (acc_scr[...] / total).astype(jnp.bfloat16)
    att = jnp.concatenate([att[g * tok:(g + 1) * tok] for g in range(GROUP)], 1)
    out_ref[...] = att
    rows = jnp.dot(place_ref[...], att, preferred_element_type=jnp.float32).astype(jnp.bfloat16)
    low_ref[...] = rows[:rows.shape[0] // 2]
    high_ref[...] = rows[rows.shape[0] // 2:]


def attend(info, queries, place, pieces, layout, moves, part, heads, tok, span=512):
    slots = tok // 4
    wide = GROUP * HD
    n = len(moves)
    hbm = pl.BlockSpec(memory_space=pl.ANY)
    scratch = pltpu.VMEM((GROUP * tok, 128), jnp.float32)
    return pl.pallas_call(
        functools.partial(attend_kernel, tok=tok, span=span, moves=moves, heads=heads, layout=layout, part=part),
        grid_spec=pltpu.PrefetchScalarGridSpec(
            num_scalar_prefetch=1,
            grid=(heads,),
            in_specs=[
                pl.BlockSpec((tok, wide), lambda c, s: (0, c + (0 if part else s[2] * heads))),
                pl.BlockSpec((2 * slots, tok), lambda c, s: (tok // (2 * slots), heads * GROUP) if part else (0, 0)),
            ] + [hbm] * len(pieces),
            out_specs=[pl.BlockSpec((r, wide), lambda c, s: (0, c)) for r in (tok, slots, slots)],
            scratch_shapes=[
                pltpu.VMEM((4 * n * tok, 2 * heads * HD), jnp.bfloat16),
                pltpu.VMEM((2 * n, 16, 2 * heads * HD), jnp.bfloat16),
                pltpu.VMEM((tok, 1), jnp.int32),
                scratch, scratch, scratch,
                pltpu.SMEM((2,), jnp.int32),
                pltpu.SemaphoreType.DMA((2 * n, 3)),
            ],
        ),
        out_shape=[jax.ShapeDtypeStruct((r, heads * wide), jnp.bfloat16) for r in (tok, slots, slots)],
        compiler_params=pltpu.CompilerParams(vmem_limit_bytes=60 << 20),
        cost_estimate=pl.CostEstimate(flops=8 * 10**9, bytes_accessed=5 << 20, transcendentals=4 * 10**6),
        name="attend",
    )(info, queries, place, *pieces)


def prepare_kernel(info_ref, kv_ref, doc_ref, send_ref, mine_ref):
    tok = kv_ref.shape[0]
    w = kv_ref.shape[1] // 4
    send_ref[tok:, :] = jnp.zeros((16, 2 * w), send_ref.dtype)
    send_ref[tok:tok + 16, :tok] = jnp.broadcast_to((doc_ref[...] + 1).astype(jnp.float32), (16, tok)).astype(send_ref.dtype)
    for yhi in range(2):
        @pl.when(info_ref[2] == yhi)
        def _(yhi=yhi):
            away = 1 - yhi
            mine_ref[:, :w] = kv_ref[:, yhi * w:(yhi + 1) * w]
            mine_ref[:, w:] = kv_ref[:, (2 + yhi) * w:(3 + yhi) * w]
            send_ref[:tok, :w] = kv_ref[:, away * w:(away + 1) * w]
            send_ref[:tok, w:] = kv_ref[:, (2 + away) * w:(3 + away) * w]


def prepare(info, keys_values, doc_ids):
    tok, width = keys_values.shape
    vm = pl.BlockSpec(memory_space=pltpu.VMEM)
    shape = lambda r, c: jax.ShapeDtypeStruct((r, c), jnp.bfloat16)
    return pl.pallas_call(
        prepare_kernel,
        in_specs=[pl.BlockSpec(memory_space=pltpu.SMEM)] + [vm] * 2,
        out_specs=[vm] * 2,
        out_shape=[shape(tok + 16, width // 2), shape(tok, width // 2)],
        compiler_params=pltpu.CompilerParams(vmem_limit_bytes=60 << 20),
        name="prepare",
    )(info, keys_values, doc_ids[None])


def plan_kernel(info_ref, ids_ref, weights_ref, q_ref, hid_ref, out_ref, place_ref, hot_ref, factor_ref, base_ref):
    tok = hid_ref.shape[0]
    slots = place_ref.shape[0] // 2
    q = q_ref.shape[1] // 2
    yhi = info_ref[2]
    below = lax.broadcasted_iota(jnp.int32, (tok, tok), 0) <= lax.broadcasted_iota(jnp.int32, (tok, tok), 1)
    below = below.astype(jnp.float32).astype(jnp.bfloat16)
    places, factors = [], []
    for flight in (yhi, 1 - yhi):
        chosen = ids_ref[...] == flight
        routed = jnp.max(jnp.where(chosen, 1.0, 0.0), axis=0, keepdims=True)
        factors.append(jnp.sum(jnp.where(chosen, weights_ref[...], 0.0), axis=0, keepdims=True))
        ranks = jnp.dot(jnp.broadcast_to(routed, (16, tok)).astype(jnp.bfloat16), below, preferred_element_type=jnp.float32)
        ranks = jnp.where(routed > 0.5, ranks[:1] - 1.0, -1.0)
        slot = lax.broadcasted_iota(jnp.int32, (slots, tok), 0).astype(jnp.float32)
        places.append(jnp.where(slot == ranks, 1.0, 0.0))
    place_f = jnp.concatenate(places, 0)
    place = place_f.astype(jnp.bfloat16)
    place_ref[...] = place
    hot_ref[...] = jnp.concatenate([place_f, jnp.zeros((tok - 2 * slots, tok), jnp.float32)], 0).T.astype(jnp.bfloat16)
    factor_ref[...] = jnp.concatenate([factors[0], factors[1], jnp.zeros((tok - 2, tok), jnp.float32)], 0).T
    rows = jnp.dot(place, hid_ref[...], preferred_element_type=jnp.float32).astype(jnp.bfloat16)
    base_ref[:slots] = rows[:slots, :q]
    base_ref[slots:] = rows[:slots, q:]
    out_ref[:tok, q:] = jnp.zeros((tok, tok), jnp.bfloat16)
    out_ref[tok:tok + slots, :q] = rows[slots:, :q]
    out_ref[tok + slots:, :q] = rows[slots:, q:]
    out_ref[tok:, q:] = place

    @pl.when(yhi == 0)
    def _():
        out_ref[:tok, :q] = q_ref[:, q:]

    @pl.when(yhi != 0)
    def _():
        out_ref[:tok, :q] = q_ref[:, :q]


def plan(info, route_ids, route_weights, queries, hidden):
    tok, d = hidden.shape
    slots = tok // 4
    vm = pl.BlockSpec(memory_space=pltpu.VMEM)
    shape = lambda r, c, t=jnp.bfloat16: jax.ShapeDtypeStruct((r, c), t)
    return pl.pallas_call(
        plan_kernel,
        in_specs=[pl.BlockSpec(memory_space=pltpu.SMEM)] + [vm] * 4,
        out_specs=[vm] * 5,
        out_shape=[
            shape(tok + 2 * slots, d // 2 + tok), shape(2 * slots, tok), shape(tok, tok), shape(tok, tok, jnp.float32), shape(2 * slots, d // 2),
        ],
        compiler_params=pltpu.CompilerParams(vmem_limit_bytes=60 << 20),
        name="plan",
    )(info, route_ids.T, route_weights.T, queries, hidden)


def join_kernel(send_ref, mine_ref, other_ref, unit_ref):
    tok = mine_ref.shape[0]
    unit_ref[:tok] = mine_ref[...]
    unit_ref[tok:2 * tok] = other_ref[:tok]
    unit_ref[2 * tok:] = send_ref[tok:]
    unit_ref[2 * tok:, tok:2 * tok] = other_ref[tok:, :tok]


def join(send, mine, other):
    tok, width = mine.shape
    vm = pl.BlockSpec(memory_space=pltpu.VMEM)
    return pl.pallas_call(
        join_kernel,
        in_specs=[vm] * 3,
        out_specs=vm,
        out_shape=jax.ShapeDtypeStruct((2 * tok + 16, width), mine.dtype),
        compiler_params=pltpu.CompilerParams(vmem_limit_bytes=60 << 20),
        name="join",
    )(send, mine, other)


def pack_kernel(info_ref, gu_ref, down_ref, out_ref, sem):
    away = 1 - info_ref[2]
    units = out_ref.shape[1]
    at = pl.ds(pl.multiple_of(info_ref[3] * units, units), units)
    one = pltpu.make_async_copy(gu_ref.at[away, :, at], out_ref.at[pl.ds(0, 2)], sem.at[0])
    two = pltpu.make_async_copy(down_ref.at[away, at], out_ref.at[2], sem.at[1])
    one.start()
    two.start()
    one.wait()
    two.wait()


def pack(info, wide_t, down, cores):
    hbm = pl.BlockSpec(memory_space=pl.ANY)
    return pl.pallas_call(
        pack_kernel,
        in_specs=[pl.BlockSpec(memory_space=pltpu.SMEM), hbm, hbm],
        out_specs=pl.BlockSpec(memory_space=pltpu.VMEM),
        out_shape=jax.ShapeDtypeStruct((3, down.shape[1] // cores, down.shape[2]), down.dtype),
        scratch_shapes=[pltpu.SemaphoreType.DMA((2,))],
        compiler_params=pltpu.CompilerParams(vmem_limit_bytes=60 << 20),
        name="pack",
    )(info, wide_t, down)


def norm_kernel(info_ref, base_ref, mine_ref, other_ref, gain_ref, out_ref):
    slots, half = mine_ref.shape

    def put(low, high):
        parts = []
        for n, att in enumerate((low, high)):
            base = base_ref[n * slots:(n + 1) * slots].astype(jnp.float32)
            parts.append((base + att.astype(jnp.float32)).astype(jnp.bfloat16).astype(jnp.float32))
        total = sum(jnp.sum(p * p, axis=1, keepdims=True) for p in parts)
        inv = lax.rsqrt(total / (2 * half) + 1e-6)
        for n, p in enumerate(parts):
            gain = gain_ref[:, n * half:(n + 1) * half].astype(jnp.float32)
            out_ref[:, n * half:(n + 1) * half] = (p * inv * gain).astype(jnp.bfloat16)

    @pl.when(info_ref[2] == 0)
    def _():
        put(mine_ref[...], other_ref[...])

    @pl.when(info_ref[2] != 0)
    def _():
        put(other_ref[...], mine_ref[...])


def norm_rows(info, base, row, mine, other, gain):
    slots, half = mine.shape
    whole = lambda x: pl.BlockSpec(x.shape, lambda i, s: (0, 0))
    return pl.pallas_call(
        norm_kernel,
        grid_spec=pltpu.PrefetchScalarGridSpec(
            num_scalar_prefetch=1,
            grid=(1,),
            in_specs=[pl.BlockSpec((2 * slots, half), lambda i, s: (row, 0)), whole(mine), whole(other), whole(gain)],
            out_specs=pl.BlockSpec((slots, 2 * half), lambda i, s: (0, 0)),
        ),
        out_shape=jax.ShapeDtypeStruct((slots, 2 * half), jnp.bfloat16),
        compiler_params=pltpu.CompilerParams(vmem_limit_bytes=60 << 20),
        name="norm_rows",
    )(info, base, mine, other, gain)


def expert_kernel(info_ref, *refs, count, rows, after):
    xs = refs[:count]
    wo_ref, do_ref, r1_ref, r2_ref = refs[count:count + 4]
    refs = refs[count + 4 + after:]
    ys = refs[:count]
    x, wg, wu, wd, sem = refs[count:]
    yhi = info_ref[2]
    n = wo_ref.shape[2]
    h = r1_ref.shape[1]
    cps = []

    def cp(src, dst):
        c = pltpu.make_async_copy(src, dst, sem.at[len(cps)])
        c.start()
        cps.append(c)

    for i in range(count):
        cp(xs[i], x.at[pl.ds(i * rows, rows)])
    for i, w in enumerate((wg, wu, wd)):
        cp(do_ref.at[yhi] if i == 2 else wo_ref.at[yhi, i], w.at[pl.ds(0, n)])
        cp(r1_ref.at[i], w.at[pl.ds(n, h)])
        cp(r2_ref.at[i], w.at[pl.ds(n + h, h)])
    nt = (((1,), (1,)), ((), ()))
    for c in cps[:count + 3]:
        c.wait()
    xv = x[...]
    gate = lax.dot_general(xv, wg[...], nt, preferred_element_type=jnp.float32)
    for c in cps[count + 3:count + 6]:
        c.wait()
    up = lax.dot_general(xv, wu[...], nt, preferred_element_type=jnp.float32)
    inner = (gate / (1 + jnp.exp(-gate)) * up).astype(jnp.bfloat16)
    for c in cps[count + 6:]:
        c.wait()
    y = jnp.dot(inner, wd[...], preferred_element_type=jnp.float32).astype(jnp.bfloat16)
    for i in range(count):
        ys[i][...] = y[i * rows:(i + 1) * rows]


def experts(info, xs, wo, do, r1, r2, after=()):
    count = len(xs)
    rows, d = xs[0].shape
    n = wo.shape[2] + r1.shape[1] + r2.shape[1]
    hbm = pl.BlockSpec(memory_space=pl.ANY)
    vm = pl.BlockSpec(memory_space=pltpu.VMEM)
    weight = pltpu.VMEM((n, d), jnp.bfloat16)
    return pl.pallas_call(
        functools.partial(expert_kernel, count=count, rows=rows, after=len(after)),
        in_specs=[pl.BlockSpec(memory_space=pltpu.SMEM)] + [hbm] * (count + 4 + len(after)),
        out_specs=[vm] * count,
        scratch_shapes=[pltpu.VMEM((count * rows, d), jnp.bfloat16), weight, weight, weight, pltpu.SemaphoreType.DMA((count + 9,))],
        out_shape=[jax.ShapeDtypeStruct((rows, d), jnp.bfloat16)] * count,
        compiler_params=pltpu.CompilerParams(vmem_limit_bytes=60 << 20),
        cost_estimate=pl.CostEstimate(flops=20 * count * rows * n * d, bytes_accessed=2 * (3 * n * d + 2 * count * rows * d), transcendentals=count * rows * n),
        name="experts",
    )(info, *xs, wo, do, r1, r2, *after)


def combine_kernel(info_ref, hid_ref, mine_ref, other_ref, a1_ref, a2_ref, a3_ref, back_ref, hot_ref, factor_ref, out_ref):
    cap = back_ref.shape[0]
    is_mine = pl.program_id(0) // 2 == info_ref[2]
    att = jnp.where(is_mine, mine_ref[...].astype(jnp.float32), other_ref[...].astype(jnp.float32))
    stream = (hid_ref[...].astype(jnp.float32) + att).astype(jnp.bfloat16).astype(jnp.float32)
    keep = a1_ref[...].astype(jnp.float32) + a2_ref[...].astype(jnp.float32) + a3_ref[...].astype(jnp.float32)
    one = jnp.dot(hot_ref[:, :cap], keep.astype(jnp.bfloat16), preferred_element_type=jnp.float32)
    two = jnp.dot(hot_ref[:, cap:2 * cap], back_ref[...], preferred_element_type=jnp.float32)
    out_ref[...] = (stream + one * factor_ref[:, 0:1] + two * factor_ref[:, 1:2]).astype(out_ref.dtype)


def combine(info, hidden, mine, other, parts, back, hot, factors):
    tok, d = hidden.shape
    cap = back.shape[0]
    wide = d // 4
    cols = lambda rows: pl.BlockSpec((rows, wide), lambda c, s: (0, c))
    half = pl.BlockSpec((tok, wide), lambda c, s: (0, lax.rem(c, 2)))
    whole = pl.BlockSpec((tok, tok), lambda c, s: (0, 0))
    return pl.pallas_call(
        combine_kernel,
        grid_spec=pltpu.PrefetchScalarGridSpec(
            num_scalar_prefetch=1,
            grid=(4,),
            in_specs=[cols(tok), half, half] + [cols(cap)] * 4 + [whole] * 2,
            out_specs=cols(tok),
        ),
        out_shape=jax.ShapeDtypeStruct((tok, d), hidden.dtype),
        compiler_params=pltpu.CompilerParams(vmem_limit_bytes=60 << 20),
        name="combine",
    )(info, hidden, mine, other, *parts, back, hot, factors)


def shift(value, axis, size, steps):
    return lax.ppermute(value, axis, [(i, (i + steps) % size) for i in range(size)])


def swap(value, axis):
    return shift(value, axis, 2, 1)


def ring_moves(size):
    out = [0]
    for s in range(1, size // 2 + 1):
        out.append(-s)
        if 2 * s < size:
            out.append(s)
    return out


def ring_gather(parts, signs, size):
    got = [{0: x} for x in parts]
    for s in range(1, size // 2 + 1):
        for g, sign in zip(got, signs):
            g[-s * sign] = shift(g[(1 - s) * sign], "z", size, sign)
            if 2 * s < size:
                g[s * sign] = shift(g[(s - 1) * sign], "z", size, -sign)
    return got


def ring_scatter(parts, signs, size):
    reach = size // 2
    ups = [p[-reach * sign] for p, sign in zip(parts, signs)]
    downs = [p[(1 - reach) * sign] for p, sign in zip(parts, signs)]
    for s in range(1, reach + 1):
        for i, (p, sign) in enumerate(zip(parts, signs)):
            ups[i] = shift(ups[i], "z", size, sign)
            if s < reach:
                ups[i] = ups[i] + p[(reach - s) * sign]
                downs[i] = shift(downs[i], "z", size, -sign)
            if s < reach - 1:
                downs[i] = downs[i] + p[(1 - reach + s) * sign]
    return [(ups[i], downs[i], p[0]) for i, p in enumerate(parts)]


def body(sizes, hidden_in, queries, keys_values, doc_ids, route_ids, route_weights, norm_gain, gate_up, down):
    tok, d = queries.shape
    capacity = tok // 4
    n_z, n_core, n_cx = sizes["z"], sizes["core"], sizes["cx"]
    yhi, z, core = lax.axis_index("yhi"), lax.axis_index("z"), lax.axis_index("core")
    half = n_z * tok
    n_ctx = n_cx * n_core
    moves = ring_moves(n_z)
    heads = keys_values.shape[1] // (4 * HD)
    info = jnp.stack([z, yhi * half, yhi, core]).astype(jnp.int32)

    send, mine = prepare(info, keys_values, doc_ids)
    other = swap(send, "yhi")
    unit = join(send, mine, other)

    q_out, place, hot, factors, base = plan(info, route_ids, route_weights, queries, hidden_in)
    q_out, unit = lax.optimization_barrier((q_out, unit))
    got = swap(q_out, "yhi")
    wide_t = jnp.swapaxes(gate_up, 2, 3)
    theirs, got = lax.optimization_barrier((pack(info, wide_t, down, n_core), got))
    got_1 = swap(theirs, "yhi")
    got_2 = swap(got_1, "core")

    own = ring_gather([unit], [1], n_z)[0]
    own = [own[m] for m in moves]
    ahead = [(i, i + 1) for i in range(n_ctx - 1)]
    groups = [range(0, 1), range(1, n_z // 2 + 1), range(n_z // 2 + 1, n_z - 1), range(n_z - 1, n_z)]
    prior, layout = [], []
    for n, group in enumerate(groups):
        block = jnp.concatenate([own[i] for i in group], 0) if len(group) > 1 else own[group[0]]
        prior.append(lax.ppermute(block, ("cx", "core"), ahead))
        layout += [(n, k * unit.shape[0]) for k in range(len(group))]
    layout += [(len(groups) + i, 0) for i in range(n_z)]
    pieces = prior + own

    gain = norm_gain[None]
    att_1, send_1, mine_1 = attend(info, got, got, pieces, layout, moves, 1, heads, tok)
    got_a = swap(send_1, "yhi")
    queries, got_1, _ = lax.optimization_barrier((queries, got_1, att_1))
    att_2, mine_2, send_2 = attend(info, queries, place, pieces, layout, moves, 0, heads, tok)
    got_b = swap(send_2, "yhi")
    rows_a = norm_rows(info, base, 0, mine_2, got_a, gain)
    rows_b = norm_rows(info, got, tok // (2 * capacity), mine_1, got_b, gain)
    att_1, rows_b = lax.optimization_barrier((att_1, rows_b))
    att_3 = swap(att_1, "yhi")

    signs = [1, -1]
    rows = ring_gather([rows_a, rows_b], signs, n_z)
    last = [-n_z // 2 * sign for sign in signs]
    early = [[m for m in r if m != l] for r, l in zip(rows, last)]
    args = (wide_t, down, got_1, got_2)
    keys = [(i, m) for i in range(2) for m in early[i]]
    first_out = experts(info, [rows[i][m] for i, m in keys], *args)
    last_out = experts(info, [rows[i][last[i]] for i in range(2)], *args, after=first_out[:1])
    outs = [{last[i]: last_out[i]} for i in range(2)]
    for (i, m), y in zip(keys, first_out):
        outs[i][m] = y
    sum_b, sum_a = ring_scatter([outs[1], outs[0]], signs[::-1], n_z)
    back = swap(sum_b[0] + sum_b[1] + sum_b[2], "yhi")
    return combine(info, hidden_in, att_2, att_3, sum_a, back, hot, factors)


def solution(mesh):
    sizes = {"cx": mesh.shape["ctx"] // 2, "core": 2, "yhi": 2, "z": mesh.shape["exp"] // 2, "dp": mesh.shape["dp"]}
    fine = Mesh(mesh.devices.reshape(tuple(sizes.values())), tuple(sizes))
    tokens = ("dp", "cx", "core", "yhi", "z")
    rows = P(tokens, None)
    hidden = ("yhi", "z")
    in_specs = (rows, rows, rows, P(tokens), rows, rows, P(), P(None, None, None, hidden), P(None, hidden, None))
    return jax.shard_map(
        functools.partial(body, sizes), mesh=fine, in_specs=in_specs, out_specs=rows, check_vma=False
    )
```

```python
import functools
import math

import jax
import jax.numpy as jnp
from jax import lax
from jax.experimental import pallas as pl
from jax.experimental.pallas import tpu as pltpu
from jax.sharding import Mesh
from jax.sharding import PartitionSpec as P

EXP_FLIGHT = 2
HD = 128
GROUP = 7
EXP2_SCALE = math.log2(math.e) / math.sqrt(HD)

def attend_kernel(info_ref, q_ref, place_ref, *refs, tok, span, moves, heads, layout, part):
    arrays, out_ref, low_ref, high_ref = refs[:-11], refs[-11], refs[-10], refs[-9]
    kv, ids, start_scr, m_scr, l_scr, acc_scr, bounds, sem = refs[-8:]
    c = pl.program_id(0)
    z = info_ref[0]
    half = len(moves) * tok
    near = pl.multiple_of(info_ref[1], half)
    far = pl.multiple_of(half - info_ref[1], half)
    first = pl.multiple_of((far if part else near) + z * tok, tok)

    @pl.when(c == 0)
    def _():
        blocks = []
        copies = []
        for n, (which, row) in enumerate(layout):
            piece = arrays[which]
            place = lax.rem(z + moves[n % len(moves)] + len(moves), len(moves)) * tok
            slab = n // len(moves) * 2 * half
            for side, base in ((0, near), (1, far)):
                at = pl.multiple_of(slab + base + place, tok)
                cp = pltpu.make_async_copy(piece.at[pl.ds(row + side * tok, tok)], kv.at[pl.ds(at, tok)], sem.at[n, side])
                blocks.append((cp, (at >= first) & (at <= first + 2 * half)))
            copies.append(pltpu.make_async_copy(piece.at[pl.ds(row + 2 * tok, 16)], ids.at[n], sem.at[n, 2]))
        for cp in copies:
            cp.start()
        for cp, needed in blocks:
            pl.when(needed)(cp.start)
        for cp in copies:
            cp.wait()
        own = ids[len(moves), 0:1, part * tok:(part + 1) * tok].astype(jnp.float32)
        own = jnp.broadcast_to(own, (tok, tok)).T
        less = jnp.zeros((tok, tok), jnp.float32)
        for n in range(len(layout)):
            for side in range(2):
                row = ids[n, 0:1, side * tok:(side + 1) * tok].astype(jnp.float32)
                less = less + jnp.where(row < own, 1.0, 0.0)
        begin = jnp.sum(less, axis=1, keepdims=True)
        start_scr[...] = begin.astype(jnp.int32)
        bounds[0] = jnp.min(begin).astype(jnp.int32)
        bounds[1] = jnp.max(begin).astype(jnp.int32)
        for cp, needed in blocks:
            pl.when(needed)(cp.wait)

    start_min, start_max = bounds[0], bounds[1]
    q = jnp.concatenate([q_ref[:, g * HD:(g + 1) * HD] for g in range(GROUP)], 0)
    start = start_scr[...]
    row = lax.broadcasted_iota(jnp.int32, (tok, 1), 0) + first + 2 * half
    key_col = pl.multiple_of(c * HD, HD)
    value_col = pl.multiple_of((heads + c) * HD, HD)

    def keys(offset, width):
        return kv[pl.ds(offset, width), pl.ds(key_col, HD)]

    def values(offset, width):
        return kv[pl.ds(offset, width), pl.ds(value_col, HD)]

    def scores(offset, width):
        return lax.dot_general(q, keys(offset, width), (((1,), (1,)), ((), ())), preferred_element_type=jnp.float32)

    def rowmax(s, width):
        t = s[:, :128]
        for j in range(1, width // 128):
            t = jnp.maximum(t, s[:, j * 128:(j + 1) * 128])
        return jnp.max(t, axis=1, keepdims=True)

    def lanesum(p, width):
        t = p[:, :128]
        for j in range(1, width // 128):
            t = t + p[:, j * 128:(j + 1) * 128]
        return t

    def masked(s, offset, width, causal):
        key = lax.broadcasted_iota(jnp.int32, (tok, width), 1) + offset
        ok = key >= start
        if causal:
            ok = ok & (key <= row)
        return jnp.where(ok[None], s.reshape(GROUP, tok, width), -1e30).reshape(GROUP * tok, width)

    own = pl.multiple_of(first + 2 * half, tok)
    s = masked(scores(own, tok), own, tok, True)
    m = rowmax(s, tok)
    p = jnp.exp2((s - m) * EXP2_SCALE)
    m_scr[...] = jnp.broadcast_to(m, m_scr.shape)
    l_scr[...] = lanesum(p, tok)
    acc_scr[...] = jnp.dot(p.astype(jnp.bfloat16), values(own, tok), preferred_element_type=jnp.float32)

    def step(i, mask):
        offset = pl.multiple_of(first + i * span, tok)
        s = scores(offset, span)
        if mask:
            s = masked(s, offset, span, False)
        old = m_scr[...]
        new = jnp.maximum(old, rowmax(s, span))
        m_scr[...] = new
        shrink = jnp.exp2((old - new) * EXP2_SCALE)
        p = jnp.exp2((s - jnp.concatenate([new] * (span // 128), 1)) * EXP2_SCALE)
        l_scr[...] = l_scr[...] * shrink + lanesum(p, span)
        acc_scr[...] = acc_scr[...] * shrink + jnp.dot(p.astype(jnp.bfloat16), values(offset, span), preferred_element_type=jnp.float32)

    steps = 2 * half // span

    def loop(i, carry):
        whole = start_max <= first + i * span

        @pl.when(whole)
        def _():
            step(i, False)

        @pl.when(jnp.logical_not(whole))
        def _():
            step(i, True)

        return carry

    lax.fori_loop(jnp.clip(lax.div(start_min - first, span), 0, steps), steps, loop, 0)

    total = jnp.sum(l_scr[...], axis=1, keepdims=True)
    att = (acc_scr[...] / total).astype(jnp.bfloat16)
    att = jnp.concatenate([att[g * tok:(g + 1) * tok] for g in range(GROUP)], 1)
    out_ref[...] = att
    rows = jnp.dot(place_ref[...], att, preferred_element_type=jnp.float32).astype(jnp.bfloat16)
    low_ref[...] = rows[:rows.shape[0] // 2]
    high_ref[...] = rows[rows.shape[0] // 2:]


def attend(info, queries, place, pieces, layout, moves, part, heads, tok, span=512):
    slots = tok // 4
    wide = GROUP * HD
    n = len(moves)
    hbm = pl.BlockSpec(memory_space=pl.ANY)
    scratch = pltpu.VMEM((GROUP * tok, 128), jnp.float32)
    return pl.pallas_call(
        functools.partial(attend_kernel, tok=tok, span=span, moves=moves, heads=heads, layout=layout, part=part),
        grid_spec=pltpu.PrefetchScalarGridSpec(
            num_scalar_prefetch=1,
            grid=(heads,),
            in_specs=[
                pl.BlockSpec((tok, wide), lambda c, s: (0, c + (0 if part else s[2] * heads))),
                pl.BlockSpec((2 * slots, tok), lambda c, s: (tok // (2 * slots), heads * GROUP) if part else (0, 0)),
            ] + [hbm] * len(pieces),
            out_specs=[pl.BlockSpec((r, wide), lambda c, s: (0, c)) for r in (tok, slots, slots)],
            scratch_shapes=[
                pltpu.VMEM((4 * n * tok, 2 * heads * HD), jnp.bfloat16),
                pltpu.VMEM((2 * n, 16, 2 * heads * HD), jnp.bfloat16),
                pltpu.VMEM((tok, 1), jnp.int32),
                scratch, scratch, scratch,
                pltpu.SMEM((2,), jnp.int32),
                pltpu.SemaphoreType.DMA((2 * n, 3)),
            ],
        ),
        out_shape=[jax.ShapeDtypeStruct((r, heads * wide), jnp.bfloat16) for r in (tok, slots, slots)],
        compiler_params=pltpu.CompilerParams(vmem_limit_bytes=60 << 20),
        cost_estimate=pl.CostEstimate(flops=8 * 10**9, bytes_accessed=5 << 20, transcendentals=4 * 10**6),
        name="attend",
    )(info, queries, place, *pieces)


def prepare_kernel(info_ref, kv_ref, doc_ref, send_ref, mine_ref):
    tok = kv_ref.shape[0]
    w = kv_ref.shape[1] // 4
    send_ref[tok:, :] = jnp.zeros((16, 2 * w), send_ref.dtype)
    send_ref[tok:tok + 16, :tok] = jnp.broadcast_to((doc_ref[...] + 1).astype(jnp.float32), (16, tok)).astype(send_ref.dtype)
    for yhi in range(2):
        @pl.when(info_ref[2] == yhi)
        def _(yhi=yhi):
            away = 1 - yhi
            mine_ref[:, :w] = kv_ref[:, yhi * w:(yhi + 1) * w]
            mine_ref[:, w:] = kv_ref[:, (2 + yhi) * w:(3 + yhi) * w]
            send_ref[:tok, :w] = kv_ref[:, away * w:(away + 1) * w]
            send_ref[:tok, w:] = kv_ref[:, (2 + away) * w:(3 + away) * w]


def prepare(info, keys_values, doc_ids):
    tok, width = keys_values.shape
    vm = pl.BlockSpec(memory_space=pltpu.VMEM)
    shape = lambda r, c: jax.ShapeDtypeStruct((r, c), jnp.bfloat16)
    return pl.pallas_call(
        prepare_kernel,
        in_specs=[pl.BlockSpec(memory_space=pltpu.SMEM)] + [vm] * 2,
        out_specs=[vm] * 2,
        out_shape=[shape(tok + 16, width // 2), shape(tok, width // 2)],
        compiler_params=pltpu.CompilerParams(vmem_limit_bytes=60 << 20),
        name="prepare",
    )(info, keys_values, doc_ids[None])


def plan_kernel(info_ref, ids_ref, weights_ref, q_ref, hid_ref, out_ref, place_ref, hot_ref, factor_ref, base_ref):
    tok = hid_ref.shape[0]
    slots = place_ref.shape[0] // 2
    q = q_ref.shape[1] // 2
    yhi = info_ref[2]
    below = lax.broadcasted_iota(jnp.int32, (tok, tok), 0) <= lax.broadcasted_iota(jnp.int32, (tok, tok), 1)
    below = below.astype(jnp.float32).astype(jnp.bfloat16)
    places, factors = [], []
    for flight in (yhi, 1 - yhi):
        chosen = ids_ref[...] == flight
        routed = jnp.max(jnp.where(chosen, 1.0, 0.0), axis=0, keepdims=True)
        factors.append(jnp.sum(jnp.where(chosen, weights_ref[...], 0.0), axis=0, keepdims=True))
        ranks = jnp.dot(jnp.broadcast_to(routed, (16, tok)).astype(jnp.bfloat16), below, preferred_element_type=jnp.float32)
        ranks = jnp.where(routed > 0.5, ranks[:1] - 1.0, -1.0)
        slot = lax.broadcasted_iota(jnp.int32, (slots, tok), 0).astype(jnp.float32)
        places.append(jnp.where(slot == ranks, 1.0, 0.0))
    place_f = jnp.concatenate(places, 0)
    place = place_f.astype(jnp.bfloat16)
    place_ref[...] = place
    hot_ref[...] = jnp.concatenate([place_f, jnp.zeros((tok - 2 * slots, tok), jnp.float32)], 0).T.astype(jnp.bfloat16)
    factor_ref[...] = jnp.concatenate([factors[0], factors[1], jnp.zeros((tok - 2, tok), jnp.float32)], 0).T
    rows = jnp.dot(place, hid_ref[...], preferred_element_type=jnp.float32).astype(jnp.bfloat16)
    base_ref[:slots] = rows[:slots, :q]
    base_ref[slots:] = rows[:slots, q:]
    out_ref[:tok, q:] = jnp.zeros((tok, tok), jnp.bfloat16)
    out_ref[tok:tok + slots, :q] = rows[slots:, :q]
    out_ref[tok + slots:, :q] = rows[slots:, q:]
    out_ref[tok:, q:] = place

    @pl.when(yhi == 0)
    def _():
        out_ref[:tok, :q] = q_ref[:, q:]

    @pl.when(yhi != 0)
    def _():
        out_ref[:tok, :q] = q_ref[:, :q]


def plan(info, route_ids, route_weights, queries, hidden):
    tok, d = hidden.shape
    slots = tok // 4
    vm = pl.BlockSpec(memory_space=pltpu.VMEM)
    shape = lambda r, c, t=jnp.bfloat16: jax.ShapeDtypeStruct((r, c), t)
    return pl.pallas_call(
        plan_kernel,
        in_specs=[pl.BlockSpec(memory_space=pltpu.SMEM)] + [vm] * 4,
        out_specs=[vm] * 5,
        out_shape=[
            shape(tok + 2 * slots, d // 2 + tok), shape(2 * slots, tok), shape(tok, tok), shape(tok, tok, jnp.float32), shape(2 * slots, d // 2),
        ],
        compiler_params=pltpu.CompilerParams(vmem_limit_bytes=60 << 20),
        name="plan",
    )(info, route_ids.T, route_weights.T, queries, hidden)


def join_kernel(send_ref, mine_ref, other_ref, unit_ref):
    tok = mine_ref.shape[0]
    unit_ref[:tok] = mine_ref[...]
    unit_ref[tok:2 * tok] = other_ref[:tok]
    unit_ref[2 * tok:] = send_ref[tok:]
    unit_ref[2 * tok:, tok:2 * tok] = other_ref[tok:, :tok]


def join(send, mine, other):
    tok, width = mine.shape
    vm = pl.BlockSpec(memory_space=pltpu.VMEM)
    return pl.pallas_call(
        join_kernel,
        in_specs=[vm] * 3,
        out_specs=vm,
        out_shape=jax.ShapeDtypeStruct((2 * tok + 16, width), mine.dtype),
        compiler_params=pltpu.CompilerParams(vmem_limit_bytes=60 << 20),
        name="join",
    )(send, mine, other)


def pack_kernel(info_ref, gu_ref, down_ref, out_ref, sem):
    away = 1 - info_ref[2]
    units = out_ref.shape[1]
    at = pl.ds(pl.multiple_of(info_ref[3] * units, units), units)
    one = pltpu.make_async_copy(gu_ref.at[away, :, at], out_ref.at[pl.ds(0, 2)], sem.at[0])
    two = pltpu.make_async_copy(down_ref.at[away, at], out_ref.at[2], sem.at[1])
    one.start()
    two.start()
    one.wait()
    two.wait()


def pack(info, wide_t, down, cores):
    hbm = pl.BlockSpec(memory_space=pl.ANY)
    return pl.pallas_call(
        pack_kernel,
        in_specs=[pl.BlockSpec(memory_space=pltpu.SMEM), hbm, hbm],
        out_specs=pl.BlockSpec(memory_space=pltpu.VMEM),
        out_shape=jax.ShapeDtypeStruct((3, down.shape[1] // cores, down.shape[2]), down.dtype),
        scratch_shapes=[pltpu.SemaphoreType.DMA((2,))],
        compiler_params=pltpu.CompilerParams(vmem_limit_bytes=60 << 20),
        name="pack",
    )(info, wide_t, down)


def norm_kernel(info_ref, base_ref, mine_ref, other_ref, gain_ref, out_ref):
    slots, half = mine_ref.shape

    def put(low, high):
        parts = []
        for n, att in enumerate((low, high)):
            base = base_ref[n * slots:(n + 1) * slots].astype(jnp.float32)
            parts.append((base + att.astype(jnp.float32)).astype(jnp.bfloat16).astype(jnp.float32))
        total = sum(jnp.sum(p * p, axis=1, keepdims=True) for p in parts)
        inv = lax.rsqrt(total / (2 * half) + 1e-6)
        for n, p in enumerate(parts):
            gain = gain_ref[:, n * half:(n + 1) * half].astype(jnp.float32)
            out_ref[:, n * half:(n + 1) * half] = (p * inv * gain).astype(jnp.bfloat16)

    @pl.when(info_ref[2] == 0)
    def _():
        put(mine_ref[...], other_ref[...])

    @pl.when(info_ref[2] != 0)
    def _():
        put(other_ref[...], mine_ref[...])


def norm_rows(info, base, row, mine, other, gain):
    slots, half = mine.shape
    whole = lambda x: pl.BlockSpec(x.shape, lambda i, s: (0, 0))
    return pl.pallas_call(
        norm_kernel,
        grid_spec=pltpu.PrefetchScalarGridSpec(
            num_scalar_prefetch=1,
            grid=(1,),
            in_specs=[pl.BlockSpec((2 * slots, half), lambda i, s: (row, 0)), whole(mine), whole(other), whole(gain)],
            out_specs=pl.BlockSpec((slots, 2 * half), lambda i, s: (0, 0)),
        ),
        out_shape=jax.ShapeDtypeStruct((slots, 2 * half), jnp.bfloat16),
        compiler_params=pltpu.CompilerParams(vmem_limit_bytes=60 << 20),
        name="norm_rows",
    )(info, base, mine, other, gain)


def expert_kernel(info_ref, *refs, count, rows, after):
    xs = refs[:count]
    wo_ref, do_ref, r1_ref, r2_ref = refs[count:count + 4]
    refs = refs[count + 4 + after:]
    ys = refs[:count]
    x, wg, wu, wd, sem = refs[count:]
    yhi = info_ref[2]
    n = wo_ref.shape[2]
    h = r1_ref.shape[1]
    cps = []

    def cp(src, dst):
        c = pltpu.make_async_copy(src, dst, sem.at[len(cps)])
        c.start()
        cps.append(c)

    for i in range(count):
        cp(xs[i], x.at[pl.ds(i * rows, rows)])
    for i, w in enumerate((wg, wu, wd)):
        cp(do_ref.at[yhi] if i == 2 else wo_ref.at[yhi, i], w.at[pl.ds(0, n)])
        cp(r1_ref.at[i], w.at[pl.ds(n, h)])
        cp(r2_ref.at[i], w.at[pl.ds(n + h, h)])
    nt = (((1,), (1,)), ((), ()))
    for c in cps[:count + 3]:
        c.wait()
    xv = x[...]
    gate = lax.dot_general(xv, wg[...], nt, preferred_element_type=jnp.float32)
    for c in cps[count + 3:count + 6]:
        c.wait()
    up = lax.dot_general(xv, wu[...], nt, preferred_element_type=jnp.float32)
    inner = (gate / (1 + jnp.exp(-gate)) * up).astype(jnp.bfloat16)
    for c in cps[count + 6:]:
        c.wait()
    y = jnp.dot(inner, wd[...], preferred_element_type=jnp.float32).astype(jnp.bfloat16)
    for i in range(count):
        ys[i][...] = y[i * rows:(i + 1) * rows]


def experts(info, xs, wo, do, r1, r2, after=()):
    count = len(xs)
    rows, d = xs[0].shape
    n = wo.shape[2] + r1.shape[1] + r2.shape[1]
    hbm = pl.BlockSpec(memory_space=pl.ANY)
    vm = pl.BlockSpec(memory_space=pltpu.VMEM)
    weight = pltpu.VMEM((n, d), jnp.bfloat16)
    return pl.pallas_call(
        functools.partial(expert_kernel, count=count, rows=rows, after=len(after)),
        in_specs=[pl.BlockSpec(memory_space=pltpu.SMEM)] + [hbm] * (count + 4 + len(after)),
        out_specs=[vm] * count,
        scratch_shapes=[pltpu.VMEM((count * rows, d), jnp.bfloat16), weight, weight, weight, pltpu.SemaphoreType.DMA((count + 9,))],
        out_shape=[jax.ShapeDtypeStruct((rows, d), jnp.bfloat16)] * count,
        compiler_params=pltpu.CompilerParams(vmem_limit_bytes=60 << 20),
        cost_estimate=pl.CostEstimate(flops=20 * count * rows * n * d, bytes_accessed=2 * (3 * n * d + 2 * count * rows * d), transcendentals=count * rows * n),
        name="experts",
    )(info, *xs, wo, do, r1, r2, *after)


def combine_kernel(info_ref, hid_ref, mine_ref, other_ref, a1_ref, a2_ref, a3_ref, back_ref, hot_ref, factor_ref, out_ref):
    cap = back_ref.shape[0]
    is_mine = pl.program_id(0) // 2 == info_ref[2]
    att = jnp.where(is_mine, mine_ref[...].astype(jnp.float32), other_ref[...].astype(jnp.float32))
    stream = (hid_ref[...].astype(jnp.float32) + att).astype(jnp.bfloat16).astype(jnp.float32)
    keep = a1_ref[...].astype(jnp.float32) + a2_ref[...].astype(jnp.float32) + a3_ref[...].astype(jnp.float32)
    one = jnp.dot(hot_ref[:, :cap], keep.astype(jnp.bfloat16), preferred_element_type=jnp.float32)
    two = jnp.dot(hot_ref[:, cap:2 * cap], back_ref[...], preferred_element_type=jnp.float32)
    out_ref[...] = (stream + one * factor_ref[:, 0:1] + two * factor_ref[:, 1:2]).astype(out_ref.dtype)


def combine(info, hidden, mine, other, parts, back, hot, factors):
    tok, d = hidden.shape
    cap = back.shape[0]
    wide = d // 4
    cols = lambda rows: pl.BlockSpec((rows, wide), lambda c, s: (0, c))
    half = pl.BlockSpec((tok, wide), lambda c, s: (0, lax.rem(c, 2)))
    whole = pl.BlockSpec((tok, tok), lambda c, s: (0, 0))
    return pl.pallas_call(
        combine_kernel,
        grid_spec=pltpu.PrefetchScalarGridSpec(
            num_scalar_prefetch=1,
            grid=(4,),
            in_specs=[cols(tok), half, half] + [cols(cap)] * 4 + [whole] * 2,
            out_specs=cols(tok),
        ),
        out_shape=jax.ShapeDtypeStruct((tok, d), hidden.dtype),
        compiler_params=pltpu.CompilerParams(vmem_limit_bytes=60 << 20),
        name="combine",
    )(info, hidden, mine, other, *parts, back, hot, factors)


def shift(value, axis, size, steps):
    return lax.ppermute(value, axis, [(i, (i + steps) % size) for i in range(size)])


def swap(value, axis):
    return shift(value, axis, 2, 1)


def ring_moves(size):
    out = [0]
    for s in range(1, size // 2 + 1):
        out.append(-s)
        if 2 * s < size:
            out.append(s)
    return out


def ring_gather(parts, signs, size):
    got = [{0: x} for x in parts]
    for s in range(1, size // 2 + 1):
        for g, sign in zip(got, signs):
            g[-s * sign] = shift(g[(1 - s) * sign], "z", size, sign)
            if 2 * s < size:
                g[s * sign] = shift(g[(s - 1) * sign], "z", size, -sign)
    return got


def ring_scatter(parts, signs, size):
    reach = size // 2
    ups = [p[-reach * sign] for p, sign in zip(parts, signs)]
    downs = [p[(1 - reach) * sign] for p, sign in zip(parts, signs)]
    for s in range(1, reach + 1):
        for i, (p, sign) in enumerate(zip(parts, signs)):
            ups[i] = shift(ups[i], "z", size, sign)
            if s < reach:
                ups[i] = ups[i] + p[(reach - s) * sign]
                downs[i] = shift(downs[i], "z", size, -sign)
            if s < reach - 1:
                downs[i] = downs[i] + p[(1 - reach + s) * sign]
    return [(ups[i], downs[i], p[0]) for i, p in enumerate(parts)]


def body(sizes, hidden_in, queries, keys_values, doc_ids, route_ids, route_weights, norm_gain, gate_up, down):
    tok, d = queries.shape
    capacity = tok // 4
    n_z, n_core, n_cx = sizes["z"], sizes["core"], sizes["cx"]
    yhi, z, core = lax.axis_index("yhi"), lax.axis_index("z"), lax.axis_index("core")
    half = n_z * tok
    n_ctx = n_cx * n_core
    moves = ring_moves(n_z)
    heads = keys_values.shape[1] // (4 * HD)
    info = jnp.stack([z, yhi * half, yhi, core]).astype(jnp.int32)

    send, mine = prepare(info, keys_values, doc_ids)
    other = swap(send, "yhi")
    unit = join(send, mine, other)

    q_out, place, hot, factors, base = plan(info, route_ids, route_weights, queries, hidden_in)
    wide_t = jnp.swapaxes(gate_up, 2, 3)
    theirs = pack(info, wide_t, down, n_core)
    q_out, theirs, unit = lax.optimization_barrier((q_out, theirs, unit))
    got = swap(q_out, "yhi")
    got_1 = swap(theirs, "yhi")
    got_2 = swap(got_1, "core")

    own = ring_gather([unit], [1], n_z)[0]
    own = [own[m] for m in moves]
    ahead = [(i, i + 1) for i in range(n_ctx - 1)]
    groups = [range(0, 1), range(1, n_z // 2 + 1), range(n_z // 2 + 1, n_z - 1), range(n_z - 1, n_z)]
    prior, layout = [], []
    for n, group in enumerate(groups):
        block = jnp.concatenate([own[i] for i in group], 0) if len(group) > 1 else own[group[0]]
        prior.append(lax.ppermute(block, ("cx", "core"), ahead))
        layout += [(n, k * unit.shape[0]) for k in range(len(group))]
    layout += [(len(groups) + i, 0) for i in range(n_z)]
    pieces = prior + own

    gain = norm_gain[None]
    att_1, send_1, mine_1 = attend(info, got, got, pieces, layout, moves, 1, heads, tok)
    got_a = swap(send_1, "yhi")
    queries, got_1, _ = lax.optimization_barrier((queries, got_1, att_1))
    att_2, mine_2, send_2 = attend(info, queries, place, pieces, layout, moves, 0, heads, tok)
    got_b = swap(send_2, "yhi")
    rows_a = norm_rows(info, base, 0, mine_2, got_a, gain)
    rows_b = norm_rows(info, got, tok // (2 * capacity), mine_1, got_b, gain)
    att_1, rows_b = lax.optimization_barrier((att_1, rows_b))
    att_3 = swap(att_1, "yhi")

    signs = [1, -1]
    rows = ring_gather([rows_a, rows_b], signs, n_z)
    last = [-n_z // 2 * sign for sign in signs]
    early = [[m for m in r if m != l] for r, l in zip(rows, last)]
    args = (wide_t, down, got_1, got_2)
    keys = [(i, m) for i in range(2) for m in early[i]]
    first_out = experts(info, [rows[i][m] for i, m in keys], *args)
    last_out = experts(info, [rows[i][last[i]] for i in range(2)], *args, after=first_out[:1])
    outs = [{last[i]: last_out[i]} for i in range(2)]
    for (i, m), y in zip(keys, first_out):
        outs[i][m] = y
    sum_b, sum_a = ring_scatter([outs[1], outs[0]], signs[::-1], n_z)
    back = swap(sum_b[0] + sum_b[1] + sum_b[2], "yhi")
    return combine(info, hidden_in, att_2, att_3, sum_a, back, hot, factors)


def solution(mesh):
    sizes = {"cx": mesh.shape["ctx"] // 2, "core": 2, "yhi": 2, "z": mesh.shape["exp"] // 2, "dp": mesh.shape["dp"]}
    fine = Mesh(mesh.devices.reshape(tuple(sizes.values())), tuple(sizes))
    tokens = ("dp", "cx", "core", "yhi", "z")
    rows = P(tokens, None)
    hidden = ("yhi", "z")
    in_specs = (rows, rows, rows, P(tokens), rows, rows, P(), P(None, None, None, hidden), P(None, hidden, None))
    return jax.shard_map(
        functools.partial(body, sizes), mesh=fine, in_specs=in_specs, out_specs=rows, check_vma=False
    )
```

```python
import functools
import math

import jax
import jax.numpy as jnp
from jax import lax
from jax.experimental import pallas as pl
from jax.experimental.pallas import tpu as pltpu
from jax.sharding import Mesh
from jax.sharding import PartitionSpec as P

EXP_FLIGHT = 2
HD = 128
GROUP = 7
EXP2_SCALE = math.log2(math.e) / math.sqrt(HD)

def attend_kernel(info_ref, q_own_ref, q_got_ref, place_own_ref, place_got_ref, *refs, tok, span, moves, heads, layout, part):
    arrays, out_ref, low_ref, high_ref = refs[:-11], refs[-11], refs[-10], refs[-9]
    kv, ids, start_scr, m_scr, l_scr, acc_scr, bounds, sem = refs[-8:]
    c = pl.program_id(0)
    z = info_ref[0]
    half = len(moves) * tok
    near = pl.multiple_of(info_ref[1], half)
    far = pl.multiple_of(half - info_ref[1], half)
    first = pl.multiple_of(part * half + z * tok, tok)
    is_own = info_ref[2] == part

    @pl.when(c == 0)
    def _():
        blocks = []
        copies = []
        for n, (which, row) in enumerate(layout):
            piece = arrays[which]
            place = lax.rem(z + moves[n % len(moves)] + len(moves), len(moves)) * tok
            slab = n // len(moves) * 2 * half
            for side, base in ((0, near), (1, far)):
                at = pl.multiple_of(slab + base + place, tok)
                cp = pltpu.make_async_copy(piece.at[pl.ds(row + side * tok, tok)], kv.at[pl.ds(at, tok)], sem.at[n, side])
                blocks.append((cp, (at >= first) & (at <= first + 2 * half)))
            copies.append(pltpu.make_async_copy(piece.at[pl.ds(row + 2 * tok, 16)], ids.at[n], sem.at[n, 2]))
        for cp in copies:
            cp.start()
        for cp, needed in blocks:
            pl.when(needed)(cp.start)
        for cp in copies:
            cp.wait()
        own = [ids[len(moves), 0:1, n * tok:(n + 1) * tok].astype(jnp.float32) for n in range(2)]
        own = jnp.where(is_own, own[0], own[1])
        own = jnp.broadcast_to(own, (tok, tok)).T
        less = jnp.zeros((tok, tok), jnp.float32)
        for n in range(len(layout)):
            for side in range(2):
                row = ids[n, 0:1, side * tok:(side + 1) * tok].astype(jnp.float32)
                less = less + jnp.where(row < own, 1.0, 0.0)
        begin = jnp.sum(less, axis=1, keepdims=True)
        start_scr[...] = begin.astype(jnp.int32)
        bounds[0] = jnp.min(begin).astype(jnp.int32)
        bounds[1] = jnp.max(begin).astype(jnp.int32)
        for cp, needed in blocks:
            pl.when(needed)(cp.wait)

    start_min, start_max = bounds[0], bounds[1]
    q = jnp.where(is_own, q_own_ref[...], q_got_ref[...])
    q = jnp.concatenate([q[:, g * HD:(g + 1) * HD] for g in range(GROUP)], 0)
    start = start_scr[...]
    row = lax.broadcasted_iota(jnp.int32, (tok, 1), 0) + first + 2 * half
    key_col = pl.multiple_of(c * HD, HD)
    value_col = pl.multiple_of((heads + c) * HD, HD)

    def keys(offset, width):
        return kv[pl.ds(offset, width), pl.ds(key_col, HD)]

    def values(offset, width):
        return kv[pl.ds(offset, width), pl.ds(value_col, HD)]

    def scores(offset, width):
        return lax.dot_general(q, keys(offset, width), (((1,), (1,)), ((), ())), preferred_element_type=jnp.float32)

    def rowmax(s, width):
        t = s[:, :128]
        for j in range(1, width // 128):
            t = jnp.maximum(t, s[:, j * 128:(j + 1) * 128])
        return jnp.max(t, axis=1, keepdims=True)

    def lanesum(p, width):
        t = p[:, :128]
        for j in range(1, width // 128):
            t = t + p[:, j * 128:(j + 1) * 128]
        return t

    def masked(s, offset, width, causal):
        key = lax.broadcasted_iota(jnp.int32, (tok, width), 1) + offset
        ok = key >= start
        if causal:
            ok = ok & (key <= row)
        return jnp.where(ok[None], s.reshape(GROUP, tok, width), -1e30).reshape(GROUP * tok, width)

    own = pl.multiple_of(first + 2 * half, tok)
    s = masked(scores(own, tok), own, tok, True)
    m = rowmax(s, tok)
    p = jnp.exp2((s - m) * EXP2_SCALE)
    m_scr[...] = jnp.broadcast_to(m, m_scr.shape)
    l_scr[...] = lanesum(p, tok)
    acc_scr[...] = jnp.dot(p.astype(jnp.bfloat16), values(own, tok), preferred_element_type=jnp.float32)

    def step(i, mask):
        offset = pl.multiple_of(first + i * span, tok)
        s = scores(offset, span)
        if mask:
            s = masked(s, offset, span, False)
        old = m_scr[...]
        new = jnp.maximum(old, rowmax(s, span))
        m_scr[...] = new
        shrink = jnp.exp2((old - new) * EXP2_SCALE)
        p = jnp.exp2((s - jnp.concatenate([new] * (span // 128), 1)) * EXP2_SCALE)
        l_scr[...] = l_scr[...] * shrink + lanesum(p, span)
        acc_scr[...] = acc_scr[...] * shrink + jnp.dot(p.astype(jnp.bfloat16), values(offset, span), preferred_element_type=jnp.float32)

    steps = 2 * half // span

    def loop(i, carry):
        whole = start_max <= first + i * span

        @pl.when(whole)
        def _():
            step(i, False)

        @pl.when(jnp.logical_not(whole))
        def _():
            step(i, True)

        return carry

    lax.fori_loop(jnp.clip(lax.div(start_min - first, span), 0, steps), steps, loop, 0)

    total = jnp.sum(l_scr[...], axis=1, keepdims=True)
    att = (acc_scr[...] / total).astype(jnp.bfloat16)
    att = jnp.concatenate([att[g * tok:(g + 1) * tok] for g in range(GROUP)], 1)
    out_ref[...] = att
    place = jnp.where(is_own, place_own_ref[...], place_got_ref[...])
    rows = jnp.dot(place, att, preferred_element_type=jnp.float32).astype(jnp.bfloat16)
    low_ref[...] = rows[:rows.shape[0] // 2]
    high_ref[...] = rows[rows.shape[0] // 2:]


def attend(info, own, got, pieces, layout, moves, part, heads, tok, span=512):
    slots = tok // 4
    wide = GROUP * HD
    n = len(moves)
    hbm = pl.BlockSpec(memory_space=pl.ANY)
    scratch = pltpu.VMEM((GROUP * tok, 128), jnp.float32)
    return pl.pallas_call(
        functools.partial(attend_kernel, tok=tok, span=span, moves=moves, heads=heads, layout=layout, part=part),
        grid_spec=pltpu.PrefetchScalarGridSpec(
            num_scalar_prefetch=1,
            grid=(heads,),
            in_specs=[
                pl.BlockSpec((tok, wide), lambda c, s: (0, c)),
                pl.BlockSpec((tok, wide), lambda c, s: (0, c)),
                pl.BlockSpec((2 * slots, tok), lambda c, s: (tok // (2 * slots), heads * GROUP)),
                pl.BlockSpec((2 * slots, tok), lambda c, s: (tok // (2 * slots), heads * GROUP)),
            ] + [hbm] * len(pieces),
            out_specs=[pl.BlockSpec((r, wide), lambda c, s: (0, c)) for r in (tok, slots, slots)],
            scratch_shapes=[
                pltpu.VMEM((4 * n * tok, 2 * heads * HD), jnp.bfloat16),
                pltpu.VMEM((2 * n, 16, 2 * heads * HD), jnp.bfloat16),
                pltpu.VMEM((tok, 1), jnp.int32),
                scratch, scratch, scratch,
                pltpu.SMEM((2,), jnp.int32),
                pltpu.SemaphoreType.DMA((2 * n, 3)),
            ],
        ),
        out_shape=[jax.ShapeDtypeStruct((r, heads * wide), jnp.bfloat16) for r in (tok, slots, slots)],
        compiler_params=pltpu.CompilerParams(vmem_limit_bytes=24 << 20),
        cost_estimate=pl.CostEstimate(flops=8 * 10**9, bytes_accessed=5 << 20, transcendentals=4 * 10**6),
        name="attend",
    )(info, own, got, own, got, *pieces)


def prepare_kernel(info_ref, kv_ref, doc_ref, send_ref, mine_ref):
    tok = kv_ref.shape[0]
    w = kv_ref.shape[1] // 4
    send_ref[tok:, :] = jnp.zeros((16, 2 * w), send_ref.dtype)
    send_ref[tok:tok + 16, :tok] = jnp.broadcast_to((doc_ref[...] + 1).astype(jnp.float32), (16, tok)).astype(send_ref.dtype)
    for yhi in range(2):
        @pl.when(info_ref[2] == yhi)
        def _(yhi=yhi):
            away = 1 - yhi
            mine_ref[:, :w] = kv_ref[:, yhi * w:(yhi + 1) * w]
            mine_ref[:, w:] = kv_ref[:, (2 + yhi) * w:(3 + yhi) * w]
            send_ref[:tok, :w] = kv_ref[:, away * w:(away + 1) * w]
            send_ref[:tok, w:] = kv_ref[:, (2 + away) * w:(3 + away) * w]


def prepare(info, keys_values, doc_ids):
    tok, width = keys_values.shape
    vm = pl.BlockSpec(memory_space=pltpu.VMEM)
    shape = lambda r, c: jax.ShapeDtypeStruct((r, c), jnp.bfloat16)
    return pl.pallas_call(
        prepare_kernel,
        in_specs=[pl.BlockSpec(memory_space=pltpu.SMEM)] + [vm] * 2,
        out_specs=[vm] * 2,
        out_shape=[shape(tok + 16, width // 2), shape(tok, width // 2)],
        compiler_params=pltpu.CompilerParams(vmem_limit_bytes=24 << 20),
        name="prepare",
    )(info, keys_values, doc_ids[None])


def plan_kernel(info_ref, ids_ref, weights_ref, q_ref, hid_ref, out_ref, own_ref, hot_ref, factor_ref):
    tok = hid_ref.shape[0]
    slots = (out_ref.shape[0] - tok) // 2
    q = q_ref.shape[1] // 2
    yhi = info_ref[2]
    below = lax.broadcasted_iota(jnp.int32, (tok, tok), 0) <= lax.broadcasted_iota(jnp.int32, (tok, tok), 1)
    below = below.astype(jnp.float32).astype(jnp.bfloat16)
    places, factors = [], []
    for flight in (yhi, 1 - yhi):
        chosen = ids_ref[...] == flight
        routed = jnp.max(jnp.where(chosen, 1.0, 0.0), axis=0, keepdims=True)
        factors.append(jnp.sum(jnp.where(chosen, weights_ref[...], 0.0), axis=0, keepdims=True))
        ranks = jnp.dot(jnp.broadcast_to(routed, (16, tok)).astype(jnp.bfloat16), below, preferred_element_type=jnp.float32)
        ranks = jnp.where(routed > 0.5, ranks[:1] - 1.0, -1.0)
        slot = lax.broadcasted_iota(jnp.int32, (slots, tok), 0).astype(jnp.float32)
        places.append(jnp.where(slot == ranks, 1.0, 0.0))
    place_f = jnp.concatenate(places, 0)
    place = place_f.astype(jnp.bfloat16)
    hot_ref[...] = jnp.concatenate([place_f, jnp.zeros((tok - 2 * slots, tok), jnp.float32)], 0).T.astype(jnp.bfloat16)
    factor_ref[...] = jnp.concatenate([factors[0], factors[1], jnp.zeros((tok - 2, tok), jnp.float32)], 0).T
    rows = jnp.dot(place, hid_ref[...], preferred_element_type=jnp.float32).astype(jnp.bfloat16)
    for n, ref in enumerate((own_ref, out_ref)):
        ref[:tok, q:] = jnp.zeros((tok, tok), jnp.bfloat16)
        ref[tok:tok + slots, :q] = rows[n * slots:(n + 1) * slots, :q]
        ref[tok + slots:, :q] = rows[n * slots:(n + 1) * slots, q:]
        ref[tok:tok + slots, q:] = place[n * slots:(n + 1) * slots]
        ref[tok + slots:, q:] = place[(1 - n) * slots:(2 - n) * slots]

    for side in range(2):
        @pl.when(yhi == side)
        def _(side=side):
            own_ref[:tok, :q] = q_ref[:, side * q:(side + 1) * q]
            out_ref[:tok, :q] = q_ref[:, (1 - side) * q:(2 - side) * q]


def plan(info, route_ids, route_weights, queries, hidden):
    tok, d = hidden.shape
    slots = tok // 4
    vm = pl.BlockSpec(memory_space=pltpu.VMEM)
    shape = lambda r, c, t=jnp.bfloat16: jax.ShapeDtypeStruct((r, c), t)
    return pl.pallas_call(
        plan_kernel,
        in_specs=[pl.BlockSpec(memory_space=pltpu.SMEM)] + [vm] * 4,
        out_specs=[vm] * 4,
        out_shape=[shape(tok + 2 * slots, d // 2 + tok)] * 2 + [shape(tok, tok), shape(tok, tok, jnp.float32)],
        compiler_params=pltpu.CompilerParams(vmem_limit_bytes=24 << 20),
        name="plan",
    )(info, route_ids.T, route_weights.T, queries, hidden)


def join_kernel(send_ref, mine_ref, other_ref, unit_ref):
    tok = mine_ref.shape[0]
    unit_ref[:tok] = mine_ref[...]
    unit_ref[tok:2 * tok] = other_ref[:tok]
    unit_ref[2 * tok:] = send_ref[tok:]
    unit_ref[2 * tok:, tok:2 * tok] = other_ref[tok:, :tok]


def join(send, mine, other):
    tok, width = mine.shape
    vm = pl.BlockSpec(memory_space=pltpu.VMEM)
    return pl.pallas_call(
        join_kernel,
        in_specs=[vm] * 3,
        out_specs=vm,
        out_shape=jax.ShapeDtypeStruct((2 * tok + 16, width), mine.dtype),
        compiler_params=pltpu.CompilerParams(vmem_limit_bytes=24 << 20),
        name="join",
    )(send, mine, other)


def pack_kernel(info_ref, gu_ref, down_ref, out_ref, sem):
    away = 1 - info_ref[2]
    units = out_ref.shape[1]
    at = pl.ds(pl.multiple_of(info_ref[3] * units, units), units)
    one = pltpu.make_async_copy(gu_ref.at[away, :, at], out_ref.at[pl.ds(0, 2)], sem.at[0])
    two = pltpu.make_async_copy(down_ref.at[away, at], out_ref.at[2], sem.at[1])
    one.start()
    two.start()
    one.wait()
    two.wait()


def pack(info, wide_t, down, cores):
    hbm = pl.BlockSpec(memory_space=pl.ANY)
    return pl.pallas_call(
        pack_kernel,
        in_specs=[pl.BlockSpec(memory_space=pltpu.SMEM), hbm, hbm],
        out_specs=pl.BlockSpec(memory_space=pltpu.VMEM),
        out_shape=jax.ShapeDtypeStruct((3, down.shape[1] // cores, down.shape[2]), down.dtype),
        scratch_shapes=[pltpu.SemaphoreType.DMA((2,))],
        compiler_params=pltpu.CompilerParams(vmem_limit_bytes=24 << 20),
        name="pack",
    )(info, wide_t, down)


def norm_kernel(info_ref, own_ref, got_ref, mine_ref, other_ref, gain_ref, out_ref, *, part):
    slots, half = mine_ref.shape
    tok = own_ref.shape[0] - 2 * slots
    is_own = info_ref[2] == part

    def put(low, high):
        parts = []
        for n, att in enumerate((low, high)):
            rows = slice(tok + n * slots, tok + (n + 1) * slots)
            base = jnp.where(is_own, own_ref[rows, :half], got_ref[rows, :half]).astype(jnp.float32)
            parts.append((base + att.astype(jnp.float32)).astype(jnp.bfloat16).astype(jnp.float32))
        total = sum(jnp.sum(p * p, axis=1, keepdims=True) for p in parts)
        inv = lax.rsqrt(total / (2 * half) + 1e-6)
        for n, p in enumerate(parts):
            gain = gain_ref[:, n * half:(n + 1) * half].astype(jnp.float32)
            out_ref[:, n * half:(n + 1) * half] = (p * inv * gain).astype(jnp.bfloat16)

    @pl.when(info_ref[2] == 0)
    def _():
        put(mine_ref[...], other_ref[...])

    @pl.when(info_ref[2] != 0)
    def _():
        put(other_ref[...], mine_ref[...])


def norm_rows(info, own, got, part, mine, other, gain):
    slots, half = mine.shape
    vm = pl.BlockSpec(memory_space=pltpu.VMEM)
    return pl.pallas_call(
        functools.partial(norm_kernel, part=part),
        in_specs=[pl.BlockSpec(memory_space=pltpu.SMEM)] + [vm] * 5,
        out_specs=vm,
        out_shape=jax.ShapeDtypeStruct((slots, 2 * half), jnp.bfloat16),
        compiler_params=pltpu.CompilerParams(vmem_limit_bytes=16 << 20),
        name="norm_rows",
    )(info, own, got, mine, other, gain)


def assemble_kernel(info_ref, wo_ref, do_ref, r1_ref, r2_ref, after_ref, w_ref, sem):
    del after_ref
    yhi = info_ref[2]
    n, h = wo_ref.shape[2], r1_ref.shape[1]
    cps = []
    for i in range(3):
        own = do_ref.at[yhi] if i == 2 else wo_ref.at[yhi, i]
        for src, at, size in ((own, 0, n), (r1_ref.at[i], n, h), (r2_ref.at[i], n + h, h)):
            cps.append(pltpu.make_async_copy(src, w_ref.at[i, pl.ds(at, size)], sem.at[len(cps)]))
    for c in cps:
        c.start()
    for c in cps:
        c.wait()


def assemble(info, wo, do, r1, r2, after):
    n, d = wo.shape[2] + r1.shape[1] + r2.shape[1], wo.shape[3]
    hbm = pl.BlockSpec(memory_space=pl.ANY)
    return pl.pallas_call(
        assemble_kernel,
        in_specs=[pl.BlockSpec(memory_space=pltpu.SMEM)] + [hbm] * 5,
        out_specs=pl.BlockSpec(memory_space=pltpu.VMEM),
        scratch_shapes=[pltpu.SemaphoreType.DMA((9,))],
        out_shape=jax.ShapeDtypeStruct((3, n, d), jnp.bfloat16),
        compiler_params=pltpu.CompilerParams(vmem_limit_bytes=16 << 20),
        cost_estimate=pl.CostEstimate(flops=0, bytes_accessed=6 * n * d, transcendentals=0),
        name="assemble",
    )(info, wo, do, r1, r2, after)


def expert_kernel(*refs, count, rows, after):
    xs, w_ref, ys = refs[:count], refs[count], refs[count + 1 + after:]
    x = jnp.concatenate([r[...] for r in xs], 0)
    nt = (((1,), (1,)), ((), ()))
    gate = lax.dot_general(x, w_ref[0], nt, preferred_element_type=jnp.float32)
    up = lax.dot_general(x, w_ref[1], nt, preferred_element_type=jnp.float32)
    inner = (gate / (1 + jnp.exp(-gate)) * up).astype(jnp.bfloat16)
    y = jnp.dot(inner, w_ref[2], preferred_element_type=jnp.float32).astype(jnp.bfloat16)
    for i in range(count):
        ys[i][...] = y[i * rows:(i + 1) * rows]


def experts(xs, w, after=()):
    count = len(xs)
    rows, d = xs[0].shape
    n = w.shape[1]
    vm = pl.BlockSpec(memory_space=pltpu.VMEM)
    return pl.pallas_call(
        functools.partial(expert_kernel, count=count, rows=rows, after=len(after)),
        in_specs=[vm] * (count + 1) + [pl.BlockSpec(memory_space=pl.ANY)] * len(after),
        out_specs=[vm] * count,
        out_shape=[jax.ShapeDtypeStruct((rows, d), jnp.bfloat16)] * count,
        compiler_params=pltpu.CompilerParams(vmem_limit_bytes=32 << 20),
        cost_estimate=pl.CostEstimate(flops=20 * count * rows * n * d, bytes_accessed=2 * (3 * n * d + 2 * count * rows * d), transcendentals=count * rows * n),
        name="experts",
    )(*xs, w, *after)


def combine_kernel(info_ref, hid_ref, mine_ref, other_ref, keep_ref, back_ref, hot_ref, factor_ref, out_ref):
    cap = back_ref.shape[0]
    is_mine = pl.program_id(0) // 2 == info_ref[2]
    att = jnp.where(is_mine, mine_ref[...].astype(jnp.float32), other_ref[...].astype(jnp.float32))
    stream = (hid_ref[...].astype(jnp.float32) + att).astype(jnp.bfloat16).astype(jnp.float32)
    one = jnp.dot(hot_ref[:, :cap], keep_ref[...], preferred_element_type=jnp.float32)
    two = jnp.dot(hot_ref[:, cap:2 * cap], back_ref[...], preferred_element_type=jnp.float32)
    out_ref[...] = (stream + one * factor_ref[:, 0:1] + two * factor_ref[:, 1:2]).astype(out_ref.dtype)


def combine(info, hidden, mine, other, keep, back, hot, factors):
    tok, d = hidden.shape
    cap = back.shape[0]
    wide = d // 4
    cols = lambda rows: pl.BlockSpec((rows, wide), lambda c, s: (0, c))
    half = pl.BlockSpec((tok, wide), lambda c, s: (0, lax.rem(c, 2)))
    whole = pl.BlockSpec((tok, tok), lambda c, s: (0, 0))
    return pl.pallas_call(
        combine_kernel,
        grid_spec=pltpu.PrefetchScalarGridSpec(
            num_scalar_prefetch=1,
            grid=(4,),
            in_specs=[cols(tok), half, half, cols(cap), cols(cap), whole, whole],
            out_specs=cols(tok),
        ),
        out_shape=jax.ShapeDtypeStruct((tok, d), hidden.dtype),
        compiler_params=pltpu.CompilerParams(vmem_limit_bytes=24 << 20),
        name="combine",
    )(info, hidden, mine, other, keep, back, hot, factors)


def shift(value, axis, size, steps):
    return lax.ppermute(value, axis, [(i, (i + steps) % size) for i in range(size)])


def swap(value, axis):
    return shift(value, axis, 2, 1)


def ring_moves(size):
    out = [0]
    for s in range(1, size // 2 + 1):
        out.append(-s)
        if 2 * s < size:
            out.append(s)
    return out


def ring_gather(parts, signs, size):
    got = [{0: x} for x in parts]
    for s in range(1, size // 2 + 1):
        for g, sign in zip(got, signs):
            g[-s * sign] = shift(g[(1 - s) * sign], "z", size, sign)
            if 2 * s < size:
                g[s * sign] = shift(g[(s - 1) * sign], "z", size, -sign)
    return got


def ring_scatter(parts, signs, size):
    reach = size // 2
    ups = [p[-reach * sign] for p, sign in zip(parts, signs)]
    downs = [p[(1 - reach) * sign] for p, sign in zip(parts, signs)]
    for s in range(1, reach + 1):
        for i, (p, sign) in enumerate(zip(parts, signs)):
            ups[i] = shift(ups[i], "z", size, sign)
            if s < reach:
                ups[i] = ups[i] + p[(reach - s) * sign]
                downs[i] = shift(downs[i], "z", size, -sign)
            if s < reach - 1:
                downs[i] = downs[i] + p[(1 - reach + s) * sign]
    return [(ups[i], downs[i], p[0]) for i, p in enumerate(parts)]


def body(sizes, hidden_in, queries, keys_values, doc_ids, route_ids, route_weights, norm_gain, gate_up, down):
    tok, d = queries.shape
    capacity = tok // 4
    n_z, n_core, n_cx = sizes["z"], sizes["core"], sizes["cx"]
    yhi, z, core = lax.axis_index("yhi"), lax.axis_index("z"), lax.axis_index("core")
    half = n_z * tok
    n_ctx = n_cx * n_core
    moves = ring_moves(n_z)
    heads = keys_values.shape[1] // (4 * HD)
    info = jnp.stack([z, yhi * half, yhi, core]).astype(jnp.int32)

    send, kept = prepare(info, keys_values, doc_ids)
    unit = join(send, kept, swap(send, "yhi"))

    out, mine, hot, factors = plan(info, route_ids, route_weights, queries, hidden_in)
    out, unit = lax.optimization_barrier((out, unit))
    got = swap(out, "yhi")
    wide_t = jnp.swapaxes(gate_up, 2, 3)
    theirs = pack(info, wide_t, down, n_core)
    own = {0: unit}
    for s in range(1, n_z // 2 + 1):
        own[-s] = shift(own[1 - s], "z", n_z, 1)
        if 2 * s < n_z:
            own[s] = shift(own[s - 1], "z", n_z, -1)
        if s == 2:
            own[-s], got, theirs = lax.optimization_barrier((own[-s], got, theirs))
    got_1 = swap(theirs, "yhi")
    got_2 = swap(got_1, "core")
    own = [own[m] for m in moves]
    ahead = [(i, i + 1) for i in range(n_ctx - 1)]
    groups = [range(0, 1), range(1, n_z // 2 + 1), range(n_z // 2 + 1, n_z - 1), range(n_z - 1, n_z)]
    prior, layout = [], []
    for n, group in enumerate(groups):
        block = jnp.concatenate([own[i] for i in group], 0) if len(group) > 1 else own[group[0]]
        prior.append(lax.ppermute(block, ("cx", "core"), ahead))
        layout += [(n, k * unit.shape[0]) for k in range(len(group))]
    layout += [(len(groups) + i, 0) for i in range(n_z)]
    pieces = prior + own

    gain = norm_gain[None]
    first = yhi == 0
    atts, rows = [], []
    for part in range(2):
        if part == 1:
            mine, _ = lax.optimization_barrier((mine, atts[0]))
        att, keep, away = attend(info, mine, got, pieces, layout, moves, part, heads, tok)
        atts.append(att)
        rows.append(norm_rows(info, mine, got, part, keep, swap(away, "yhi"), gain))
    own_att = jnp.where(first, atts[0], atts[1])
    away_att, rows[1] = lax.optimization_barrier((jnp.where(first, atts[1], atts[0]), rows[1]))
    other_att = swap(away_att, "yhi")

    signs = [1, -1]
    weights = assemble(info, wide_t, down, got_1, got_2, rows[1])
    rows = ring_gather(rows, signs, n_z)
    last = [-n_z // 2 * sign for sign in signs]
    early = [[m for m in g if m != l] for g, l in zip(rows, last)]
    keys = [(i, m) for i in range(2) for m in early[i]]
    first_out = experts([rows[i][m] for i, m in keys], weights)
    last_out = experts([rows[i][last[i]] for i in range(2)], weights, after=first_out[:1])
    outs = [{last[i]: last_out[i]} for i in range(2)]
    for (i, m), y in zip(keys, first_out):
        outs[i][m] = y
    sums = [ups.astype(jnp.float32) + downs + here for ups, downs, here in ring_scatter(outs, signs, n_z)]
    back = swap(jnp.where(first, sums[1], sums[0]).astype(jnp.bfloat16), "yhi")
    keep = jnp.where(first, sums[0], sums[1]).astype(jnp.bfloat16)
    return combine(info, hidden_in, own_att, other_att, keep, back, hot, factors)


def solution(mesh):
    sizes = {"cx": mesh.shape["ctx"] // 2, "core": 2, "yhi": 2, "z": mesh.shape["exp"] // 2, "dp": mesh.shape["dp"]}
    fine = Mesh(mesh.devices.reshape(tuple(sizes.values())), tuple(sizes))
    tokens = ("dp", "cx", "core", "yhi", "z")
    rows = P(tokens, None)
    hidden = ("yhi", "z")
    in_specs = (rows, rows, rows, P(tokens), rows, rows, P(), P(None, None, None, hidden), P(None, hidden, None))
    return jax.shard_map(
        functools.partial(body, sizes), mesh=fine, in_specs=in_specs, out_specs=rows, check_vma=False
    )
```

```python
import functools
import math

import jax
import jax.numpy as jnp
from jax import lax
from jax.experimental import pallas as pl
from jax.experimental.pallas import tpu as pltpu
from jax.sharding import Mesh
from jax.sharding import PartitionSpec as P

EXP_FLIGHT = 2
HD = 128
GROUP = 7
EXP2_SCALE = math.log2(math.e) / math.sqrt(HD)

def attend_kernel(info_ref, q_own_ref, q_got_ref, place_own_ref, place_got_ref, *refs, tok, span, moves, heads, layout, part):
    arrays, out_ref, low_ref, high_ref = refs[:-11], refs[-11], refs[-10], refs[-9]
    kv, ids, start_scr, m_scr, l_scr, acc_scr, bounds, sem = refs[-8:]
    c = pl.program_id(0)
    z = info_ref[0]
    half = len(moves) * tok
    near = pl.multiple_of(info_ref[1], half)
    far = pl.multiple_of(half - info_ref[1], half)
    first = pl.multiple_of(part * half + z * tok, tok)
    is_own = info_ref[2] == part

    @pl.when(c == 0)
    def _():
        blocks = []
        copies = []
        for n, (which, row) in enumerate(layout):
            piece = arrays[which]
            place = lax.rem(z + moves[n % len(moves)] + len(moves), len(moves)) * tok
            slab = n // len(moves) * 2 * half
            for side, base in ((0, near), (1, far)):
                at = pl.multiple_of(slab + base + place, tok)
                cp = pltpu.make_async_copy(piece.at[pl.ds(row + side * tok, tok)], kv.at[pl.ds(at, tok)], sem.at[n, side])
                blocks.append((cp, (at >= first) & (at <= first + 2 * half)))
            copies.append(pltpu.make_async_copy(piece.at[pl.ds(row + 2 * tok, 16)], ids.at[n], sem.at[n, 2]))
        for cp in copies:
            cp.start()
        for cp, needed in blocks:
            pl.when(needed)(cp.start)
        for cp in copies:
            cp.wait()
        own = [ids[len(moves), 0:1, n * tok:(n + 1) * tok].astype(jnp.float32) for n in range(2)]
        own = jnp.where(is_own, own[0], own[1])
        own = jnp.broadcast_to(own, (tok, tok)).T
        less = jnp.zeros((tok, tok), jnp.float32)
        for n in range(len(layout)):
            for side in range(2):
                row = ids[n, 0:1, side * tok:(side + 1) * tok].astype(jnp.float32)
                less = less + jnp.where(row < own, 1.0, 0.0)
        begin = jnp.sum(less, axis=1, keepdims=True)
        start_scr[...] = begin.astype(jnp.int32)
        bounds[0] = jnp.min(begin).astype(jnp.int32)
        bounds[1] = jnp.max(begin).astype(jnp.int32)
        for cp, needed in blocks:
            pl.when(needed)(cp.wait)

    start_min, start_max = bounds[0], bounds[1]
    q = jnp.where(is_own, q_own_ref[...], q_got_ref[...])
    q = jnp.concatenate([q[:, g * HD:(g + 1) * HD] for g in range(GROUP)], 0)
    start = start_scr[...]
    row = lax.broadcasted_iota(jnp.int32, (tok, 1), 0) + first + 2 * half
    key_col = pl.multiple_of(c * HD, HD)
    value_col = pl.multiple_of((heads + c) * HD, HD)

    def keys(offset, width):
        return kv[pl.ds(offset, width), pl.ds(key_col, HD)]

    def values(offset, width):
        return kv[pl.ds(offset, width), pl.ds(value_col, HD)]

    def scores(offset, width):
        return lax.dot_general(q, keys(offset, width), (((1,), (1,)), ((), ())), preferred_element_type=jnp.float32)

    def rowmax(s, width):
        t = s[:, :128]
        for j in range(1, width // 128):
            t = jnp.maximum(t, s[:, j * 128:(j + 1) * 128])
        return jnp.max(t, axis=1, keepdims=True)

    def lanesum(p, width):
        t = p[:, :128]
        for j in range(1, width // 128):
            t = t + p[:, j * 128:(j + 1) * 128]
        return t

    def masked(s, offset, width, causal):
        key = lax.broadcasted_iota(jnp.int32, (tok, width), 1) + offset
        ok = key >= start
        if causal:
            ok = ok & (key <= row)
        return jnp.where(ok[None], s.reshape(GROUP, tok, width), -1e30).reshape(GROUP * tok, width)

    own = pl.multiple_of(first + 2 * half, tok)
    s = masked(scores(own, tok), own, tok, True)
    m = rowmax(s, tok)
    p = jnp.exp2((s - m) * EXP2_SCALE)
    m_scr[...] = jnp.broadcast_to(m, m_scr.shape)
    l_scr[...] = lanesum(p, tok)
    acc_scr[...] = jnp.dot(p.astype(jnp.bfloat16), values(own, tok), preferred_element_type=jnp.float32)

    def step(i, mask):
        offset = pl.multiple_of(first + i * span, tok)
        s = scores(offset, span)
        if mask:
            s = masked(s, offset, span, False)
        old = m_scr[...]
        new = jnp.maximum(old, rowmax(s, span))
        m_scr[...] = new
        shrink = jnp.exp2((old - new) * EXP2_SCALE)
        p = jnp.exp2((s - jnp.concatenate([new] * (span // 128), 1)) * EXP2_SCALE)
        l_scr[...] = l_scr[...] * shrink + lanesum(p, span)
        acc_scr[...] = acc_scr[...] * shrink + jnp.dot(p.astype(jnp.bfloat16), values(offset, span), preferred_element_type=jnp.float32)

    steps = 2 * half // span

    def loop(i, carry):
        whole = start_max <= first + i * span

        @pl.when(whole)
        def _():
            step(i, False)

        @pl.when(jnp.logical_not(whole))
        def _():
            step(i, True)

        return carry

    lax.fori_loop(jnp.clip(lax.div(start_min - first, span), 0, steps), steps, loop, 0)

    total = jnp.sum(l_scr[...], axis=1, keepdims=True)
    att = (acc_scr[...] / total).astype(jnp.bfloat16)
    att = jnp.concatenate([att[g * tok:(g + 1) * tok] for g in range(GROUP)], 1)
    out_ref[...] = att
    place = jnp.where(is_own, place_own_ref[...], place_got_ref[...])
    rows = jnp.dot(place, att, preferred_element_type=jnp.float32).astype(jnp.bfloat16)
    low_ref[...] = rows[:rows.shape[0] // 2]
    high_ref[...] = rows[rows.shape[0] // 2:]


def attend(info, own, got, pieces, layout, moves, part, heads, tok, span=512):
    slots = tok // 4
    wide = GROUP * HD
    n = len(moves)
    hbm = pl.BlockSpec(memory_space=pl.ANY)
    scratch = pltpu.VMEM((GROUP * tok, 128), jnp.float32)
    return pl.pallas_call(
        functools.partial(attend_kernel, tok=tok, span=span, moves=moves, heads=heads, layout=layout, part=part),
        grid_spec=pltpu.PrefetchScalarGridSpec(
            num_scalar_prefetch=1,
            grid=(heads,),
            in_specs=[
                pl.BlockSpec((tok, wide), lambda c, s: (0, c)),
                pl.BlockSpec((tok, wide), lambda c, s: (0, c)),
                pl.BlockSpec((2 * slots, tok), lambda c, s: (tok // (2 * slots), heads * GROUP)),
                pl.BlockSpec((2 * slots, tok), lambda c, s: (tok // (2 * slots), heads * GROUP)),
            ] + [hbm] * len(pieces),
            out_specs=[pl.BlockSpec((r, wide), lambda c, s: (0, c)) for r in (tok, slots, slots)],
            scratch_shapes=[
                pltpu.VMEM((4 * n * tok, 2 * heads * HD), jnp.bfloat16),
                pltpu.VMEM((2 * n, 16, 2 * heads * HD), jnp.bfloat16),
                pltpu.VMEM((tok, 1), jnp.int32),
                scratch, scratch, scratch,
                pltpu.SMEM((2,), jnp.int32),
                pltpu.SemaphoreType.DMA((2 * n, 3)),
            ],
        ),
        out_shape=[jax.ShapeDtypeStruct((r, heads * wide), jnp.bfloat16) for r in (tok, slots, slots)],
        compiler_params=pltpu.CompilerParams(vmem_limit_bytes=60 << 20),
        cost_estimate=pl.CostEstimate(flops=8 * 10**9, bytes_accessed=5 << 20, transcendentals=4 * 10**6),
        name="attend",
    )(info, own, got, own, got, *pieces)


def prepare_kernel(info_ref, kv_ref, doc_ref, send_ref, mine_ref):
    tok = kv_ref.shape[0]
    w = kv_ref.shape[1] // 4
    send_ref[tok:, :] = jnp.zeros((16, 2 * w), send_ref.dtype)
    send_ref[tok:tok + 16, :tok] = jnp.broadcast_to((doc_ref[...] + 1).astype(jnp.float32), (16, tok)).astype(send_ref.dtype)
    for yhi in range(2):
        @pl.when(info_ref[2] == yhi)
        def _(yhi=yhi):
            away = 1 - yhi
            mine_ref[:, :w] = kv_ref[:, yhi * w:(yhi + 1) * w]
            mine_ref[:, w:] = kv_ref[:, (2 + yhi) * w:(3 + yhi) * w]
            send_ref[:tok, :w] = kv_ref[:, away * w:(away + 1) * w]
            send_ref[:tok, w:] = kv_ref[:, (2 + away) * w:(3 + away) * w]


def prepare(info, keys_values, doc_ids):
    tok, width = keys_values.shape
    vm = pl.BlockSpec(memory_space=pltpu.VMEM)
    shape = lambda r, c: jax.ShapeDtypeStruct((r, c), jnp.bfloat16)
    return pl.pallas_call(
        prepare_kernel,
        in_specs=[pl.BlockSpec(memory_space=pltpu.SMEM)] + [vm] * 2,
        out_specs=[vm] * 2,
        out_shape=[shape(tok + 16, width // 2), shape(tok, width // 2)],
        compiler_params=pltpu.CompilerParams(vmem_limit_bytes=24 << 20),
        name="prepare",
    )(info, keys_values, doc_ids[None])


def plan_kernel(info_ref, ids_ref, weights_ref, q_ref, hid_ref, out_ref, own_ref, hot_ref, factor_ref):
    tok = hid_ref.shape[0]
    slots = (out_ref.shape[0] - tok) // 2
    q = q_ref.shape[1] // 2
    yhi = info_ref[2]
    below = lax.broadcasted_iota(jnp.int32, (tok, tok), 0) <= lax.broadcasted_iota(jnp.int32, (tok, tok), 1)
    below = below.astype(jnp.float32).astype(jnp.bfloat16)
    places, factors = [], []
    for flight in (yhi, 1 - yhi):
        chosen = ids_ref[...] == flight
        routed = jnp.max(jnp.where(chosen, 1.0, 0.0), axis=0, keepdims=True)
        factors.append(jnp.sum(jnp.where(chosen, weights_ref[...], 0.0), axis=0, keepdims=True))
        ranks = jnp.dot(jnp.broadcast_to(routed, (16, tok)).astype(jnp.bfloat16), below, preferred_element_type=jnp.float32)
        ranks = jnp.where(routed > 0.5, ranks[:1] - 1.0, -1.0)
        slot = lax.broadcasted_iota(jnp.int32, (slots, tok), 0).astype(jnp.float32)
        places.append(jnp.where(slot == ranks, 1.0, 0.0))
    place_f = jnp.concatenate(places, 0)
    place = place_f.astype(jnp.bfloat16)
    hot_ref[...] = jnp.concatenate([place_f, jnp.zeros((tok - 2 * slots, tok), jnp.float32)], 0).T.astype(jnp.bfloat16)
    factor_ref[...] = jnp.concatenate([factors[0], factors[1], jnp.zeros((tok - 2, tok), jnp.float32)], 0).T
    rows = jnp.dot(place, hid_ref[...], preferred_element_type=jnp.float32).astype(jnp.bfloat16)
    for n, ref in enumerate((own_ref, out_ref)):
        ref[:tok, q:] = jnp.zeros((tok, tok), jnp.bfloat16)
        ref[tok:tok + slots, :q] = rows[n * slots:(n + 1) * slots, :q]
        ref[tok + slots:, :q] = rows[n * slots:(n + 1) * slots, q:]
        ref[tok:tok + slots, q:] = place[n * slots:(n + 1) * slots]
        ref[tok + slots:, q:] = place[(1 - n) * slots:(2 - n) * slots]

    for side in range(2):
        @pl.when(yhi == side)
        def _(side=side):
            own_ref[:tok, :q] = q_ref[:, side * q:(side + 1) * q]
            out_ref[:tok, :q] = q_ref[:, (1 - side) * q:(2 - side) * q]


def plan(info, route_ids, route_weights, queries, hidden):
    tok, d = hidden.shape
    slots = tok // 4
    vm = pl.BlockSpec(memory_space=pltpu.VMEM)
    shape = lambda r, c, t=jnp.bfloat16: jax.ShapeDtypeStruct((r, c), t)
    return pl.pallas_call(
        plan_kernel,
        in_specs=[pl.BlockSpec(memory_space=pltpu.SMEM)] + [vm] * 4,
        out_specs=[vm] * 4,
        out_shape=[shape(tok + 2 * slots, d // 2 + tok)] * 2 + [shape(tok, tok), shape(tok, tok, jnp.float32)],
        compiler_params=pltpu.CompilerParams(vmem_limit_bytes=24 << 20),
        name="plan",
    )(info, route_ids.T, route_weights.T, queries, hidden)


def join_kernel(send_ref, mine_ref, other_ref, unit_ref):
    tok = mine_ref.shape[0]
    unit_ref[:tok] = mine_ref[...]
    unit_ref[tok:2 * tok] = other_ref[:tok]
    unit_ref[2 * tok:] = send_ref[tok:]
    unit_ref[2 * tok:, tok:2 * tok] = other_ref[tok:, :tok]


def join(send, mine, other):
    tok, width = mine.shape
    vm = pl.BlockSpec(memory_space=pltpu.VMEM)
    return pl.pallas_call(
        join_kernel,
        in_specs=[vm] * 3,
        out_specs=vm,
        out_shape=jax.ShapeDtypeStruct((2 * tok + 16, width), mine.dtype),
        compiler_params=pltpu.CompilerParams(vmem_limit_bytes=24 << 20),
        name="join",
    )(send, mine, other)


def pack_kernel(info_ref, gu_ref, down_ref, out_ref, far_ref, sem):
    yhi = info_ref[2]
    away = 1 - yhi
    pick = jnp.where(info_ref[5] == 0, yhi, away)
    units = out_ref.shape[1]
    wide = far_ref.shape[2]
    at = pl.ds(pl.multiple_of(info_ref[3] * units, units), units)
    cols = pl.ds(pl.multiple_of(info_ref[4] * wide, wide), wide)
    cps = [
        pltpu.make_async_copy(gu_ref.at[away, :, at], out_ref.at[pl.ds(0, 2)], sem.at[0]),
        pltpu.make_async_copy(down_ref.at[away, at], out_ref.at[2], sem.at[1]),
        pltpu.make_async_copy(gu_ref.at[pick, :, at, cols], far_ref.at[pl.ds(0, 2)], sem.at[2]),
        pltpu.make_async_copy(down_ref.at[pick, at, cols], far_ref.at[2], sem.at[3]),
    ]
    for c in cps:
        c.start()
    for c in cps:
        c.wait()


def pack(info, wide_t, down, cores, columns):
    hbm = pl.BlockSpec(memory_space=pl.ANY)
    units, d = down.shape[1] // cores, down.shape[2]
    return pl.pallas_call(
        pack_kernel,
        in_specs=[pl.BlockSpec(memory_space=pltpu.SMEM), hbm, hbm],
        out_specs=[pl.BlockSpec(memory_space=pltpu.VMEM)] * 2,
        out_shape=[jax.ShapeDtypeStruct((3, units, d), down.dtype), jax.ShapeDtypeStruct((3, units, d // columns), down.dtype)],
        scratch_shapes=[pltpu.SemaphoreType.DMA((4,))],
        compiler_params=pltpu.CompilerParams(vmem_limit_bytes=60 << 20),
        name="pack",
    )(info, wide_t, down)


def norm_kernel(info_ref, own_ref, got_ref, mine_ref, other_ref, gain_ref, out_ref, *, part):
    slots, half = mine_ref.shape
    tok = own_ref.shape[0] - 2 * slots
    is_own = info_ref[2] == part

    def put(low, high):
        parts = []
        for n, att in enumerate((low, high)):
            rows = slice(tok + n * slots, tok + (n + 1) * slots)
            base = jnp.where(is_own, own_ref[rows, :half], got_ref[rows, :half]).astype(jnp.float32)
            parts.append((base + att.astype(jnp.float32)).astype(jnp.bfloat16).astype(jnp.float32))
        total = sum(jnp.sum(p * p, axis=1, keepdims=True) for p in parts)
        inv = lax.rsqrt(total / (2 * half) + 1e-6)
        for n, p in enumerate(parts):
            gain = gain_ref[:, n * half:(n + 1) * half].astype(jnp.float32)
            out_ref[:, n * half:(n + 1) * half] = (p * inv * gain).astype(jnp.bfloat16)

    @pl.when(info_ref[2] == 0)
    def _():
        put(mine_ref[...], other_ref[...])

    @pl.when(info_ref[2] != 0)
    def _():
        put(other_ref[...], mine_ref[...])


def norm_rows(info, own, got, part, mine, other, gain):
    slots, half = mine.shape
    vm = pl.BlockSpec(memory_space=pltpu.VMEM)
    return pl.pallas_call(
        functools.partial(norm_kernel, part=part),
        in_specs=[pl.BlockSpec(memory_space=pltpu.SMEM)] + [vm] * 5,
        out_specs=vm,
        out_shape=jax.ShapeDtypeStruct((slots, 2 * half), jnp.bfloat16),
        compiler_params=pltpu.CompilerParams(vmem_limit_bytes=16 << 20),
        name="norm_rows",
    )(info, own, got, mine, other, gain)


def assemble_kernel(info_ref, wo_ref, do_ref, r1_ref, r2_ref, *refs, steps):
    count = 2 * len(steps)
    blocks, w_ref, sem = refs[:count], refs[-2], refs[-1]
    yhi = info_ref[2]
    n, h = wo_ref.shape[2], r1_ref.shape[1]
    cps = []

    def cp(src, dst):
        cps.append(pltpu.make_async_copy(src, dst, sem.at[len(cps)]))

    for i in range(3):
        own = do_ref.at[yhi] if i == 2 else wo_ref.at[yhi, i]
        for src, at, size in ((own, 0, n), (r1_ref.at[i], n, h), (r2_ref.at[i], n + h, h)):
            cp(src, w_ref.at[i, pl.ds(at, size)])
        for k, block in enumerate(blocks):
            core, step = divmod(k, len(steps))
            wide = block.shape[2]
            col = lax.rem(info_ref[4] + steps[step] + len(steps), len(steps)) * wide
            for u in range(2):
                at = n + 2 * h + (2 * core + u) * h
                cp(block.at[3 * u + i], w_ref.at[i, pl.ds(at, h), pl.ds(pl.multiple_of(col, wide), wide)])
    for c in cps:
        c.start()
    for c in cps:
        c.wait()


def assemble(info, wo, do, r1, r2, blocks, steps, after):
    n, d = 2 * (wo.shape[2] + r1.shape[1] + r2.shape[1]), wo.shape[3]
    hbm = pl.BlockSpec(memory_space=pl.ANY)
    return pl.pallas_call(
        functools.partial(assemble_kernel, steps=steps),
        in_specs=[pl.BlockSpec(memory_space=pltpu.SMEM)] + [hbm] * (5 + len(blocks)),
        out_specs=pl.BlockSpec(memory_space=pltpu.VMEM),
        scratch_shapes=[pltpu.SemaphoreType.DMA((9 + 6 * len(blocks),))],
        out_shape=jax.ShapeDtypeStruct((3, n, d), jnp.bfloat16),
        compiler_params=pltpu.CompilerParams(vmem_limit_bytes=20 << 20),
        cost_estimate=pl.CostEstimate(flops=0, bytes_accessed=6 * n * d, transcendentals=0),
        name="assemble",
    )(info, wo, do, r1, r2, *blocks, after)


def expert_kernel(*refs, count, rows, after):
    xs, w_ref, ys = refs[:count], refs[count], refs[count + 1 + after:]
    x = jnp.concatenate([r[...] for r in xs], 0)
    nt = (((1,), (1,)), ((), ()))
    gate = lax.dot_general(x, w_ref[0], nt, preferred_element_type=jnp.float32)
    up = lax.dot_general(x, w_ref[1], nt, preferred_element_type=jnp.float32)
    inner = (gate / (1 + jnp.exp(-gate)) * up).astype(jnp.bfloat16)
    y = jnp.dot(inner, w_ref[2], preferred_element_type=jnp.float32).astype(jnp.bfloat16)
    for i in range(count):
        ys[i][...] = y[i * rows:(i + 1) * rows]


def experts(xs, w, after=()):
    count = len(xs)
    rows, d = xs[0].shape
    n = w.shape[1]
    vm = pl.BlockSpec(memory_space=pltpu.VMEM)
    return pl.pallas_call(
        functools.partial(expert_kernel, count=count, rows=rows, after=len(after)),
        in_specs=[vm] * (count + 1) + [pl.BlockSpec(memory_space=pl.ANY)] * len(after),
        out_specs=[vm] * count,
        out_shape=[jax.ShapeDtypeStruct((rows, d), jnp.bfloat16)] * count,
        compiler_params=pltpu.CompilerParams(vmem_limit_bytes=26 << 20),
        cost_estimate=pl.CostEstimate(flops=20 * count * rows * n * d, bytes_accessed=2 * (3 * n * d + 2 * count * rows * d), transcendentals=count * rows * n),
        name="experts",
    )(*xs, w, *after)


def combine_kernel(info_ref, hid_ref, mine_ref, other_ref, keep_ref, back_ref, hot_ref, factor_ref, out_ref):
    cap = back_ref.shape[0]
    is_mine = pl.program_id(0) // 2 == info_ref[2]
    att = jnp.where(is_mine, mine_ref[...].astype(jnp.float32), other_ref[...].astype(jnp.float32))
    stream = (hid_ref[...].astype(jnp.float32) + att).astype(jnp.bfloat16).astype(jnp.float32)
    one = jnp.dot(hot_ref[:, :cap], keep_ref[...], preferred_element_type=jnp.float32)
    two = jnp.dot(hot_ref[:, cap:2 * cap], back_ref[...], preferred_element_type=jnp.float32)
    out_ref[...] = (stream + one * factor_ref[:, 0:1] + two * factor_ref[:, 1:2]).astype(out_ref.dtype)


def combine(info, hidden, mine, other, keep, back, hot, factors):
    tok, d = hidden.shape
    cap = back.shape[0]
    wide = d // 4
    cols = lambda rows: pl.BlockSpec((rows, wide), lambda c, s: (0, c))
    half = pl.BlockSpec((tok, wide), lambda c, s: (0, lax.rem(c, 2)))
    whole = pl.BlockSpec((tok, tok), lambda c, s: (0, 0))
    return pl.pallas_call(
        combine_kernel,
        grid_spec=pltpu.PrefetchScalarGridSpec(
            num_scalar_prefetch=1,
            grid=(4,),
            in_specs=[cols(tok), half, half, cols(cap), cols(cap), whole, whole],
            out_specs=cols(tok),
        ),
        out_shape=jax.ShapeDtypeStruct((tok, d), hidden.dtype),
        compiler_params=pltpu.CompilerParams(vmem_limit_bytes=24 << 20),
        name="combine",
    )(info, hidden, mine, other, keep, back, hot, factors)


def shift(value, axis, size, steps):
    return lax.ppermute(value, axis, [(i, (i + steps) % size) for i in range(size)])


def swap(value, axis):
    return shift(value, axis, 2, 1)


def ring_moves(size):
    out = [0]
    for s in range(1, size // 2 + 1):
        out.append(-s)
        if 2 * s < size:
            out.append(s)
    return out


def ring_scatter(parts, signs, size):
    ups = [p[-2 * sign] for p, sign in zip(parts, signs)]
    downs = [shift(p[sign], "z", size, sign) for p, sign in zip(parts, signs)]
    for i, (p, sign) in enumerate(zip(parts, signs)):
        ups[i] = shift(ups[i], "z", size, -sign) + p[-sign]
    ups = [shift(u, "z", size, -sign) for u, sign in zip(ups, signs)]
    return [(ups[i], downs[i], p[0]) for i, p in enumerate(parts)]


def body(sizes, hidden_in, queries, keys_values, doc_ids, route_ids, route_weights, norm_gain, gate_up, down):
    tok, d = queries.shape
    capacity = tok // 4
    n_z, n_core, n_cx = sizes["z"], sizes["core"], sizes["cx"]
    yhi, z, core = lax.axis_index("yhi"), lax.axis_index("z"), lax.axis_index("core")
    half = n_z * tok
    n_ctx = n_cx * n_core
    moves = ring_moves(n_z)
    heads = keys_values.shape[1] // (4 * HD)
    cx, dp = lax.axis_index("cx"), lax.axis_index("dp")
    info = jnp.stack([z, yhi * half, yhi, core, cx, dp]).astype(jnp.int32)

    send, kept = prepare(info, keys_values, doc_ids)
    unit = join(send, kept, swap(send, "yhi"))

    out, mine, hot, factors = plan(info, route_ids, route_weights, queries, hidden_in)
    wide_t = jnp.swapaxes(gate_up, 2, 3)
    theirs, far = pack(info, wide_t, down, n_core, n_cx)
    out, far, unit = lax.optimization_barrier((out, far, unit))
    got = swap(out, "yhi")
    place = lambda y, k, l: (y * n_z + k) * 2 + l
    across = [
        (place(y, k, l), place(y if l == 0 else 1 - y, (k + n_z // 2) % n_z, l)) for y in range(2) for k in range(n_z) for l in range(2)
    ]
    far = lax.ppermute(far, ("yhi", "z", "dp"), across)
    own = {0: unit}
    for s in range(1, n_z // 2 + 1):
        own[-s] = shift(own[1 - s], "z", n_z, 1)
        if 2 * s < n_z:
            own[s] = shift(own[s - 1], "z", n_z, -1)
        if s == 2:
            own[-s], got, theirs = lax.optimization_barrier((own[-s], got, theirs))
        if s == 3:
            own[-s], far = lax.optimization_barrier((own[-s], far))
    got_1 = swap(theirs, "yhi")
    got_2 = swap(got_1, "core")
    share = jnp.concatenate([far, swap(far, "dp")], 0)
    own = [own[m] for m in moves]
    ahead = [(i, i + 1) for i in range(n_ctx - 1)]
    groups = [range(0, 1), range(1, n_z // 2 + 1), range(n_z // 2 + 1, n_z - 1), range(n_z - 1, n_z)]
    prior, layout = [], []
    for n, group in enumerate(groups):
        block = jnp.concatenate([own[i] for i in group], 0) if len(group) > 1 else own[group[0]]
        prior.append(lax.ppermute(block, ("cx", "core"), ahead))
        layout += [(n, k * unit.shape[0]) for k in range(len(group))]
    layout += [(len(groups) + i, 0) for i in range(n_z)]
    pieces = prior + own

    gain = norm_gain[None]
    first = yhi == 0
    atts, rows = [], []
    mine, share = lax.optimization_barrier((mine, share))
    steps = [0, -1, 1, 2]
    shares = [share, shift(share, "cx", n_cx, 1), shift(share, "cx", n_cx, -1)]
    for part in range(2):
        if part == 1:
            mine, shares[2], _ = lax.optimization_barrier((mine, shares[2], atts[0]))
            shares.append(shift(shares[2], "cx", n_cx, -1))
        att, keep, away = attend(info, mine, got, pieces, layout, moves, part, heads, tok)
        atts.append(att)
        rows.append(norm_rows(info, mine, got, part, keep, swap(away, "yhi"), gain))
    own_att = jnp.where(first, atts[0], atts[1])
    away_att, rows[1] = lax.optimization_barrier((jnp.where(first, atts[1], atts[0]), rows[1]))
    other_att = swap(away_att, "yhi")

    signs = [1, -1]
    rows = [{0: x, -sign: shift(x, "z", n_z, sign), sign: shift(x, "z", n_z, -sign)} for x, sign in zip(rows, signs)]
    rows[1][1], shares[3] = lax.optimization_barrier((rows[1][1], shares[3]))
    for g, sign in zip(rows, signs):
        g[-2 * sign] = shift(g[-sign], "z", n_z, sign)
    blocks = shares + [swap(x, "core") for x in shares]
    weights = assemble(info, wide_t, down, got_1, got_2, blocks, steps, rows[1][0])
    keys = [(i, m) for i in range(2) for m in (0, -1, 1)]
    first_out = experts([rows[i][m] for i, m in keys], weights)
    last_out = experts([g[-2 * sign] for g, sign in zip(rows, signs)], weights, after=first_out[:1])
    outs = [{-2 * sign: y} for sign, y in zip(signs, last_out)]
    for (i, m), y in zip(keys, first_out):
        outs[i][m] = y
    sums = [ups.astype(jnp.float32) + downs + here for ups, downs, here in ring_scatter(outs, signs, n_z)]
    back = swap(jnp.where(first, sums[1], sums[0]).astype(jnp.bfloat16), "yhi")
    keep = jnp.where(first, sums[0], sums[1]).astype(jnp.bfloat16)
    return combine(info, hidden_in, own_att, other_att, keep, back, hot, factors)


def solution(mesh):
    sizes = {"cx": mesh.shape["ctx"] // 2, "core": 2, "yhi": 2, "z": mesh.shape["exp"] // 2, "dp": mesh.shape["dp"]}
    fine = Mesh(mesh.devices.reshape(tuple(sizes.values())), tuple(sizes))
    tokens = ("dp", "cx", "core", "yhi", "z")
    rows = P(tokens, None)
    hidden = ("yhi", "z")
    in_specs = (rows, rows, rows, P(tokens), rows, rows, P(), P(None, None, None, hidden), P(None, hidden, None))
    return jax.shard_map(
        functools.partial(body, sizes), mesh=fine, in_specs=in_specs, out_specs=rows, check_vma=False
    )
```

```python
import functools
import math

import jax
import jax.numpy as jnp
from jax import lax
from jax.experimental import pallas as pl
from jax.experimental.pallas import tpu as pltpu
from jax.sharding import Mesh
from jax.sharding import PartitionSpec as P

EXP_FLIGHT = 2
HD = 128
GROUP = 7
EXP2_SCALE = math.log2(math.e) / math.sqrt(HD)

def attend_kernel(info_ref, q_own_ref, q_got_ref, place_own_ref, place_got_ref, *refs, tok, span, moves, heads, layout, part):
    arrays, out_ref, low_ref, high_ref = refs[:-11], refs[-11], refs[-10], refs[-9]
    kv, ids, start_scr, m_scr, l_scr, acc_scr, bounds, sem = refs[-8:]
    c = pl.program_id(0)
    z = info_ref[0]
    half = len(moves) * tok
    near = pl.multiple_of(info_ref[1], half)
    far = pl.multiple_of(half - info_ref[1], half)
    first = pl.multiple_of(part * half + z * tok, tok)
    is_own = info_ref[2] == part

    @pl.when(c == 0)
    def _():
        blocks = []
        copies = []
        for n, (which, row) in enumerate(layout):
            piece = arrays[which]
            place = lax.rem(z + moves[n % len(moves)] + len(moves), len(moves)) * tok
            slab = n // len(moves) * 2 * half
            for side, base in ((0, near), (1, far)):
                at = pl.multiple_of(slab + base + place, tok)
                cp = pltpu.make_async_copy(piece.at[pl.ds(row + side * tok, tok)], kv.at[pl.ds(at, tok)], sem.at[n, side])
                blocks.append((cp, (at >= first) & (at <= first + 2 * half)))
            copies.append(pltpu.make_async_copy(piece.at[pl.ds(row + 2 * tok, 16)], ids.at[n], sem.at[n, 2]))
        for cp in copies:
            cp.start()
        for cp, needed in blocks:
            pl.when(needed)(cp.start)
        for cp in copies:
            cp.wait()
        own = [ids[len(moves), 0:1, n * tok:(n + 1) * tok].astype(jnp.float32) for n in range(2)]
        own = jnp.where(is_own, own[0], own[1])
        own = jnp.broadcast_to(own, (tok, tok)).T
        less = jnp.zeros((tok, tok), jnp.float32)
        for n in range(len(layout)):
            for side in range(2):
                row = ids[n, 0:1, side * tok:(side + 1) * tok].astype(jnp.float32)
                less = less + jnp.where(row < own, 1.0, 0.0)
        begin = jnp.sum(less, axis=1, keepdims=True)
        start_scr[...] = begin.astype(jnp.int32)
        bounds[0] = jnp.min(begin).astype(jnp.int32)
        bounds[1] = jnp.max(begin).astype(jnp.int32)
        for cp, needed in blocks:
            pl.when(needed)(cp.wait)

    start_min, start_max = bounds[0], bounds[1]
    q = jnp.where(is_own, q_own_ref[...], q_got_ref[...])
    q = jnp.concatenate([q[:, g * HD:(g + 1) * HD] for g in range(GROUP)], 0)
    start = start_scr[...]
    row = lax.broadcasted_iota(jnp.int32, (tok, 1), 0) + first + 2 * half
    key_col = pl.multiple_of(c * HD, HD)
    value_col = pl.multiple_of((heads + c) * HD, HD)

    def keys(offset, width):
        return kv[pl.ds(offset, width), pl.ds(key_col, HD)]

    def values(offset, width):
        return kv[pl.ds(offset, width), pl.ds(value_col, HD)]

    def scores(offset, width):
        return lax.dot_general(q, keys(offset, width), (((1,), (1,)), ((), ())), preferred_element_type=jnp.float32)

    def rowmax(s, width):
        t = s[:, :128]
        for j in range(1, width // 128):
            t = jnp.maximum(t, s[:, j * 128:(j + 1) * 128])
        return jnp.max(t, axis=1, keepdims=True)

    def lanesum(p, width):
        t = p[:, :128]
        for j in range(1, width // 128):
            t = t + p[:, j * 128:(j + 1) * 128]
        return t

    def masked(s, offset, width, causal):
        key = lax.broadcasted_iota(jnp.int32, (tok, width), 1) + offset
        ok = key >= start
        if causal:
            ok = ok & (key <= row)
        return jnp.where(ok[None], s.reshape(GROUP, tok, width), -1e30).reshape(GROUP * tok, width)

    own = pl.multiple_of(first + 2 * half, tok)
    s = masked(scores(own, tok), own, tok, True)
    m = rowmax(s, tok)
    p = jnp.exp2((s - m) * EXP2_SCALE)
    m_scr[...] = jnp.broadcast_to(m, m_scr.shape)
    l_scr[...] = lanesum(p, tok)
    acc_scr[...] = jnp.dot(p.astype(jnp.bfloat16), values(own, tok), preferred_element_type=jnp.float32)

    def step(i, mask):
        offset = pl.multiple_of(first + i * span, tok)
        s = scores(offset, span)
        if mask:
            s = masked(s, offset, span, False)
        old = m_scr[...]
        new = jnp.maximum(old, rowmax(s, span))
        m_scr[...] = new
        shrink = jnp.exp2((old - new) * EXP2_SCALE)
        p = jnp.exp2((s - jnp.concatenate([new] * (span // 128), 1)) * EXP2_SCALE)
        l_scr[...] = l_scr[...] * shrink + lanesum(p, span)
        acc_scr[...] = acc_scr[...] * shrink + jnp.dot(p.astype(jnp.bfloat16), values(offset, span), preferred_element_type=jnp.float32)

    steps = 2 * half // span

    def loop(i, carry):
        whole = start_max <= first + i * span

        @pl.when(whole)
        def _():
            step(i, False)

        @pl.when(jnp.logical_not(whole))
        def _():
            step(i, True)

        return carry

    lax.fori_loop(jnp.clip(lax.div(start_min - first, span), 0, steps), steps, loop, 0)

    total = jnp.sum(l_scr[...], axis=1, keepdims=True)
    att = (acc_scr[...] / total).astype(jnp.bfloat16)
    att = jnp.concatenate([att[g * tok:(g + 1) * tok] for g in range(GROUP)], 1)
    out_ref[...] = att
    place = jnp.where(is_own, place_own_ref[...], place_got_ref[...])
    rows = jnp.dot(place, att, preferred_element_type=jnp.float32).astype(jnp.bfloat16)
    low_ref[...] = rows[:rows.shape[0] // 2]
    high_ref[...] = rows[rows.shape[0] // 2:]


def attend(info, own, got, pieces, layout, moves, part, heads, tok, span=512):
    slots = tok // 4
    wide = GROUP * HD
    n = len(moves)
    hbm = pl.BlockSpec(memory_space=pl.ANY)
    scratch = pltpu.VMEM((GROUP * tok, 128), jnp.float32)
    return pl.pallas_call(
        functools.partial(attend_kernel, tok=tok, span=span, moves=moves, heads=heads, layout=layout, part=part),
        grid_spec=pltpu.PrefetchScalarGridSpec(
            num_scalar_prefetch=1,
            grid=(heads,),
            in_specs=[
                pl.BlockSpec((tok, wide), lambda c, s: (0, c)),
                pl.BlockSpec((tok, wide), lambda c, s: (0, c)),
                pl.BlockSpec((2 * slots, tok), lambda c, s: (tok // (2 * slots), heads * GROUP)),
                pl.BlockSpec((2 * slots, tok), lambda c, s: (tok // (2 * slots), heads * GROUP)),
            ] + [hbm] * len(pieces),
            out_specs=[pl.BlockSpec((r, wide), lambda c, s: (0, c)) for r in (tok, slots, slots)],
            scratch_shapes=[
                pltpu.VMEM((4 * n * tok, 2 * heads * HD), jnp.bfloat16),
                pltpu.VMEM((2 * n, 16, 2 * heads * HD), jnp.bfloat16),
                pltpu.VMEM((tok, 1), jnp.int32),
                scratch, scratch, scratch,
                pltpu.SMEM((2,), jnp.int32),
                pltpu.SemaphoreType.DMA((2 * n, 3)),
            ],
        ),
        out_shape=[jax.ShapeDtypeStruct((r, heads * wide), jnp.bfloat16) for r in (tok, slots, slots)],
        compiler_params=pltpu.CompilerParams(vmem_limit_bytes=60 << 20),
        cost_estimate=pl.CostEstimate(flops=8 * 10**9, bytes_accessed=5 << 20, transcendentals=4 * 10**6),
        name="attend",
    )(info, own, got, own, got, *pieces)


def prepare_kernel(info_ref, kv_ref, doc_ref, send_ref, mine_ref):
    tok = kv_ref.shape[0]
    w = kv_ref.shape[1] // 4
    send_ref[tok:, :] = jnp.zeros((16, 2 * w), send_ref.dtype)
    send_ref[tok:tok + 16, :tok] = jnp.broadcast_to((doc_ref[...] + 1).astype(jnp.float32), (16, tok)).astype(send_ref.dtype)
    for yhi in range(2):
        @pl.when(info_ref[2] == yhi)
        def _(yhi=yhi):
            away = 1 - yhi
            mine_ref[:, :w] = kv_ref[:, yhi * w:(yhi + 1) * w]
            mine_ref[:, w:] = kv_ref[:, (2 + yhi) * w:(3 + yhi) * w]
            send_ref[:tok, :w] = kv_ref[:, away * w:(away + 1) * w]
            send_ref[:tok, w:] = kv_ref[:, (2 + away) * w:(3 + away) * w]


def prepare(info, keys_values, doc_ids):
    tok, width = keys_values.shape
    vm = pl.BlockSpec(memory_space=pltpu.VMEM)
    shape = lambda r, c: jax.ShapeDtypeStruct((r, c), jnp.bfloat16)
    return pl.pallas_call(
        prepare_kernel,
        in_specs=[pl.BlockSpec(memory_space=pltpu.SMEM)] + [vm] * 2,
        out_specs=[vm] * 2,
        out_shape=[shape(tok + 16, width // 2), shape(tok, width // 2)],
        compiler_params=pltpu.CompilerParams(vmem_limit_bytes=24 << 20),
        name="prepare",
    )(info, keys_values, doc_ids[None])


def plan_kernel(info_ref, ids_ref, weights_ref, q_ref, hid_ref, out_ref, own_ref, hot_ref, factor_ref):
    tok = hid_ref.shape[0]
    slots = (out_ref.shape[0] - tok) // 2
    q = q_ref.shape[1] // 2
    yhi = info_ref[2]
    below = lax.broadcasted_iota(jnp.int32, (tok, tok), 0) <= lax.broadcasted_iota(jnp.int32, (tok, tok), 1)
    below = below.astype(jnp.float32).astype(jnp.bfloat16)
    places, factors = [], []
    for flight in (yhi, 1 - yhi):
        chosen = ids_ref[...] == flight
        routed = jnp.max(jnp.where(chosen, 1.0, 0.0), axis=0, keepdims=True)
        factors.append(jnp.sum(jnp.where(chosen, weights_ref[...], 0.0), axis=0, keepdims=True))
        ranks = jnp.dot(jnp.broadcast_to(routed, (16, tok)).astype(jnp.bfloat16), below, preferred_element_type=jnp.float32)
        ranks = jnp.where(routed > 0.5, ranks[:1] - 1.0, -1.0)
        slot = lax.broadcasted_iota(jnp.int32, (slots, tok), 0).astype(jnp.float32)
        places.append(jnp.where(slot == ranks, 1.0, 0.0))
    place_f = jnp.concatenate(places, 0)
    place = place_f.astype(jnp.bfloat16)
    hot_ref[...] = jnp.concatenate([place_f, jnp.zeros((tok - 2 * slots, tok), jnp.float32)], 0).T.astype(jnp.bfloat16)
    factor_ref[...] = jnp.concatenate([factors[0], factors[1], jnp.zeros((tok - 2, tok), jnp.float32)], 0).T
    rows = jnp.dot(place, hid_ref[...], preferred_element_type=jnp.float32).astype(jnp.bfloat16)
    for n, ref in enumerate((own_ref, out_ref)):
        ref[:tok, q:] = jnp.zeros((tok, tok), jnp.bfloat16)
        ref[tok:tok + slots, :q] = rows[n * slots:(n + 1) * slots, :q]
        ref[tok + slots:, :q] = rows[n * slots:(n + 1) * slots, q:]
        ref[tok:tok + slots, q:] = place[n * slots:(n + 1) * slots]
        ref[tok + slots:, q:] = place[(1 - n) * slots:(2 - n) * slots]

    for side in range(2):
        @pl.when(yhi == side)
        def _(side=side):
            own_ref[:tok, :q] = q_ref[:, side * q:(side + 1) * q]
            out_ref[:tok, :q] = q_ref[:, (1 - side) * q:(2 - side) * q]


def plan(info, route_ids, route_weights, queries, hidden):
    tok, d = hidden.shape
    slots = tok // 4
    vm = pl.BlockSpec(memory_space=pltpu.VMEM)
    shape = lambda r, c, t=jnp.bfloat16: jax.ShapeDtypeStruct((r, c), t)
    return pl.pallas_call(
        plan_kernel,
        in_specs=[pl.BlockSpec(memory_space=pltpu.SMEM)] + [vm] * 4,
        out_specs=[vm] * 4,
        out_shape=[shape(tok + 2 * slots, d // 2 + tok)] * 2 + [shape(tok, tok), shape(tok, tok, jnp.float32)],
        compiler_params=pltpu.CompilerParams(vmem_limit_bytes=24 << 20),
        name="plan",
    )(info, route_ids.T, route_weights.T, queries, hidden)


def join_kernel(send_ref, mine_ref, other_ref, unit_ref):
    tok = mine_ref.shape[0]
    unit_ref[:tok] = mine_ref[...]
    unit_ref[tok:2 * tok] = other_ref[:tok]
    unit_ref[2 * tok:] = send_ref[tok:]
    unit_ref[2 * tok:, tok:2 * tok] = other_ref[tok:, :tok]


def join(send, mine, other):
    tok, width = mine.shape
    vm = pl.BlockSpec(memory_space=pltpu.VMEM)
    return pl.pallas_call(
        join_kernel,
        in_specs=[vm] * 3,
        out_specs=vm,
        out_shape=jax.ShapeDtypeStruct((2 * tok + 16, width), mine.dtype),
        compiler_params=pltpu.CompilerParams(vmem_limit_bytes=24 << 20),
        name="join",
    )(send, mine, other)


def pack_kernel(info_ref, gu_ref, down_ref, out_ref, sem):
    yhi = info_ref[2]
    units, wide = out_ref.shape[1], out_ref.shape[2]
    at = pl.ds(pl.multiple_of(info_ref[3] * units, units), units)
    if wide == down_ref.shape[2]:
        away, cols = 1 - yhi, pl.ds(0, wide)
    else:
        away = jnp.where(info_ref[5] == 0, yhi, 1 - yhi)
        cols = pl.ds(pl.multiple_of(info_ref[4] * wide, wide), wide)
    one = pltpu.make_async_copy(gu_ref.at[away, :, at, cols], out_ref.at[pl.ds(0, 2)], sem.at[0])
    two = pltpu.make_async_copy(down_ref.at[away, at, cols], out_ref.at[2], sem.at[1])
    one.start()
    two.start()
    one.wait()
    two.wait()


def pack(info, wide_t, down, cores, columns):
    hbm = pl.BlockSpec(memory_space=pl.ANY)
    units, d = down.shape[1] // cores, down.shape[2]
    return pl.pallas_call(
        pack_kernel,
        in_specs=[pl.BlockSpec(memory_space=pltpu.SMEM), hbm, hbm],
        out_specs=pl.BlockSpec(memory_space=pltpu.VMEM),
        out_shape=jax.ShapeDtypeStruct((3, units, d // columns), down.dtype),
        scratch_shapes=[pltpu.SemaphoreType.DMA((2,))],
        compiler_params=pltpu.CompilerParams(vmem_limit_bytes=60 << 20),
        name="pack",
    )(info, wide_t, down)


def norm_kernel(info_ref, own_ref, got_ref, mine_ref, other_ref, gain_ref, out_ref, *, part):
    slots, half = mine_ref.shape
    tok = own_ref.shape[0] - 2 * slots
    is_own = info_ref[2] == part

    def put(low, high):
        parts = []
        for n, att in enumerate((low, high)):
            rows = slice(tok + n * slots, tok + (n + 1) * slots)
            base = jnp.where(is_own, own_ref[rows, :half], got_ref[rows, :half]).astype(jnp.float32)
            parts.append((base + att.astype(jnp.float32)).astype(jnp.bfloat16).astype(jnp.float32))
        total = sum(jnp.sum(p * p, axis=1, keepdims=True) for p in parts)
        inv = lax.rsqrt(total / (2 * half) + 1e-6)
        for n, p in enumerate(parts):
            gain = gain_ref[:, n * half:(n + 1) * half].astype(jnp.float32)
            out_ref[:, n * half:(n + 1) * half] = (p * inv * gain).astype(jnp.bfloat16)

    @pl.when(info_ref[2] == 0)
    def _():
        put(mine_ref[...], other_ref[...])

    @pl.when(info_ref[2] != 0)
    def _():
        put(other_ref[...], mine_ref[...])


def norm_rows(info, own, got, part, mine, other, gain):
    slots, half = mine.shape
    vm = pl.BlockSpec(memory_space=pltpu.VMEM)
    return pl.pallas_call(
        functools.partial(norm_kernel, part=part),
        in_specs=[pl.BlockSpec(memory_space=pltpu.SMEM)] + [vm] * 5,
        out_specs=vm,
        out_shape=jax.ShapeDtypeStruct((slots, 2 * half), jnp.bfloat16),
        compiler_params=pltpu.CompilerParams(vmem_limit_bytes=16 << 20),
        name="norm_rows",
    )(info, own, got, mine, other, gain)


def assemble_kernel(info_ref, wo_ref, do_ref, r1_ref, r2_ref, *refs, steps):
    count = 2 * len(steps)
    blocks, w_ref, sem = refs[:count], refs[-2], refs[-1]
    yhi = info_ref[2]
    n, h = wo_ref.shape[2], r1_ref.shape[1]
    cps = []

    def cp(src, dst):
        cps.append(pltpu.make_async_copy(src, dst, sem.at[len(cps)]))

    for i in range(3):
        own = do_ref.at[yhi] if i == 2 else wo_ref.at[yhi, i]
        for src, at, size in ((own, 0, n), (r1_ref.at[i], n, h), (r2_ref.at[i], n + h, h)):
            cp(src, w_ref.at[i, pl.ds(at, size)])
        for k, block in enumerate(blocks):
            core, step = divmod(k, len(steps))
            wide = block.shape[2]
            col = lax.rem(info_ref[4] + steps[step] + len(steps), len(steps)) * wide
            for u in range(2):
                at = n + 2 * h + (2 * core + u) * h
                cp(block.at[3 * u + i], w_ref.at[i, pl.ds(at, h), pl.ds(pl.multiple_of(col, wide), wide)])
    for c in cps:
        c.start()
    for c in cps:
        c.wait()


def assemble(info, wo, do, r1, r2, blocks, steps, after):
    n, d = 2 * (wo.shape[2] + r1.shape[1] + r2.shape[1]), wo.shape[3]
    hbm = pl.BlockSpec(memory_space=pl.ANY)
    return pl.pallas_call(
        functools.partial(assemble_kernel, steps=steps),
        in_specs=[pl.BlockSpec(memory_space=pltpu.SMEM)] + [hbm] * (5 + len(blocks)),
        out_specs=pl.BlockSpec(memory_space=pltpu.VMEM),
        scratch_shapes=[pltpu.SemaphoreType.DMA((9 + 6 * len(blocks),))],
        out_shape=jax.ShapeDtypeStruct((3, n, d), jnp.bfloat16),
        compiler_params=pltpu.CompilerParams(vmem_limit_bytes=46 << 20),
        cost_estimate=pl.CostEstimate(flops=0, bytes_accessed=6 * n * d, transcendentals=0),
        name="assemble",
    )(info, wo, do, r1, r2, *blocks, after)


def expert_kernel(*refs, count, rows, after):
    xs, w_ref, ys = refs[:count], refs[count], refs[count + 1 + after:]
    x = jnp.concatenate([r[...] for r in xs], 0)
    nt = (((1,), (1,)), ((), ()))
    gate = lax.dot_general(x, w_ref[0], nt, preferred_element_type=jnp.float32)
    up = lax.dot_general(x, w_ref[1], nt, preferred_element_type=jnp.float32)
    inner = (gate / (1 + jnp.exp(-gate)) * up).astype(jnp.bfloat16)
    y = jnp.dot(inner, w_ref[2], preferred_element_type=jnp.float32).astype(jnp.bfloat16)
    for i in range(count):
        ys[i][...] = y[i * rows:(i + 1) * rows]


def experts(xs, w, after=()):
    count = len(xs)
    rows, d = xs[0].shape
    n = w.shape[1]
    vm = pl.BlockSpec(memory_space=pltpu.VMEM)
    return pl.pallas_call(
        functools.partial(expert_kernel, count=count, rows=rows, after=len(after)),
        in_specs=[vm] * (count + 1) + [pl.BlockSpec(memory_space=pl.ANY)] * len(after),
        out_specs=[vm] * count,
        out_shape=[jax.ShapeDtypeStruct((rows, d), jnp.bfloat16)] * count,
        compiler_params=pltpu.CompilerParams(vmem_limit_bytes=26 << 20),
        cost_estimate=pl.CostEstimate(flops=20 * count * rows * n * d, bytes_accessed=2 * (3 * n * d + 2 * count * rows * d), transcendentals=count * rows * n),
        name="experts",
    )(*xs, w, *after)


def combine_kernel(info_ref, hid_ref, mine_ref, other_ref, keep_ref, back_ref, hot_ref, factor_ref, out_ref):
    cap = back_ref.shape[0]
    is_mine = pl.program_id(0) // 2 == info_ref[2]
    att = jnp.where(is_mine, mine_ref[...].astype(jnp.float32), other_ref[...].astype(jnp.float32))
    stream = (hid_ref[...].astype(jnp.float32) + att).astype(jnp.bfloat16).astype(jnp.float32)
    one = jnp.dot(hot_ref[:, :cap], keep_ref[...], preferred_element_type=jnp.float32)
    two = jnp.dot(hot_ref[:, cap:2 * cap], back_ref[...], preferred_element_type=jnp.float32)
    out_ref[...] = (stream + one * factor_ref[:, 0:1] + two * factor_ref[:, 1:2]).astype(out_ref.dtype)


def combine(info, hidden, mine, other, keep, back, hot, factors):
    tok, d = hidden.shape
    cap = back.shape[0]
    wide = d // 4
    cols = lambda rows: pl.BlockSpec((rows, wide), lambda c, s: (0, c))
    half = pl.BlockSpec((tok, wide), lambda c, s: (0, lax.rem(c, 2)))
    whole = pl.BlockSpec((tok, tok), lambda c, s: (0, 0))
    return pl.pallas_call(
        combine_kernel,
        grid_spec=pltpu.PrefetchScalarGridSpec(
            num_scalar_prefetch=1,
            grid=(4,),
            in_specs=[cols(tok), half, half, cols(cap), cols(cap), whole, whole],
            out_specs=cols(tok),
        ),
        out_shape=jax.ShapeDtypeStruct((tok, d), hidden.dtype),
        compiler_params=pltpu.CompilerParams(vmem_limit_bytes=24 << 20),
        name="combine",
    )(info, hidden, mine, other, keep, back, hot, factors)


def shift(value, axis, size, steps):
    return lax.ppermute(value, axis, [(i, (i + steps) % size) for i in range(size)])


def swap(value, axis):
    return shift(value, axis, 2, 1)


def ring_moves(size):
    out = [0]
    for s in range(1, size // 2 + 1):
        out.append(-s)
        if 2 * s < size:
            out.append(s)
    return out


def ring_scatter(parts, signs, size):
    ups = [p[-2 * sign] for p, sign in zip(parts, signs)]
    downs = [shift(p[sign], "z", size, sign) for p, sign in zip(parts, signs)]
    for i, (p, sign) in enumerate(zip(parts, signs)):
        ups[i] = shift(ups[i], "z", size, -sign) + p[-sign]
    ups = [shift(u, "z", size, -sign) for u, sign in zip(ups, signs)]
    return [(ups[i], downs[i], p[0]) for i, p in enumerate(parts)]


def body(sizes, hidden_in, queries, keys_values, doc_ids, route_ids, route_weights, norm_gain, gate_up, down):
    tok, d = queries.shape
    capacity = tok // 4
    n_z, n_core, n_cx = sizes["z"], sizes["core"], sizes["cx"]
    yhi, z, core = lax.axis_index("yhi"), lax.axis_index("z"), lax.axis_index("core")
    half = n_z * tok
    n_ctx = n_cx * n_core
    moves = ring_moves(n_z)
    heads = keys_values.shape[1] // (4 * HD)
    cx, dp = lax.axis_index("cx"), lax.axis_index("dp")
    info = jnp.stack([z, yhi * half, yhi, core, cx, dp]).astype(jnp.int32)

    wide_t = jnp.swapaxes(gate_up, 2, 3)
    far = pack(info, wide_t, down, n_core, n_cx)
    place = lambda y, k, l: (y * n_z + k) * 2 + l
    across = [
        (place(y, k, l), place(y if l == 0 else 1 - y, (k + n_z // 2) % n_z, l)) for y in range(2) for k in range(n_z) for l in range(2)
    ]
    keys_values, far = lax.optimization_barrier((keys_values, far))
    far = lax.ppermute(far, ("yhi", "z", "dp"), across)

    send, kept = prepare(info, keys_values, doc_ids)
    unit = join(send, kept, swap(send, "yhi"))

    out, mine, hot, factors = plan(info, route_ids, route_weights, queries, hidden_in)
    theirs = pack(info, wide_t, down, n_core, 1)
    out, theirs, unit = lax.optimization_barrier((out, theirs, unit))
    got = swap(out, "yhi")
    ahead = [(i, i + 1) for i in range(n_ctx - 1)]
    onward = lambda x: lax.ppermute(x, ("cx", "core"), ahead)
    own = {0: unit}
    prior = [onward(unit)]
    for s in range(1, n_z // 2 + 1):
        own[-s] = shift(own[1 - s], "z", n_z, 1)
        if 2 * s < n_z:
            own[s] = shift(own[s - 1], "z", n_z, -1)
        if s == 1:
            own[-s], far = lax.optimization_barrier((own[-s], far))
            far_2 = swap(far, "dp")
        if s == 2:
            own[-s], got, theirs, prior[0] = lax.optimization_barrier((own[-s], got, theirs, prior[0]))
        if s == 3:
            own[-s], far, far_2 = lax.optimization_barrier((own[-s], far, far_2))
    got_1 = swap(theirs, "yhi")
    share = jnp.concatenate([far, far_2], 0)
    shares = [share, shift(share, "cx", n_cx, 1), shift(share, "cx", n_cx, -1)]
    own = [own[m] for m in moves]
    groups = [range(0, 1), range(1, n_z // 2 + 1), range(n_z // 2 + 1, n_z - 1), range(n_z - 1, n_z)]
    layout = []
    for n, group in enumerate(groups):
        if n > 0:
            prior.append(onward(jnp.concatenate([own[i] for i in group], 0) if len(group) > 1 else own[group[0]]))
        layout += [(n, k * unit.shape[0]) for k in range(len(group))]
    layout += [(len(groups) + i, 0) for i in range(n_z)]
    pieces = prior + own

    gain = norm_gain[None]
    first = yhi == 0
    atts, rows = [], []
    mine, got_1, shares[2] = lax.optimization_barrier((mine, got_1, shares[2]))
    steps = [0, -1, 1, 2]
    got_2 = swap(got_1, "core")
    shares.append(shift(shares[2], "cx", n_cx, -1))
    for part in range(2):
        if part == 1:
            mine, _ = lax.optimization_barrier((mine, atts[0]))
        att, keep, away = attend(info, mine, got, pieces, layout, moves, part, heads, tok)
        atts.append(att)
        rows.append(norm_rows(info, mine, got, part, keep, swap(away, "yhi"), gain))
    rows[1], shares[3] = lax.optimization_barrier((rows[1], shares[3]))
    own_att = jnp.where(first, atts[0], atts[1])
    away_att, rows[1] = lax.optimization_barrier((jnp.where(first, atts[1], atts[0]), rows[1]))
    other_att = swap(away_att, "yhi")

    signs = [1, -1]
    rows = [{0: x, -sign: shift(x, "z", n_z, sign), sign: shift(x, "z", n_z, -sign)} for x, sign in zip(rows, signs)]
    for g, sign in zip(rows, signs):
        g[-2 * sign] = shift(g[-sign], "z", n_z, sign)
    blocks = shares + [swap(x, "core") for x in shares]
    weights = assemble(info, wide_t, down, got_1, got_2, blocks, steps, rows[1][0])
    keys = [(i, m) for i in range(2) for m in (0, -1, 1)]
    first_out = experts([rows[i][m] for i, m in keys], weights)
    last_out = experts([g[-2 * sign] for g, sign in zip(rows, signs)], weights, after=first_out[:1])
    outs = [{-2 * sign: y} for sign, y in zip(signs, last_out)]
    for (i, m), y in zip(keys, first_out):
        outs[i][m] = y
    sums = [ups.astype(jnp.float32) + downs + here for ups, downs, here in ring_scatter(outs, signs, n_z)]
    back = swap(jnp.where(first, sums[1], sums[0]).astype(jnp.bfloat16), "yhi")
    keep = jnp.where(first, sums[0], sums[1]).astype(jnp.bfloat16)
    return combine(info, hidden_in, own_att, other_att, keep, back, hot, factors)


def solution(mesh):
    sizes = {"cx": mesh.shape["ctx"] // 2, "core": 2, "yhi": 2, "z": mesh.shape["exp"] // 2, "dp": mesh.shape["dp"]}
    fine = Mesh(mesh.devices.reshape(tuple(sizes.values())), tuple(sizes))
    tokens = ("dp", "cx", "core", "yhi", "z")
    rows = P(tokens, None)
    hidden = ("yhi", "z")
    in_specs = (rows, rows, rows, P(tokens), rows, rows, P(), P(None, None, None, hidden), P(None, hidden, None))
    return jax.shard_map(
        functools.partial(body, sizes), mesh=fine, in_specs=in_specs, out_specs=rows, check_vma=False
    )
```

```python
import functools
import math

import jax
import jax.numpy as jnp
from jax import lax
from jax.experimental import pallas as pl
from jax.experimental.pallas import tpu as pltpu
from jax.sharding import Mesh
from jax.sharding import PartitionSpec as P

EXP_FLIGHT = 2
HD = 128
GROUP = 7
EXP2_SCALE = math.log2(math.e) / math.sqrt(HD)

def attend_kernel(info_ref, q_own_ref, q_got_ref, place_own_ref, place_got_ref, *refs, tok, span, moves, heads, layout, part):
    arrays, out_ref, low_ref, high_ref = refs[:-11], refs[-11], refs[-10], refs[-9]
    kv, ids, start_scr, m_scr, l_scr, acc_scr, bounds, sem = refs[-8:]
    c = pl.program_id(0)
    z = info_ref[0]
    half = len(moves) * tok
    near = pl.multiple_of(info_ref[1], half)
    far = pl.multiple_of(half - info_ref[1], half)
    first = pl.multiple_of(part * half + z * tok, tok)
    is_own = info_ref[2] == part

    @pl.when(c == 0)
    def _():
        blocks = []
        copies = []
        for n, (which, row) in enumerate(layout):
            piece = arrays[which]
            place = lax.rem(z + moves[n % len(moves)] + len(moves), len(moves)) * tok
            slab = n // len(moves) * 2 * half
            for side, base in ((0, near), (1, far)):
                at = pl.multiple_of(slab + base + place, tok)
                cp = pltpu.make_async_copy(piece.at[pl.ds(row + side * tok, tok)], kv.at[pl.ds(at, tok)], sem.at[n, side])
                blocks.append((cp, (at >= first) & (at <= first + 2 * half)))
            copies.append(pltpu.make_async_copy(piece.at[pl.ds(row + 2 * tok, 16)], ids.at[n], sem.at[n, 2]))
        for cp in copies:
            cp.start()
        for cp, needed in blocks:
            pl.when(needed)(cp.start)
        for cp in copies:
            cp.wait()
        own = [ids[len(moves), 0:1, n * tok:(n + 1) * tok].astype(jnp.float32) for n in range(2)]
        own = jnp.where(is_own, own[0], own[1])
        own = jnp.broadcast_to(own, (tok, tok)).T
        less = jnp.zeros((tok, tok), jnp.float32)
        for n in range(len(layout)):
            for side in range(2):
                row = ids[n, 0:1, side * tok:(side + 1) * tok].astype(jnp.float32)
                less = less + jnp.where(row < own, 1.0, 0.0)
        begin = jnp.sum(less, axis=1, keepdims=True)
        start_scr[...] = begin.astype(jnp.int32)
        bounds[0] = jnp.min(begin).astype(jnp.int32)
        bounds[1] = jnp.max(begin).astype(jnp.int32)
        for cp, needed in blocks:
            pl.when(needed)(cp.wait)

    start_min, start_max = bounds[0], bounds[1]
    q = jnp.where(is_own, q_own_ref[...], q_got_ref[...])
    q = jnp.concatenate([q[:, g * HD:(g + 1) * HD] for g in range(GROUP)], 0)
    start = start_scr[...]
    row = lax.broadcasted_iota(jnp.int32, (tok, 1), 0) + first + 2 * half
    key_col = pl.multiple_of(c * HD, HD)
    value_col = pl.multiple_of((heads + c) * HD, HD)

    def keys(offset, width):
        return kv[pl.ds(offset, width), pl.ds(key_col, HD)]

    def values(offset, width):
        return kv[pl.ds(offset, width), pl.ds(value_col, HD)]

    def scores(offset, width):
        return lax.dot_general(q, keys(offset, width), (((1,), (1,)), ((), ())), preferred_element_type=jnp.float32)

    def rowmax(s, width):
        t = s[:, :128]
        for j in range(1, width // 128):
            t = jnp.maximum(t, s[:, j * 128:(j + 1) * 128])
        return jnp.max(t, axis=1, keepdims=True)

    def lanesum(p, width):
        t = p[:, :128]
        for j in range(1, width // 128):
            t = t + p[:, j * 128:(j + 1) * 128]
        return t

    def masked(s, offset, width, causal):
        key = lax.broadcasted_iota(jnp.int32, (tok, width), 1) + offset
        ok = key >= start
        if causal:
            ok = ok & (key <= row)
        return jnp.where(ok[None], s.reshape(GROUP, tok, width), -1e30).reshape(GROUP * tok, width)

    own = pl.multiple_of(first + 2 * half, tok)
    s = masked(scores(own, tok), own, tok, True)
    m = rowmax(s, tok)
    p = jnp.exp2((s - m) * EXP2_SCALE)
    m_scr[...] = jnp.broadcast_to(m, m_scr.shape)
    l_scr[...] = lanesum(p, tok)
    acc_scr[...] = jnp.dot(p.astype(jnp.bfloat16), values(own, tok), preferred_element_type=jnp.float32)

    def step(i, mask):
        offset = pl.multiple_of(first + i * span, tok)
        s = scores(offset, span)
        if mask:
            s = masked(s, offset, span, False)
        old = m_scr[...]
        new = jnp.maximum(old, rowmax(s, span))
        m_scr[...] = new
        shrink = jnp.exp2((old - new) * EXP2_SCALE)
        p = jnp.exp2((s - jnp.concatenate([new] * (span // 128), 1)) * EXP2_SCALE)
        l_scr[...] = l_scr[...] * shrink + lanesum(p, span)
        acc_scr[...] = acc_scr[...] * shrink + jnp.dot(p.astype(jnp.bfloat16), values(offset, span), preferred_element_type=jnp.float32)

    steps = 2 * half // span

    def loop(i, carry):
        whole = start_max <= first + i * span

        @pl.when(whole)
        def _():
            step(i, False)

        @pl.when(jnp.logical_not(whole))
        def _():
            step(i, True)

        return carry

    lax.fori_loop(jnp.clip(lax.div(start_min - first, span), 0, steps), steps, loop, 0)

    total = jnp.sum(l_scr[...], axis=1, keepdims=True)
    att = (acc_scr[...] / total).astype(jnp.bfloat16)
    att = jnp.concatenate([att[g * tok:(g + 1) * tok] for g in range(GROUP)], 1)
    out_ref[...] = att
    place = jnp.where(is_own, place_own_ref[...], place_got_ref[...])
    rows = jnp.dot(place, att, preferred_element_type=jnp.float32).astype(jnp.bfloat16)
    low_ref[...] = rows[:rows.shape[0] // 2]
    high_ref[...] = rows[rows.shape[0] // 2:]


def attend(info, own, got, pieces, layout, moves, part, heads, tok, span=512):
    slots = tok // 4
    wide = GROUP * HD
    n = len(moves)
    hbm = pl.BlockSpec(memory_space=pl.ANY)
    scratch = pltpu.VMEM((GROUP * tok, 128), jnp.float32)
    return pl.pallas_call(
        functools.partial(attend_kernel, tok=tok, span=span, moves=moves, heads=heads, layout=layout, part=part),
        grid_spec=pltpu.PrefetchScalarGridSpec(
            num_scalar_prefetch=1,
            grid=(heads,),
            in_specs=[
                pl.BlockSpec((tok, wide), lambda c, s: (0, c)),
                pl.BlockSpec((tok, wide), lambda c, s: (0, c)),
                pl.BlockSpec((2 * slots, tok), lambda c, s: (tok // (2 * slots), heads * GROUP)),
                pl.BlockSpec((2 * slots, tok), lambda c, s: (tok // (2 * slots), heads * GROUP)),
            ] + [hbm] * len(pieces),
            out_specs=[pl.BlockSpec((r, wide), lambda c, s: (0, c)) for r in (tok, slots, slots)],
            scratch_shapes=[
                pltpu.VMEM((4 * n * tok, 2 * heads * HD), jnp.bfloat16),
                pltpu.VMEM((2 * n, 16, 2 * heads * HD), jnp.bfloat16),
                pltpu.VMEM((tok, 1), jnp.int32),
                scratch, scratch, scratch,
                pltpu.SMEM((2,), jnp.int32),
                pltpu.SemaphoreType.DMA((2 * n, 3)),
            ],
        ),
        out_shape=[jax.ShapeDtypeStruct((r, heads * wide), jnp.bfloat16) for r in (tok, slots, slots)],
        compiler_params=pltpu.CompilerParams(vmem_limit_bytes=60 << 20),
        cost_estimate=pl.CostEstimate(flops=8 * 10**9, bytes_accessed=5 << 20, transcendentals=4 * 10**6),
        name="attend",
    )(info, own, got, own, got, *pieces)


def prepare_kernel(info_ref, kv_ref, doc_ref, send_ref, mine_ref):
    tok = kv_ref.shape[0]
    w = kv_ref.shape[1] // 4
    send_ref[tok:, :] = jnp.zeros((16, 2 * w), send_ref.dtype)
    send_ref[tok:tok + 16, :tok] = jnp.broadcast_to((doc_ref[...] + 1).astype(jnp.float32), (16, tok)).astype(send_ref.dtype)
    for yhi in range(2):
        @pl.when(info_ref[2] == yhi)
        def _(yhi=yhi):
            away = 1 - yhi
            mine_ref[:, :w] = kv_ref[:, yhi * w:(yhi + 1) * w]
            mine_ref[:, w:] = kv_ref[:, (2 + yhi) * w:(3 + yhi) * w]
            send_ref[:tok, :w] = kv_ref[:, away * w:(away + 1) * w]
            send_ref[:tok, w:] = kv_ref[:, (2 + away) * w:(3 + away) * w]


def prepare(info, keys_values, doc_ids):
    tok, width = keys_values.shape
    vm = pl.BlockSpec(memory_space=pltpu.VMEM)
    shape = lambda r, c: jax.ShapeDtypeStruct((r, c), jnp.bfloat16)
    return pl.pallas_call(
        prepare_kernel,
        in_specs=[pl.BlockSpec(memory_space=pltpu.SMEM)] + [vm] * 2,
        out_specs=[vm] * 2,
        out_shape=[shape(tok + 16, width // 2), shape(tok, width // 2)],
        compiler_params=pltpu.CompilerParams(vmem_limit_bytes=24 << 20),
        name="prepare",
    )(info, keys_values, doc_ids[None])


def plan_kernel(info_ref, ids_ref, weights_ref, q_ref, hid_ref, out_ref, own_ref, hot_ref, factor_ref):
    tok = hid_ref.shape[0]
    slots = (out_ref.shape[0] - tok) // 2
    q = q_ref.shape[1] // 2
    yhi = info_ref[2]
    below = lax.broadcasted_iota(jnp.int32, (tok, tok), 0) <= lax.broadcasted_iota(jnp.int32, (tok, tok), 1)
    below = below.astype(jnp.float32).astype(jnp.bfloat16)
    places, factors = [], []
    for flight in (yhi, 1 - yhi):
        chosen = ids_ref[...] == flight
        routed = jnp.max(jnp.where(chosen, 1.0, 0.0), axis=0, keepdims=True)
        factors.append(jnp.sum(jnp.where(chosen, weights_ref[...], 0.0), axis=0, keepdims=True))
        ranks = jnp.dot(jnp.broadcast_to(routed, (16, tok)).astype(jnp.bfloat16), below, preferred_element_type=jnp.float32)
        ranks = jnp.where(routed > 0.5, ranks[:1] - 1.0, -1.0)
        slot = lax.broadcasted_iota(jnp.int32, (slots, tok), 0).astype(jnp.float32)
        places.append(jnp.where(slot == ranks, 1.0, 0.0))
    place_f = jnp.concatenate(places, 0)
    place = place_f.astype(jnp.bfloat16)
    hot_ref[...] = jnp.concatenate([place_f, jnp.zeros((tok - 2 * slots, tok), jnp.float32)], 0).T.astype(jnp.bfloat16)
    factor_ref[...] = jnp.concatenate([factors[0], factors[1], jnp.zeros((tok - 2, tok), jnp.float32)], 0).T
    rows = jnp.dot(place, hid_ref[...], preferred_element_type=jnp.float32).astype(jnp.bfloat16)
    for n, ref in enumerate((own_ref, out_ref)):
        ref[:tok, q:] = jnp.zeros((tok, tok), jnp.bfloat16)
        ref[tok:tok + slots, :q] = rows[n * slots:(n + 1) * slots, :q]
        ref[tok + slots:, :q] = rows[n * slots:(n + 1) * slots, q:]
        ref[tok:tok + slots, q:] = place[n * slots:(n + 1) * slots]
        ref[tok + slots:, q:] = place[(1 - n) * slots:(2 - n) * slots]

    for side in range(2):
        @pl.when(yhi == side)
        def _(side=side):
            own_ref[:tok, :q] = q_ref[:, side * q:(side + 1) * q]
            out_ref[:tok, :q] = q_ref[:, (1 - side) * q:(2 - side) * q]


def plan(info, route_ids, route_weights, queries, hidden):
    tok, d = hidden.shape
    slots = tok // 4
    vm = pl.BlockSpec(memory_space=pltpu.VMEM)
    shape = lambda r, c, t=jnp.bfloat16: jax.ShapeDtypeStruct((r, c), t)
    return pl.pallas_call(
        plan_kernel,
        in_specs=[pl.BlockSpec(memory_space=pltpu.SMEM)] + [vm] * 4,
        out_specs=[vm] * 4,
        out_shape=[shape(tok + 2 * slots, d // 2 + tok)] * 2 + [shape(tok, tok), shape(tok, tok, jnp.float32)],
        compiler_params=pltpu.CompilerParams(vmem_limit_bytes=24 << 20),
        name="plan",
    )(info, route_ids.T, route_weights.T, queries, hidden)


def join_kernel(send_ref, mine_ref, other_ref, unit_ref):
    tok = mine_ref.shape[0]
    unit_ref[:tok] = mine_ref[...]
    unit_ref[tok:2 * tok] = other_ref[:tok]
    unit_ref[2 * tok:] = send_ref[tok:]
    unit_ref[2 * tok:, tok:2 * tok] = other_ref[tok:, :tok]


def join(send, mine, other):
    tok, width = mine.shape
    vm = pl.BlockSpec(memory_space=pltpu.VMEM)
    return pl.pallas_call(
        join_kernel,
        in_specs=[vm] * 3,
        out_specs=vm,
        out_shape=jax.ShapeDtypeStruct((2 * tok + 16, width), mine.dtype),
        compiler_params=pltpu.CompilerParams(vmem_limit_bytes=24 << 20),
        name="join",
    )(send, mine, other)


def pack_kernel(info_ref, gu_ref, down_ref, out_ref, sem):
    yhi = info_ref[2]
    units, wide = out_ref.shape[1], out_ref.shape[2]
    at = pl.ds(pl.multiple_of(info_ref[3] * units, units), units)
    if wide == down_ref.shape[2]:
        away, cols = 1 - yhi, pl.ds(0, wide)
    else:
        away = jnp.where(info_ref[5] == 0, yhi, 1 - yhi)
        cols = pl.ds(pl.multiple_of(info_ref[4] * wide, wide), wide)
    one = pltpu.make_async_copy(gu_ref.at[away, :, at, cols], out_ref.at[pl.ds(0, 2)], sem.at[0])
    two = pltpu.make_async_copy(down_ref.at[away, at, cols], out_ref.at[2], sem.at[1])
    one.start()
    two.start()
    one.wait()
    two.wait()


def pack(info, wide_t, down, cores, columns):
    hbm = pl.BlockSpec(memory_space=pl.ANY)
    units, d = down.shape[1] // cores, down.shape[2]
    return pl.pallas_call(
        pack_kernel,
        in_specs=[pl.BlockSpec(memory_space=pltpu.SMEM), hbm, hbm],
        out_specs=pl.BlockSpec(memory_space=pltpu.VMEM),
        out_shape=jax.ShapeDtypeStruct((3, units, d // columns), down.dtype),
        scratch_shapes=[pltpu.SemaphoreType.DMA((2,))],
        compiler_params=pltpu.CompilerParams(vmem_limit_bytes=60 << 20),
        name="pack",
    )(info, wide_t, down)


def norm_kernel(info_ref, own_ref, got_ref, mine_ref, other_ref, gain_ref, out_ref, *, part):
    slots, half = mine_ref.shape
    tok = own_ref.shape[0] - 2 * slots
    is_own = info_ref[2] == part

    def put(low, high):
        parts = []
        for n, att in enumerate((low, high)):
            rows = slice(tok + n * slots, tok + (n + 1) * slots)
            base = jnp.where(is_own, own_ref[rows, :half], got_ref[rows, :half]).astype(jnp.float32)
            parts.append((base + att.astype(jnp.float32)).astype(jnp.bfloat16).astype(jnp.float32))
        total = sum(jnp.sum(p * p, axis=1, keepdims=True) for p in parts)
        inv = lax.rsqrt(total / (2 * half) + 1e-6)
        for n, p in enumerate(parts):
            gain = gain_ref[:, n * half:(n + 1) * half].astype(jnp.float32)
            out_ref[:, n * half:(n + 1) * half] = (p * inv * gain).astype(jnp.bfloat16)

    @pl.when(info_ref[2] == 0)
    def _():
        put(mine_ref[...], other_ref[...])

    @pl.when(info_ref[2] != 0)
    def _():
        put(other_ref[...], mine_ref[...])


def norm_rows(info, own, got, part, mine, other, gain):
    slots, half = mine.shape
    vm = pl.BlockSpec(memory_space=pltpu.VMEM)
    return pl.pallas_call(
        functools.partial(norm_kernel, part=part),
        in_specs=[pl.BlockSpec(memory_space=pltpu.SMEM)] + [vm] * 5,
        out_specs=vm,
        out_shape=jax.ShapeDtypeStruct((slots, 2 * half), jnp.bfloat16),
        compiler_params=pltpu.CompilerParams(vmem_limit_bytes=16 << 20),
        name="norm_rows",
    )(info, own, got, mine, other, gain)


def assemble_kernel(info_ref, wo_ref, do_ref, r1_ref, r2_ref, *refs, steps):
    count = 2 * len(steps)
    blocks, w_ref, sem = refs[:count], refs[-2], refs[-1]
    yhi = info_ref[2]
    n, h = wo_ref.shape[2], r1_ref.shape[1]
    cps = []

    def cp(src, dst):
        cps.append(pltpu.make_async_copy(src, dst, sem.at[len(cps)]))

    for i in range(3):
        own = do_ref.at[yhi] if i == 2 else wo_ref.at[yhi, i]
        for src, at, size in ((own, 0, n), (r1_ref.at[i], n, h), (r2_ref.at[i], n + h, h)):
            cp(src, w_ref.at[i, pl.ds(at, size)])
        for k, block in enumerate(blocks):
            core, step = divmod(k, len(steps))
            wide = block.shape[2]
            col = lax.rem(info_ref[4] + steps[step] + len(steps), len(steps)) * wide
            for u in range(2):
                at = n + 2 * h + (2 * core + u) * h
                cp(block.at[3 * u + i], w_ref.at[i, pl.ds(at, h), pl.ds(pl.multiple_of(col, wide), wide)])
    for c in cps:
        c.start()
    for c in cps:
        c.wait()


def assemble(info, wo, do, r1, r2, blocks, steps, after):
    n, d = 2 * (wo.shape[2] + r1.shape[1] + r2.shape[1]), wo.shape[3]
    hbm = pl.BlockSpec(memory_space=pl.ANY)
    return pl.pallas_call(
        functools.partial(assemble_kernel, steps=steps),
        in_specs=[pl.BlockSpec(memory_space=pltpu.SMEM)] + [hbm] * (5 + len(blocks)),
        out_specs=pl.BlockSpec(memory_space=pltpu.VMEM),
        scratch_shapes=[pltpu.SemaphoreType.DMA((9 + 6 * len(blocks),))],
        out_shape=jax.ShapeDtypeStruct((3, n, d), jnp.bfloat16),
        compiler_params=pltpu.CompilerParams(vmem_limit_bytes=20 << 20),
        cost_estimate=pl.CostEstimate(flops=0, bytes_accessed=6 * n * d, transcendentals=0),
        name="assemble",
    )(info, wo, do, r1, r2, *blocks, after)


def expert_kernel(*refs, count, rows, after):
    xs, w_ref, ys = refs[:count], refs[count], refs[count + 1 + after:]
    x = jnp.concatenate([r[...] for r in xs], 0)
    nt = (((1,), (1,)), ((), ()))
    gate = lax.dot_general(x, w_ref[0], nt, preferred_element_type=jnp.float32)
    up = lax.dot_general(x, w_ref[1], nt, preferred_element_type=jnp.float32)
    inner = (gate / (1 + jnp.exp(-gate)) * up).astype(jnp.bfloat16)
    y = jnp.dot(inner, w_ref[2], preferred_element_type=jnp.float32).astype(jnp.bfloat16)
    for i in range(count):
        ys[i][...] = y[i * rows:(i + 1) * rows]


def experts(xs, w, after=()):
    count = len(xs)
    rows, d = xs[0].shape
    n = w.shape[1]
    vm = pl.BlockSpec(memory_space=pltpu.VMEM)
    return pl.pallas_call(
        functools.partial(expert_kernel, count=count, rows=rows, after=len(after)),
        in_specs=[vm] * (count + 1) + [pl.BlockSpec(memory_space=pl.ANY)] * len(after),
        out_specs=[vm] * count,
        out_shape=[jax.ShapeDtypeStruct((rows, d), jnp.bfloat16)] * count,
        compiler_params=pltpu.CompilerParams(vmem_limit_bytes=26 << 20),
        cost_estimate=pl.CostEstimate(flops=20 * count * rows * n * d, bytes_accessed=2 * (3 * n * d + 2 * count * rows * d), transcendentals=count * rows * n),
        name="experts",
    )(*xs, w, *after)


def combine_kernel(info_ref, hid_ref, mine_ref, other_ref, keep_ref, back_ref, hot_ref, factor_ref, out_ref):
    cap = back_ref.shape[0]
    is_mine = pl.program_id(0) // 2 == info_ref[2]
    att = jnp.where(is_mine, mine_ref[...].astype(jnp.float32), other_ref[...].astype(jnp.float32))
    stream = (hid_ref[...].astype(jnp.float32) + att).astype(jnp.bfloat16).astype(jnp.float32)
    one = jnp.dot(hot_ref[:, :cap], keep_ref[...], preferred_element_type=jnp.float32)
    two = jnp.dot(hot_ref[:, cap:2 * cap], back_ref[...], preferred_element_type=jnp.float32)
    out_ref[...] = (stream + one * factor_ref[:, 0:1] + two * factor_ref[:, 1:2]).astype(out_ref.dtype)


def combine(info, hidden, mine, other, keep, back, hot, factors):
    tok, d = hidden.shape
    cap = back.shape[0]
    wide = d // 4
    cols = lambda rows: pl.BlockSpec((rows, wide), lambda c, s: (0, c))
    half = pl.BlockSpec((tok, wide), lambda c, s: (0, lax.rem(c, 2)))
    whole = pl.BlockSpec((tok, tok), lambda c, s: (0, 0))
    return pl.pallas_call(
        combine_kernel,
        grid_spec=pltpu.PrefetchScalarGridSpec(
            num_scalar_prefetch=1,
            grid=(4,),
            in_specs=[cols(tok), half, half, cols(cap), cols(cap), whole, whole],
            out_specs=cols(tok),
        ),
        out_shape=jax.ShapeDtypeStruct((tok, d), hidden.dtype),
        compiler_params=pltpu.CompilerParams(vmem_limit_bytes=24 << 20),
        name="combine",
    )(info, hidden, mine, other, keep, back, hot, factors)


def shift(value, axis, size, steps):
    return lax.ppermute(value, axis, [(i, (i + steps) % size) for i in range(size)])


def swap(value, axis):
    return shift(value, axis, 2, 1)


def ring_moves(size):
    out = [0]
    for s in range(1, size // 2 + 1):
        out.append(-s)
        if 2 * s < size:
            out.append(s)
    return out


def ring_scatter(parts, signs, size):
    ups = [p[-2 * sign] for p, sign in zip(parts, signs)]
    downs = [shift(p[sign], "z", size, sign) for p, sign in zip(parts, signs)]
    for i, (p, sign) in enumerate(zip(parts, signs)):
        ups[i] = shift(ups[i], "z", size, -sign) + p[-sign]
    ups = [shift(u, "z", size, -sign) for u, sign in zip(ups, signs)]
    return [(ups[i], downs[i], p[0]) for i, p in enumerate(parts)]


def body(sizes, hidden_in, queries, keys_values, doc_ids, route_ids, route_weights, norm_gain, gate_up, down):
    tok, d = queries.shape
    capacity = tok // 4
    n_z, n_core, n_cx = sizes["z"], sizes["core"], sizes["cx"]
    yhi, z, core = lax.axis_index("yhi"), lax.axis_index("z"), lax.axis_index("core")
    half = n_z * tok
    n_ctx = n_cx * n_core
    moves = ring_moves(n_z)
    heads = keys_values.shape[1] // (4 * HD)
    cx, dp = lax.axis_index("cx"), lax.axis_index("dp")
    info = jnp.stack([z, yhi * half, yhi, core, cx, dp]).astype(jnp.int32)

    wide_t = jnp.swapaxes(gate_up, 2, 3)
    far = pack(info, wide_t, down, n_core, n_cx)
    place = lambda y, k, l: (y * n_z + k) * 2 + l
    across = [
        (place(y, k, l), place(y if l == 0 else 1 - y, (k + n_z // 2) % n_z, l)) for y in range(2) for k in range(n_z) for l in range(2)
    ]
    far = lax.ppermute(far, ("yhi", "z", "dp"), across)

    send, kept = prepare(info, keys_values, doc_ids)
    other, far = lax.optimization_barrier((swap(send, "yhi"), far))
    unit = join(send, kept, other)
    far_2 = swap(far, "dp")

    out, mine, hot, factors = plan(info, route_ids, route_weights, queries, hidden_in)
    theirs = pack(info, wide_t, down, n_core, 1)
    ahead = [(i, i + 1) for i in range(n_ctx - 1)]
    onward = lambda x: lax.ppermute(x, ("cx", "core"), ahead)
    own = {0: unit}
    prior = [onward(unit)]
    for s in range(1, n_z // 2 + 1):
        own[-s] = shift(own[1 - s], "z", n_z, 1)
        if 2 * s < n_z:
            own[s] = shift(own[s - 1], "z", n_z, -1)
        if s == 1:
            own[-s], far, far_2, out = lax.optimization_barrier((own[-s], far, far_2, out))
            got = swap(out, "yhi")
            share = jnp.concatenate([far, far_2], 0)
            shares = [share, shift(share, "cx", n_cx, 1), shift(share, "cx", n_cx, -1)]
        if s == 2:
            own[-s], prior[0] = lax.optimization_barrier((own[-s], prior[0]))
        if s == 3:
            own[-s], got, theirs, shares[1], shares[2] = lax.optimization_barrier((own[-s], got, theirs, shares[1], shares[2]))
            got_1 = swap(theirs, "yhi")
            shares.append(shift(shares[2], "cx", n_cx, -1))
    own = [own[m] for m in moves]
    groups = [range(0, 1), range(1, n_z // 2 + 1), range(n_z // 2 + 1, n_z - 1), range(n_z - 1, n_z)]
    layout = []
    for n, group in enumerate(groups):
        if n > 0:
            prior.append(onward(jnp.concatenate([own[i] for i in group], 0) if len(group) > 1 else own[group[0]]))
        layout += [(n, k * unit.shape[0]) for k in range(len(group))]
    layout += [(len(groups) + i, 0) for i in range(n_z)]
    pieces = prior + own

    gain = norm_gain[None]
    first = yhi == 0
    atts, rows = [], []
    steps = [0, -1, 1, 2]
    for part in range(2):
        if part == 1:
            mine, _ = lax.optimization_barrier((mine, atts[0]))
        att, keep, away = attend(info, mine, got, pieces, layout, moves, part, heads, tok)
        atts.append(att)
        rows.append(norm_rows(info, mine, got, part, keep, swap(away, "yhi"), gain))
    rows[1], shares[3], got_1 = lax.optimization_barrier((rows[1], shares[3], got_1))
    got_2 = swap(got_1, "core")
    own_att = jnp.where(first, atts[0], atts[1])
    away_att, rows[1] = lax.optimization_barrier((jnp.where(first, atts[1], atts[0]), rows[1]))
    other_att = swap(away_att, "yhi")

    signs = [1, -1]
    rows = [{0: x, -sign: shift(x, "z", n_z, sign), sign: shift(x, "z", n_z, -sign)} for x, sign in zip(rows, signs)]
    for g, sign in zip(rows, signs):
        g[-2 * sign] = shift(g[-sign], "z", n_z, sign)
    blocks = shares + [swap(x, "core") for x in shares]
    weights = assemble(info, wide_t, down, got_1, got_2, blocks, steps, rows[1][0])
    keys = [(i, m) for i in range(2) for m in (0, -1, 1)]
    first_out = experts([rows[i][m] for i, m in keys], weights)
    last_out = experts([g[-2 * sign] for g, sign in zip(rows, signs)], weights, after=first_out[:1])
    outs = [{-2 * sign: y} for sign, y in zip(signs, last_out)]
    for (i, m), y in zip(keys, first_out):
        outs[i][m] = y
    sums = [ups.astype(jnp.float32) + downs + here for ups, downs, here in ring_scatter(outs, signs, n_z)]
    back = swap(jnp.where(first, sums[1], sums[0]).astype(jnp.bfloat16), "yhi")
    keep = jnp.where(first, sums[0], sums[1]).astype(jnp.bfloat16)
    return combine(info, hidden_in, own_att, other_att, keep, back, hot, factors)


def solution(mesh):
    sizes = {"cx": mesh.shape["ctx"] // 2, "core": 2, "yhi": 2, "z": mesh.shape["exp"] // 2, "dp": mesh.shape["dp"]}
    fine = Mesh(mesh.devices.reshape(tuple(sizes.values())), tuple(sizes))
    tokens = ("dp", "cx", "core", "yhi", "z")
    rows = P(tokens, None)
    hidden = ("yhi", "z")
    in_specs = (rows, rows, rows, P(tokens), rows, rows, P(), P(None, None, None, hidden), P(None, hidden, None))
    return jax.shard_map(
        functools.partial(body, sizes), mesh=fine, in_specs=in_specs, out_specs=rows, check_vma=False
    )
```

```python
import functools
import math

import jax
import jax.numpy as jnp
from jax import lax
from jax.experimental import pallas as pl
from jax.experimental.pallas import tpu as pltpu
from jax.sharding import Mesh
from jax.sharding import PartitionSpec as P

EXP_FLIGHT = 2
HD = 128
GROUP = 7
EXP2_SCALE = math.log2(math.e) / math.sqrt(HD)

def attend_kernel(info_ref, q_own_ref, q_got_ref, place_own_ref, place_got_ref, *refs, tok, span, moves, heads, layout, part):
    arrays, out_ref, low_ref, high_ref = refs[:-11], refs[-11], refs[-10], refs[-9]
    kv, ids, start_scr, m_scr, l_scr, acc_scr, bounds, sem = refs[-8:]
    c = pl.program_id(0)
    z = info_ref[0]
    half = len(moves) * tok
    near = pl.multiple_of(info_ref[1], half)
    far = pl.multiple_of(half - info_ref[1], half)
    first = pl.multiple_of(part * half + z * tok, tok)
    is_own = info_ref[2] == part

    @pl.when(c == 0)
    def _():
        blocks = []
        copies = []
        for n, (which, row) in enumerate(layout):
            piece = arrays[which]
            place = lax.rem(z + moves[n % len(moves)] + len(moves), len(moves)) * tok
            slab = n // len(moves) * 2 * half
            for side, base in ((0, near), (1, far)):
                at = pl.multiple_of(slab + base + place, tok)
                cp = pltpu.make_async_copy(piece.at[pl.ds(row + side * tok, tok)], kv.at[pl.ds(at, tok)], sem.at[n, side])
                blocks.append((cp, (at >= first) & (at <= first + 2 * half)))
            copies.append(pltpu.make_async_copy(piece.at[pl.ds(row + 2 * tok, 16)], ids.at[n], sem.at[n, 2]))
        for cp in copies:
            cp.start()
        for cp, needed in blocks:
            pl.when(needed)(cp.start)
        for cp in copies:
            cp.wait()
        own = [ids[len(moves), 0:1, n * tok:(n + 1) * tok].astype(jnp.float32) for n in range(2)]
        own = jnp.where(is_own, own[0], own[1])
        own = jnp.broadcast_to(own, (tok, tok)).T
        less = jnp.zeros((tok, tok), jnp.float32)
        for n in range(len(layout)):
            for side in range(2):
                row = ids[n, 0:1, side * tok:(side + 1) * tok].astype(jnp.float32)
                less = less + jnp.where(row < own, 1.0, 0.0)
        begin = jnp.sum(less, axis=1, keepdims=True)
        start_scr[...] = begin.astype(jnp.int32)
        bounds[0] = jnp.min(begin).astype(jnp.int32)
        bounds[1] = jnp.max(begin).astype(jnp.int32)
        for cp, needed in blocks:
            pl.when(needed)(cp.wait)

    start_min, start_max = bounds[0], bounds[1]
    q = jnp.where(is_own, q_own_ref[...], q_got_ref[...])
    q = jnp.concatenate([q[:, g * HD:(g + 1) * HD] for g in range(GROUP)], 0)
    start = start_scr[...]
    row = lax.broadcasted_iota(jnp.int32, (tok, 1), 0) + first + 2 * half
    key_col = pl.multiple_of(c * HD, HD)
    value_col = pl.multiple_of((heads + c) * HD, HD)

    def keys(offset, width):
        return kv[pl.ds(offset, width), pl.ds(key_col, HD)]

    def values(offset, width):
        return kv[pl.ds(offset, width), pl.ds(value_col, HD)]

    def scores(offset, width):
        return lax.dot_general(q, keys(offset, width), (((1,), (1,)), ((), ())), preferred_element_type=jnp.float32)

    def rowmax(s, width):
        t = s[:, :128]
        for j in range(1, width // 128):
            t = jnp.maximum(t, s[:, j * 128:(j + 1) * 128])
        return jnp.max(t, axis=1, keepdims=True)

    def lanesum(p, width):
        t = p[:, :128]
        for j in range(1, width // 128):
            t = t + p[:, j * 128:(j + 1) * 128]
        return t

    def masked(s, offset, width, causal):
        key = lax.broadcasted_iota(jnp.int32, (tok, width), 1) + offset
        ok = key >= start
        if causal:
            ok = ok & (key <= row)
        return jnp.where(ok[None], s.reshape(GROUP, tok, width), -1e30).reshape(GROUP * tok, width)

    own = pl.multiple_of(first + 2 * half, tok)
    s = masked(scores(own, tok), own, tok, True)
    m = rowmax(s, tok)
    p = jnp.exp2((s - m) * EXP2_SCALE)
    m_scr[...] = jnp.broadcast_to(m, m_scr.shape)
    l_scr[...] = lanesum(p, tok)
    acc_scr[...] = jnp.dot(p.astype(jnp.bfloat16), values(own, tok), preferred_element_type=jnp.float32)

    def step(i, mask):
        offset = pl.multiple_of(first + i * span, tok)
        s = scores(offset, span)
        if mask:
            s = masked(s, offset, span, False)
        old = m_scr[...]
        new = jnp.maximum(old, rowmax(s, span))
        m_scr[...] = new
        shrink = jnp.exp2((old - new) * EXP2_SCALE)
        p = jnp.exp2((s - jnp.concatenate([new] * (span // 128), 1)) * EXP2_SCALE)
        l_scr[...] = l_scr[...] * shrink + lanesum(p, span)
        acc_scr[...] = acc_scr[...] * shrink + jnp.dot(p.astype(jnp.bfloat16), values(offset, span), preferred_element_type=jnp.float32)

    steps = 2 * half // span

    def loop(i, carry):
        whole = start_max <= first + i * span

        @pl.when(whole)
        def _():
            step(i, False)

        @pl.when(jnp.logical_not(whole))
        def _():
            step(i, True)

        return carry

    lax.fori_loop(jnp.clip(lax.div(start_min - first, span), 0, steps), steps, loop, 0)

    total = jnp.sum(l_scr[...], axis=1, keepdims=True)
    att = (acc_scr[...] / total).astype(jnp.bfloat16)
    att = jnp.concatenate([att[g * tok:(g + 1) * tok] for g in range(GROUP)], 1)
    out_ref[...] = att
    place = jnp.where(is_own, place_own_ref[...], place_got_ref[...])
    rows = jnp.dot(place, att, preferred_element_type=jnp.float32).astype(jnp.bfloat16)
    low_ref[...] = rows[:rows.shape[0] // 2]
    high_ref[...] = rows[rows.shape[0] // 2:]


def attend(info, own, got, pieces, layout, moves, part, heads, tok, span=512):
    slots = tok // 4
    wide = GROUP * HD
    n = len(moves)
    hbm = pl.BlockSpec(memory_space=pl.ANY)
    scratch = pltpu.VMEM((GROUP * tok, 128), jnp.float32)
    return pl.pallas_call(
        functools.partial(attend_kernel, tok=tok, span=span, moves=moves, heads=heads, layout=layout, part=part),
        grid_spec=pltpu.PrefetchScalarGridSpec(
            num_scalar_prefetch=1,
            grid=(heads,),
            in_specs=[
                pl.BlockSpec((tok, wide), lambda c, s: (0, c)),
                pl.BlockSpec((tok, wide), lambda c, s: (0, c)),
                pl.BlockSpec((2 * slots, tok), lambda c, s: (tok // (2 * slots), heads * GROUP)),
                pl.BlockSpec((2 * slots, tok), lambda c, s: (tok // (2 * slots), heads * GROUP)),
            ] + [hbm] * len(pieces),
            out_specs=[pl.BlockSpec((r, wide), lambda c, s: (0, c)) for r in (tok, slots, slots)],
            scratch_shapes=[
                pltpu.VMEM((4 * n * tok, 2 * heads * HD), jnp.bfloat16),
                pltpu.VMEM((2 * n, 16, 2 * heads * HD), jnp.bfloat16),
                pltpu.VMEM((tok, 1), jnp.int32),
                scratch, scratch, scratch,
                pltpu.SMEM((2,), jnp.int32),
                pltpu.SemaphoreType.DMA((2 * n, 3)),
            ],
        ),
        out_shape=[jax.ShapeDtypeStruct((r, heads * wide), jnp.bfloat16) for r in (tok, slots, slots)],
        compiler_params=pltpu.CompilerParams(vmem_limit_bytes=60 << 20),
        cost_estimate=pl.CostEstimate(flops=8 * 10**9, bytes_accessed=5 << 20, transcendentals=4 * 10**6),
        name="attend",
    )(info, own, got, own, got, *pieces)


def prepare_kernel(info_ref, kv_ref, doc_ref, send_ref, mine_ref):
    tok = kv_ref.shape[0]
    w = kv_ref.shape[1] // 4
    send_ref[tok:, :] = jnp.zeros((16, 2 * w), send_ref.dtype)
    send_ref[tok:tok + 16, :tok] = jnp.broadcast_to((doc_ref[...] + 1).astype(jnp.float32), (16, tok)).astype(send_ref.dtype)
    for yhi in range(2):
        @pl.when(info_ref[2] == yhi)
        def _(yhi=yhi):
            away = 1 - yhi
            mine_ref[:, :w] = kv_ref[:, yhi * w:(yhi + 1) * w]
            mine_ref[:, w:] = kv_ref[:, (2 + yhi) * w:(3 + yhi) * w]
            send_ref[:tok, :w] = kv_ref[:, away * w:(away + 1) * w]
            send_ref[:tok, w:] = kv_ref[:, (2 + away) * w:(3 + away) * w]


def prepare(info, keys_values, doc_ids):
    tok, width = keys_values.shape
    vm = pl.BlockSpec(memory_space=pltpu.VMEM)
    shape = lambda r, c: jax.ShapeDtypeStruct((r, c), jnp.bfloat16)
    return pl.pallas_call(
        prepare_kernel,
        in_specs=[pl.BlockSpec(memory_space=pltpu.SMEM)] + [vm] * 2,
        out_specs=[vm] * 2,
        out_shape=[shape(tok + 16, width // 2), shape(tok, width // 2)],
        compiler_params=pltpu.CompilerParams(vmem_limit_bytes=24 << 20),
        name="prepare",
    )(info, keys_values, doc_ids[None])


def plan_kernel(info_ref, ids_ref, weights_ref, q_ref, hid_ref, out_ref, own_ref, hot_ref, factor_ref):
    tok = hid_ref.shape[0]
    slots = (out_ref.shape[0] - tok) // 2
    q = q_ref.shape[1] // 2
    yhi = info_ref[2]
    below = lax.broadcasted_iota(jnp.int32, (tok, tok), 0) <= lax.broadcasted_iota(jnp.int32, (tok, tok), 1)
    below = below.astype(jnp.float32).astype(jnp.bfloat16)
    places, factors = [], []
    for flight in (yhi, 1 - yhi):
        chosen = ids_ref[...] == flight
        routed = jnp.max(jnp.where(chosen, 1.0, 0.0), axis=0, keepdims=True)
        factors.append(jnp.sum(jnp.where(chosen, weights_ref[...], 0.0), axis=0, keepdims=True))
        ranks = jnp.dot(jnp.broadcast_to(routed, (16, tok)).astype(jnp.bfloat16), below, preferred_element_type=jnp.float32)
        ranks = jnp.where(routed > 0.5, ranks[:1] - 1.0, -1.0)
        slot = lax.broadcasted_iota(jnp.int32, (slots, tok), 0).astype(jnp.float32)
        places.append(jnp.where(slot == ranks, 1.0, 0.0))
    place_f = jnp.concatenate(places, 0)
    place = place_f.astype(jnp.bfloat16)
    hot_ref[...] = jnp.concatenate([place_f, jnp.zeros((tok - 2 * slots, tok), jnp.float32)], 0).T.astype(jnp.bfloat16)
    factor_ref[...] = jnp.concatenate([factors[0], factors[1], jnp.zeros((tok - 2, tok), jnp.float32)], 0).T
    rows = jnp.dot(place, hid_ref[...], preferred_element_type=jnp.float32).astype(jnp.bfloat16)
    for n, ref in enumerate((own_ref, out_ref)):
        ref[:tok, q:] = jnp.zeros((tok, tok), jnp.bfloat16)
        ref[tok:tok + slots, :q] = rows[n * slots:(n + 1) * slots, :q]
        ref[tok + slots:, :q] = rows[n * slots:(n + 1) * slots, q:]
        ref[tok:tok + slots, q:] = place[n * slots:(n + 1) * slots]
        ref[tok + slots:, q:] = place[(1 - n) * slots:(2 - n) * slots]

    for side in range(2):
        @pl.when(yhi == side)
        def _(side=side):
            own_ref[:tok, :q] = q_ref[:, side * q:(side + 1) * q]
            out_ref[:tok, :q] = q_ref[:, (1 - side) * q:(2 - side) * q]


def plan(info, route_ids, route_weights, queries, hidden):
    tok, d = hidden.shape
    slots = tok // 4
    vm = pl.BlockSpec(memory_space=pltpu.VMEM)
    shape = lambda r, c, t=jnp.bfloat16: jax.ShapeDtypeStruct((r, c), t)
    return pl.pallas_call(
        plan_kernel,
        in_specs=[pl.BlockSpec(memory_space=pltpu.SMEM)] + [vm] * 4,
        out_specs=[vm] * 4,
        out_shape=[shape(tok + 2 * slots, d // 2 + tok)] * 2 + [shape(tok, tok), shape(tok, tok, jnp.float32)],
        compiler_params=pltpu.CompilerParams(vmem_limit_bytes=24 << 20),
        name="plan",
    )(info, route_ids.T, route_weights.T, queries, hidden)


def join_kernel(send_ref, mine_ref, other_ref, unit_ref):
    tok = mine_ref.shape[0]
    unit_ref[:tok] = mine_ref[...]
    unit_ref[tok:2 * tok] = other_ref[:tok]
    unit_ref[2 * tok:] = send_ref[tok:]
    unit_ref[2 * tok:, tok:2 * tok] = other_ref[tok:, :tok]


def join(send, mine, other):
    tok, width = mine.shape
    vm = pl.BlockSpec(memory_space=pltpu.VMEM)
    return pl.pallas_call(
        join_kernel,
        in_specs=[vm] * 3,
        out_specs=vm,
        out_shape=jax.ShapeDtypeStruct((2 * tok + 16, width), mine.dtype),
        compiler_params=pltpu.CompilerParams(vmem_limit_bytes=24 << 20),
        name="join",
    )(send, mine, other)


def pack_kernel(info_ref, gu_ref, down_ref, out_ref, sem):
    yhi = info_ref[2]
    units, wide = out_ref.shape[1], out_ref.shape[2]
    at = pl.ds(pl.multiple_of(info_ref[3] * units, units), units)
    if wide == down_ref.shape[2]:
        away, cols = 1 - yhi, pl.ds(0, wide)
    else:
        away = jnp.where(info_ref[5] == 0, yhi, 1 - yhi)
        cols = pl.ds(pl.multiple_of(info_ref[4] * wide, wide), wide)
    one = pltpu.make_async_copy(gu_ref.at[away, :, at, cols], out_ref.at[pl.ds(0, 2)], sem.at[0])
    two = pltpu.make_async_copy(down_ref.at[away, at, cols], out_ref.at[2], sem.at[1])
    one.start()
    two.start()
    one.wait()
    two.wait()


def pack(info, wide_t, down, cores, columns):
    hbm = pl.BlockSpec(memory_space=pl.ANY)
    units, d = down.shape[1] // cores, down.shape[2]
    return pl.pallas_call(
        pack_kernel,
        in_specs=[pl.BlockSpec(memory_space=pltpu.SMEM), hbm, hbm],
        out_specs=pl.BlockSpec(memory_space=pltpu.VMEM),
        out_shape=jax.ShapeDtypeStruct((3, units, d // columns), down.dtype),
        scratch_shapes=[pltpu.SemaphoreType.DMA((2,))],
        compiler_params=pltpu.CompilerParams(vmem_limit_bytes=60 << 20),
        name="pack",
    )(info, wide_t, down)


def norm_kernel(info_ref, own_ref, got_ref, mine_ref, other_ref, gain_ref, out_ref, *, part):
    slots, half = mine_ref.shape
    tok = own_ref.shape[0] - 2 * slots
    is_own = info_ref[2] == part

    def put(low, high):
        parts = []
        for n, att in enumerate((low, high)):
            rows = slice(tok + n * slots, tok + (n + 1) * slots)
            base = jnp.where(is_own, own_ref[rows, :half], got_ref[rows, :half]).astype(jnp.float32)
            parts.append((base + att.astype(jnp.float32)).astype(jnp.bfloat16).astype(jnp.float32))
        total = sum(jnp.sum(p * p, axis=1, keepdims=True) for p in parts)
        inv = lax.rsqrt(total / (2 * half) + 1e-6)
        for n, p in enumerate(parts):
            gain = gain_ref[:, n * half:(n + 1) * half].astype(jnp.float32)
            out_ref[:, n * half:(n + 1) * half] = (p * inv * gain).astype(jnp.bfloat16)

    @pl.when(info_ref[2] == 0)
    def _():
        put(mine_ref[...], other_ref[...])

    @pl.when(info_ref[2] != 0)
    def _():
        put(other_ref[...], mine_ref[...])


def norm_rows(info, own, got, part, mine, other, gain):
    slots, half = mine.shape
    vm = pl.BlockSpec(memory_space=pltpu.VMEM)
    return pl.pallas_call(
        functools.partial(norm_kernel, part=part),
        in_specs=[pl.BlockSpec(memory_space=pltpu.SMEM)] + [vm] * 5,
        out_specs=vm,
        out_shape=jax.ShapeDtypeStruct((slots, 2 * half), jnp.bfloat16),
        compiler_params=pltpu.CompilerParams(vmem_limit_bytes=16 << 20),
        name="norm_rows",
    )(info, own, got, mine, other, gain)


def assemble_kernel(info_ref, wo_ref, do_ref, r1_ref, r2_ref, *refs, steps):
    count = 2 * len(steps)
    blocks, w_ref, sem = refs[:count], refs[-2], refs[-1]
    yhi = info_ref[2]
    n, h = wo_ref.shape[2], r1_ref.shape[1]
    cps = []

    def cp(src, dst):
        cps.append(pltpu.make_async_copy(src, dst, sem.at[len(cps)]))

    for i in range(3):
        own = do_ref.at[yhi] if i == 2 else wo_ref.at[yhi, i]
        for src, at, size in ((own, 0, n), (r1_ref.at[i], n, h), (r2_ref.at[i], n + h, h)):
            cp(src, w_ref.at[i, pl.ds(at, size)])
        for k, block in enumerate(blocks):
            core, step = divmod(k, len(steps))
            wide = block.shape[2]
            col = lax.rem(info_ref[4] + steps[step] + len(steps), len(steps)) * wide
            for u in range(2):
                at = n + 2 * h + (2 * core + u) * h
                cp(block.at[3 * u + i], w_ref.at[i, pl.ds(at, h), pl.ds(pl.multiple_of(col, wide), wide)])
    for c in cps:
        c.start()
    for c in cps:
        c.wait()


def assemble(info, wo, do, r1, r2, blocks, steps, after):
    n, d = 2 * (wo.shape[2] + r1.shape[1] + r2.shape[1]), wo.shape[3]
    hbm = pl.BlockSpec(memory_space=pl.ANY)
    return pl.pallas_call(
        functools.partial(assemble_kernel, steps=steps),
        in_specs=[pl.BlockSpec(memory_space=pltpu.SMEM)] + [hbm] * (5 + len(blocks)),
        out_specs=pl.BlockSpec(memory_space=pltpu.VMEM),
        scratch_shapes=[pltpu.SemaphoreType.DMA((9 + 6 * len(blocks),))],
        out_shape=jax.ShapeDtypeStruct((3, n, d), jnp.bfloat16),
        compiler_params=pltpu.CompilerParams(vmem_limit_bytes=42 << 20),
        cost_estimate=pl.CostEstimate(flops=0, bytes_accessed=6 * n * d, transcendentals=0),
        name="assemble",
    )(info, wo, do, r1, r2, *blocks, after)


def expert_kernel(*refs, count, rows, after):
    xs, w_ref, ys = refs[:count], refs[count], refs[count + 1 + after:]
    x = jnp.concatenate([r[...] for r in xs], 0)
    nt = (((1,), (1,)), ((), ()))
    gate = lax.dot_general(x, w_ref[0], nt, preferred_element_type=jnp.float32)
    up = lax.dot_general(x, w_ref[1], nt, preferred_element_type=jnp.float32)
    inner = (gate / (1 + jnp.exp(-gate)) * up).astype(jnp.bfloat16)
    y = jnp.dot(inner, w_ref[2], preferred_element_type=jnp.float32).astype(jnp.bfloat16)
    for i in range(count):
        ys[i][...] = y[i * rows:(i + 1) * rows]


def experts(xs, w, after=()):
    count = len(xs)
    rows, d = xs[0].shape
    n = w.shape[1]
    vm = pl.BlockSpec(memory_space=pltpu.VMEM)
    return pl.pallas_call(
        functools.partial(expert_kernel, count=count, rows=rows, after=len(after)),
        in_specs=[vm] * (count + 1) + [pl.BlockSpec(memory_space=pl.ANY)] * len(after),
        out_specs=[vm] * count,
        out_shape=[jax.ShapeDtypeStruct((rows, d), jnp.bfloat16)] * count,
        compiler_params=pltpu.CompilerParams(vmem_limit_bytes=26 << 20),
        cost_estimate=pl.CostEstimate(flops=20 * count * rows * n * d, bytes_accessed=2 * (3 * n * d + 2 * count * rows * d), transcendentals=count * rows * n),
        name="experts",
    )(*xs, w, *after)


def combine_kernel(info_ref, hid_ref, mine_ref, other_ref, keep_ref, back_ref, hot_ref, factor_ref, out_ref):
    cap = back_ref.shape[0]
    is_mine = pl.program_id(0) // 2 == info_ref[2]
    att = jnp.where(is_mine, mine_ref[...].astype(jnp.float32), other_ref[...].astype(jnp.float32))
    stream = (hid_ref[...].astype(jnp.float32) + att).astype(jnp.bfloat16).astype(jnp.float32)
    one = jnp.dot(hot_ref[:, :cap], keep_ref[...], preferred_element_type=jnp.float32)
    two = jnp.dot(hot_ref[:, cap:2 * cap], back_ref[...], preferred_element_type=jnp.float32)
    out_ref[...] = (stream + one * factor_ref[:, 0:1] + two * factor_ref[:, 1:2]).astype(out_ref.dtype)


def combine(info, hidden, mine, other, keep, back, hot, factors):
    tok, d = hidden.shape
    cap = back.shape[0]
    wide = d // 4
    cols = lambda rows: pl.BlockSpec((rows, wide), lambda c, s: (0, c))
    half = pl.BlockSpec((tok, wide), lambda c, s: (0, lax.rem(c, 2)))
    whole = pl.BlockSpec((tok, tok), lambda c, s: (0, 0))
    return pl.pallas_call(
        combine_kernel,
        grid_spec=pltpu.PrefetchScalarGridSpec(
            num_scalar_prefetch=1,
            grid=(4,),
            in_specs=[cols(tok), half, half, cols(cap), cols(cap), whole, whole],
            out_specs=cols(tok),
        ),
        out_shape=jax.ShapeDtypeStruct((tok, d), hidden.dtype),
        compiler_params=pltpu.CompilerParams(vmem_limit_bytes=24 << 20),
        name="combine",
    )(info, hidden, mine, other, keep, back, hot, factors)


def shift(value, axis, size, steps):
    return lax.ppermute(value, axis, [(i, (i + steps) % size) for i in range(size)])


def swap(value, axis):
    return shift(value, axis, 2, 1)


def ring_moves(size):
    out = [0]
    for s in range(1, size // 2 + 1):
        out.append(-s)
        if 2 * s < size:
            out.append(s)
    return out


def ring_scatter(parts, signs, size):
    ups = [p[-2 * sign] for p, sign in zip(parts, signs)]
    downs = [shift(p[sign], "z", size, sign) for p, sign in zip(parts, signs)]
    for i, (p, sign) in enumerate(zip(parts, signs)):
        ups[i] = shift(ups[i], "z", size, -sign) + p[-sign]
    ups = [shift(u, "z", size, -sign) for u, sign in zip(ups, signs)]
    return [(ups[i], downs[i], p[0]) for i, p in enumerate(parts)]


def body(sizes, hidden_in, queries, keys_values, doc_ids, route_ids, route_weights, norm_gain, gate_up, down):
    tok, d = queries.shape
    capacity = tok // 4
    n_z, n_core, n_cx = sizes["z"], sizes["core"], sizes["cx"]
    yhi, z, core = lax.axis_index("yhi"), lax.axis_index("z"), lax.axis_index("core")
    half = n_z * tok
    n_ctx = n_cx * n_core
    moves = ring_moves(n_z)
    heads = keys_values.shape[1] // (4 * HD)
    cx, dp = lax.axis_index("cx"), lax.axis_index("dp")
    info = jnp.stack([z, yhi * half, yhi, core, cx, dp]).astype(jnp.int32)

    wide_t = jnp.swapaxes(gate_up, 2, 3)
    far = pack(info, wide_t, down, n_core, n_cx)
    place = lambda y, k, l: (y * n_z + k) * 2 + l
    across = [
        (place(y, k, l), place(y if l == 0 else 1 - y, (k + n_z // 2) % n_z, l)) for y in range(2) for k in range(n_z) for l in range(2)
    ]
    far = lax.ppermute(far, ("yhi", "z", "dp"), across)

    out, mine, hot, factors = plan(info, route_ids, route_weights, queries, hidden_in)
    got = swap(out, "yhi")

    send, kept = prepare(info, keys_values, doc_ids)
    other, far, got = lax.optimization_barrier((swap(send, "yhi"), far, got))
    unit = join(send, kept, other)
    far_2 = swap(far, "dp")
    theirs = pack(info, wide_t, down, n_core, 1)
    ahead = [(i, i + 1) for i in range(n_ctx - 1)]
    onward = lambda x: lax.ppermute(x, ("cx", "core"), ahead)
    own = {0: unit}
    prior = [onward(unit)]
    for s in range(1, n_z // 2 + 1):
        own[-s] = shift(own[1 - s], "z", n_z, 1)
        if 2 * s < n_z:
            own[s] = shift(own[s - 1], "z", n_z, -1)
        if s == 1:
            own[-s], far, far_2, theirs = lax.optimization_barrier((own[-s], far, far_2, theirs))
            got_1 = swap(theirs, "yhi")
            share = jnp.concatenate([far, far_2], 0)
            right = shift(share, "cx", n_cx, -1)
        if s == 2:
            own[-s], prior[0] = lax.optimization_barrier((own[-s], prior[0]))
        if s == 4:
            own[-s], right = lax.optimization_barrier((own[-s], right))
            far_right = shift(right, "cx", n_cx, -1)
    own = [own[m] for m in moves]
    groups = [range(0, 1), range(1, n_z // 2 + 1), range(n_z // 2 + 1, n_z - 1), range(n_z - 1, n_z)]
    layout = []
    for n, group in enumerate(groups):
        if n > 0:
            prior.append(onward(jnp.concatenate([own[i] for i in group], 0) if len(group) > 1 else own[group[0]]))
        layout += [(n, k * unit.shape[0]) for k in range(len(group))]
    layout += [(len(groups) + i, 0) for i in range(n_z)]
    prior[-1], mine, share = lax.optimization_barrier((prior[-1], mine, share))
    left = shift(share, "cx", n_cx, 1)
    pieces = prior + own

    gain = norm_gain[None]
    first = yhi == 0
    atts, rows = [], []
    steps = [0, -1, 1, 2]
    for part in range(2):
        if part == 1:
            mine, got_1, _ = lax.optimization_barrier((mine, got_1, atts[0]))
        att, keep, away = attend(info, mine, got, pieces, layout, moves, part, heads, tok)
        atts.append(att)
        rows.append(norm_rows(info, mine, got, part, keep, swap(away, "yhi"), gain))
    rows[1], left, far_right = lax.optimization_barrier((rows[1], left, far_right))
    shares = [share, left, right, far_right]
    got_2 = swap(got_1, "core")
    own_att = jnp.where(first, atts[0], atts[1])
    away_att, rows[1] = lax.optimization_barrier((jnp.where(first, atts[1], atts[0]), rows[1]))
    other_att = swap(away_att, "yhi")

    signs = [1, -1]
    rows = [{0: x, -sign: shift(x, "z", n_z, sign), sign: shift(x, "z", n_z, -sign)} for x, sign in zip(rows, signs)]
    for g, sign in zip(rows, signs):
        g[-2 * sign] = shift(g[-sign], "z", n_z, sign)
    blocks = shares + [swap(x, "core") for x in shares]
    weights = assemble(info, wide_t, down, got_1, got_2, blocks, steps, rows[1][0])
    keys = [(i, m) for i in range(2) for m in (0, -1, 1)]
    first_out = experts([rows[i][m] for i, m in keys], weights)
    last_out = experts([g[-2 * sign] for g, sign in zip(rows, signs)], weights, after=[first_out[0], other_att])
    outs = [{-2 * sign: y} for sign, y in zip(signs, last_out)]
    for (i, m), y in zip(keys, first_out):
        outs[i][m] = y
    sums = [ups.astype(jnp.float32) + downs + here for ups, downs, here in ring_scatter(outs, signs, n_z)]
    back = swap(jnp.where(first, sums[1], sums[0]).astype(jnp.bfloat16), "yhi")
    keep = jnp.where(first, sums[0], sums[1]).astype(jnp.bfloat16)
    return combine(info, hidden_in, own_att, other_att, keep, back, hot, factors)


def solution(mesh):
    sizes = {"cx": mesh.shape["ctx"] // 2, "core": 2, "yhi": 2, "z": mesh.shape["exp"] // 2, "dp": mesh.shape["dp"]}
    fine = Mesh(mesh.devices.reshape(tuple(sizes.values())), tuple(sizes))
    tokens = ("dp", "cx", "core", "yhi", "z")
    rows = P(tokens, None)
    hidden = ("yhi", "z")
    in_specs = (rows, rows, rows, P(tokens), rows, rows, P(), P(None, None, None, hidden), P(None, hidden, None))
    return jax.shard_map(
        functools.partial(body, sizes), mesh=fine, in_specs=in_specs, out_specs=rows, check_vma=False
    )
```

```python
import functools
import math

import jax
import jax.numpy as jnp
from jax import lax
from jax.experimental import pallas as pl
from jax.experimental.pallas import tpu as pltpu
from jax.sharding import Mesh
from jax.sharding import PartitionSpec as P

EXP_FLIGHT = 2
HD = 128
GROUP = 7
EXP2_SCALE = math.log2(math.e) / math.sqrt(HD)

def attend_kernel(info_ref, q_own_ref, q_got_ref, place_own_ref, place_got_ref, *refs, tok, span, moves, heads, layout, part):
    arrays, out_ref, low_ref, high_ref = refs[:-11], refs[-11], refs[-10], refs[-9]
    kv, ids, start_scr, m_scr, l_scr, acc_scr, bounds, sem = refs[-8:]
    c = pl.program_id(0)
    z = info_ref[0]
    half = len(moves) * tok
    near = pl.multiple_of(info_ref[1], half)
    far = pl.multiple_of(half - info_ref[1], half)
    first = pl.multiple_of(part * half + z * tok, tok)
    is_own = info_ref[2] == part

    @pl.when(c == 0)
    def _():
        blocks = []
        copies = []
        for n, (which, row) in enumerate(layout):
            piece = arrays[which]
            place = lax.rem(z + moves[n % len(moves)] + len(moves), len(moves)) * tok
            slab = n // len(moves) * 2 * half
            for side, base in ((0, near), (1, far)):
                at = pl.multiple_of(slab + base + place, tok)
                cp = pltpu.make_async_copy(piece.at[pl.ds(row + side * tok, tok)], kv.at[pl.ds(at, tok)], sem.at[n, side])
                blocks.append((cp, (at >= first) & (at <= first + 2 * half)))
            copies.append(pltpu.make_async_copy(piece.at[pl.ds(row + 2 * tok, 16)], ids.at[n], sem.at[n, 2]))
        for cp in copies:
            cp.start()
        for cp, needed in blocks:
            pl.when(needed)(cp.start)
        for cp in copies:
            cp.wait()
        own = [ids[len(moves), 0:1, n * tok:(n + 1) * tok].astype(jnp.float32) for n in range(2)]
        own = jnp.where(is_own, own[0], own[1])
        own = jnp.broadcast_to(own, (tok, tok)).T
        less = jnp.zeros((tok, tok), jnp.float32)
        for n in range(len(layout)):
            for side in range(2):
                row = ids[n, 0:1, side * tok:(side + 1) * tok].astype(jnp.float32)
                less = less + jnp.where(row < own, 1.0, 0.0)
        begin = jnp.sum(less, axis=1, keepdims=True)
        start_scr[...] = begin.astype(jnp.int32)
        bounds[0] = jnp.min(begin).astype(jnp.int32)
        bounds[1] = jnp.max(begin).astype(jnp.int32)
        for cp, needed in blocks:
            pl.when(needed)(cp.wait)

    start_min, start_max = bounds[0], bounds[1]
    q = jnp.where(is_own, q_own_ref[...], q_got_ref[...])
    q = jnp.concatenate([q[:, g * HD:(g + 1) * HD] for g in range(GROUP)], 0)
    start = start_scr[...]
    row = lax.broadcasted_iota(jnp.int32, (tok, 1), 0) + first + 2 * half
    key_col = pl.multiple_of(c * HD, HD)
    value_col = pl.multiple_of((heads + c) * HD, HD)

    def keys(offset, width):
        return kv[pl.ds(offset, width), pl.ds(key_col, HD)]

    def values(offset, width):
        return kv[pl.ds(offset, width), pl.ds(value_col, HD)]

    def scores(offset, width):
        return lax.dot_general(q, keys(offset, width), (((1,), (1,)), ((), ())), preferred_element_type=jnp.float32)

    def rowmax(s, width):
        t = s[:, :128]
        for j in range(1, width // 128):
            t = jnp.maximum(t, s[:, j * 128:(j + 1) * 128])
        return jnp.max(t, axis=1, keepdims=True)

    def lanesum(p, width):
        t = p[:, :128]
        for j in range(1, width // 128):
            t = t + p[:, j * 128:(j + 1) * 128]
        return t

    def masked(s, offset, width, causal):
        key = lax.broadcasted_iota(jnp.int32, (tok, width), 1) + offset
        ok = key >= start
        if causal:
            ok = ok & (key <= row)
        return jnp.where(ok[None], s.reshape(GROUP, tok, width), -1e30).reshape(GROUP * tok, width)

    own = pl.multiple_of(first + 2 * half, tok)
    s = masked(scores(own, tok), own, tok, True)
    m = rowmax(s, tok)
    p = jnp.exp2((s - m) * EXP2_SCALE)
    m_scr[...] = jnp.broadcast_to(m, m_scr.shape)
    l_scr[...] = lanesum(p, tok)
    acc_scr[...] = jnp.dot(p.astype(jnp.bfloat16), values(own, tok), preferred_element_type=jnp.float32)

    def step(i, mask):
        offset = pl.multiple_of(first + i * span, tok)
        s = scores(offset, span)
        if mask:
            s = masked(s, offset, span, False)
        old = m_scr[...]
        new = jnp.maximum(old, rowmax(s, span))
        m_scr[...] = new
        shrink = jnp.exp2((old - new) * EXP2_SCALE)
        p = jnp.exp2((s - jnp.concatenate([new] * (span // 128), 1)) * EXP2_SCALE)
        l_scr[...] = l_scr[...] * shrink + lanesum(p, span)
        acc_scr[...] = acc_scr[...] * shrink + jnp.dot(p.astype(jnp.bfloat16), values(offset, span), preferred_element_type=jnp.float32)

    steps = 2 * half // span

    def loop(i, carry):
        whole = start_max <= first + i * span

        @pl.when(whole)
        def _():
            step(i, False)

        @pl.when(jnp.logical_not(whole))
        def _():
            step(i, True)

        return carry

    lax.fori_loop(jnp.clip(lax.div(start_min - first, span), 0, steps), steps, loop, 0)

    total = jnp.sum(l_scr[...], axis=1, keepdims=True)
    att = (acc_scr[...] / total).astype(jnp.bfloat16)
    att = jnp.concatenate([att[g * tok:(g + 1) * tok] for g in range(GROUP)], 1)
    out_ref[...] = att
    place = jnp.where(is_own, place_own_ref[...], place_got_ref[...])
    rows = jnp.dot(place, att, preferred_element_type=jnp.float32).astype(jnp.bfloat16)
    low_ref[...] = rows[:rows.shape[0] // 2]
    high_ref[...] = rows[rows.shape[0] // 2:]


def attend(info, own, got, pieces, layout, moves, part, heads, tok, span=512):
    slots = tok // 4
    wide = GROUP * HD
    n = len(moves)
    hbm = pl.BlockSpec(memory_space=pl.ANY)
    scratch = pltpu.VMEM((GROUP * tok, 128), jnp.float32)
    return pl.pallas_call(
        functools.partial(attend_kernel, tok=tok, span=span, moves=moves, heads=heads, layout=layout, part=part),
        grid_spec=pltpu.PrefetchScalarGridSpec(
            num_scalar_prefetch=1,
            grid=(heads,),
            in_specs=[
                pl.BlockSpec((tok, wide), lambda c, s: (0, c)),
                pl.BlockSpec((tok, wide), lambda c, s: (0, c)),
                pl.BlockSpec((2 * slots, tok), lambda c, s: (tok // (2 * slots), heads * GROUP)),
                pl.BlockSpec((2 * slots, tok), lambda c, s: (tok // (2 * slots), heads * GROUP)),
            ] + [hbm] * len(pieces),
            out_specs=[pl.BlockSpec((r, wide), lambda c, s: (0, c)) for r in (tok, slots, slots)],
            scratch_shapes=[
                pltpu.VMEM((4 * n * tok, 2 * heads * HD), jnp.bfloat16),
                pltpu.VMEM((2 * n, 16, 2 * heads * HD), jnp.bfloat16),
                pltpu.VMEM((tok, 1), jnp.int32),
                scratch, scratch, scratch,
                pltpu.SMEM((2,), jnp.int32),
                pltpu.SemaphoreType.DMA((2 * n, 3)),
            ],
        ),
        out_shape=[jax.ShapeDtypeStruct((r, heads * wide), jnp.bfloat16) for r in (tok, slots, slots)],
        compiler_params=pltpu.CompilerParams(vmem_limit_bytes=60 << 20),
        cost_estimate=pl.CostEstimate(flops=8 * 10**9, bytes_accessed=5 << 20, transcendentals=4 * 10**6),
        name="attend",
    )(info, own, got, own, got, *pieces)


def prepare_kernel(info_ref, kv_ref, doc_ref, send_ref, mine_ref):
    tok = kv_ref.shape[0]
    w = kv_ref.shape[1] // 4
    send_ref[tok:, :] = jnp.zeros((16, 2 * w), send_ref.dtype)
    send_ref[tok:tok + 16, :tok] = jnp.broadcast_to((doc_ref[...] + 1).astype(jnp.float32), (16, tok)).astype(send_ref.dtype)
    for yhi in range(2):
        @pl.when(info_ref[2] == yhi)
        def _(yhi=yhi):
            away = 1 - yhi
            mine_ref[:, :w] = kv_ref[:, yhi * w:(yhi + 1) * w]
            mine_ref[:, w:] = kv_ref[:, (2 + yhi) * w:(3 + yhi) * w]
            send_ref[:tok, :w] = kv_ref[:, away * w:(away + 1) * w]
            send_ref[:tok, w:] = kv_ref[:, (2 + away) * w:(3 + away) * w]


def prepare(info, keys_values, doc_ids):
    tok, width = keys_values.shape
    vm = pl.BlockSpec(memory_space=pltpu.VMEM)
    shape = lambda r, c: jax.ShapeDtypeStruct((r, c), jnp.bfloat16)
    return pl.pallas_call(
        prepare_kernel,
        in_specs=[pl.BlockSpec(memory_space=pltpu.SMEM)] + [vm] * 2,
        out_specs=[vm] * 2,
        out_shape=[shape(tok + 16, width // 2), shape(tok, width // 2)],
        compiler_params=pltpu.CompilerParams(vmem_limit_bytes=24 << 20),
        name="prepare",
    )(info, keys_values, doc_ids[None])


def plan_kernel(info_ref, ids_ref, weights_ref, q_ref, hid_ref, out_ref, own_ref, hot_ref, factor_ref):
    tok = hid_ref.shape[0]
    slots = (out_ref.shape[0] - tok) // 2
    q = q_ref.shape[1] // 2
    yhi = info_ref[2]
    below = lax.broadcasted_iota(jnp.int32, (tok, tok), 0) <= lax.broadcasted_iota(jnp.int32, (tok, tok), 1)
    below = below.astype(jnp.float32).astype(jnp.bfloat16)
    places, factors = [], []
    for flight in (yhi, 1 - yhi):
        chosen = ids_ref[...] == flight
        routed = jnp.max(jnp.where(chosen, 1.0, 0.0), axis=0, keepdims=True)
        factors.append(jnp.sum(jnp.where(chosen, weights_ref[...], 0.0), axis=0, keepdims=True))
        ranks = jnp.dot(jnp.broadcast_to(routed, (16, tok)).astype(jnp.bfloat16), below, preferred_element_type=jnp.float32)
        ranks = jnp.where(routed > 0.5, ranks[:1] - 1.0, -1.0)
        slot = lax.broadcasted_iota(jnp.int32, (slots, tok), 0).astype(jnp.float32)
        places.append(jnp.where(slot == ranks, 1.0, 0.0))
    place_f = jnp.concatenate(places, 0)
    place = place_f.astype(jnp.bfloat16)
    hot_ref[...] = jnp.concatenate([place_f, jnp.zeros((tok - 2 * slots, tok), jnp.float32)], 0).T.astype(jnp.bfloat16)
    factor_ref[...] = jnp.concatenate([factors[0], factors[1], jnp.zeros((tok - 2, tok), jnp.float32)], 0).T
    rows = jnp.dot(place, hid_ref[...], preferred_element_type=jnp.float32).astype(jnp.bfloat16)
    for n, ref in enumerate((own_ref, out_ref)):
        ref[:tok, q:] = jnp.zeros((tok, tok), jnp.bfloat16)
        ref[tok:tok + slots, :q] = rows[n * slots:(n + 1) * slots, :q]
        ref[tok + slots:, :q] = rows[n * slots:(n + 1) * slots, q:]
        ref[tok:tok + slots, q:] = place[n * slots:(n + 1) * slots]
        ref[tok + slots:, q:] = place[(1 - n) * slots:(2 - n) * slots]

    for side in range(2):
        @pl.when(yhi == side)
        def _(side=side):
            own_ref[:tok, :q] = q_ref[:, side * q:(side + 1) * q]
            out_ref[:tok, :q] = q_ref[:, (1 - side) * q:(2 - side) * q]


def plan(info, route_ids, route_weights, queries, hidden):
    tok, d = hidden.shape
    slots = tok // 4
    vm = pl.BlockSpec(memory_space=pltpu.VMEM)
    shape = lambda r, c, t=jnp.bfloat16: jax.ShapeDtypeStruct((r, c), t)
    return pl.pallas_call(
        plan_kernel,
        in_specs=[pl.BlockSpec(memory_space=pltpu.SMEM)] + [vm] * 4,
        out_specs=[vm] * 4,
        out_shape=[shape(tok + 2 * slots, d // 2 + tok)] * 2 + [shape(tok, tok), shape(tok, tok, jnp.float32)],
        compiler_params=pltpu.CompilerParams(vmem_limit_bytes=24 << 20),
        name="plan",
    )(info, route_ids.T, route_weights.T, queries, hidden)


def join_kernel(send_ref, mine_ref, other_ref, unit_ref):
    tok = mine_ref.shape[0]
    unit_ref[:tok] = mine_ref[...]
    unit_ref[tok:2 * tok] = other_ref[:tok]
    unit_ref[2 * tok:] = send_ref[tok:]
    unit_ref[2 * tok:, tok:2 * tok] = other_ref[tok:, :tok]


def join(send, mine, other):
    tok, width = mine.shape
    vm = pl.BlockSpec(memory_space=pltpu.VMEM)
    return pl.pallas_call(
        join_kernel,
        in_specs=[vm] * 3,
        out_specs=vm,
        out_shape=jax.ShapeDtypeStruct((2 * tok + 16, width), mine.dtype),
        compiler_params=pltpu.CompilerParams(vmem_limit_bytes=24 << 20),
        name="join",
    )(send, mine, other)


def pack_kernel(info_ref, gu_ref, down_ref, out_ref, sem):
    yhi = info_ref[2]
    units, wide = out_ref.shape[1], out_ref.shape[2]
    at = pl.ds(pl.multiple_of(info_ref[3] * units, units), units)
    if wide == down_ref.shape[2]:
        away, cols = 1 - yhi, pl.ds(0, wide)
    else:
        away = jnp.where(info_ref[5] == 0, yhi, 1 - yhi)
        cols = pl.ds(pl.multiple_of(info_ref[4] * wide, wide), wide)
    one = pltpu.make_async_copy(gu_ref.at[away, :, at, cols], out_ref.at[pl.ds(0, 2)], sem.at[0])
    two = pltpu.make_async_copy(down_ref.at[away, at, cols], out_ref.at[2], sem.at[1])
    one.start()
    two.start()
    one.wait()
    two.wait()


def pack(info, wide_t, down, cores, columns):
    hbm = pl.BlockSpec(memory_space=pl.ANY)
    units, d = down.shape[1] // cores, down.shape[2]
    return pl.pallas_call(
        pack_kernel,
        in_specs=[pl.BlockSpec(memory_space=pltpu.SMEM), hbm, hbm],
        out_specs=pl.BlockSpec(memory_space=pltpu.VMEM),
        out_shape=jax.ShapeDtypeStruct((3, units, d // columns), down.dtype),
        scratch_shapes=[pltpu.SemaphoreType.DMA((2,))],
        compiler_params=pltpu.CompilerParams(vmem_limit_bytes=60 << 20),
        name="pack",
    )(info, wide_t, down)


def norm_kernel(info_ref, own_ref, got_ref, mine_ref, other_ref, gain_ref, out_ref, *, part):
    slots, half = mine_ref.shape
    tok = own_ref.shape[0] - 2 * slots
    is_own = info_ref[2] == part

    def put(low, high):
        parts = []
        for n, att in enumerate((low, high)):
            rows = slice(tok + n * slots, tok + (n + 1) * slots)
            base = jnp.where(is_own, own_ref[rows, :half], got_ref[rows, :half]).astype(jnp.float32)
            parts.append((base + att.astype(jnp.float32)).astype(jnp.bfloat16).astype(jnp.float32))
        total = sum(jnp.sum(p * p, axis=1, keepdims=True) for p in parts)
        inv = lax.rsqrt(total / (2 * half) + 1e-6)
        for n, p in enumerate(parts):
            gain = gain_ref[:, n * half:(n + 1) * half].astype(jnp.float32)
            out_ref[:, n * half:(n + 1) * half] = (p * inv * gain).astype(jnp.bfloat16)

    @pl.when(info_ref[2] == 0)
    def _():
        put(mine_ref[...], other_ref[...])

    @pl.when(info_ref[2] != 0)
    def _():
        put(other_ref[...], mine_ref[...])


def norm_rows(info, own, got, part, mine, other, gain):
    slots, half = mine.shape
    vm = pl.BlockSpec(memory_space=pltpu.VMEM)
    return pl.pallas_call(
        functools.partial(norm_kernel, part=part),
        in_specs=[pl.BlockSpec(memory_space=pltpu.SMEM)] + [vm] * 5,
        out_specs=vm,
        out_shape=jax.ShapeDtypeStruct((slots, 2 * half), jnp.bfloat16),
        compiler_params=pltpu.CompilerParams(vmem_limit_bytes=16 << 20),
        name="norm_rows",
    )(info, own, got, mine, other, gain)


def assemble_kernel(info_ref, wo_ref, do_ref, r1_ref, r2_ref, *refs, steps):
    count = 2 * len(steps)
    blocks, w_ref, sem = refs[:count], refs[-2], refs[-1]
    yhi = info_ref[2]
    n, h = wo_ref.shape[2], r1_ref.shape[1]
    cps = []

    def cp(src, dst):
        cps.append(pltpu.make_async_copy(src, dst, sem.at[len(cps)]))

    for i in range(3):
        own = do_ref.at[yhi] if i == 2 else wo_ref.at[yhi, i]
        for src, at, size in ((own, 0, n), (r1_ref.at[i], n, h), (r2_ref.at[i], n + h, h)):
            cp(src, w_ref.at[i, pl.ds(at, size)])
        for k, block in enumerate(blocks):
            core, step = divmod(k, len(steps))
            wide = block.shape[2]
            col = lax.rem(info_ref[4] + steps[step] + len(steps), len(steps)) * wide
            for u in range(2):
                at = n + 2 * h + (2 * core + u) * h
                cp(block.at[3 * u + i], w_ref.at[i, pl.ds(at, h), pl.ds(pl.multiple_of(col, wide), wide)])
    for c in cps:
        c.start()
    for c in cps:
        c.wait()


def assemble(info, wo, do, r1, r2, blocks, steps, after):
    n, d = 2 * (wo.shape[2] + r1.shape[1] + r2.shape[1]), wo.shape[3]
    hbm = pl.BlockSpec(memory_space=pl.ANY)
    return pl.pallas_call(
        functools.partial(assemble_kernel, steps=steps),
        in_specs=[pl.BlockSpec(memory_space=pltpu.SMEM)] + [hbm] * (5 + len(blocks)),
        out_specs=pl.BlockSpec(memory_space=pltpu.VMEM),
        scratch_shapes=[pltpu.SemaphoreType.DMA((9 + 6 * len(blocks),))],
        out_shape=jax.ShapeDtypeStruct((3, n, d), jnp.bfloat16),
        compiler_params=pltpu.CompilerParams(vmem_limit_bytes=20 << 20),
        cost_estimate=pl.CostEstimate(flops=0, bytes_accessed=6 * n * d, transcendentals=0),
        name="assemble",
    )(info, wo, do, r1, r2, *blocks, after)


def expert_kernel(*refs, count, rows, after):
    xs, w_ref, ys = refs[:count], refs[count], refs[count + 1 + after:]
    x = jnp.concatenate([r[...] for r in xs], 0)
    nt = (((1,), (1,)), ((), ()))
    gate = lax.dot_general(x, w_ref[0], nt, preferred_element_type=jnp.float32)
    up = lax.dot_general(x, w_ref[1], nt, preferred_element_type=jnp.float32)
    inner = (gate / (1 + jnp.exp(-gate)) * up).astype(jnp.bfloat16)
    y = jnp.dot(inner, w_ref[2], preferred_element_type=jnp.float32).astype(jnp.bfloat16)
    for i in range(count):
        ys[i][...] = y[i * rows:(i + 1) * rows]


def experts(xs, w, after=()):
    count = len(xs)
    rows, d = xs[0].shape
    n = w.shape[1]
    vm = pl.BlockSpec(memory_space=pltpu.VMEM)
    return pl.pallas_call(
        functools.partial(expert_kernel, count=count, rows=rows, after=len(after)),
        in_specs=[vm] * (count + 1) + [pl.BlockSpec(memory_space=pl.ANY)] * len(after),
        out_specs=[vm] * count,
        out_shape=[jax.ShapeDtypeStruct((rows, d), jnp.bfloat16)] * count,
        compiler_params=pltpu.CompilerParams(vmem_limit_bytes=26 << 20),
        cost_estimate=pl.CostEstimate(flops=20 * count * rows * n * d, bytes_accessed=2 * (3 * n * d + 2 * count * rows * d), transcendentals=count * rows * n),
        name="experts",
    )(*xs, w, *after)


def combine_kernel(info_ref, hid_ref, mine_ref, other_ref, keep_ref, back_ref, hot_ref, factor_ref, out_ref):
    cap = back_ref.shape[0]
    is_mine = pl.program_id(0) // 2 == info_ref[2]
    att = jnp.where(is_mine, mine_ref[...].astype(jnp.float32), other_ref[...].astype(jnp.float32))
    stream = (hid_ref[...].astype(jnp.float32) + att).astype(jnp.bfloat16).astype(jnp.float32)
    one = jnp.dot(hot_ref[:, :cap], keep_ref[...], preferred_element_type=jnp.float32)
    two = jnp.dot(hot_ref[:, cap:2 * cap], back_ref[...], preferred_element_type=jnp.float32)
    out_ref[...] = (stream + one * factor_ref[:, 0:1] + two * factor_ref[:, 1:2]).astype(out_ref.dtype)


def combine(info, hidden, mine, other, keep, back, hot, factors):
    tok, d = hidden.shape
    cap = back.shape[0]
    wide = d // 4
    cols = lambda rows: pl.BlockSpec((rows, wide), lambda c, s: (0, c))
    half = pl.BlockSpec((tok, wide), lambda c, s: (0, lax.rem(c, 2)))
    whole = pl.BlockSpec((tok, tok), lambda c, s: (0, 0))
    return pl.pallas_call(
        combine_kernel,
        grid_spec=pltpu.PrefetchScalarGridSpec(
            num_scalar_prefetch=1,
            grid=(4,),
            in_specs=[cols(tok), half, half, cols(cap), cols(cap), whole, whole],
            out_specs=cols(tok),
        ),
        out_shape=jax.ShapeDtypeStruct((tok, d), hidden.dtype),
        compiler_params=pltpu.CompilerParams(vmem_limit_bytes=24 << 20),
        name="combine",
    )(info, hidden, mine, other, keep, back, hot, factors)


def shift(value, axis, size, steps):
    return lax.ppermute(value, axis, [(i, (i + steps) % size) for i in range(size)])


def swap(value, axis):
    return shift(value, axis, 2, 1)


def ring_moves(size):
    out = [0]
    for s in range(1, size // 2 + 1):
        out.append(-s)
        if 2 * s < size:
            out.append(s)
    return out


def ring_scatter(parts, signs, size):
    ups = [p[-2 * sign] for p, sign in zip(parts, signs)]
    downs = [shift(p[sign], "z", size, sign) for p, sign in zip(parts, signs)]
    for i, (p, sign) in enumerate(zip(parts, signs)):
        ups[i] = shift(ups[i], "z", size, -sign) + p[-sign]
    ups = [shift(u, "z", size, -sign) for u, sign in zip(ups, signs)]
    return [(ups[i], downs[i], p[0]) for i, p in enumerate(parts)]


def body(sizes, hidden_in, queries, keys_values, doc_ids, route_ids, route_weights, norm_gain, gate_up, down):
    tok, d = queries.shape
    capacity = tok // 4
    n_z, n_core, n_cx = sizes["z"], sizes["core"], sizes["cx"]
    yhi, z, core = lax.axis_index("yhi"), lax.axis_index("z"), lax.axis_index("core")
    half = n_z * tok
    n_ctx = n_cx * n_core
    moves = ring_moves(n_z)
    heads = keys_values.shape[1] // (4 * HD)
    cx, dp = lax.axis_index("cx"), lax.axis_index("dp")
    info = jnp.stack([z, yhi * half, yhi, core, cx, dp]).astype(jnp.int32)

    wide_t = jnp.swapaxes(gate_up, 2, 3)
    far = pack(info, wide_t, down, n_core, n_cx)
    place = lambda y, k, l: (y * n_z + k) * 2 + l
    across = [
        (place(y, k, l), place(y if l == 0 else 1 - y, (k + n_z // 2) % n_z, l)) for y in range(2) for k in range(n_z) for l in range(2)
    ]
    far = lax.ppermute(far, ("yhi", "z", "dp"), across)

    send, kept = prepare(info, keys_values, doc_ids)
    other = swap(send, "yhi")

    out, mine, hot, factors = plan(info, route_ids, route_weights, queries, hidden_in)
    out, other = lax.optimization_barrier((out, other))
    got = swap(out, "yhi")
    other, far = lax.optimization_barrier((other, far))
    unit = join(send, kept, other)
    far_2 = swap(far, "dp")
    theirs = pack(info, wide_t, down, n_core, 1)
    ahead = [(i, i + 1) for i in range(n_ctx - 1)]
    onward = lambda x: lax.ppermute(x, ("cx", "core"), ahead)
    own = {0: unit}
    prior = [onward(unit)]
    for s in range(1, n_z // 2 + 1):
        own[-s] = shift(own[1 - s], "z", n_z, 1)
        if 2 * s < n_z:
            own[s] = shift(own[s - 1], "z", n_z, -1)
        if s == 1:
            own[-s], far, far_2, theirs = lax.optimization_barrier((own[-s], far, far_2, theirs))
            got_1 = swap(theirs, "yhi")
            share = jnp.concatenate([far, far_2], 0)
            right = shift(share, "cx", n_cx, -1)
        if s == 2:
            own[-s], prior[0], got = lax.optimization_barrier((own[-s], prior[0], got))
        if s == 4:
            own[-s], right = lax.optimization_barrier((own[-s], right))
            far_right = shift(right, "cx", n_cx, -1)
    own = [own[m] for m in moves]
    groups = [range(0, 1), range(1, n_z // 2 + 1), range(n_z // 2 + 1, n_z - 1), range(n_z - 1, n_z)]
    layout = []
    for n, group in enumerate(groups):
        if n > 0:
            prior.append(onward(jnp.concatenate([own[i] for i in group], 0) if len(group) > 1 else own[group[0]]))
        layout += [(n, k * unit.shape[0]) for k in range(len(group))]
    layout += [(len(groups) + i, 0) for i in range(n_z)]
    prior[-1], mine, share = lax.optimization_barrier((prior[-1], mine, share))
    left = shift(share, "cx", n_cx, 1)
    pieces = prior + own

    gain = norm_gain[None]
    first = yhi == 0
    atts, rows = [], []
    steps = [0, -1, 1, 2]
    for part in range(2):
        if part == 1:
            mine, got_1, _ = lax.optimization_barrier((mine, got_1, atts[0]))
        att, keep, away = attend(info, mine, got, pieces, layout, moves, part, heads, tok)
        atts.append(att)
        rows.append(norm_rows(info, mine, got, part, keep, swap(away, "yhi"), gain))
    rows[1], left, far_right = lax.optimization_barrier((rows[1], left, far_right))
    shares = [share, left, right, far_right]
    got_2 = swap(got_1, "core")
    own_att = jnp.where(first, atts[0], atts[1])
    away_att, rows[1] = lax.optimization_barrier((jnp.where(first, atts[1], atts[0]), rows[1]))
    other_att = swap(away_att, "yhi")

    signs = [1, -1]
    rows = [{0: x, -sign: shift(x, "z", n_z, sign), sign: shift(x, "z", n_z, -sign)} for x, sign in zip(rows, signs)]
    for g, sign in zip(rows, signs):
        g[-2 * sign] = shift(g[-sign], "z", n_z, sign)
    blocks = shares + [swap(x, "core") for x in shares]
    weights = assemble(info, wide_t, down, got_1, got_2, blocks, steps, rows[1][0])
    keys = [(i, m) for i in range(2) for m in (0, -1, 1)]
    first_out = experts([rows[i][m] for i, m in keys], weights)
    last_out = experts([g[-2 * sign] for g, sign in zip(rows, signs)], weights, after=[first_out[0], other_att])
    outs = [{-2 * sign: y} for sign, y in zip(signs, last_out)]
    for (i, m), y in zip(keys, first_out):
        outs[i][m] = y
    sums = [ups.astype(jnp.float32) + downs + here for ups, downs, here in ring_scatter(outs, signs, n_z)]
    back = swap(jnp.where(first, sums[1], sums[0]).astype(jnp.bfloat16), "yhi")
    keep = jnp.where(first, sums[0], sums[1]).astype(jnp.bfloat16)
    return combine(info, hidden_in, own_att, other_att, keep, back, hot, factors)


def solution(mesh):
    sizes = {"cx": mesh.shape["ctx"] // 2, "core": 2, "yhi": 2, "z": mesh.shape["exp"] // 2, "dp": mesh.shape["dp"]}
    fine = Mesh(mesh.devices.reshape(tuple(sizes.values())), tuple(sizes))
    tokens = ("dp", "cx", "core", "yhi", "z")
    rows = P(tokens, None)
    hidden = ("yhi", "z")
    in_specs = (rows, rows, rows, P(tokens), rows, rows, P(), P(None, None, None, hidden), P(None, hidden, None))
    return jax.shard_map(
        functools.partial(body, sizes), mesh=fine, in_specs=in_specs, out_specs=rows, check_vma=False
    )
```

```python
import functools
import math

import jax
import jax.numpy as jnp
from jax import lax
from jax.experimental import pallas as pl
from jax.experimental.pallas import tpu as pltpu
from jax.sharding import Mesh
from jax.sharding import PartitionSpec as P

EXP_FLIGHT = 2
HD = 128
GROUP = 7
EXP2_SCALE = math.log2(math.e) / math.sqrt(HD)

def attend_kernel(info_ref, q_own_ref, q_got_ref, place_own_ref, place_got_ref, *refs, tok, span, moves, heads, layout, part):
    arrays, out_ref, low_ref, high_ref = refs[:-11], refs[-11], refs[-10], refs[-9]
    kv, ids, start_scr, m_scr, l_scr, acc_scr, bounds, sem = refs[-8:]
    c = pl.program_id(0)
    z = info_ref[0]
    half = len(moves) * tok
    near = pl.multiple_of(info_ref[1], half)
    far = pl.multiple_of(half - info_ref[1], half)
    first = pl.multiple_of(part * half + z * tok, tok)
    is_own = info_ref[2] == part

    @pl.when(c == 0)
    def _():
        blocks = []
        copies = []
        for n, (which, row) in enumerate(layout):
            piece = arrays[which]
            place = lax.rem(z + moves[n % len(moves)] + len(moves), len(moves)) * tok
            slab = n // len(moves) * 2 * half
            for side, base in ((0, near), (1, far)):
                at = pl.multiple_of(slab + base + place, tok)
                cp = pltpu.make_async_copy(piece.at[pl.ds(row + side * tok, tok)], kv.at[pl.ds(at, tok)], sem.at[n, side])
                blocks.append((cp, (at >= first) & (at <= first + 2 * half)))
            copies.append(pltpu.make_async_copy(piece.at[pl.ds(row + 2 * tok, 16)], ids.at[n], sem.at[n, 2]))
        for cp in copies:
            cp.start()
        for cp, needed in blocks:
            pl.when(needed)(cp.start)
        for cp in copies:
            cp.wait()
        own = [ids[len(moves), 0:1, n * tok:(n + 1) * tok].astype(jnp.float32) for n in range(2)]
        own = jnp.where(is_own, own[0], own[1])
        own = jnp.broadcast_to(own, (tok, tok)).T
        less = jnp.zeros((tok, tok), jnp.float32)
        for n in range(len(layout)):
            for side in range(2):
                row = ids[n, 0:1, side * tok:(side + 1) * tok].astype(jnp.float32)
                less = less + jnp.where(row < own, 1.0, 0.0)
        begin = jnp.sum(less, axis=1, keepdims=True)
        start_scr[...] = begin.astype(jnp.int32)
        bounds[0] = jnp.min(begin).astype(jnp.int32)
        bounds[1] = jnp.max(begin).astype(jnp.int32)
        for cp, needed in blocks:
            pl.when(needed)(cp.wait)

    start_min, start_max = bounds[0], bounds[1]
    q = jnp.where(is_own, q_own_ref[...], q_got_ref[...])
    q = jnp.concatenate([q[:, g * HD:(g + 1) * HD] for g in range(GROUP)], 0)
    start = start_scr[...]
    row = lax.broadcasted_iota(jnp.int32, (tok, 1), 0) + first + 2 * half
    key_col = pl.multiple_of(c * HD, HD)
    value_col = pl.multiple_of((heads + c) * HD, HD)

    def keys(offset, width):
        return kv[pl.ds(offset, width), pl.ds(key_col, HD)]

    def values(offset, width):
        return kv[pl.ds(offset, width), pl.ds(value_col, HD)]

    def scores(offset, width):
        return lax.dot_general(q, keys(offset, width), (((1,), (1,)), ((), ())), preferred_element_type=jnp.float32)

    def rowmax(s, width):
        t = s[:, :128]
        for j in range(1, width // 128):
            t = jnp.maximum(t, s[:, j * 128:(j + 1) * 128])
        return jnp.max(t, axis=1, keepdims=True)

    def lanesum(p, width):
        t = p[:, :128]
        for j in range(1, width // 128):
            t = t + p[:, j * 128:(j + 1) * 128]
        return t

    def masked(s, offset, width, causal):
        key = lax.broadcasted_iota(jnp.int32, (tok, width), 1) + offset
        ok = key >= start
        if causal:
            ok = ok & (key <= row)
        return jnp.where(ok[None], s.reshape(GROUP, tok, width), -1e30).reshape(GROUP * tok, width)

    own = pl.multiple_of(first + 2 * half, tok)
    s = masked(scores(own, tok), own, tok, True)
    m = rowmax(s, tok)
    p = jnp.exp2((s - m) * EXP2_SCALE)
    m_scr[...] = jnp.broadcast_to(m, m_scr.shape)
    l_scr[...] = lanesum(p, tok)
    acc_scr[...] = jnp.dot(p.astype(jnp.bfloat16), values(own, tok), preferred_element_type=jnp.float32)

    def step(i, mask):
        offset = pl.multiple_of(first + i * span, tok)
        s = scores(offset, span)
        if mask:
            s = masked(s, offset, span, False)
        old = m_scr[...]
        new = jnp.maximum(old, rowmax(s, span))
        m_scr[...] = new
        shrink = jnp.exp2((old - new) * EXP2_SCALE)
        p = jnp.exp2((s - jnp.concatenate([new] * (span // 128), 1)) * EXP2_SCALE)
        l_scr[...] = l_scr[...] * shrink + lanesum(p, span)
        acc_scr[...] = acc_scr[...] * shrink + jnp.dot(p.astype(jnp.bfloat16), values(offset, span), preferred_element_type=jnp.float32)

    steps = 2 * half // span

    def loop(i, carry):
        whole = start_max <= first + i * span

        @pl.when(whole)
        def _():
            step(i, False)

        @pl.when(jnp.logical_not(whole))
        def _():
            step(i, True)

        return carry

    lax.fori_loop(jnp.clip(lax.div(start_min - first, span), 0, steps), steps, loop, 0)

    total = jnp.sum(l_scr[...], axis=1, keepdims=True)
    att = (acc_scr[...] / total).astype(jnp.bfloat16)
    att = jnp.concatenate([att[g * tok:(g + 1) * tok] for g in range(GROUP)], 1)
    out_ref[...] = att
    place = jnp.where(is_own, place_own_ref[...], place_got_ref[...])
    rows = jnp.dot(place, att, preferred_element_type=jnp.float32).astype(jnp.bfloat16)
    low_ref[...] = rows[:rows.shape[0] // 2]
    high_ref[...] = rows[rows.shape[0] // 2:]


def attend(info, own, got, pieces, layout, moves, part, heads, tok, span=512):
    slots = tok // 4
    wide = GROUP * HD
    n = len(moves)
    hbm = pl.BlockSpec(memory_space=pl.ANY)
    scratch = pltpu.VMEM((GROUP * tok, 128), jnp.float32)
    return pl.pallas_call(
        functools.partial(attend_kernel, tok=tok, span=span, moves=moves, heads=heads, layout=layout, part=part),
        grid_spec=pltpu.PrefetchScalarGridSpec(
            num_scalar_prefetch=1,
            grid=(heads,),
            in_specs=[
                pl.BlockSpec((tok, wide), lambda c, s: (0, c)),
                pl.BlockSpec((tok, wide), lambda c, s: (0, c)),
                pl.BlockSpec((2 * slots, tok), lambda c, s: (tok // (2 * slots), heads * GROUP)),
                pl.BlockSpec((2 * slots, tok), lambda c, s: (tok // (2 * slots), heads * GROUP)),
            ] + [hbm] * len(pieces),
            out_specs=[pl.BlockSpec((r, wide), lambda c, s: (0, c)) for r in (tok, slots, slots)],
            scratch_shapes=[
                pltpu.VMEM((4 * n * tok, 2 * heads * HD), jnp.bfloat16),
                pltpu.VMEM((2 * n, 16, 2 * heads * HD), jnp.bfloat16),
                pltpu.VMEM((tok, 1), jnp.int32),
                scratch, scratch, scratch,
                pltpu.SMEM((2,), jnp.int32),
                pltpu.SemaphoreType.DMA((2 * n, 3)),
            ],
        ),
        out_shape=[jax.ShapeDtypeStruct((r, heads * wide), jnp.bfloat16) for r in (tok, slots, slots)],
        compiler_params=pltpu.CompilerParams(vmem_limit_bytes=60 << 20),
        cost_estimate=pl.CostEstimate(flops=2 * 10**9, bytes_accessed=1 << 20, transcendentals=10**5),
        name="attend",
    )(info, own, got, own, got, *pieces)


def prepare_kernel(info_ref, kv_ref, doc_ref, send_ref, mine_ref):
    tok = kv_ref.shape[0]
    w = kv_ref.shape[1] // 4
    send_ref[tok:, :] = jnp.zeros((16, 2 * w), send_ref.dtype)
    send_ref[tok:tok + 16, :tok] = jnp.broadcast_to((doc_ref[...] + 1).astype(jnp.float32), (16, tok)).astype(send_ref.dtype)
    for yhi in range(2):
        @pl.when(info_ref[2] == yhi)
        def _(yhi=yhi):
            away = 1 - yhi
            mine_ref[:, :w] = kv_ref[:, yhi * w:(yhi + 1) * w]
            mine_ref[:, w:] = kv_ref[:, (2 + yhi) * w:(3 + yhi) * w]
            send_ref[:tok, :w] = kv_ref[:, away * w:(away + 1) * w]
            send_ref[:tok, w:] = kv_ref[:, (2 + away) * w:(3 + away) * w]


def prepare(info, keys_values, doc_ids):
    tok, width = keys_values.shape
    vm = pl.BlockSpec(memory_space=pltpu.VMEM)
    shape = lambda r, c: jax.ShapeDtypeStruct((r, c), jnp.bfloat16)
    return pl.pallas_call(
        prepare_kernel,
        in_specs=[pl.BlockSpec(memory_space=pltpu.SMEM)] + [vm] * 2,
        out_specs=[vm] * 2,
        out_shape=[shape(tok + 16, width // 2), shape(tok, width // 2)],
        compiler_params=pltpu.CompilerParams(vmem_limit_bytes=24 << 20),
        name="prepare",
    )(info, keys_values, doc_ids[None])


def plan_kernel(info_ref, ids_ref, weights_ref, q_ref, hid_ref, out_ref, own_ref, hot_ref, factor_ref):
    tok = hid_ref.shape[0]
    slots = (out_ref.shape[0] - tok) // 2
    q = q_ref.shape[1] // 2
    yhi = info_ref[2]
    below = lax.broadcasted_iota(jnp.int32, (tok, tok), 0) <= lax.broadcasted_iota(jnp.int32, (tok, tok), 1)
    below = below.astype(jnp.float32).astype(jnp.bfloat16)
    places, factors = [], []
    for flight in (yhi, 1 - yhi):
        chosen = ids_ref[...] == flight
        routed = jnp.max(jnp.where(chosen, 1.0, 0.0), axis=0, keepdims=True)
        factors.append(jnp.sum(jnp.where(chosen, weights_ref[...], 0.0), axis=0, keepdims=True))
        ranks = jnp.dot(jnp.broadcast_to(routed, (16, tok)).astype(jnp.bfloat16), below, preferred_element_type=jnp.float32)
        ranks = jnp.where(routed > 0.5, ranks[:1] - 1.0, -1.0)
        slot = lax.broadcasted_iota(jnp.int32, (slots, tok), 0).astype(jnp.float32)
        places.append(jnp.where(slot == ranks, 1.0, 0.0))
    place_f = jnp.concatenate(places, 0)
    place = place_f.astype(jnp.bfloat16)
    hot_ref[...] = jnp.concatenate([place_f, jnp.zeros((tok - 2 * slots, tok), jnp.float32)], 0).T.astype(jnp.bfloat16)
    factor_ref[...] = jnp.concatenate([factors[0], factors[1], jnp.zeros((tok - 2, tok), jnp.float32)], 0).T
    rows = jnp.dot(place, hid_ref[...], preferred_element_type=jnp.float32).astype(jnp.bfloat16)
    for n, ref in enumerate((own_ref, out_ref)):
        ref[:tok, q:] = jnp.zeros((tok, tok), jnp.bfloat16)
        ref[tok:tok + slots, :q] = rows[n * slots:(n + 1) * slots, :q]
        ref[tok + slots:, :q] = rows[n * slots:(n + 1) * slots, q:]
        ref[tok:tok + slots, q:] = place[n * slots:(n + 1) * slots]
        ref[tok + slots:, q:] = place[(1 - n) * slots:(2 - n) * slots]

    for side in range(2):
        @pl.when(yhi == side)
        def _(side=side):
            own_ref[:tok, :q] = q_ref[:, side * q:(side + 1) * q]
            out_ref[:tok, :q] = q_ref[:, (1 - side) * q:(2 - side) * q]


def plan(info, route_ids, route_weights, queries, hidden):
    tok, d = hidden.shape
    slots = tok // 4
    vm = pl.BlockSpec(memory_space=pltpu.VMEM)
    shape = lambda r, c, t=jnp.bfloat16: jax.ShapeDtypeStruct((r, c), t)
    return pl.pallas_call(
        plan_kernel,
        in_specs=[pl.BlockSpec(memory_space=pltpu.SMEM)] + [vm] * 4,
        out_specs=[vm] * 4,
        out_shape=[shape(tok + 2 * slots, d // 2 + tok)] * 2 + [shape(tok, tok), shape(tok, tok, jnp.float32)],
        compiler_params=pltpu.CompilerParams(vmem_limit_bytes=24 << 20),
        name="plan",
    )(info, route_ids.T, route_weights.T, queries, hidden)


def join_kernel(send_ref, mine_ref, other_ref, unit_ref):
    tok = mine_ref.shape[0]
    unit_ref[:tok] = mine_ref[...]
    unit_ref[tok:2 * tok] = other_ref[:tok]
    unit_ref[2 * tok:] = send_ref[tok:]
    unit_ref[2 * tok:, tok:2 * tok] = other_ref[tok:, :tok]


def join(send, mine, other):
    tok, width = mine.shape
    vm = pl.BlockSpec(memory_space=pltpu.VMEM)
    return pl.pallas_call(
        join_kernel,
        in_specs=[vm] * 3,
        out_specs=vm,
        out_shape=jax.ShapeDtypeStruct((2 * tok + 16, width), mine.dtype),
        compiler_params=pltpu.CompilerParams(vmem_limit_bytes=24 << 20),
        name="join",
    )(send, mine, other)


def pack_kernel(info_ref, gu_ref, down_ref, out_ref, sem):
    yhi = info_ref[2]
    units, wide = out_ref.shape[1], out_ref.shape[2]
    at = pl.ds(pl.multiple_of(info_ref[3] * units, units), units)
    if wide == down_ref.shape[2]:
        away, cols = 1 - yhi, pl.ds(0, wide)
    else:
        away = jnp.where(info_ref[5] == 0, yhi, 1 - yhi)
        cols = pl.ds(pl.multiple_of(info_ref[4] * wide, wide), wide)
    one = pltpu.make_async_copy(gu_ref.at[away, :, at, cols], out_ref.at[pl.ds(0, 2)], sem.at[0])
    two = pltpu.make_async_copy(down_ref.at[away, at, cols], out_ref.at[2], sem.at[1])
    one.start()
    two.start()
    one.wait()
    two.wait()


def pack(info, wide_t, down, cores, columns):
    hbm = pl.BlockSpec(memory_space=pl.ANY)
    units, d = down.shape[1] // cores, down.shape[2]
    return pl.pallas_call(
        pack_kernel,
        in_specs=[pl.BlockSpec(memory_space=pltpu.SMEM), hbm, hbm],
        out_specs=pl.BlockSpec(memory_space=pltpu.VMEM),
        out_shape=jax.ShapeDtypeStruct((3, units, d // columns), down.dtype),
        scratch_shapes=[pltpu.SemaphoreType.DMA((2,))],
        compiler_params=pltpu.CompilerParams(vmem_limit_bytes=60 << 20),
        name="pack",
    )(info, wide_t, down)


def norm_kernel(info_ref, own_ref, got_ref, mine_ref, other_ref, gain_ref, out_ref, *, part):
    slots, half = mine_ref.shape
    tok = own_ref.shape[0] - 2 * slots
    is_own = info_ref[2] == part

    def put(low, high):
        parts = []
        for n, att in enumerate((low, high)):
            rows = slice(tok + n * slots, tok + (n + 1) * slots)
            base = jnp.where(is_own, own_ref[rows, :half], got_ref[rows, :half]).astype(jnp.float32)
            parts.append((base + att.astype(jnp.float32)).astype(jnp.bfloat16).astype(jnp.float32))
        total = sum(jnp.sum(p * p, axis=1, keepdims=True) for p in parts)
        inv = lax.rsqrt(total / (2 * half) + 1e-6)
        for n, p in enumerate(parts):
            gain = gain_ref[:, n * half:(n + 1) * half].astype(jnp.float32)
            out_ref[:, n * half:(n + 1) * half] = (p * inv * gain).astype(jnp.bfloat16)

    @pl.when(info_ref[2] == 0)
    def _():
        put(mine_ref[...], other_ref[...])

    @pl.when(info_ref[2] != 0)
    def _():
        put(other_ref[...], mine_ref[...])


def norm_rows(info, own, got, part, mine, other, gain):
    slots, half = mine.shape
    vm = pl.BlockSpec(memory_space=pltpu.VMEM)
    return pl.pallas_call(
        functools.partial(norm_kernel, part=part),
        in_specs=[pl.BlockSpec(memory_space=pltpu.SMEM)] + [vm] * 5,
        out_specs=vm,
        out_shape=jax.ShapeDtypeStruct((slots, 2 * half), jnp.bfloat16),
        compiler_params=pltpu.CompilerParams(vmem_limit_bytes=16 << 20),
        name="norm_rows",
    )(info, own, got, mine, other, gain)


def assemble_kernel(info_ref, wo_ref, do_ref, r1_ref, r2_ref, *refs, plan, columns):
    blocks, w_ref, sem = refs[:len(plan)], refs[-2], refs[-1]
    yhi = info_ref[2]
    n, h = wo_ref.shape[2], r1_ref.shape[1]
    cps = []

    def cp(src, dst):
        cps.append(pltpu.make_async_copy(src, dst, sem.at[len(cps)]))

    for i in range(3):
        own = do_ref.at[yhi] if i == 2 else wo_ref.at[yhi, i]
        for src, at, size in ((own, 0, n), (r1_ref.at[i], n, h), (r2_ref.at[i], n + h, h)):
            cp(src, w_ref.at[i, pl.ds(at, size)])
        for block, (core, step, first) in zip(blocks, plan):
            wide = block.shape[2]
            col = lax.rem(info_ref[4] + step + columns, columns) * wide
            for u in range(block.shape[0] // 3):
                at = n + 2 * h + (2 * core + first + u) * h
                cp(block.at[3 * u + i], w_ref.at[i, pl.ds(at, h), pl.ds(pl.multiple_of(col, wide), wide)])
    for c in cps:
        c.start()
    for c in cps:
        c.wait()


def assemble(info, wo, do, r1, r2, blocks, plan, columns, after):
    n, d = 2 * (wo.shape[2] + r1.shape[1] + r2.shape[1]), wo.shape[3]
    hbm = pl.BlockSpec(memory_space=pl.ANY)
    return pl.pallas_call(
        functools.partial(assemble_kernel, plan=plan, columns=columns),
        in_specs=[pl.BlockSpec(memory_space=pltpu.SMEM)] + [hbm] * (5 + len(blocks)),
        out_specs=pl.BlockSpec(memory_space=pltpu.VMEM),
        scratch_shapes=[pltpu.SemaphoreType.DMA((9 + 6 * len(blocks),))],
        out_shape=jax.ShapeDtypeStruct((3, n, d), jnp.bfloat16),
        compiler_params=pltpu.CompilerParams(vmem_limit_bytes=20 << 20),
        cost_estimate=pl.CostEstimate(flops=0, bytes_accessed=n * d, transcendentals=0),
        name="assemble",
    )(info, wo, do, r1, r2, *blocks, after)


def expert_kernel(*refs, count, rows, after):
    xs, w_ref, ys = refs[:count], refs[count], refs[count + 1 + after:]
    x = jnp.concatenate([r[...] for r in xs], 0)
    nt = (((1,), (1,)), ((), ()))
    gate = lax.dot_general(x, w_ref[0], nt, preferred_element_type=jnp.float32)
    up = lax.dot_general(x, w_ref[1], nt, preferred_element_type=jnp.float32)
    inner = (gate / (1 + jnp.exp(-gate)) * up).astype(jnp.bfloat16)
    y = jnp.dot(inner, w_ref[2], preferred_element_type=jnp.float32).astype(jnp.bfloat16)
    for i in range(count):
        ys[i][...] = y[i * rows:(i + 1) * rows]


def experts(xs, w, after=()):
    count = len(xs)
    rows, d = xs[0].shape
    n = w.shape[1]
    vm = pl.BlockSpec(memory_space=pltpu.VMEM)
    return pl.pallas_call(
        functools.partial(expert_kernel, count=count, rows=rows, after=len(after)),
        in_specs=[vm] * (count + 1) + [pl.BlockSpec(memory_space=pl.ANY)] * len(after),
        out_specs=[vm] * count,
        out_shape=[jax.ShapeDtypeStruct((rows, d), jnp.bfloat16)] * count,
        compiler_params=pltpu.CompilerParams(vmem_limit_bytes=26 << 20),
        cost_estimate=pl.CostEstimate(flops=2 * count * rows * n * d, bytes_accessed=n * d, transcendentals=count * rows),
        name="experts",
    )(*xs, w, *after)


def combine_kernel(info_ref, hid_ref, mine_ref, other_ref, keep_ref, back_ref, hot_ref, factor_ref, out_ref):
    cap = back_ref.shape[0]
    is_mine = pl.program_id(0) // 2 == info_ref[2]
    att = jnp.where(is_mine, mine_ref[...].astype(jnp.float32), other_ref[...].astype(jnp.float32))
    stream = (hid_ref[...].astype(jnp.float32) + att).astype(jnp.bfloat16).astype(jnp.float32)
    one = jnp.dot(hot_ref[:, :cap], keep_ref[...], preferred_element_type=jnp.float32)
    two = jnp.dot(hot_ref[:, cap:2 * cap], back_ref[...], preferred_element_type=jnp.float32)
    out_ref[...] = (stream + one * factor_ref[:, 0:1] + two * factor_ref[:, 1:2]).astype(out_ref.dtype)


def combine(info, hidden, mine, other, keep, back, hot, factors):
    tok, d = hidden.shape
    cap = back.shape[0]
    wide = d // 4
    cols = lambda rows: pl.BlockSpec((rows, wide), lambda c, s: (0, c))
    half = pl.BlockSpec((tok, wide), lambda c, s: (0, lax.rem(c, 2)))
    whole = pl.BlockSpec((tok, tok), lambda c, s: (0, 0))
    return pl.pallas_call(
        combine_kernel,
        grid_spec=pltpu.PrefetchScalarGridSpec(
            num_scalar_prefetch=1,
            grid=(4,),
            in_specs=[cols(tok), half, half, cols(cap), cols(cap), whole, whole],
            out_specs=cols(tok),
        ),
        out_shape=jax.ShapeDtypeStruct((tok, d), hidden.dtype),
        compiler_params=pltpu.CompilerParams(vmem_limit_bytes=24 << 20),
        name="combine",
    )(info, hidden, mine, other, keep, back, hot, factors)


def shift(value, axis, size, steps):
    return lax.ppermute(value, axis, [(i, (i + steps) % size) for i in range(size)])


def swap(value, axis):
    return shift(value, axis, 2, 1)


def ring_moves(size):
    out = [0]
    for s in range(1, size // 2 + 1):
        out.append(-s)
        if 2 * s < size:
            out.append(s)
    return out


def ring_scatter(parts, signs, size):
    ups = [p[-2 * sign] for p, sign in zip(parts, signs)]
    downs = [shift(p[sign], "z", size, sign) for p, sign in zip(parts, signs)]
    for i, (p, sign) in enumerate(zip(parts, signs)):
        ups[i] = shift(ups[i], "z", size, -sign) + p[-sign]
    ups = [shift(u, "z", size, -sign) for u, sign in zip(ups, signs)]
    return [(ups[i], downs[i], p[0]) for i, p in enumerate(parts)]


def body(sizes, hidden_in, queries, keys_values, doc_ids, route_ids, route_weights, norm_gain, gate_up, down):
    tok, d = queries.shape
    capacity = tok // 4
    n_z, n_core, n_cx = sizes["z"], sizes["core"], sizes["cx"]
    yhi, z, core = lax.axis_index("yhi"), lax.axis_index("z"), lax.axis_index("core")
    half = n_z * tok
    n_ctx = n_cx * n_core
    moves = ring_moves(n_z)
    heads = keys_values.shape[1] // (4 * HD)
    cx, dp = lax.axis_index("cx"), lax.axis_index("dp")
    info = jnp.stack([z, yhi * half, yhi, core, cx, dp]).astype(jnp.int32)

    wide_t = jnp.swapaxes(gate_up, 2, 3)
    far = pack(info, wide_t, down, n_core, n_cx)
    place = lambda y, k, l: (y * n_z + k) * 2 + l
    across = [
        (place(y, k, l), place(y if l == 0 else 1 - y, (k + n_z // 2) % n_z, l)) for y in range(2) for k in range(n_z) for l in range(2)
    ]

    send, kept = prepare(info, keys_values, doc_ids)
    other = swap(send, "yhi")

    out, mine, hot, factors = plan(info, route_ids, route_weights, queries, hidden_in)
    out, other = lax.optimization_barrier((out, other))
    got = swap(out, "yhi")
    unit = join(send, kept, other)
    theirs = pack(info, wide_t, down, n_core, 1)
    ahead = [(i, i + 1) for i in range(n_ctx - 1)]
    onward = lambda x: lax.ppermute(x, ("cx", "core"), ahead)
    own = {0: unit}
    prior = [onward(unit)]
    for s in range(1, n_z // 2 + 1):
        own[-s] = shift(own[1 - s], "z", n_z, 1)
        if 2 * s < n_z:
            own[s] = shift(own[s - 1], "z", n_z, -1)
        if s == 1:
            own[-s], theirs = lax.optimization_barrier((own[-s], theirs))
            got_1 = swap(theirs, "yhi")
        if s == 2:
            own[-s], prior[0], got = lax.optimization_barrier((own[-s], prior[0], got))
        if s == 4:
            own[-s], far = lax.optimization_barrier((own[-s], far))
            far = lax.ppermute(far, ("yhi", "z", "dp"), across)
    own = [own[m] for m in moves]
    groups = [range(0, 1), range(1, n_z // 2 + 1), range(n_z // 2 + 1, n_z - 1), range(n_z - 1, n_z)]
    layout = []
    for n, group in enumerate(groups):
        if n > 0:
            prior.append(onward(jnp.concatenate([own[i] for i in group], 0) if len(group) > 1 else own[group[0]]))
        layout += [(n, k * unit.shape[0]) for k in range(len(group))]
    layout += [(len(groups) + i, 0) for i in range(n_z)]
    pieces = prior + own

    gain = norm_gain[None]
    first = yhi == 0
    atts, rows = [], []
    for part in range(2):
        if part == 1:
            mine, got_1, far, _ = lax.optimization_barrier((mine, got_1, far, atts[0]))
            far_2 = swap(far, "dp")
        att, keep, away = attend(info, mine, got, pieces, layout, moves, part, heads, tok)
        if part == 1:
            away, far, far_2 = lax.optimization_barrier((away, far, far_2))
            share = jnp.concatenate([far, far_2], 0)
            left, right = shift(share, "cx", n_cx, 1), shift(share, "cx", n_cx, -1)
        atts.append(att)
        rows.append(norm_rows(info, mine, got, part, keep, swap(away, "yhi"), gain))
    got_2 = swap(got_1, "core")
    own_att = jnp.where(first, atts[0], atts[1])
    away_att, rows[1] = lax.optimization_barrier((jnp.where(first, atts[1], atts[0]), rows[1]))
    other_att = swap(away_att, "yhi")

    signs = [1, -1]
    rows = [{0: x, -sign: shift(x, "z", n_z, sign), sign: shift(x, "z", n_z, -sign)} for x, sign in zip(rows, signs)]
    rows[0][-1], left, right = lax.optimization_barrier((rows[0][-1], left, right))
    cut = share.shape[0] // 2
    blocks = [share, left, right, shift(right[:cut], "cx", n_cx, -1), shift(left[cut:], "cx", n_cx, 1)]
    steps = [(0, 0), (-1, 0), (1, 0), (2, 0), (2, 1)]
    for g, sign in zip(rows, signs):
        g[-2 * sign] = shift(g[-sign], "z", n_z, sign)
    blocks = blocks + [swap(x, "core") for x in blocks]
    layout = [(c,) + step for c in range(n_core) for step in steps]
    weights = assemble(info, wide_t, down, got_1, got_2, blocks, layout, n_cx, rows[1][0])
    keys = [(i, m) for i in range(2) for m in (0, -1, 1)]
    first_out = experts([rows[i][m] for i, m in keys], weights)
    last_out = experts([g[-2 * sign] for g, sign in zip(rows, signs)], weights, after=[first_out[0], other_att])
    outs = [{-2 * sign: y} for sign, y in zip(signs, last_out)]
    for (i, m), y in zip(keys, first_out):
        outs[i][m] = y
    sums = [ups.astype(jnp.float32) + downs + here for ups, downs, here in ring_scatter(outs, signs, n_z)]
    back = swap(jnp.where(first, sums[1], sums[0]).astype(jnp.bfloat16), "yhi")
    keep = jnp.where(first, sums[0], sums[1]).astype(jnp.bfloat16)
    return combine(info, hidden_in, own_att, other_att, keep, back, hot, factors)


def solution(mesh):
    sizes = {"cx": mesh.shape["ctx"] // 2, "core": 2, "yhi": 2, "z": mesh.shape["exp"] // 2, "dp": mesh.shape["dp"]}
    fine = Mesh(mesh.devices.reshape(tuple(sizes.values())), tuple(sizes))
    tokens = ("dp", "cx", "core", "yhi", "z")
    rows = P(tokens, None)
    hidden = ("yhi", "z")
    in_specs = (rows, rows, rows, P(tokens), rows, rows, P(), P(None, None, None, hidden), P(None, hidden, None))
    return jax.shard_map(
        functools.partial(body, sizes), mesh=fine, in_specs=in_specs, out_specs=rows, check_vma=False
    )
```

```python
import functools
import math

import jax
import jax.numpy as jnp
from jax import lax
from jax.experimental import pallas as pl
from jax.experimental.pallas import tpu as pltpu
from jax.sharding import Mesh
from jax.sharding import PartitionSpec as P

EXP_FLIGHT = 2
HD = 128
GROUP = 7
EXP2_SCALE = math.log2(math.e) / math.sqrt(HD)

def attend_kernel(info_ref, q_own_ref, q_got_ref, place_own_ref, place_got_ref, *refs, tok, span, moves, heads, layout, part):
    arrays, out_ref, low_ref, high_ref = refs[:-11], refs[-11], refs[-10], refs[-9]
    kv, ids, start_scr, m_scr, l_scr, acc_scr, bounds, sem = refs[-8:]
    c = pl.program_id(0)
    z = info_ref[0]
    half = len(moves) * tok
    near = pl.multiple_of(info_ref[1], half)
    far = pl.multiple_of(half - info_ref[1], half)
    first = pl.multiple_of(part * half + z * tok, tok)
    is_own = info_ref[2] == part

    @pl.when(c == 0)
    def _():
        blocks = []
        copies = []
        for n, (which, row) in enumerate(layout):
            piece = arrays[which]
            place = lax.rem(z + moves[n % len(moves)] + len(moves), len(moves)) * tok
            slab = n // len(moves) * 2 * half
            for side, base in ((0, near), (1, far)):
                at = pl.multiple_of(slab + base + place, tok)
                cp = pltpu.make_async_copy(piece.at[pl.ds(row + side * tok, tok)], kv.at[pl.ds(at, tok)], sem.at[n, side])
                blocks.append((cp, (at >= first) & (at <= first + 2 * half)))
            copies.append(pltpu.make_async_copy(piece.at[pl.ds(row + 2 * tok, 16)], ids.at[n], sem.at[n, 2]))
        for cp in copies:
            cp.start()
        for cp, needed in blocks:
            pl.when(needed)(cp.start)
        for cp in copies:
            cp.wait()
        own = [ids[len(moves), 0:1, n * tok:(n + 1) * tok].astype(jnp.float32) for n in range(2)]
        own = jnp.where(is_own, own[0], own[1])
        own = jnp.broadcast_to(own, (tok, tok)).T
        less = jnp.zeros((tok, tok), jnp.float32)
        for n in range(len(layout)):
            for side in range(2):
                row = ids[n, 0:1, side * tok:(side + 1) * tok].astype(jnp.float32)
                less = less + jnp.where(row < own, 1.0, 0.0)
        begin = jnp.sum(less, axis=1, keepdims=True)
        start_scr[...] = begin.astype(jnp.int32)
        bounds[0] = jnp.min(begin).astype(jnp.int32)
        bounds[1] = jnp.max(begin).astype(jnp.int32)
        for cp, needed in blocks:
            pl.when(needed)(cp.wait)

    start_min, start_max = bounds[0], bounds[1]
    q = jnp.where(is_own, q_own_ref[...], q_got_ref[...])
    q = jnp.concatenate([q[:, g * HD:(g + 1) * HD] for g in range(GROUP)], 0)
    start = start_scr[...]
    row = lax.broadcasted_iota(jnp.int32, (tok, 1), 0) + first + 2 * half
    key_col = pl.multiple_of(c * HD, HD)
    value_col = pl.multiple_of((heads + c) * HD, HD)

    def keys(offset, width):
        return kv[pl.ds(offset, width), pl.ds(key_col, HD)]

    def values(offset, width):
        return kv[pl.ds(offset, width), pl.ds(value_col, HD)]

    def scores(offset, width):
        return lax.dot_general(q, keys(offset, width), (((1,), (1,)), ((), ())), preferred_element_type=jnp.float32)

    def rowmax(s, width):
        t = s[:, :128]
        for j in range(1, width // 128):
            t = jnp.maximum(t, s[:, j * 128:(j + 1) * 128])
        return jnp.max(t, axis=1, keepdims=True)

    def lanesum(p, width):
        t = p[:, :128]
        for j in range(1, width // 128):
            t = t + p[:, j * 128:(j + 1) * 128]
        return t

    def masked(s, offset, width, causal):
        key = lax.broadcasted_iota(jnp.int32, (tok, width), 1) + offset
        ok = key >= start
        if causal:
            ok = ok & (key <= row)
        return jnp.where(ok[None], s.reshape(GROUP, tok, width), -1e30).reshape(GROUP * tok, width)

    own = pl.multiple_of(first + 2 * half, tok)
    s = masked(scores(own, tok), own, tok, True)
    m = rowmax(s, tok)
    p = jnp.exp2((s - m) * EXP2_SCALE)
    m_scr[...] = jnp.broadcast_to(m, m_scr.shape)
    l_scr[...] = lanesum(p, tok)
    acc_scr[...] = jnp.dot(p.astype(jnp.bfloat16), values(own, tok), preferred_element_type=jnp.float32)

    def step(i, mask):
        offset = pl.multiple_of(first + i * span, tok)
        s = scores(offset, span)
        if mask:
            s = masked(s, offset, span, False)
        old = m_scr[...]
        new = jnp.maximum(old, rowmax(s, span))
        m_scr[...] = new
        shrink = jnp.exp2((old - new) * EXP2_SCALE)
        p = jnp.exp2((s - jnp.concatenate([new] * (span // 128), 1)) * EXP2_SCALE)
        l_scr[...] = l_scr[...] * shrink + lanesum(p, span)
        acc_scr[...] = acc_scr[...] * shrink + jnp.dot(p.astype(jnp.bfloat16), values(offset, span), preferred_element_type=jnp.float32)

    steps = 2 * half // span

    def loop(i, carry):
        whole = start_max <= first + i * span

        @pl.when(whole)
        def _():
            step(i, False)

        @pl.when(jnp.logical_not(whole))
        def _():
            step(i, True)

        return carry

    lax.fori_loop(jnp.clip(lax.div(start_min - first, span), 0, steps), steps, loop, 0)

    total = jnp.sum(l_scr[...], axis=1, keepdims=True)
    att = (acc_scr[...] / total).astype(jnp.bfloat16)
    att = jnp.concatenate([att[g * tok:(g + 1) * tok] for g in range(GROUP)], 1)
    out_ref[...] = att
    place = jnp.where(is_own, place_own_ref[...], place_got_ref[...])
    rows = jnp.dot(place, att, preferred_element_type=jnp.float32).astype(jnp.bfloat16)
    low_ref[...] = rows[:rows.shape[0] // 2]
    high_ref[...] = rows[rows.shape[0] // 2:]


def attend(info, own, got, pieces, layout, moves, part, heads, tok, span=512):
    slots = tok // 4
    wide = GROUP * HD
    n = len(moves)
    hbm = pl.BlockSpec(memory_space=pl.ANY)
    scratch = pltpu.VMEM((GROUP * tok, 128), jnp.float32)
    return pl.pallas_call(
        functools.partial(attend_kernel, tok=tok, span=span, moves=moves, heads=heads, layout=layout, part=part),
        grid_spec=pltpu.PrefetchScalarGridSpec(
            num_scalar_prefetch=1,
            grid=(heads,),
            in_specs=[
                pl.BlockSpec((tok, wide), lambda c, s: (0, c)),
                pl.BlockSpec((tok, wide), lambda c, s: (0, c)),
                pl.BlockSpec((2 * slots, tok), lambda c, s: (tok // (2 * slots), heads * GROUP)),
                pl.BlockSpec((2 * slots, tok), lambda c, s: (tok // (2 * slots), heads * GROUP)),
            ] + [hbm] * len(pieces),
            out_specs=[pl.BlockSpec((r, wide), lambda c, s: (0, c)) for r in (tok, slots, slots)],
            scratch_shapes=[
                pltpu.VMEM((4 * n * tok, 2 * heads * HD), jnp.bfloat16),
                pltpu.VMEM((2 * n, 16, 2 * heads * HD), jnp.bfloat16),
                pltpu.VMEM((tok, 1), jnp.int32),
                scratch, scratch, scratch,
                pltpu.SMEM((2,), jnp.int32),
                pltpu.SemaphoreType.DMA((2 * n, 3)),
            ],
        ),
        out_shape=[jax.ShapeDtypeStruct((r, heads * wide), jnp.bfloat16) for r in (tok, slots, slots)],
        compiler_params=pltpu.CompilerParams(vmem_limit_bytes=60 << 20),
        cost_estimate=pl.CostEstimate(flops=2 * 10**9, bytes_accessed=1 << 20, transcendentals=10**5),
        name="attend",
    )(info, own, got, own, got, *pieces)


def prepare_kernel(info_ref, kv_ref, doc_ref, send_ref, mine_ref):
    tok = kv_ref.shape[0]
    w = kv_ref.shape[1] // 4
    send_ref[tok:, :] = jnp.zeros((16, 2 * w), send_ref.dtype)
    send_ref[tok:tok + 16, :tok] = jnp.broadcast_to((doc_ref[...] + 1).astype(jnp.float32), (16, tok)).astype(send_ref.dtype)
    for yhi in range(2):
        @pl.when(info_ref[2] == yhi)
        def _(yhi=yhi):
            away = 1 - yhi
            mine_ref[:, :w] = kv_ref[:, yhi * w:(yhi + 1) * w]
            mine_ref[:, w:] = kv_ref[:, (2 + yhi) * w:(3 + yhi) * w]
            send_ref[:tok, :w] = kv_ref[:, away * w:(away + 1) * w]
            send_ref[:tok, w:] = kv_ref[:, (2 + away) * w:(3 + away) * w]


def prepare(info, keys_values, doc_ids):
    tok, width = keys_values.shape
    vm = pl.BlockSpec(memory_space=pltpu.VMEM)
    shape = lambda r, c: jax.ShapeDtypeStruct((r, c), jnp.bfloat16)
    return pl.pallas_call(
        prepare_kernel,
        in_specs=[pl.BlockSpec(memory_space=pltpu.SMEM)] + [vm] * 2,
        out_specs=[vm] * 2,
        out_shape=[shape(tok + 16, width // 2), shape(tok, width // 2)],
        compiler_params=pltpu.CompilerParams(vmem_limit_bytes=24 << 20),
        name="prepare",
    )(info, keys_values, doc_ids[None])


def plan_kernel(info_ref, ids_ref, weights_ref, q_ref, hid_ref, out_ref, own_ref, hot_ref, factor_ref):
    tok = hid_ref.shape[0]
    slots = (out_ref.shape[0] - tok) // 2
    q = q_ref.shape[1] // 2
    yhi = info_ref[2]
    below = lax.broadcasted_iota(jnp.int32, (tok, tok), 0) <= lax.broadcasted_iota(jnp.int32, (tok, tok), 1)
    below = below.astype(jnp.float32).astype(jnp.bfloat16)
    places, factors = [], []
    for flight in (yhi, 1 - yhi):
        chosen = ids_ref[...] == flight
        routed = jnp.max(jnp.where(chosen, 1.0, 0.0), axis=0, keepdims=True)
        factors.append(jnp.sum(jnp.where(chosen, weights_ref[...], 0.0), axis=0, keepdims=True))
        ranks = jnp.dot(jnp.broadcast_to(routed, (16, tok)).astype(jnp.bfloat16), below, preferred_element_type=jnp.float32)
        ranks = jnp.where(routed > 0.5, ranks[:1] - 1.0, -1.0)
        slot = lax.broadcasted_iota(jnp.int32, (slots, tok), 0).astype(jnp.float32)
        places.append(jnp.where(slot == ranks, 1.0, 0.0))
    place_f = jnp.concatenate(places, 0)
    place = place_f.astype(jnp.bfloat16)
    hot_ref[...] = jnp.concatenate([place_f, jnp.zeros((tok - 2 * slots, tok), jnp.float32)], 0).T.astype(jnp.bfloat16)
    factor_ref[...] = jnp.concatenate([factors[0], factors[1], jnp.zeros((tok - 2, tok), jnp.float32)], 0).T
    rows = jnp.dot(place, hid_ref[...], preferred_element_type=jnp.float32).astype(jnp.bfloat16)
    for n, ref in enumerate((own_ref, out_ref)):
        ref[:tok, q:] = jnp.zeros((tok, tok), jnp.bfloat16)
        ref[tok:tok + slots, :q] = rows[n * slots:(n + 1) * slots, :q]
        ref[tok + slots:, :q] = rows[n * slots:(n + 1) * slots, q:]
        ref[tok:tok + slots, q:] = place[n * slots:(n + 1) * slots]
        ref[tok + slots:, q:] = place[(1 - n) * slots:(2 - n) * slots]

    for side in range(2):
        @pl.when(yhi == side)
        def _(side=side):
            own_ref[:tok, :q] = q_ref[:, side * q:(side + 1) * q]
            out_ref[:tok, :q] = q_ref[:, (1 - side) * q:(2 - side) * q]


def plan(info, route_ids, route_weights, queries, hidden):
    tok, d = hidden.shape
    slots = tok // 4
    vm = pl.BlockSpec(memory_space=pltpu.VMEM)
    shape = lambda r, c, t=jnp.bfloat16: jax.ShapeDtypeStruct((r, c), t)
    return pl.pallas_call(
        plan_kernel,
        in_specs=[pl.BlockSpec(memory_space=pltpu.SMEM)] + [vm] * 4,
        out_specs=[vm] * 4,
        out_shape=[shape(tok + 2 * slots, d // 2 + tok)] * 2 + [shape(tok, tok), shape(tok, tok, jnp.float32)],
        compiler_params=pltpu.CompilerParams(vmem_limit_bytes=24 << 20),
        name="plan",
    )(info, route_ids.T, route_weights.T, queries, hidden)


def join_kernel(send_ref, mine_ref, other_ref, unit_ref):
    tok = mine_ref.shape[0]
    unit_ref[:tok] = mine_ref[...]
    unit_ref[tok:2 * tok] = other_ref[:tok]
    unit_ref[2 * tok:] = send_ref[tok:]
    unit_ref[2 * tok:, tok:2 * tok] = other_ref[tok:, :tok]


def join(send, mine, other):
    tok, width = mine.shape
    vm = pl.BlockSpec(memory_space=pltpu.VMEM)
    return pl.pallas_call(
        join_kernel,
        in_specs=[vm] * 3,
        out_specs=vm,
        out_shape=jax.ShapeDtypeStruct((2 * tok + 16, width), mine.dtype),
        compiler_params=pltpu.CompilerParams(vmem_limit_bytes=24 << 20),
        name="join",
    )(send, mine, other)


def pack_kernel(info_ref, gu_ref, down_ref, out_ref, sem):
    yhi = info_ref[2]
    units, wide = out_ref.shape[1], out_ref.shape[2]
    at = pl.ds(pl.multiple_of(info_ref[3] * units, units), units)
    if wide == down_ref.shape[2]:
        away, cols = 1 - yhi, pl.ds(0, wide)
    else:
        away = jnp.where(info_ref[5] == 0, yhi, 1 - yhi)
        cols = pl.ds(pl.multiple_of(info_ref[4] * wide, wide), wide)
    one = pltpu.make_async_copy(gu_ref.at[away, :, at, cols], out_ref.at[pl.ds(0, 2)], sem.at[0])
    two = pltpu.make_async_copy(down_ref.at[away, at, cols], out_ref.at[2], sem.at[1])
    one.start()
    two.start()
    one.wait()
    two.wait()


def pack(info, wide_t, down, cores, columns):
    hbm = pl.BlockSpec(memory_space=pl.ANY)
    units, d = down.shape[1] // cores, down.shape[2]
    return pl.pallas_call(
        pack_kernel,
        in_specs=[pl.BlockSpec(memory_space=pltpu.SMEM), hbm, hbm],
        out_specs=pl.BlockSpec(memory_space=pltpu.VMEM),
        out_shape=jax.ShapeDtypeStruct((3, units, d // columns), down.dtype),
        scratch_shapes=[pltpu.SemaphoreType.DMA((2,))],
        compiler_params=pltpu.CompilerParams(vmem_limit_bytes=60 << 20),
        name="pack",
    )(info, wide_t, down)


def norm_kernel(info_ref, own_ref, got_ref, mine_ref, other_ref, gain_ref, out_ref, *, part):
    slots, half = mine_ref.shape
    tok = own_ref.shape[0] - 2 * slots
    is_own = info_ref[2] == part

    def put(low, high):
        parts = []
        for n, att in enumerate((low, high)):
            rows = slice(tok + n * slots, tok + (n + 1) * slots)
            base = jnp.where(is_own, own_ref[rows, :half], got_ref[rows, :half]).astype(jnp.float32)
            parts.append((base + att.astype(jnp.float32)).astype(jnp.bfloat16).astype(jnp.float32))
        total = sum(jnp.sum(p * p, axis=1, keepdims=True) for p in parts)
        inv = lax.rsqrt(total / (2 * half) + 1e-6)
        for n, p in enumerate(parts):
            gain = gain_ref[:, n * half:(n + 1) * half].astype(jnp.float32)
            out_ref[:, n * half:(n + 1) * half] = (p * inv * gain).astype(jnp.bfloat16)

    @pl.when(info_ref[2] == 0)
    def _():
        put(mine_ref[...], other_ref[...])

    @pl.when(info_ref[2] != 0)
    def _():
        put(other_ref[...], mine_ref[...])


def norm_rows(info, own, got, part, mine, other, gain):
    slots, half = mine.shape
    vm = pl.BlockSpec(memory_space=pltpu.VMEM)
    return pl.pallas_call(
        functools.partial(norm_kernel, part=part),
        in_specs=[pl.BlockSpec(memory_space=pltpu.SMEM)] + [vm] * 5,
        out_specs=vm,
        out_shape=jax.ShapeDtypeStruct((slots, 2 * half), jnp.bfloat16),
        compiler_params=pltpu.CompilerParams(vmem_limit_bytes=16 << 20),
        name="norm_rows",
    )(info, own, got, mine, other, gain)


def assemble_kernel(info_ref, wo_ref, do_ref, r1_ref, r2_ref, *refs, plan, columns):
    blocks, w_ref, sem = refs[:len(plan)], refs[-2], refs[-1]
    yhi = info_ref[2]
    n, h = wo_ref.shape[2], r1_ref.shape[1]
    cps = []

    def cp(src, dst):
        cps.append(pltpu.make_async_copy(src, dst, sem.at[len(cps)]))

    for i in range(3):
        own = do_ref.at[yhi] if i == 2 else wo_ref.at[yhi, i]
        for src, at, size in ((own, 0, n), (r1_ref.at[i], n, h), (r2_ref.at[i], n + h, h)):
            cp(src, w_ref.at[i, pl.ds(at, size)])
        for block, (core, step, first) in zip(blocks, plan):
            wide = block.shape[2]
            col = lax.rem(info_ref[4] + step + columns, columns) * wide
            for u in range(block.shape[0] // 3):
                at = n + 2 * h + (2 * core + first + u) * h
                cp(block.at[3 * u + i], w_ref.at[i, pl.ds(at, h), pl.ds(pl.multiple_of(col, wide), wide)])
    for c in cps:
        c.start()
    for c in cps:
        c.wait()


def assemble(info, wo, do, r1, r2, blocks, plan, columns, after):
    n, d = 2 * (wo.shape[2] + r1.shape[1] + r2.shape[1]), wo.shape[3]
    hbm = pl.BlockSpec(memory_space=pl.ANY)
    return pl.pallas_call(
        functools.partial(assemble_kernel, plan=plan, columns=columns),
        in_specs=[pl.BlockSpec(memory_space=pltpu.SMEM)] + [hbm] * (5 + len(blocks)),
        out_specs=pl.BlockSpec(memory_space=pltpu.VMEM),
        scratch_shapes=[pltpu.SemaphoreType.DMA((9 + 6 * len(blocks),))],
        out_shape=jax.ShapeDtypeStruct((3, n, d), jnp.bfloat16),
        compiler_params=pltpu.CompilerParams(vmem_limit_bytes=20 << 20),
        cost_estimate=pl.CostEstimate(flops=0, bytes_accessed=n * d, transcendentals=0),
        name="assemble",
    )(info, wo, do, r1, r2, *blocks, after)


def expert_kernel(*refs, count, rows, after):
    xs, w_ref, ys = refs[:count], refs[count], refs[count + 1 + after:]
    x = jnp.concatenate([r[...] for r in xs], 0)
    nt = (((1,), (1,)), ((), ()))
    gate = lax.dot_general(x, w_ref[0], nt, preferred_element_type=jnp.float32)
    up = lax.dot_general(x, w_ref[1], nt, preferred_element_type=jnp.float32)
    inner = (gate / (1 + jnp.exp(-gate)) * up).astype(jnp.bfloat16)
    y = jnp.dot(inner, w_ref[2], preferred_element_type=jnp.float32).astype(jnp.bfloat16)
    for i in range(count):
        ys[i][...] = y[i * rows:(i + 1) * rows]


def experts(xs, w, after=()):
    count = len(xs)
    rows, d = xs[0].shape
    n = w.shape[1]
    vm = pl.BlockSpec(memory_space=pltpu.VMEM)
    return pl.pallas_call(
        functools.partial(expert_kernel, count=count, rows=rows, after=len(after)),
        in_specs=[vm] * (count + 1) + [pl.BlockSpec(memory_space=pl.ANY)] * len(after),
        out_specs=[vm] * count,
        out_shape=[jax.ShapeDtypeStruct((rows, d), jnp.bfloat16)] * count,
        compiler_params=pltpu.CompilerParams(vmem_limit_bytes=26 << 20),
        cost_estimate=pl.CostEstimate(flops=2 * count * rows * n * d, bytes_accessed=n * d, transcendentals=count * rows),
        name="experts",
    )(*xs, w, *after)


def combine_kernel(info_ref, hid_ref, mine_ref, other_ref, keep_ref, back_ref, hot_ref, factor_ref, out_ref):
    cap = back_ref.shape[0]
    is_mine = pl.program_id(0) // 2 == info_ref[2]
    att = jnp.where(is_mine, mine_ref[...].astype(jnp.float32), other_ref[...].astype(jnp.float32))
    stream = (hid_ref[...].astype(jnp.float32) + att).astype(jnp.bfloat16).astype(jnp.float32)
    one = jnp.dot(hot_ref[:, :cap], keep_ref[...], preferred_element_type=jnp.float32)
    two = jnp.dot(hot_ref[:, cap:2 * cap], back_ref[...], preferred_element_type=jnp.float32)
    out_ref[...] = (stream + one * factor_ref[:, 0:1] + two * factor_ref[:, 1:2]).astype(out_ref.dtype)


def combine(info, hidden, mine, other, keep, back, hot, factors):
    tok, d = hidden.shape
    cap = back.shape[0]
    wide = d // 4
    cols = lambda rows: pl.BlockSpec((rows, wide), lambda c, s: (0, c))
    half = pl.BlockSpec((tok, wide), lambda c, s: (0, lax.rem(c, 2)))
    whole = pl.BlockSpec((tok, tok), lambda c, s: (0, 0))
    return pl.pallas_call(
        combine_kernel,
        grid_spec=pltpu.PrefetchScalarGridSpec(
            num_scalar_prefetch=1,
            grid=(4,),
            in_specs=[cols(tok), half, half, cols(cap), cols(cap), whole, whole],
            out_specs=cols(tok),
        ),
        out_shape=jax.ShapeDtypeStruct((tok, d), hidden.dtype),
        compiler_params=pltpu.CompilerParams(vmem_limit_bytes=24 << 20),
        name="combine",
    )(info, hidden, mine, other, keep, back, hot, factors)


def shift(value, axis, size, steps):
    return lax.ppermute(value, axis, [(i, (i + steps) % size) for i in range(size)])


def swap(value, axis):
    return shift(value, axis, 2, 1)


def ring_moves(size):
    out = [0]
    for s in range(1, size // 2 + 1):
        out.append(-s)
        if 2 * s < size:
            out.append(s)
    return out


def ring_scatter(parts, signs, size):
    ups = [p[-2 * sign] for p, sign in zip(parts, signs)]
    downs = [shift(p[sign], "z", size, sign) for p, sign in zip(parts, signs)]
    for i, (p, sign) in enumerate(zip(parts, signs)):
        ups[i] = shift(ups[i], "z", size, -sign) + p[-sign]
    ups = [shift(u, "z", size, -sign) for u, sign in zip(ups, signs)]
    return [(ups[i], downs[i], p[0]) for i, p in enumerate(parts)]


def body(sizes, hidden_in, queries, keys_values, doc_ids, route_ids, route_weights, norm_gain, gate_up, down):
    tok, d = queries.shape
    capacity = tok // 4
    n_z, n_core, n_cx = sizes["z"], sizes["core"], sizes["cx"]
    yhi, z, core = lax.axis_index("yhi"), lax.axis_index("z"), lax.axis_index("core")
    half = n_z * tok
    n_ctx = n_cx * n_core
    moves = ring_moves(n_z)
    heads = keys_values.shape[1] // (4 * HD)
    cx, dp = lax.axis_index("cx"), lax.axis_index("dp")
    info = jnp.stack([z, yhi * half, yhi, core, cx, dp]).astype(jnp.int32)

    wide_t = jnp.swapaxes(gate_up, 2, 3)
    far = pack(info, wide_t, down, n_core, n_cx)
    place = lambda y, k, l: (y * n_z + k) * 2 + l
    across = [
        (place(y, k, l), place(y if l == 0 else 1 - y, (k + n_z // 2) % n_z, l)) for y in range(2) for k in range(n_z) for l in range(2)
    ]

    send, kept = prepare(info, keys_values, doc_ids)
    other = swap(send, "yhi")

    out, mine, hot, factors = plan(info, route_ids, route_weights, queries, hidden_in)
    out, other = lax.optimization_barrier((out, other))
    got = swap(out, "yhi")
    unit = join(send, kept, other)
    theirs = pack(info, wide_t, down, n_core, 1)
    ahead = [(i, i + 1) for i in range(n_ctx - 1)]
    onward = lambda x: lax.ppermute(x, ("cx", "core"), ahead)
    own = {0: unit}
    prior = [onward(unit)]
    for s in range(1, n_z // 2 + 1):
        own[-s] = shift(own[1 - s], "z", n_z, 1)
        if 2 * s < n_z:
            own[s] = shift(own[s - 1], "z", n_z, -1)
        if s == 1:
            own[-s], theirs = lax.optimization_barrier((own[-s], theirs))
            got_1 = swap(theirs, "yhi")
        if s == 2:
            own[-s], prior[0], got = lax.optimization_barrier((own[-s], prior[0], got))
        if s == 3:
            own[-s], far = lax.optimization_barrier((own[-s], far))
            far = lax.ppermute(far, ("yhi", "z", "dp"), across)
    own = [own[m] for m in moves]
    groups = [range(0, 1), range(1, n_z // 2 + 1), range(n_z // 2 + 1, n_z - 1), range(n_z - 1, n_z)]
    layout = []
    for n, group in enumerate(groups):
        if n > 0:
            prior.append(onward(jnp.concatenate([own[i] for i in group], 0) if len(group) > 1 else own[group[0]]))
        layout += [(n, k * unit.shape[0]) for k in range(len(group))]
    layout += [(len(groups) + i, 0) for i in range(n_z)]
    pieces = prior + own

    gain = norm_gain[None]
    first = yhi == 0
    atts, rows = [], []
    mine, far = lax.optimization_barrier((mine, far))
    far_2 = swap(far, "dp")
    for part in range(2):
        if part == 1:
            mine, got_1, far, far_2, _ = lax.optimization_barrier((mine, got_1, far, far_2, atts[0]))
            share = jnp.concatenate([far, far_2], 0)
            mine, share = lax.optimization_barrier((mine, share))
            left, right = shift(share, "cx", n_cx, 1), shift(share, "cx", n_cx, -1)
        att, keep, away = attend(info, mine, got, pieces, layout, moves, part, heads, tok)
        atts.append(att)
        rows.append(norm_rows(info, mine, got, part, keep, swap(away, "yhi"), gain))
    rows[1], left, right = lax.optimization_barrier((rows[1], left, right))
    got_2 = swap(got_1, "core")
    own_att = jnp.where(first, atts[0], atts[1])
    away_att, rows[1] = lax.optimization_barrier((jnp.where(first, atts[1], atts[0]), rows[1]))
    other_att = swap(away_att, "yhi")

    signs = [1, -1]
    rows = [{0: x, -sign: shift(x, "z", n_z, sign), sign: shift(x, "z", n_z, -sign)} for x, sign in zip(rows, signs)]
    cut = share.shape[0] // 2
    halves = [shift(right[:cut], "cx", n_cx, -1), shift(left[cut:], "cx", n_cx, 1)]
    near = [g[m] for g in rows for m in (-1, 1)]
    near, halves = lax.optimization_barrier((near, halves))
    rows = [{0: g[0], -1: near[2 * i], 1: near[2 * i + 1]} for i, g in enumerate(rows)]
    blocks = [share, left, right] + halves
    steps = [(0, 0), (-1, 0), (1, 0), (2, 0), (2, 1)]
    for g, sign in zip(rows, signs):
        g[-2 * sign] = shift(g[-sign], "z", n_z, sign)
    blocks = blocks + [swap(x, "core") for x in blocks]
    layout = [(c,) + step for c in range(n_core) for step in steps]
    weights = assemble(info, wide_t, down, got_1, got_2, blocks, layout, n_cx, rows[1][0])
    keys = [(i, m) for i in range(2) for m in (0, -1, 1)]
    first_out = experts([rows[i][m] for i, m in keys], weights)
    last_out = experts([g[-2 * sign] for g, sign in zip(rows, signs)], weights, after=[first_out[0], other_att])
    outs = [{-2 * sign: y} for sign, y in zip(signs, last_out)]
    for (i, m), y in zip(keys, first_out):
        outs[i][m] = y
    sums = [ups.astype(jnp.float32) + downs + here for ups, downs, here in ring_scatter(outs, signs, n_z)]
    back = swap(jnp.where(first, sums[1], sums[0]).astype(jnp.bfloat16), "yhi")
    keep = jnp.where(first, sums[0], sums[1]).astype(jnp.bfloat16)
    return combine(info, hidden_in, own_att, other_att, keep, back, hot, factors)


def solution(mesh):
    sizes = {"cx": mesh.shape["ctx"] // 2, "core": 2, "yhi": 2, "z": mesh.shape["exp"] // 2, "dp": mesh.shape["dp"]}
    fine = Mesh(mesh.devices.reshape(tuple(sizes.values())), tuple(sizes))
    tokens = ("dp", "cx", "core", "yhi", "z")
    rows = P(tokens, None)
    hidden = ("yhi", "z")
    in_specs = (rows, rows, rows, P(tokens), rows, rows, P(), P(None, None, None, hidden), P(None, hidden, None))
    return jax.shard_map(
        functools.partial(body, sizes), mesh=fine, in_specs=in_specs, out_specs=rows, check_vma=False
    )
```

```python
import functools
import math

import jax
import jax.numpy as jnp
from jax import lax
from jax.experimental import pallas as pl
from jax.experimental.pallas import tpu as pltpu
from jax.sharding import Mesh
from jax.sharding import PartitionSpec as P

EXP_FLIGHT = 2
HD = 128
GROUP = 7
EXP2_SCALE = math.log2(math.e) / math.sqrt(HD)

def attend_kernel(info_ref, q_own_ref, q_got_ref, place_own_ref, place_got_ref, *refs, tok, span, moves, heads, layout, part):
    arrays, out_ref, low_ref, high_ref = refs[:-11], refs[-11], refs[-10], refs[-9]
    kv, ids, start_scr, m_scr, l_scr, acc_scr, bounds, sem = refs[-8:]
    c = pl.program_id(0)
    z = info_ref[0]
    half = len(moves) * tok
    near = pl.multiple_of(info_ref[1], half)
    far = pl.multiple_of(half - info_ref[1], half)
    first = pl.multiple_of(part * half + z * tok, tok)
    is_own = info_ref[2] == part

    @pl.when(c == 0)
    def _():
        blocks = []
        copies = []
        for n, (which, row) in enumerate(layout):
            piece = arrays[which]
            place = lax.rem(z + moves[n % len(moves)] + len(moves), len(moves)) * tok
            slab = n // len(moves) * 2 * half
            for side, base in ((0, near), (1, far)):
                at = pl.multiple_of(slab + base + place, tok)
                cp = pltpu.make_async_copy(piece.at[pl.ds(row + side * tok, tok)], kv.at[pl.ds(at, tok)], sem.at[n, side])
                blocks.append((cp, (at >= first) & (at <= first + 2 * half)))
            copies.append(pltpu.make_async_copy(piece.at[pl.ds(row + 2 * tok, 16)], ids.at[n], sem.at[n, 2]))
        for cp in copies:
            cp.start()
        for cp, needed in blocks:
            pl.when(needed)(cp.start)
        for cp in copies:
            cp.wait()
        own = [ids[len(moves), 0:1, n * tok:(n + 1) * tok].astype(jnp.float32) for n in range(2)]
        own = jnp.where(is_own, own[0], own[1])
        own = jnp.broadcast_to(own, (tok, tok)).T
        less = jnp.zeros((tok, tok), jnp.float32)
        for n in range(len(layout)):
            for side in range(2):
                row = ids[n, 0:1, side * tok:(side + 1) * tok].astype(jnp.float32)
                less = less + jnp.where(row < own, 1.0, 0.0)
        begin = jnp.sum(less, axis=1, keepdims=True)
        start_scr[...] = begin.astype(jnp.int32)
        bounds[0] = jnp.min(begin).astype(jnp.int32)
        bounds[1] = jnp.max(begin).astype(jnp.int32)
        for cp, needed in blocks:
            pl.when(needed)(cp.wait)

    start_min, start_max = bounds[0], bounds[1]
    q = jnp.where(is_own, q_own_ref[...], q_got_ref[...])
    q = jnp.concatenate([q[:, g * HD:(g + 1) * HD] for g in range(GROUP)], 0)
    start = start_scr[...]
    row = lax.broadcasted_iota(jnp.int32, (tok, 1), 0) + first + 2 * half
    key_col = pl.multiple_of(c * HD, HD)
    value_col = pl.multiple_of((heads + c) * HD, HD)

    def keys(offset, width):
        return kv[pl.ds(offset, width), pl.ds(key_col, HD)]

    def values(offset, width):
        return kv[pl.ds(offset, width), pl.ds(value_col, HD)]

    def scores(offset, width):
        return lax.dot_general(q, keys(offset, width), (((1,), (1,)), ((), ())), preferred_element_type=jnp.float32)

    def rowmax(s, width):
        t = s[:, :128]
        for j in range(1, width // 128):
            t = jnp.maximum(t, s[:, j * 128:(j + 1) * 128])
        return jnp.max(t, axis=1, keepdims=True)

    def lanesum(p, width):
        t = p[:, :128]
        for j in range(1, width // 128):
            t = t + p[:, j * 128:(j + 1) * 128]
        return t

    def masked(s, offset, width, causal):
        key = lax.broadcasted_iota(jnp.int32, (tok, width), 1) + offset
        ok = key >= start
        if causal:
            ok = ok & (key <= row)
        return jnp.where(ok[None], s.reshape(GROUP, tok, width), -1e30).reshape(GROUP * tok, width)

    own = pl.multiple_of(first + 2 * half, tok)
    s = masked(scores(own, tok), own, tok, True)
    m = rowmax(s, tok)
    p = jnp.exp2((s - m) * EXP2_SCALE)
    m_scr[...] = jnp.broadcast_to(m, m_scr.shape)
    l_scr[...] = lanesum(p, tok)
    acc_scr[...] = jnp.dot(p.astype(jnp.bfloat16), values(own, tok), preferred_element_type=jnp.float32)

    def step(i, mask):
        offset = pl.multiple_of(first + i * span, tok)
        s = scores(offset, span)
        if mask:
            s = masked(s, offset, span, False)
        old = m_scr[...]
        new = jnp.maximum(old, rowmax(s, span))
        m_scr[...] = new
        shrink = jnp.exp2((old - new) * EXP2_SCALE)
        p = jnp.exp2((s - jnp.concatenate([new] * (span // 128), 1)) * EXP2_SCALE)
        l_scr[...] = l_scr[...] * shrink + lanesum(p, span)
        acc_scr[...] = acc_scr[...] * shrink + jnp.dot(p.astype(jnp.bfloat16), values(offset, span), preferred_element_type=jnp.float32)

    steps = 2 * half // span

    def loop(i, carry):
        whole = start_max <= first + i * span

        @pl.when(whole)
        def _():
            step(i, False)

        @pl.when(jnp.logical_not(whole))
        def _():
            step(i, True)

        return carry

    lax.fori_loop(jnp.clip(lax.div(start_min - first, span), 0, steps), steps, loop, 0)

    total = jnp.sum(l_scr[...], axis=1, keepdims=True)
    att = (acc_scr[...] / total).astype(jnp.bfloat16)
    att = jnp.concatenate([att[g * tok:(g + 1) * tok] for g in range(GROUP)], 1)
    out_ref[...] = att
    place = jnp.where(is_own, place_own_ref[...], place_got_ref[...])
    rows = jnp.dot(place, att, preferred_element_type=jnp.float32).astype(jnp.bfloat16)
    low_ref[...] = rows[:rows.shape[0] // 2]
    high_ref[...] = rows[rows.shape[0] // 2:]


def attend(info, own, got, pieces, layout, moves, part, heads, tok, span=512):
    slots = tok // 4
    wide = GROUP * HD
    n = len(moves)
    hbm = pl.BlockSpec(memory_space=pl.ANY)
    scratch = pltpu.VMEM((GROUP * tok, 128), jnp.float32)
    return pl.pallas_call(
        functools.partial(attend_kernel, tok=tok, span=span, moves=moves, heads=heads, layout=layout, part=part),
        grid_spec=pltpu.PrefetchScalarGridSpec(
            num_scalar_prefetch=1,
            grid=(heads,),
            in_specs=[
                pl.BlockSpec((tok, wide), lambda c, s: (0, c)),
                pl.BlockSpec((tok, wide), lambda c, s: (0, c)),
                pl.BlockSpec((2 * slots, tok), lambda c, s: (tok // (2 * slots), heads * GROUP)),
                pl.BlockSpec((2 * slots, tok), lambda c, s: (tok // (2 * slots), heads * GROUP)),
            ] + [hbm] * len(pieces),
            out_specs=[pl.BlockSpec((r, wide), lambda c, s: (0, c)) for r in (tok, slots, slots)],
            scratch_shapes=[
                pltpu.VMEM((4 * n * tok, 2 * heads * HD), jnp.bfloat16),
                pltpu.VMEM((2 * n, 16, 2 * heads * HD), jnp.bfloat16),
                pltpu.VMEM((tok, 1), jnp.int32),
                scratch, scratch, scratch,
                pltpu.SMEM((2,), jnp.int32),
                pltpu.SemaphoreType.DMA((2 * n, 3)),
            ],
        ),
        out_shape=[jax.ShapeDtypeStruct((r, heads * wide), jnp.bfloat16) for r in (tok, slots, slots)],
        compiler_params=pltpu.CompilerParams(vmem_limit_bytes=60 << 20),
        cost_estimate=pl.CostEstimate(flops=2 * 10**9, bytes_accessed=1 << 20, transcendentals=10**5),
        name="attend",
    )(info, own, got, own, got, *pieces)


def prepare_kernel(info_ref, kv_ref, doc_ref, send_ref, mine_ref):
    tok = kv_ref.shape[0]
    w = kv_ref.shape[1] // 4
    send_ref[tok:, :] = jnp.zeros((16, 2 * w), send_ref.dtype)
    send_ref[tok:tok + 16, :tok] = jnp.broadcast_to((doc_ref[...] + 1).astype(jnp.float32), (16, tok)).astype(send_ref.dtype)
    for yhi in range(2):
        @pl.when(info_ref[2] == yhi)
        def _(yhi=yhi):
            away = 1 - yhi
            mine_ref[:, :w] = kv_ref[:, yhi * w:(yhi + 1) * w]
            mine_ref[:, w:] = kv_ref[:, (2 + yhi) * w:(3 + yhi) * w]
            send_ref[:tok, :w] = kv_ref[:, away * w:(away + 1) * w]
            send_ref[:tok, w:] = kv_ref[:, (2 + away) * w:(3 + away) * w]


def prepare(info, keys_values, doc_ids):
    tok, width = keys_values.shape
    vm = pl.BlockSpec(memory_space=pltpu.VMEM)
    shape = lambda r, c: jax.ShapeDtypeStruct((r, c), jnp.bfloat16)
    return pl.pallas_call(
        prepare_kernel,
        in_specs=[pl.BlockSpec(memory_space=pltpu.SMEM)] + [vm] * 2,
        out_specs=[vm] * 2,
        out_shape=[shape(tok + 16, width // 2), shape(tok, width // 2)],
        compiler_params=pltpu.CompilerParams(vmem_limit_bytes=24 << 20),
        name="prepare",
    )(info, keys_values, doc_ids[None])


def plan_kernel(info_ref, ids_ref, weights_ref, q_ref, hid_ref, out_ref, own_ref, hot_ref, factor_ref):
    tok = hid_ref.shape[0]
    slots = (out_ref.shape[0] - tok) // 2
    q = q_ref.shape[1] // 2
    yhi = info_ref[2]
    below = lax.broadcasted_iota(jnp.int32, (tok, tok), 0) <= lax.broadcasted_iota(jnp.int32, (tok, tok), 1)
    below = below.astype(jnp.float32).astype(jnp.bfloat16)
    places, factors = [], []
    for flight in (yhi, 1 - yhi):
        chosen = ids_ref[...] == flight
        routed = jnp.max(jnp.where(chosen, 1.0, 0.0), axis=0, keepdims=True)
        factors.append(jnp.sum(jnp.where(chosen, weights_ref[...], 0.0), axis=0, keepdims=True))
        ranks = jnp.dot(jnp.broadcast_to(routed, (16, tok)).astype(jnp.bfloat16), below, preferred_element_type=jnp.float32)
        ranks = jnp.where(routed > 0.5, ranks[:1] - 1.0, -1.0)
        slot = lax.broadcasted_iota(jnp.int32, (slots, tok), 0).astype(jnp.float32)
        places.append(jnp.where(slot == ranks, 1.0, 0.0))
    place_f = jnp.concatenate(places, 0)
    place = place_f.astype(jnp.bfloat16)
    hot_ref[...] = jnp.concatenate([place_f, jnp.zeros((tok - 2 * slots, tok), jnp.float32)], 0).T.astype(jnp.bfloat16)
    factor_ref[...] = jnp.concatenate([factors[0], factors[1], jnp.zeros((tok - 2, tok), jnp.float32)], 0).T
    rows = jnp.dot(place, hid_ref[...], preferred_element_type=jnp.float32).astype(jnp.bfloat16)
    for n, ref in enumerate((own_ref, out_ref)):
        ref[:tok, q:] = jnp.zeros((tok, tok), jnp.bfloat16)
        ref[tok:tok + slots, :q] = rows[n * slots:(n + 1) * slots, :q]
        ref[tok + slots:, :q] = rows[n * slots:(n + 1) * slots, q:]
        ref[tok:tok + slots, q:] = place[n * slots:(n + 1) * slots]
        ref[tok + slots:, q:] = place[(1 - n) * slots:(2 - n) * slots]

    for side in range(2):
        @pl.when(yhi == side)
        def _(side=side):
            own_ref[:tok, :q] = q_ref[:, side * q:(side + 1) * q]
            out_ref[:tok, :q] = q_ref[:, (1 - side) * q:(2 - side) * q]


def plan(info, route_ids, route_weights, queries, hidden):
    tok, d = hidden.shape
    slots = tok // 4
    vm = pl.BlockSpec(memory_space=pltpu.VMEM)
    shape = lambda r, c, t=jnp.bfloat16: jax.ShapeDtypeStruct((r, c), t)
    return pl.pallas_call(
        plan_kernel,
        in_specs=[pl.BlockSpec(memory_space=pltpu.SMEM)] + [vm] * 4,
        out_specs=[vm] * 4,
        out_shape=[shape(tok + 2 * slots, d // 2 + tok)] * 2 + [shape(tok, tok), shape(tok, tok, jnp.float32)],
        compiler_params=pltpu.CompilerParams(vmem_limit_bytes=24 << 20),
        name="plan",
    )(info, route_ids.T, route_weights.T, queries, hidden)


def join_kernel(send_ref, mine_ref, other_ref, unit_ref):
    tok = mine_ref.shape[0]
    unit_ref[:tok] = mine_ref[...]
    unit_ref[tok:2 * tok] = other_ref[:tok]
    unit_ref[2 * tok:] = send_ref[tok:]
    unit_ref[2 * tok:, tok:2 * tok] = other_ref[tok:, :tok]


def join(send, mine, other):
    tok, width = mine.shape
    vm = pl.BlockSpec(memory_space=pltpu.VMEM)
    return pl.pallas_call(
        join_kernel,
        in_specs=[vm] * 3,
        out_specs=vm,
        out_shape=jax.ShapeDtypeStruct((2 * tok + 16, width), mine.dtype),
        compiler_params=pltpu.CompilerParams(vmem_limit_bytes=24 << 20),
        name="join",
    )(send, mine, other)


def pack_kernel(info_ref, gu_ref, down_ref, out_ref, sem):
    yhi = info_ref[2]
    units, wide = out_ref.shape[1], out_ref.shape[2]
    at = pl.ds(pl.multiple_of(info_ref[3] * units, units), units)
    if wide == down_ref.shape[2]:
        away, cols = 1 - yhi, pl.ds(0, wide)
    else:
        away = jnp.where(info_ref[5] == 0, yhi, 1 - yhi)
        cols = pl.ds(pl.multiple_of(info_ref[4] * wide, wide), wide)
    one = pltpu.make_async_copy(gu_ref.at[away, :, at, cols], out_ref.at[pl.ds(0, 2)], sem.at[0])
    two = pltpu.make_async_copy(down_ref.at[away, at, cols], out_ref.at[2], sem.at[1])
    one.start()
    two.start()
    one.wait()
    two.wait()


def pack(info, wide_t, down, cores, columns):
    hbm = pl.BlockSpec(memory_space=pl.ANY)
    units, d = down.shape[1] // cores, down.shape[2]
    return pl.pallas_call(
        pack_kernel,
        in_specs=[pl.BlockSpec(memory_space=pltpu.SMEM), hbm, hbm],
        out_specs=pl.BlockSpec(memory_space=pltpu.VMEM),
        out_shape=jax.ShapeDtypeStruct((3, units, d // columns), down.dtype),
        scratch_shapes=[pltpu.SemaphoreType.DMA((2,))],
        compiler_params=pltpu.CompilerParams(vmem_limit_bytes=60 << 20),
        name="pack",
    )(info, wide_t, down)


def norm_kernel(info_ref, own_ref, got_ref, mine_ref, other_ref, gain_ref, out_ref, *, part):
    slots, half = mine_ref.shape
    tok = own_ref.shape[0] - 2 * slots
    is_own = info_ref[2] == part

    def put(low, high):
        parts = []
        for n, att in enumerate((low, high)):
            rows = slice(tok + n * slots, tok + (n + 1) * slots)
            base = jnp.where(is_own, own_ref[rows, :half], got_ref[rows, :half]).astype(jnp.float32)
            parts.append((base + att.astype(jnp.float32)).astype(jnp.bfloat16).astype(jnp.float32))
        total = sum(jnp.sum(p * p, axis=1, keepdims=True) for p in parts)
        inv = lax.rsqrt(total / (2 * half) + 1e-6)
        for n, p in enumerate(parts):
            gain = gain_ref[:, n * half:(n + 1) * half].astype(jnp.float32)
            out_ref[:, n * half:(n + 1) * half] = (p * inv * gain).astype(jnp.bfloat16)

    @pl.when(info_ref[2] == 0)
    def _():
        put(mine_ref[...], other_ref[...])

    @pl.when(info_ref[2] != 0)
    def _():
        put(other_ref[...], mine_ref[...])


def norm_rows(info, own, got, part, mine, other, gain):
    slots, half = mine.shape
    vm = pl.BlockSpec(memory_space=pltpu.VMEM)
    return pl.pallas_call(
        functools.partial(norm_kernel, part=part),
        in_specs=[pl.BlockSpec(memory_space=pltpu.SMEM)] + [vm] * 5,
        out_specs=vm,
        out_shape=jax.ShapeDtypeStruct((slots, 2 * half), jnp.bfloat16),
        compiler_params=pltpu.CompilerParams(vmem_limit_bytes=16 << 20),
        name="norm_rows",
    )(info, own, got, mine, other, gain)


def assemble_kernel(info_ref, wo_ref, do_ref, r1_ref, r2_ref, *refs, plan, columns):
    blocks, w_ref, sem = refs[:len(plan)], refs[-2], refs[-1]
    yhi = info_ref[2]
    n, h = wo_ref.shape[2], r1_ref.shape[1]
    cps = []

    def cp(src, dst):
        cps.append(pltpu.make_async_copy(src, dst, sem.at[len(cps)]))

    for i in range(3):
        own = do_ref.at[yhi] if i == 2 else wo_ref.at[yhi, i]
        for src, at, size in ((own, 0, n), (r1_ref.at[i], n, h), (r2_ref.at[i], n + h, h)):
            cp(src, w_ref.at[i, pl.ds(at, size)])
        for block, (core, step, first) in zip(blocks, plan):
            wide = block.shape[2]
            col = lax.rem(info_ref[4] + step + columns, columns) * wide
            for u in range(block.shape[0] // 3):
                at = n + 2 * h + (2 * core + first + u) * h
                cp(block.at[3 * u + i], w_ref.at[i, pl.ds(at, h), pl.ds(pl.multiple_of(col, wide), wide)])
    for c in cps:
        c.start()
    for c in cps:
        c.wait()


def assemble(info, wo, do, r1, r2, blocks, plan, columns, after):
    n, d = 2 * (wo.shape[2] + r1.shape[1] + r2.shape[1]), wo.shape[3]
    hbm = pl.BlockSpec(memory_space=pl.ANY)
    return pl.pallas_call(
        functools.partial(assemble_kernel, plan=plan, columns=columns),
        in_specs=[pl.BlockSpec(memory_space=pltpu.SMEM)] + [hbm] * (5 + len(blocks)),
        out_specs=pl.BlockSpec(memory_space=pltpu.VMEM),
        scratch_shapes=[pltpu.SemaphoreType.DMA((9 + 6 * len(blocks),))],
        out_shape=jax.ShapeDtypeStruct((3, n, d), jnp.bfloat16),
        compiler_params=pltpu.CompilerParams(vmem_limit_bytes=20 << 20),
        cost_estimate=pl.CostEstimate(flops=0, bytes_accessed=n * d, transcendentals=0),
        name="assemble",
    )(info, wo, do, r1, r2, *blocks, after)


def expert_kernel(*refs, count, rows, after):
    xs, w_ref, ys = refs[:count], refs[count], refs[count + 1 + after:]
    x = jnp.concatenate([r[...] for r in xs], 0)
    nt = (((1,), (1,)), ((), ()))
    gate = lax.dot_general(x, w_ref[0], nt, preferred_element_type=jnp.float32)
    up = lax.dot_general(x, w_ref[1], nt, preferred_element_type=jnp.float32)
    inner = (gate / (1 + jnp.exp(-gate)) * up).astype(jnp.bfloat16)
    y = jnp.dot(inner, w_ref[2], preferred_element_type=jnp.float32).astype(jnp.bfloat16)
    for i in range(count):
        ys[i][...] = y[i * rows:(i + 1) * rows]


def experts(xs, w, after=()):
    count = len(xs)
    rows, d = xs[0].shape
    n = w.shape[1]
    vm = pl.BlockSpec(memory_space=pltpu.VMEM)
    return pl.pallas_call(
        functools.partial(expert_kernel, count=count, rows=rows, after=len(after)),
        in_specs=[vm] * (count + 1) + [pl.BlockSpec(memory_space=pl.ANY)] * len(after),
        out_specs=[vm] * count,
        out_shape=[jax.ShapeDtypeStruct((rows, d), jnp.bfloat16)] * count,
        compiler_params=pltpu.CompilerParams(vmem_limit_bytes=26 << 20),
        cost_estimate=pl.CostEstimate(flops=2 * count * rows * n * d, bytes_accessed=n * d, transcendentals=count * rows),
        name="experts",
    )(*xs, w, *after)


def combine_kernel(info_ref, hid_ref, mine_ref, other_ref, keep_ref, back_ref, hot_ref, factor_ref, out_ref):
    cap = back_ref.shape[0]
    is_mine = pl.program_id(0) // 2 == info_ref[2]
    att = jnp.where(is_mine, mine_ref[...].astype(jnp.float32), other_ref[...].astype(jnp.float32))
    stream = (hid_ref[...].astype(jnp.float32) + att).astype(jnp.bfloat16).astype(jnp.float32)
    one = jnp.dot(hot_ref[:, :cap], keep_ref[...], preferred_element_type=jnp.float32)
    two = jnp.dot(hot_ref[:, cap:2 * cap], back_ref[...], preferred_element_type=jnp.float32)
    out_ref[...] = (stream + one * factor_ref[:, 0:1] + two * factor_ref[:, 1:2]).astype(out_ref.dtype)


def combine(info, hidden, mine, other, keep, back, hot, factors):
    tok, d = hidden.shape
    cap = back.shape[0]
    wide = d // 4
    cols = lambda rows: pl.BlockSpec((rows, wide), lambda c, s: (0, c))
    half = pl.BlockSpec((tok, wide), lambda c, s: (0, lax.rem(c, 2)))
    whole = pl.BlockSpec((tok, tok), lambda c, s: (0, 0))
    return pl.pallas_call(
        combine_kernel,
        grid_spec=pltpu.PrefetchScalarGridSpec(
            num_scalar_prefetch=1,
            grid=(4,),
            in_specs=[cols(tok), half, half, cols(cap), cols(cap), whole, whole],
            out_specs=cols(tok),
        ),
        out_shape=jax.ShapeDtypeStruct((tok, d), hidden.dtype),
        compiler_params=pltpu.CompilerParams(vmem_limit_bytes=24 << 20),
        name="combine",
    )(info, hidden, mine, other, keep, back, hot, factors)


def shift(value, axis, size, steps):
    return lax.ppermute(value, axis, [(i, (i + steps) % size) for i in range(size)])


def swap(value, axis):
    return shift(value, axis, 2, 1)


def ring_moves(size):
    out = [0]
    for s in range(1, size // 2 + 1):
        out.append(-s)
        if 2 * s < size:
            out.append(s)
    return out


def ring_scatter(parts, signs, size):
    ups = [p[-2 * sign] for p, sign in zip(parts, signs)]
    downs = [shift(p[sign], "z", size, sign) for p, sign in zip(parts, signs)]
    for i, (p, sign) in enumerate(zip(parts, signs)):
        ups[i] = shift(ups[i], "z", size, -sign) + p[-sign]
    ups = [shift(u, "z", size, -sign) for u, sign in zip(ups, signs)]
    return [(ups[i], downs[i], p[0]) for i, p in enumerate(parts)]


def body(sizes, hidden_in, queries, keys_values, doc_ids, route_ids, route_weights, norm_gain, gate_up, down):
    tok, d = queries.shape
    capacity = tok // 4
    n_z, n_core, n_cx = sizes["z"], sizes["core"], sizes["cx"]
    yhi, z, core = lax.axis_index("yhi"), lax.axis_index("z"), lax.axis_index("core")
    half = n_z * tok
    n_ctx = n_cx * n_core
    moves = ring_moves(n_z)
    heads = keys_values.shape[1] // (4 * HD)
    cx, dp = lax.axis_index("cx"), lax.axis_index("dp")
    info = jnp.stack([z, yhi * half, yhi, core, cx, dp]).astype(jnp.int32)

    wide_t = jnp.swapaxes(gate_up, 2, 3)
    far = pack(info, wide_t, down, n_core, n_cx)
    place = lambda y, k, l: (y * n_z + k) * 2 + l
    across = [
        (place(y, k, l), place(y if l == 0 else 1 - y, (k + n_z // 2) % n_z, l)) for y in range(2) for k in range(n_z) for l in range(2)
    ]

    send, kept = prepare(info, keys_values, doc_ids)
    other = swap(send, "yhi")

    out, mine, hot, factors = plan(info, route_ids, route_weights, queries, hidden_in)
    out, other = lax.optimization_barrier((out, other))
    got = swap(out, "yhi")
    unit = join(send, kept, other)
    theirs = pack(info, wide_t, down, n_core, 1)
    ahead = [(i, i + 1) for i in range(n_ctx - 1)]
    onward = lambda x: lax.ppermute(x, ("cx", "core"), ahead)
    own = {0: unit}
    prior = [onward(unit)]
    for s in range(1, n_z // 2 + 1):
        own[-s] = shift(own[1 - s], "z", n_z, 1)
        if 2 * s < n_z:
            own[s] = shift(own[s - 1], "z", n_z, -1)
        if s == 1:
            own[-s], theirs = lax.optimization_barrier((own[-s], theirs))
            got_1 = swap(theirs, "yhi")
        if s == 2:
            own[-s], prior[0], got = lax.optimization_barrier((own[-s], prior[0], got))
        if s == 4:
            own[-s], far = lax.optimization_barrier((own[-s], far))
            far = lax.ppermute(far, ("yhi", "z", "dp"), across)
    own = [own[m] for m in moves]
    groups = [range(0, 1), range(1, n_z // 2 + 1), range(n_z // 2 + 1, n_z - 1), range(n_z - 1, n_z)]
    layout = []
    for n, group in enumerate(groups):
        if n > 0:
            prior.append(onward(jnp.concatenate([own[i] for i in group], 0) if len(group) > 1 else own[group[0]]))
        layout += [(n, k * unit.shape[0]) for k in range(len(group))]
    layout += [(len(groups) + i, 0) for i in range(n_z)]
    pieces = prior + own

    gain = norm_gain[None]
    first = yhi == 0
    atts, rows = [], []
    for part in range(2):
        if part == 1:
            mine, got_1, _ = lax.optimization_barrier((mine, got_1, atts[0]))
        att, keep, away = attend(info, mine, got, pieces, layout, moves, part, heads, tok)
        if part == 1:
            away, far = lax.optimization_barrier((away, far))
            share = jnp.concatenate([far, swap(far, "dp")], 0)
            left, right = shift(share, "cx", n_cx, 1), shift(share, "cx", n_cx, -1)
        atts.append(att)
        rows.append(norm_rows(info, mine, got, part, keep, swap(away, "yhi"), gain))
    got_2 = swap(got_1, "core")
    own_att = jnp.where(first, atts[0], atts[1])
    away_att, rows[1] = lax.optimization_barrier((jnp.where(first, atts[1], atts[0]), rows[1]))
    other_att = swap(away_att, "yhi")

    signs = [1, -1]
    rows = [{0: x, -sign: shift(x, "z", n_z, sign), sign: shift(x, "z", n_z, -sign)} for x, sign in zip(rows, signs)]
    cut = share.shape[0] // 2
    blocks = [share, left, right, shift(right[:cut], "cx", n_cx, -1), shift(left[cut:], "cx", n_cx, 1)]
    steps = [(0, 0), (-1, 0), (1, 0), (2, 0), (2, 1)]
    for g, sign in zip(rows, signs):
        g[-2 * sign] = shift(g[-sign], "z", n_z, sign)
    blocks = blocks + [swap(x, "core") for x in blocks]
    layout = [(c,) + step for c in range(n_core) for step in steps]
    weights = assemble(info, wide_t, down, got_1, got_2, blocks, layout, n_cx, rows[1][0])
    keys = [(i, m) for i, sign in enumerate(signs) for m in (0, -1, 1, -2 * sign)]
    outs = [{}, {}]
    for (i, m), y in zip(keys, experts([rows[i][m] for i, m in keys], weights, after=[other_att])):
        outs[i][m] = y
    sums = [ups.astype(jnp.float32) + downs + here for ups, downs, here in ring_scatter(outs, signs, n_z)]
    back = swap(jnp.where(first, sums[1], sums[0]).astype(jnp.bfloat16), "yhi")
    keep = jnp.where(first, sums[0], sums[1]).astype(jnp.bfloat16)
    return combine(info, hidden_in, own_att, other_att, keep, back, hot, factors)


def solution(mesh):
    sizes = {"cx": mesh.shape["ctx"] // 2, "core": 2, "yhi": 2, "z": mesh.shape["exp"] // 2, "dp": mesh.shape["dp"]}
    fine = Mesh(mesh.devices.reshape(tuple(sizes.values())), tuple(sizes))
    tokens = ("dp", "cx", "core", "yhi", "z")
    rows = P(tokens, None)
    hidden = ("yhi", "z")
    in_specs = (rows, rows, rows, P(tokens), rows, rows, P(), P(None, None, None, hidden), P(None, hidden, None))
    return jax.shard_map(
        functools.partial(body, sizes), mesh=fine, in_specs=in_specs, out_specs=rows, check_vma=False
    )
```

```python
import functools
import math

import jax
import jax.numpy as jnp
from jax import lax
from jax.experimental import pallas as pl
from jax.experimental.pallas import tpu as pltpu
from jax.sharding import Mesh
from jax.sharding import PartitionSpec as P

EXP_FLIGHT = 2
HD = 128
GROUP = 7
EXP2_SCALE = math.log2(math.e) / math.sqrt(HD)

def attend_kernel(info_ref, q_own_ref, q_got_ref, place_own_ref, place_got_ref, *refs, tok, span, moves, heads, layout, part):
    arrays, out_ref, low_ref, high_ref = refs[:-11], refs[-11], refs[-10], refs[-9]
    kv, ids, start_scr, m_scr, l_scr, acc_scr, bounds, sem = refs[-8:]
    c = pl.program_id(0)
    z = info_ref[0]
    half = len(moves) * tok
    near = pl.multiple_of(info_ref[1], half)
    far = pl.multiple_of(half - info_ref[1], half)
    first = pl.multiple_of(part * half + z * tok, tok)
    is_own = info_ref[2] == part

    @pl.when(c == 0)
    def _():
        blocks = []
        copies = []
        for n, (which, row) in enumerate(layout):
            piece = arrays[which]
            place = lax.rem(z + moves[n % len(moves)] + len(moves), len(moves)) * tok
            slab = n // len(moves) * 2 * half
            for side, base in ((0, near), (1, far)):
                at = pl.multiple_of(slab + base + place, tok)
                cp = pltpu.make_async_copy(piece.at[pl.ds(row + side * tok, tok)], kv.at[pl.ds(at, tok)], sem.at[n, side])
                blocks.append((cp, (at >= first) & (at <= first + 2 * half)))
            copies.append(pltpu.make_async_copy(piece.at[pl.ds(row + 2 * tok, 16)], ids.at[n], sem.at[n, 2]))
        for cp in copies:
            cp.start()
        for cp, needed in blocks:
            pl.when(needed)(cp.start)
        for cp in copies:
            cp.wait()
        own = [ids[len(moves), 0:1, n * tok:(n + 1) * tok].astype(jnp.float32) for n in range(2)]
        own = jnp.where(is_own, own[0], own[1])
        own = jnp.broadcast_to(own, (tok, tok)).T
        less = jnp.zeros((tok, tok), jnp.float32)
        for n in range(len(layout)):
            for side in range(2):
                row = ids[n, 0:1, side * tok:(side + 1) * tok].astype(jnp.float32)
                less = less + jnp.where(row < own, 1.0, 0.0)
        begin = jnp.sum(less, axis=1, keepdims=True)
        start_scr[...] = begin.astype(jnp.int32)
        bounds[0] = jnp.min(begin).astype(jnp.int32)
        bounds[1] = jnp.max(begin).astype(jnp.int32)
        for cp, needed in blocks:
            pl.when(needed)(cp.wait)

    start_min, start_max = bounds[0], bounds[1]
    q = jnp.where(is_own, q_own_ref[...], q_got_ref[...])
    q = jnp.concatenate([q[:, g * HD:(g + 1) * HD] for g in range(GROUP)], 0)
    start = start_scr[...]
    row = lax.broadcasted_iota(jnp.int32, (tok, 1), 0) + first + 2 * half
    key_col = pl.multiple_of(c * HD, HD)
    value_col = pl.multiple_of((heads + c) * HD, HD)

    def keys(offset, width):
        return kv[pl.ds(offset, width), pl.ds(key_col, HD)]

    def values(offset, width):
        return kv[pl.ds(offset, width), pl.ds(value_col, HD)]

    def scores(offset, width):
        return lax.dot_general(q, keys(offset, width), (((1,), (1,)), ((), ())), preferred_element_type=jnp.float32)

    def rowmax(s, width):
        t = s[:, :128]
        for j in range(1, width // 128):
            t = jnp.maximum(t, s[:, j * 128:(j + 1) * 128])
        return jnp.max(t, axis=1, keepdims=True)

    def lanesum(p, width):
        t = p[:, :128]
        for j in range(1, width // 128):
            t = t + p[:, j * 128:(j + 1) * 128]
        return t

    def masked(s, offset, width, causal):
        key = lax.broadcasted_iota(jnp.int32, (tok, width), 1) + offset
        ok = key >= start
        if causal:
            ok = ok & (key <= row)
        return jnp.where(ok[None], s.reshape(GROUP, tok, width), -1e30).reshape(GROUP * tok, width)

    own = pl.multiple_of(first + 2 * half, tok)
    s = masked(scores(own, tok), own, tok, True)
    m = rowmax(s, tok)
    p = jnp.exp2((s - m) * EXP2_SCALE)
    m_scr[...] = jnp.broadcast_to(m, m_scr.shape)
    l_scr[...] = lanesum(p, tok)
    acc_scr[...] = jnp.dot(p.astype(jnp.bfloat16), values(own, tok), preferred_element_type=jnp.float32)

    def step(i, mask):
        offset = pl.multiple_of(first + i * span, tok)
        s = scores(offset, span)
        if mask:
            s = masked(s, offset, span, False)
        old = m_scr[...]
        new = jnp.maximum(old, rowmax(s, span))
        m_scr[...] = new
        shrink = jnp.exp2((old - new) * EXP2_SCALE)
        p = jnp.exp2((s - jnp.concatenate([new] * (span // 128), 1)) * EXP2_SCALE)
        l_scr[...] = l_scr[...] * shrink + lanesum(p, span)
        acc_scr[...] = acc_scr[...] * shrink + jnp.dot(p.astype(jnp.bfloat16), values(offset, span), preferred_element_type=jnp.float32)

    steps = 2 * half // span

    def loop(i, carry):
        whole = start_max <= first + i * span

        @pl.when(whole)
        def _():
            step(i, False)

        @pl.when(jnp.logical_not(whole))
        def _():
            step(i, True)

        return carry

    lax.fori_loop(jnp.clip(lax.div(start_min - first, span), 0, steps), steps, loop, 0)

    total = jnp.sum(l_scr[...], axis=1, keepdims=True)
    att = (acc_scr[...] / total).astype(jnp.bfloat16)
    att = jnp.concatenate([att[g * tok:(g + 1) * tok] for g in range(GROUP)], 1)
    out_ref[...] = att
    place = jnp.where(is_own, place_own_ref[...], place_got_ref[...])
    rows = jnp.dot(place, att, preferred_element_type=jnp.float32).astype(jnp.bfloat16)
    low_ref[...] = rows[:rows.shape[0] // 2]
    high_ref[...] = rows[rows.shape[0] // 2:]


def attend(info, own, got, pieces, layout, moves, part, heads, tok, span=512):
    slots = tok // 4
    wide = GROUP * HD
    n = len(moves)
    hbm = pl.BlockSpec(memory_space=pl.ANY)
    scratch = pltpu.VMEM((GROUP * tok, 128), jnp.float32)
    return pl.pallas_call(
        functools.partial(attend_kernel, tok=tok, span=span, moves=moves, heads=heads, layout=layout, part=part),
        grid_spec=pltpu.PrefetchScalarGridSpec(
            num_scalar_prefetch=1,
            grid=(heads,),
            in_specs=[
                pl.BlockSpec((tok, wide), lambda c, s: (0, c)),
                pl.BlockSpec((tok, wide), lambda c, s: (0, c)),
                pl.BlockSpec((2 * slots, tok), lambda c, s: (tok // (2 * slots), heads * GROUP)),
                pl.BlockSpec((2 * slots, tok), lambda c, s: (tok // (2 * slots), heads * GROUP)),
            ] + [hbm] * len(pieces),
            out_specs=[pl.BlockSpec((r, wide), lambda c, s: (0, c)) for r in (tok, slots, slots)],
            scratch_shapes=[
                pltpu.VMEM((4 * n * tok, 2 * heads * HD), jnp.bfloat16),
                pltpu.VMEM((2 * n, 16, 2 * heads * HD), jnp.bfloat16),
                pltpu.VMEM((tok, 1), jnp.int32),
                scratch, scratch, scratch,
                pltpu.SMEM((2,), jnp.int32),
                pltpu.SemaphoreType.DMA((2 * n, 3)),
            ],
        ),
        out_shape=[jax.ShapeDtypeStruct((r, heads * wide), jnp.bfloat16) for r in (tok, slots, slots)],
        compiler_params=pltpu.CompilerParams(vmem_limit_bytes=60 << 20),
        cost_estimate=pl.CostEstimate(flops=2 * 10**9, bytes_accessed=1 << 20, transcendentals=10**5),
        name="attend",
    )(info, own, got, own, got, *pieces)


def prepare_kernel(info_ref, kv_ref, doc_ref, send_ref, mine_ref):
    tok = kv_ref.shape[0]
    w = kv_ref.shape[1] // 4
    send_ref[tok:, :] = jnp.zeros((16, 2 * w), send_ref.dtype)
    send_ref[tok:tok + 16, :tok] = jnp.broadcast_to((doc_ref[...] + 1).astype(jnp.float32), (16, tok)).astype(send_ref.dtype)
    for yhi in range(2):
        @pl.when(info_ref[2] == yhi)
        def _(yhi=yhi):
            away = 1 - yhi
            mine_ref[:, :w] = kv_ref[:, yhi * w:(yhi + 1) * w]
            mine_ref[:, w:] = kv_ref[:, (2 + yhi) * w:(3 + yhi) * w]
            send_ref[:tok, :w] = kv_ref[:, away * w:(away + 1) * w]
            send_ref[:tok, w:] = kv_ref[:, (2 + away) * w:(3 + away) * w]


def prepare(info, keys_values, doc_ids):
    tok, width = keys_values.shape
    vm = pl.BlockSpec(memory_space=pltpu.VMEM)
    shape = lambda r, c: jax.ShapeDtypeStruct((r, c), jnp.bfloat16)
    return pl.pallas_call(
        prepare_kernel,
        in_specs=[pl.BlockSpec(memory_space=pltpu.SMEM)] + [vm] * 2,
        out_specs=[vm] * 2,
        out_shape=[shape(tok + 16, width // 2), shape(tok, width // 2)],
        compiler_params=pltpu.CompilerParams(vmem_limit_bytes=24 << 20),
        name="prepare",
    )(info, keys_values, doc_ids[None])


def plan_kernel(info_ref, ids_ref, weights_ref, q_ref, hid_ref, out_ref, own_ref, hot_ref, factor_ref):
    tok = hid_ref.shape[0]
    slots = (out_ref.shape[0] - tok) // 2
    q = q_ref.shape[1] // 2
    yhi = info_ref[2]
    below = lax.broadcasted_iota(jnp.int32, (tok, tok), 0) <= lax.broadcasted_iota(jnp.int32, (tok, tok), 1)
    below = below.astype(jnp.float32).astype(jnp.bfloat16)
    places, factors = [], []
    for flight in (yhi, 1 - yhi):
        chosen = ids_ref[...] == flight
        routed = jnp.max(jnp.where(chosen, 1.0, 0.0), axis=0, keepdims=True)
        factors.append(jnp.sum(jnp.where(chosen, weights_ref[...], 0.0), axis=0, keepdims=True))
        ranks = jnp.dot(jnp.broadcast_to(routed, (16, tok)).astype(jnp.bfloat16), below, preferred_element_type=jnp.float32)
        ranks = jnp.where(routed > 0.5, ranks[:1] - 1.0, -1.0)
        slot = lax.broadcasted_iota(jnp.int32, (slots, tok), 0).astype(jnp.float32)
        places.append(jnp.where(slot == ranks, 1.0, 0.0))
    place_f = jnp.concatenate(places, 0)
    place = place_f.astype(jnp.bfloat16)
    hot_ref[...] = jnp.concatenate([place_f, jnp.zeros((tok - 2 * slots, tok), jnp.float32)], 0).T.astype(jnp.bfloat16)
    factor_ref[...] = jnp.concatenate([factors[0], factors[1], jnp.zeros((tok - 2, tok), jnp.float32)], 0).T
    rows = jnp.dot(place, hid_ref[...], preferred_element_type=jnp.float32).astype(jnp.bfloat16)
    for n, ref in enumerate((own_ref, out_ref)):
        ref[:tok, q:] = jnp.zeros((tok, tok), jnp.bfloat16)
        ref[tok:tok + slots, :q] = rows[n * slots:(n + 1) * slots, :q]
        ref[tok + slots:, :q] = rows[n * slots:(n + 1) * slots, q:]
        ref[tok:tok + slots, q:] = place[n * slots:(n + 1) * slots]
        ref[tok + slots:, q:] = place[(1 - n) * slots:(2 - n) * slots]

    for side in range(2):
        @pl.when(yhi == side)
        def _(side=side):
            own_ref[:tok, :q] = q_ref[:, side * q:(side + 1) * q]
            out_ref[:tok, :q] = q_ref[:, (1 - side) * q:(2 - side) * q]


def plan(info, route_ids, route_weights, queries, hidden):
    tok, d = hidden.shape
    slots = tok // 4
    vm = pl.BlockSpec(memory_space=pltpu.VMEM)
    shape = lambda r, c, t=jnp.bfloat16: jax.ShapeDtypeStruct((r, c), t)
    return pl.pallas_call(
        plan_kernel,
        in_specs=[pl.BlockSpec(memory_space=pltpu.SMEM)] + [vm] * 4,
        out_specs=[vm] * 4,
        out_shape=[shape(tok + 2 * slots, d // 2 + tok)] * 2 + [shape(tok, tok), shape(tok, tok, jnp.float32)],
        compiler_params=pltpu.CompilerParams(vmem_limit_bytes=24 << 20),
        name="plan",
    )(info, route_ids.T, route_weights.T, queries, hidden)


def join_kernel(send_ref, mine_ref, other_ref, unit_ref):
    tok = mine_ref.shape[0]
    unit_ref[:tok] = mine_ref[...]
    unit_ref[tok:2 * tok] = other_ref[:tok]
    unit_ref[2 * tok:] = send_ref[tok:]
    unit_ref[2 * tok:, tok:2 * tok] = other_ref[tok:, :tok]


def join(send, mine, other):
    tok, width = mine.shape
    vm = pl.BlockSpec(memory_space=pltpu.VMEM)
    return pl.pallas_call(
        join_kernel,
        in_specs=[vm] * 3,
        out_specs=vm,
        out_shape=jax.ShapeDtypeStruct((2 * tok + 16, width), mine.dtype),
        compiler_params=pltpu.CompilerParams(vmem_limit_bytes=24 << 20),
        name="join",
    )(send, mine, other)


def pack_kernel(info_ref, gu_ref, down_ref, out_ref, sem):
    yhi = info_ref[2]
    units, wide = out_ref.shape[1], out_ref.shape[2]
    at = pl.ds(pl.multiple_of(info_ref[3] * units, units), units)
    if wide == down_ref.shape[2]:
        away, cols = 1 - yhi, pl.ds(0, wide)
    else:
        away = jnp.where(info_ref[5] == 0, yhi, 1 - yhi)
        cols = pl.ds(pl.multiple_of(info_ref[4] * wide, wide), wide)
    one = pltpu.make_async_copy(gu_ref.at[away, :, at, cols], out_ref.at[pl.ds(0, 2)], sem.at[0])
    two = pltpu.make_async_copy(down_ref.at[away, at, cols], out_ref.at[2], sem.at[1])
    one.start()
    two.start()
    one.wait()
    two.wait()


def pack(info, wide_t, down, cores, columns):
    hbm = pl.BlockSpec(memory_space=pl.ANY)
    units, d = down.shape[1] // cores, down.shape[2]
    return pl.pallas_call(
        pack_kernel,
        in_specs=[pl.BlockSpec(memory_space=pltpu.SMEM), hbm, hbm],
        out_specs=pl.BlockSpec(memory_space=pltpu.VMEM),
        out_shape=jax.ShapeDtypeStruct((3, units, d // columns), down.dtype),
        scratch_shapes=[pltpu.SemaphoreType.DMA((2,))],
        compiler_params=pltpu.CompilerParams(vmem_limit_bytes=60 << 20),
        name="pack",
    )(info, wide_t, down)


def norm_kernel(info_ref, own_ref, got_ref, mine_ref, other_ref, gain_ref, out_ref, *, part):
    slots, half = mine_ref.shape
    tok = own_ref.shape[0] - 2 * slots
    is_own = info_ref[2] == part

    def put(low, high):
        parts = []
        for n, att in enumerate((low, high)):
            rows = slice(tok + n * slots, tok + (n + 1) * slots)
            base = jnp.where(is_own, own_ref[rows, :half], got_ref[rows, :half]).astype(jnp.float32)
            parts.append((base + att.astype(jnp.float32)).astype(jnp.bfloat16).astype(jnp.float32))
        total = sum(jnp.sum(p * p, axis=1, keepdims=True) for p in parts)
        inv = lax.rsqrt(total / (2 * half) + 1e-6)
        for n, p in enumerate(parts):
            gain = gain_ref[:, n * half:(n + 1) * half].astype(jnp.float32)
            out_ref[:, n * half:(n + 1) * half] = (p * inv * gain).astype(jnp.bfloat16)

    @pl.when(info_ref[2] == 0)
    def _():
        put(mine_ref[...], other_ref[...])

    @pl.when(info_ref[2] != 0)
    def _():
        put(other_ref[...], mine_ref[...])


def norm_rows(info, own, got, part, mine, other, gain):
    slots, half = mine.shape
    vm = pl.BlockSpec(memory_space=pltpu.VMEM)
    return pl.pallas_call(
        functools.partial(norm_kernel, part=part),
        in_specs=[pl.BlockSpec(memory_space=pltpu.SMEM)] + [vm] * 5,
        out_specs=vm,
        out_shape=jax.ShapeDtypeStruct((slots, 2 * half), jnp.bfloat16),
        compiler_params=pltpu.CompilerParams(vmem_limit_bytes=16 << 20),
        name="norm_rows",
    )(info, own, got, mine, other, gain)


def assemble_kernel(info_ref, wo_ref, do_ref, r1_ref, r2_ref, *refs, plan, columns):
    blocks, w_ref, sem = refs[:len(plan)], refs[-2], refs[-1]
    yhi = info_ref[2]
    n, h = wo_ref.shape[2], r1_ref.shape[1]
    cps = []

    def cp(src, dst):
        cps.append(pltpu.make_async_copy(src, dst, sem.at[len(cps)]))

    for i in range(3):
        own = do_ref.at[yhi] if i == 2 else wo_ref.at[yhi, i]
        for src, at, size in ((own, 0, n), (r1_ref.at[i], n, h), (r2_ref.at[i], n + h, h)):
            cp(src, w_ref.at[i, pl.ds(at, size)])
        for block, (core, step, first) in zip(blocks, plan):
            wide = block.shape[2]
            col = lax.rem(info_ref[4] + step + columns, columns) * wide
            for u in range(block.shape[0] // 3):
                at = n + 2 * h + (2 * core + first + u) * h
                cp(block.at[3 * u + i], w_ref.at[i, pl.ds(at, h), pl.ds(pl.multiple_of(col, wide), wide)])
    for c in cps:
        c.start()
    for c in cps:
        c.wait()


def assemble(info, wo, do, r1, r2, blocks, plan, columns, after):
    n, d = 2 * (wo.shape[2] + r1.shape[1] + r2.shape[1]), wo.shape[3]
    hbm = pl.BlockSpec(memory_space=pl.ANY)
    return pl.pallas_call(
        functools.partial(assemble_kernel, plan=plan, columns=columns),
        in_specs=[pl.BlockSpec(memory_space=pltpu.SMEM)] + [hbm] * (4 + len(blocks) + len(after)),
        out_specs=pl.BlockSpec(memory_space=pltpu.VMEM),
        scratch_shapes=[pltpu.SemaphoreType.DMA((9 + 6 * len(blocks),))],
        out_shape=jax.ShapeDtypeStruct((3, n, d), jnp.bfloat16),
        compiler_params=pltpu.CompilerParams(vmem_limit_bytes=20 << 20),
        cost_estimate=pl.CostEstimate(flops=0, bytes_accessed=n * d, transcendentals=0),
        name="assemble",
    )(info, wo, do, r1, r2, *blocks, *after)


def expert_kernel(*refs, count, rows, after):
    xs, w_ref, ys = refs[:count], refs[count], refs[count + 1 + after:]
    x = jnp.concatenate([r[...] for r in xs], 0)
    nt = (((1,), (1,)), ((), ()))
    gate = lax.dot_general(x, w_ref[0], nt, preferred_element_type=jnp.float32)
    up = lax.dot_general(x, w_ref[1], nt, preferred_element_type=jnp.float32)
    inner = (gate / (1 + jnp.exp(-gate)) * up).astype(jnp.bfloat16)
    y = jnp.dot(inner, w_ref[2], preferred_element_type=jnp.float32).astype(jnp.bfloat16)
    for i in range(count):
        ys[i][...] = y[i * rows:(i + 1) * rows]


def experts(xs, w, after=()):
    count = len(xs)
    rows, d = xs[0].shape
    n = w.shape[1]
    vm = pl.BlockSpec(memory_space=pltpu.VMEM)
    return pl.pallas_call(
        functools.partial(expert_kernel, count=count, rows=rows, after=len(after)),
        in_specs=[vm] * (count + 1) + [pl.BlockSpec(memory_space=pl.ANY)] * len(after),
        out_specs=[vm] * count,
        out_shape=[jax.ShapeDtypeStruct((rows, d), jnp.bfloat16)] * count,
        compiler_params=pltpu.CompilerParams(vmem_limit_bytes=26 << 20),
        cost_estimate=pl.CostEstimate(flops=2 * count * rows * n * d, bytes_accessed=n * d, transcendentals=count * rows),
        name="experts",
    )(*xs, w, *after)


def combine_kernel(info_ref, hid_ref, mine_ref, other_ref, keep_ref, back_ref, hot_ref, factor_ref, out_ref):
    cap = back_ref.shape[0]
    is_mine = pl.program_id(0) // 2 == info_ref[2]
    att = jnp.where(is_mine, mine_ref[...].astype(jnp.float32), other_ref[...].astype(jnp.float32))
    stream = (hid_ref[...].astype(jnp.float32) + att).astype(jnp.bfloat16).astype(jnp.float32)
    one = jnp.dot(hot_ref[:, :cap], keep_ref[...], preferred_element_type=jnp.float32)
    two = jnp.dot(hot_ref[:, cap:2 * cap], back_ref[...], preferred_element_type=jnp.float32)
    out_ref[...] = (stream + one * factor_ref[:, 0:1] + two * factor_ref[:, 1:2]).astype(out_ref.dtype)


def combine(info, hidden, mine, other, keep, back, hot, factors):
    tok, d = hidden.shape
    cap = back.shape[0]
    wide = d // 4
    cols = lambda rows: pl.BlockSpec((rows, wide), lambda c, s: (0, c))
    half = pl.BlockSpec((tok, wide), lambda c, s: (0, lax.rem(c, 2)))
    whole = pl.BlockSpec((tok, tok), lambda c, s: (0, 0))
    return pl.pallas_call(
        combine_kernel,
        grid_spec=pltpu.PrefetchScalarGridSpec(
            num_scalar_prefetch=1,
            grid=(4,),
            in_specs=[cols(tok), half, half, cols(cap), cols(cap), whole, whole],
            out_specs=cols(tok),
        ),
        out_shape=jax.ShapeDtypeStruct((tok, d), hidden.dtype),
        compiler_params=pltpu.CompilerParams(vmem_limit_bytes=24 << 20),
        name="combine",
    )(info, hidden, mine, other, keep, back, hot, factors)


def shift(value, axis, size, steps):
    return lax.ppermute(value, axis, [(i, (i + steps) % size) for i in range(size)])


def swap(value, axis):
    return shift(value, axis, 2, 1)


def ring_moves(size):
    out = [0]
    for s in range(1, size // 2 + 1):
        out.append(-s)
        if 2 * s < size:
            out.append(s)
    return out


def ring_scatter(parts, signs, size):
    ups = [p[-2 * sign] for p, sign in zip(parts, signs)]
    downs = [shift(p[sign], "z", size, sign) for p, sign in zip(parts, signs)]
    for i, (p, sign) in enumerate(zip(parts, signs)):
        ups[i] = shift(ups[i], "z", size, -sign) + p[-sign]
    ups = [shift(u, "z", size, -sign) for u, sign in zip(ups, signs)]
    return [(ups[i], downs[i], p[0]) for i, p in enumerate(parts)]


def body(sizes, hidden_in, queries, keys_values, doc_ids, route_ids, route_weights, norm_gain, gate_up, down):
    tok, d = queries.shape
    capacity = tok // 4
    n_z, n_core, n_cx = sizes["z"], sizes["core"], sizes["cx"]
    yhi, z, core = lax.axis_index("yhi"), lax.axis_index("z"), lax.axis_index("core")
    half = n_z * tok
    n_ctx = n_cx * n_core
    moves = ring_moves(n_z)
    heads = keys_values.shape[1] // (4 * HD)
    cx, dp = lax.axis_index("cx"), lax.axis_index("dp")
    info = jnp.stack([z, yhi * half, yhi, core, cx, dp]).astype(jnp.int32)

    wide_t = jnp.swapaxes(gate_up, 2, 3)
    far = pack(info, wide_t, down, n_core, n_cx)
    place = lambda y, k, l: (y * n_z + k) * 2 + l
    across = [
        (place(y, k, l), place(y if l == 0 else 1 - y, (k + n_z // 2) % n_z, l)) for y in range(2) for k in range(n_z) for l in range(2)
    ]

    send, kept = prepare(info, keys_values, doc_ids)
    other = swap(send, "yhi")

    out, mine, hot, factors = plan(info, route_ids, route_weights, queries, hidden_in)
    out, other = lax.optimization_barrier((out, other))
    got = swap(out, "yhi")
    unit = join(send, kept, other)
    theirs = pack(info, wide_t, down, n_core, 1)
    ahead = [(i, i + 1) for i in range(n_ctx - 1)]
    onward = lambda x: lax.ppermute(x, ("cx", "core"), ahead)
    own = {0: unit}
    prior = [onward(unit)]
    for s in range(1, n_z // 2 + 1):
        own[-s] = shift(own[1 - s], "z", n_z, 1)
        if 2 * s < n_z:
            own[s] = shift(own[s - 1], "z", n_z, -1)
        if s == 1:
            own[-s], theirs = lax.optimization_barrier((own[-s], theirs))
            got_1 = swap(theirs, "yhi")
        if s == 2:
            own[-s], prior[0], got = lax.optimization_barrier((own[-s], prior[0], got))
        if s == 4:
            own[-s], far = lax.optimization_barrier((own[-s], far))
            far = lax.ppermute(far, ("yhi", "z", "dp"), across)
    own = [own[m] for m in moves]
    groups = [range(0, 1), range(1, n_z // 2 + 1), range(n_z // 2 + 1, n_z - 1), range(n_z - 1, n_z)]
    layout = []
    for n, group in enumerate(groups):
        if n > 0:
            prior.append(onward(jnp.concatenate([own[i] for i in group], 0) if len(group) > 1 else own[group[0]]))
        layout += [(n, k * unit.shape[0]) for k in range(len(group))]
    layout += [(len(groups) + i, 0) for i in range(n_z)]
    pieces = prior + own

    gain = norm_gain[None]
    first = yhi == 0
    atts, rows = [], []
    for part in range(2):
        if part == 1:
            mine, got_1, _ = lax.optimization_barrier((mine, got_1, atts[0]))
        att, keep, away = attend(info, mine, got, pieces, layout, moves, part, heads, tok)
        atts.append(att)
        rows.append((keep, away))
    away, far = lax.optimization_barrier((rows[1][1], far))
    others = [swap(rows[0][1], "yhi"), swap(away, "yhi")]
    others, far, far_2 = lax.optimization_barrier((others, far, swap(far, "dp")))
    share = jnp.concatenate([far, far_2], 0)
    left, right = shift(share, "cx", n_cx, 1), shift(share, "cx", n_cx, -1)
    rows = [norm_rows(info, mine, got, part, rows[part][0], others[part], gain) for part in range(2)]
    got_2 = swap(got_1, "core")
    own_att = jnp.where(first, atts[0], atts[1])
    away_att, rows[1] = lax.optimization_barrier((jnp.where(first, atts[1], atts[0]), rows[1]))
    other_att = swap(away_att, "yhi")

    signs = [1, -1]
    rows = [{0: x, -sign: shift(x, "z", n_z, sign), sign: shift(x, "z", n_z, -sign)} for x, sign in zip(rows, signs)]
    cut = share.shape[0] // 2
    halves = [shift(right[:cut], "cx", n_cx, -1), shift(left[cut:], "cx", n_cx, 1)]
    near = [g[m] for g in rows for m in (-1, 1)]
    near, halves = lax.optimization_barrier((near, halves))
    rows = [
        {0: g[0], -1: near[2 * i], 1: near[2 * i + 1], -2 * sign: shift(g[-sign], "z", n_z, sign)} for i, (g, sign) in enumerate(zip(rows, signs))
    ]
    blocks = [share, left, right] + halves
    steps = [(0, 0), (-1, 0), (1, 0), (2, 0), (2, 1)]
    blocks = blocks + [swap(x, "core") for x in blocks]
    layout = [(c,) + step for c in range(n_core) for step in steps]
    weights = assemble(info, wide_t, down, got_1, got_2, blocks, layout, n_cx, [g[-2 * sign] for g, sign in zip(rows, signs)])
    keys = [(i, m) for i, sign in enumerate(signs) for m in (0, -1, 1, -2 * sign)]
    outs = [{}, {}]
    for (i, m), y in zip(keys, experts([rows[i][m] for i, m in keys], weights, after=[other_att])):
        outs[i][m] = y
    sums = [ups.astype(jnp.float32) + downs + here for ups, downs, here in ring_scatter(outs, signs, n_z)]
    back = swap(jnp.where(first, sums[1], sums[0]).astype(jnp.bfloat16), "yhi")
    keep = jnp.where(first, sums[0], sums[1]).astype(jnp.bfloat16)
    return combine(info, hidden_in, own_att, other_att, keep, back, hot, factors)


def solution(mesh):
    sizes = {"cx": mesh.shape["ctx"] // 2, "core": 2, "yhi": 2, "z": mesh.shape["exp"] // 2, "dp": mesh.shape["dp"]}
    fine = Mesh(mesh.devices.reshape(tuple(sizes.values())), tuple(sizes))
    tokens = ("dp", "cx", "core", "yhi", "z")
    rows = P(tokens, None)
    hidden = ("yhi", "z")
    in_specs = (rows, rows, rows, P(tokens), rows, rows, P(), P(None, None, None, hidden), P(None, hidden, None))
    return jax.shard_map(
        functools.partial(body, sizes), mesh=fine, in_specs=in_specs, out_specs=rows, check_vma=False
    )
```

```python
import functools
import math

import jax
import jax.numpy as jnp
from jax import lax
from jax.experimental import pallas as pl
from jax.experimental.pallas import tpu as pltpu
from jax.sharding import Mesh
from jax.sharding import PartitionSpec as P

EXP_FLIGHT = 2
HD = 128
GROUP = 7
EXP2_SCALE = math.log2(math.e) / math.sqrt(HD)

def attend_kernel(info_ref, q_own_ref, q_got_ref, place_own_ref, place_got_ref, *refs, tok, span, moves, heads, layout, part):
    arrays, out_ref, low_ref, high_ref = refs[:-11], refs[-11], refs[-10], refs[-9]
    kv, ids, start_scr, m_scr, l_scr, acc_scr, bounds, sem = refs[-8:]
    c = pl.program_id(0)
    z = info_ref[0]
    half = len(moves) * tok
    near = pl.multiple_of(info_ref[1], half)
    far = pl.multiple_of(half - info_ref[1], half)
    first = pl.multiple_of(part * half + z * tok, tok)
    is_own = info_ref[2] == part

    @pl.when(c == 0)
    def _():
        blocks = []
        copies = []
        for n, (which, row) in enumerate(layout):
            piece = arrays[which]
            place = lax.rem(z + moves[n % len(moves)] + len(moves), len(moves)) * tok
            slab = n // len(moves) * 2 * half
            for side, base in ((0, near), (1, far)):
                at = pl.multiple_of(slab + base + place, tok)
                cp = pltpu.make_async_copy(piece.at[pl.ds(row + side * tok, tok)], kv.at[pl.ds(at, tok)], sem.at[n, side])
                blocks.append((cp, (at >= first) & (at <= first + 2 * half)))
            copies.append(pltpu.make_async_copy(piece.at[pl.ds(row + 2 * tok, 16)], ids.at[n], sem.at[n, 2]))
        for cp in copies:
            cp.start()
        for cp, needed in blocks:
            pl.when(needed)(cp.start)
        for cp in copies:
            cp.wait()
        own = [ids[len(moves), 0:1, n * tok:(n + 1) * tok].astype(jnp.float32) for n in range(2)]
        own = jnp.where(is_own, own[0], own[1])
        own = jnp.broadcast_to(own, (tok, tok)).T
        less = jnp.zeros((tok, tok), jnp.float32)
        for n in range(len(layout)):
            for side in range(2):
                row = ids[n, 0:1, side * tok:(side + 1) * tok].astype(jnp.float32)
                less = less + jnp.where(row < own, 1.0, 0.0)
        begin = jnp.sum(less, axis=1, keepdims=True)
        start_scr[...] = begin.astype(jnp.int32)
        bounds[0] = jnp.min(begin).astype(jnp.int32)
        bounds[1] = jnp.max(begin).astype(jnp.int32)
        for cp, needed in blocks:
            pl.when(needed)(cp.wait)

    start_min, start_max = bounds[0], bounds[1]
    q = jnp.where(is_own, q_own_ref[...], q_got_ref[...])
    q = jnp.concatenate([q[:, g * HD:(g + 1) * HD] for g in range(GROUP)], 0)
    start = start_scr[...]
    row = lax.broadcasted_iota(jnp.int32, (tok, 1), 0) + first + 2 * half
    key_col = pl.multiple_of(c * HD, HD)
    value_col = pl.multiple_of((heads + c) * HD, HD)

    def keys(offset, width):
        return kv[pl.ds(offset, width), pl.ds(key_col, HD)]

    def values(offset, width):
        return kv[pl.ds(offset, width), pl.ds(value_col, HD)]

    def scores(offset, width):
        return lax.dot_general(q, keys(offset, width), (((1,), (1,)), ((), ())), preferred_element_type=jnp.float32)

    def rowmax(s, width):
        t = s[:, :128]
        for j in range(1, width // 128):
            t = jnp.maximum(t, s[:, j * 128:(j + 1) * 128])
        return jnp.max(t, axis=1, keepdims=True)

    def lanesum(p, width):
        t = p[:, :128]
        for j in range(1, width // 128):
            t = t + p[:, j * 128:(j + 1) * 128]
        return t

    def masked(s, offset, width, causal):
        key = lax.broadcasted_iota(jnp.int32, (tok, width), 1) + offset
        ok = key >= start
        if causal:
            ok = ok & (key <= row)
        return jnp.where(ok[None], s.reshape(GROUP, tok, width), -1e30).reshape(GROUP * tok, width)

    own = pl.multiple_of(first + 2 * half, tok)
    s = masked(scores(own, tok), own, tok, True)
    m = rowmax(s, tok)
    p = jnp.exp2((s - m) * EXP2_SCALE)
    m_scr[...] = jnp.broadcast_to(m, m_scr.shape)
    l_scr[...] = lanesum(p, tok)
    acc_scr[...] = jnp.dot(p.astype(jnp.bfloat16), values(own, tok), preferred_element_type=jnp.float32)

    def step(i, mask):
        offset = pl.multiple_of(first + i * span, tok)
        s = scores(offset, span)
        if mask:
            s = masked(s, offset, span, False)
        old = m_scr[...]
        new = jnp.maximum(old, rowmax(s, span))
        m_scr[...] = new
        shrink = jnp.exp2((old - new) * EXP2_SCALE)
        p = jnp.exp2((s - jnp.concatenate([new] * (span // 128), 1)) * EXP2_SCALE)
        l_scr[...] = l_scr[...] * shrink + lanesum(p, span)
        acc_scr[...] = acc_scr[...] * shrink + jnp.dot(p.astype(jnp.bfloat16), values(offset, span), preferred_element_type=jnp.float32)

    steps = 2 * half // span

    def loop(i, carry):
        whole = start_max <= first + i * span

        @pl.when(whole)
        def _():
            step(i, False)

        @pl.when(jnp.logical_not(whole))
        def _():
            step(i, True)

        return carry

    lax.fori_loop(jnp.clip(lax.div(start_min - first, span), 0, steps), steps, loop, 0)

    total = jnp.sum(l_scr[...], axis=1, keepdims=True)
    att = (acc_scr[...] / total).astype(jnp.bfloat16)
    att = jnp.concatenate([att[g * tok:(g + 1) * tok] for g in range(GROUP)], 1)
    out_ref[...] = att
    place = jnp.where(is_own, place_own_ref[...], place_got_ref[...])
    rows = jnp.dot(place, att, preferred_element_type=jnp.float32).astype(jnp.bfloat16)
    low_ref[...] = rows[:rows.shape[0] // 2]
    high_ref[...] = rows[rows.shape[0] // 2:]


def attend(info, own, got, pieces, layout, moves, part, heads, tok, span=512):
    slots = tok // 4
    wide = GROUP * HD
    n = len(moves)
    hbm = pl.BlockSpec(memory_space=pl.ANY)
    scratch = pltpu.VMEM((GROUP * tok, 128), jnp.float32)
    return pl.pallas_call(
        functools.partial(attend_kernel, tok=tok, span=span, moves=moves, heads=heads, layout=layout, part=part),
        grid_spec=pltpu.PrefetchScalarGridSpec(
            num_scalar_prefetch=1,
            grid=(heads,),
            in_specs=[
                pl.BlockSpec((tok, wide), lambda c, s: (0, c)),
                pl.BlockSpec((tok, wide), lambda c, s: (0, c)),
                pl.BlockSpec((2 * slots, tok), lambda c, s: (tok // (2 * slots), heads * GROUP)),
                pl.BlockSpec((2 * slots, tok), lambda c, s: (tok // (2 * slots), heads * GROUP)),
            ] + [hbm] * len(pieces),
            out_specs=[pl.BlockSpec((r, wide), lambda c, s: (0, c)) for r in (tok, slots, slots)],
            scratch_shapes=[
                pltpu.VMEM((4 * n * tok, 2 * heads * HD), jnp.bfloat16),
                pltpu.VMEM((2 * n, 16, 2 * heads * HD), jnp.bfloat16),
                pltpu.VMEM((tok, 1), jnp.int32),
                scratch, scratch, scratch,
                pltpu.SMEM((2,), jnp.int32),
                pltpu.SemaphoreType.DMA((2 * n, 3)),
            ],
        ),
        out_shape=[jax.ShapeDtypeStruct((r, heads * wide), jnp.bfloat16) for r in (tok, slots, slots)],
        compiler_params=pltpu.CompilerParams(vmem_limit_bytes=60 << 20),
        cost_estimate=pl.CostEstimate(flops=2 * 10**9, bytes_accessed=1 << 20, transcendentals=10**5),
        name="attend",
    )(info, own, got, own, got, *pieces)


def prepare_kernel(info_ref, kv_ref, doc_ref, send_ref, mine_ref):
    tok = kv_ref.shape[0]
    w = kv_ref.shape[1] // 4
    send_ref[tok:, :] = jnp.zeros((16, 2 * w), send_ref.dtype)
    send_ref[tok:tok + 16, :tok] = jnp.broadcast_to((doc_ref[...] + 1).astype(jnp.float32), (16, tok)).astype(send_ref.dtype)
    for yhi in range(2):
        @pl.when(info_ref[2] == yhi)
        def _(yhi=yhi):
            away = 1 - yhi
            mine_ref[:, :w] = kv_ref[:, yhi * w:(yhi + 1) * w]
            mine_ref[:, w:] = kv_ref[:, (2 + yhi) * w:(3 + yhi) * w]
            send_ref[:tok, :w] = kv_ref[:, away * w:(away + 1) * w]
            send_ref[:tok, w:] = kv_ref[:, (2 + away) * w:(3 + away) * w]


def prepare(info, keys_values, doc_ids):
    tok, width = keys_values.shape
    vm = pl.BlockSpec(memory_space=pltpu.VMEM)
    shape = lambda r, c: jax.ShapeDtypeStruct((r, c), jnp.bfloat16)
    return pl.pallas_call(
        prepare_kernel,
        in_specs=[pl.BlockSpec(memory_space=pltpu.SMEM)] + [vm] * 2,
        out_specs=[vm] * 2,
        out_shape=[shape(tok + 16, width // 2), shape(tok, width // 2)],
        compiler_params=pltpu.CompilerParams(vmem_limit_bytes=24 << 20),
        name="prepare",
    )(info, keys_values, doc_ids[None])


def plan_kernel(info_ref, ids_ref, weights_ref, q_ref, hid_ref, out_ref, own_ref, hot_ref, factor_ref):
    tok = hid_ref.shape[0]
    slots = (out_ref.shape[0] - tok) // 2
    q = q_ref.shape[1] // 2
    yhi = info_ref[2]
    below = lax.broadcasted_iota(jnp.int32, (tok, tok), 0) <= lax.broadcasted_iota(jnp.int32, (tok, tok), 1)
    below = below.astype(jnp.float32).astype(jnp.bfloat16)
    places, factors = [], []
    for flight in (yhi, 1 - yhi):
        chosen = ids_ref[...] == flight
        routed = jnp.max(jnp.where(chosen, 1.0, 0.0), axis=0, keepdims=True)
        factors.append(jnp.sum(jnp.where(chosen, weights_ref[...], 0.0), axis=0, keepdims=True))
        ranks = jnp.dot(jnp.broadcast_to(routed, (16, tok)).astype(jnp.bfloat16), below, preferred_element_type=jnp.float32)
        ranks = jnp.where(routed > 0.5, ranks[:1] - 1.0, -1.0)
        slot = lax.broadcasted_iota(jnp.int32, (slots, tok), 0).astype(jnp.float32)
        places.append(jnp.where(slot == ranks, 1.0, 0.0))
    place_f = jnp.concatenate(places, 0)
    place = place_f.astype(jnp.bfloat16)
    hot_ref[...] = jnp.concatenate([place_f, jnp.zeros((tok - 2 * slots, tok), jnp.float32)], 0).T.astype(jnp.bfloat16)
    factor_ref[...] = jnp.concatenate([factors[0], factors[1], jnp.zeros((tok - 2, tok), jnp.float32)], 0).T
    rows = jnp.dot(place, hid_ref[...], preferred_element_type=jnp.float32).astype(jnp.bfloat16)
    for n, ref in enumerate((own_ref, out_ref)):
        ref[:tok, q:] = jnp.zeros((tok, tok), jnp.bfloat16)
        ref[tok:tok + slots, :q] = rows[n * slots:(n + 1) * slots, :q]
        ref[tok + slots:, :q] = rows[n * slots:(n + 1) * slots, q:]
        ref[tok:tok + slots, q:] = place[n * slots:(n + 1) * slots]
        ref[tok + slots:, q:] = place[(1 - n) * slots:(2 - n) * slots]

    for side in range(2):
        @pl.when(yhi == side)
        def _(side=side):
            own_ref[:tok, :q] = q_ref[:, side * q:(side + 1) * q]
            out_ref[:tok, :q] = q_ref[:, (1 - side) * q:(2 - side) * q]


def plan(info, route_ids, route_weights, queries, hidden):
    tok, d = hidden.shape
    slots = tok // 4
    vm = pl.BlockSpec(memory_space=pltpu.VMEM)
    shape = lambda r, c, t=jnp.bfloat16: jax.ShapeDtypeStruct((r, c), t)
    return pl.pallas_call(
        plan_kernel,
        in_specs=[pl.BlockSpec(memory_space=pltpu.SMEM)] + [vm] * 4,
        out_specs=[vm] * 4,
        out_shape=[shape(tok + 2 * slots, d // 2 + tok)] * 2 + [shape(tok, tok), shape(tok, tok, jnp.float32)],
        compiler_params=pltpu.CompilerParams(vmem_limit_bytes=24 << 20),
        name="plan",
    )(info, route_ids.T, route_weights.T, queries, hidden)


def join_kernel(send_ref, mine_ref, other_ref, unit_ref):
    tok = mine_ref.shape[0]
    unit_ref[:tok] = mine_ref[...]
    unit_ref[tok:2 * tok] = other_ref[:tok]
    unit_ref[2 * tok:] = send_ref[tok:]
    unit_ref[2 * tok:, tok:2 * tok] = other_ref[tok:, :tok]


def join(send, mine, other):
    tok, width = mine.shape
    vm = pl.BlockSpec(memory_space=pltpu.VMEM)
    return pl.pallas_call(
        join_kernel,
        in_specs=[vm] * 3,
        out_specs=vm,
        out_shape=jax.ShapeDtypeStruct((2 * tok + 16, width), mine.dtype),
        compiler_params=pltpu.CompilerParams(vmem_limit_bytes=24 << 20),
        name="join",
    )(send, mine, other)


def pack_kernel(info_ref, gu_ref, down_ref, out_ref, sem):
    yhi = info_ref[2]
    units, wide = out_ref.shape[1], out_ref.shape[2]
    at = pl.ds(pl.multiple_of(info_ref[3] * units, units), units)
    if wide == down_ref.shape[2]:
        away, cols = 1 - yhi, pl.ds(0, wide)
    else:
        away = jnp.where(info_ref[5] == 0, yhi, 1 - yhi)
        cols = pl.ds(pl.multiple_of(info_ref[4] * wide, wide), wide)
    one = pltpu.make_async_copy(gu_ref.at[away, :, at, cols], out_ref.at[pl.ds(0, 2)], sem.at[0])
    two = pltpu.make_async_copy(down_ref.at[away, at, cols], out_ref.at[2], sem.at[1])
    one.start()
    two.start()
    one.wait()
    two.wait()


def pack(info, wide_t, down, cores, columns):
    hbm = pl.BlockSpec(memory_space=pl.ANY)
    units, d = down.shape[1] // cores, down.shape[2]
    return pl.pallas_call(
        pack_kernel,
        in_specs=[pl.BlockSpec(memory_space=pltpu.SMEM), hbm, hbm],
        out_specs=pl.BlockSpec(memory_space=pltpu.VMEM),
        out_shape=jax.ShapeDtypeStruct((3, units, d // columns), down.dtype),
        scratch_shapes=[pltpu.SemaphoreType.DMA((2,))],
        compiler_params=pltpu.CompilerParams(vmem_limit_bytes=60 << 20),
        name="pack",
    )(info, wide_t, down)


def norm_kernel(info_ref, own_ref, got_ref, mine_ref, other_ref, gain_ref, out_ref, *, part):
    slots, half = mine_ref.shape
    tok = own_ref.shape[0] - 2 * slots
    is_own = info_ref[2] == part

    def put(low, high):
        parts = []
        for n, att in enumerate((low, high)):
            rows = slice(tok + n * slots, tok + (n + 1) * slots)
            base = jnp.where(is_own, own_ref[rows, :half], got_ref[rows, :half]).astype(jnp.float32)
            parts.append((base + att.astype(jnp.float32)).astype(jnp.bfloat16).astype(jnp.float32))
        total = sum(jnp.sum(p * p, axis=1, keepdims=True) for p in parts)
        inv = lax.rsqrt(total / (2 * half) + 1e-6)
        for n, p in enumerate(parts):
            gain = gain_ref[:, n * half:(n + 1) * half].astype(jnp.float32)
            out_ref[:, n * half:(n + 1) * half] = (p * inv * gain).astype(jnp.bfloat16)

    @pl.when(info_ref[2] == 0)
    def _():
        put(mine_ref[...], other_ref[...])

    @pl.when(info_ref[2] != 0)
    def _():
        put(other_ref[...], mine_ref[...])


def norm_rows(info, own, got, part, mine, other, gain):
    slots, half = mine.shape
    vm = pl.BlockSpec(memory_space=pltpu.VMEM)
    return pl.pallas_call(
        functools.partial(norm_kernel, part=part),
        in_specs=[pl.BlockSpec(memory_space=pltpu.SMEM)] + [vm] * 5,
        out_specs=vm,
        out_shape=jax.ShapeDtypeStruct((slots, 2 * half), jnp.bfloat16),
        compiler_params=pltpu.CompilerParams(vmem_limit_bytes=16 << 20),
        name="norm_rows",
    )(info, own, got, mine, other, gain)


def assemble_kernel(info_ref, wo_ref, do_ref, r1_ref, r2_ref, *refs, plan, columns):
    blocks, w_ref, sem = refs[:len(plan)], refs[-2], refs[-1]
    yhi = info_ref[2]
    n, h = wo_ref.shape[2], r1_ref.shape[1]
    cps = []

    def cp(src, dst):
        cps.append(pltpu.make_async_copy(src, dst, sem.at[len(cps)]))

    for i in range(3):
        own = do_ref.at[yhi] if i == 2 else wo_ref.at[yhi, i]
        for src, at, size in ((own, 0, n), (r1_ref.at[i], n, h), (r2_ref.at[i], n + h, h)):
            cp(src, w_ref.at[i, pl.ds(at, size)])
        for block, (core, step, first) in zip(blocks, plan):
            wide = block.shape[2]
            col = lax.rem(info_ref[4] + step + columns, columns) * wide
            for u in range(block.shape[0] // 3):
                at = n + 2 * h + (2 * core + first + u) * h
                cp(block.at[3 * u + i], w_ref.at[i, pl.ds(at, h), pl.ds(pl.multiple_of(col, wide), wide)])
    for c in cps:
        c.start()
    for c in cps:
        c.wait()


def assemble(info, wo, do, r1, r2, blocks, plan, columns, after):
    n, d = 2 * (wo.shape[2] + r1.shape[1] + r2.shape[1]), wo.shape[3]
    hbm = pl.BlockSpec(memory_space=pl.ANY)
    return pl.pallas_call(
        functools.partial(assemble_kernel, plan=plan, columns=columns),
        in_specs=[pl.BlockSpec(memory_space=pltpu.SMEM)] + [hbm] * (5 + len(blocks)),
        out_specs=pl.BlockSpec(memory_space=pltpu.VMEM),
        scratch_shapes=[pltpu.SemaphoreType.DMA((9 + 6 * len(blocks),))],
        out_shape=jax.ShapeDtypeStruct((3, n, d), jnp.bfloat16),
        compiler_params=pltpu.CompilerParams(vmem_limit_bytes=20 << 20),
        cost_estimate=pl.CostEstimate(flops=0, bytes_accessed=n * d, transcendentals=0),
        name="assemble",
    )(info, wo, do, r1, r2, *blocks, after)


def expert_kernel(*refs, count, rows, after):
    xs, w_ref, ys = refs[:count], refs[count], refs[count + 1 + after:]
    x = jnp.concatenate([r[...] for r in xs], 0)
    nt = (((1,), (1,)), ((), ()))
    gate = lax.dot_general(x, w_ref[0], nt, preferred_element_type=jnp.float32)
    up = lax.dot_general(x, w_ref[1], nt, preferred_element_type=jnp.float32)
    inner = (gate / (1 + jnp.exp(-gate)) * up).astype(jnp.bfloat16)
    y = jnp.dot(inner, w_ref[2], preferred_element_type=jnp.float32).astype(jnp.bfloat16)
    for i in range(count):
        ys[i][...] = y[i * rows:(i + 1) * rows]


def experts(xs, w, after=()):
    count = len(xs)
    rows, d = xs[0].shape
    n = w.shape[1]
    vm = pl.BlockSpec(memory_space=pltpu.VMEM)
    return pl.pallas_call(
        functools.partial(expert_kernel, count=count, rows=rows, after=len(after)),
        in_specs=[vm] * (count + 1) + [pl.BlockSpec(memory_space=pl.ANY)] * len(after),
        out_specs=[vm] * count,
        out_shape=[jax.ShapeDtypeStruct((rows, d), jnp.bfloat16)] * count,
        compiler_params=pltpu.CompilerParams(vmem_limit_bytes=26 << 20),
        cost_estimate=pl.CostEstimate(flops=2 * count * rows * n * d, bytes_accessed=n * d, transcendentals=count * rows),
        name="experts",
    )(*xs, w, *after)


def combine_kernel(info_ref, hid_ref, mine_ref, other_ref, keep_ref, back_ref, hot_ref, factor_ref, out_ref):
    cap = back_ref.shape[0]
    is_mine = pl.program_id(0) // 2 == info_ref[2]
    att = jnp.where(is_mine, mine_ref[...].astype(jnp.float32), other_ref[...].astype(jnp.float32))
    stream = (hid_ref[...].astype(jnp.float32) + att).astype(jnp.bfloat16).astype(jnp.float32)
    one = jnp.dot(hot_ref[:, :cap], keep_ref[...], preferred_element_type=jnp.float32)
    two = jnp.dot(hot_ref[:, cap:2 * cap], back_ref[...], preferred_element_type=jnp.float32)
    out_ref[...] = (stream + one * factor_ref[:, 0:1] + two * factor_ref[:, 1:2]).astype(out_ref.dtype)


def combine(info, hidden, mine, other, keep, back, hot, factors):
    tok, d = hidden.shape
    cap = back.shape[0]
    wide = d // 4
    cols = lambda rows: pl.BlockSpec((rows, wide), lambda c, s: (0, c))
    half = pl.BlockSpec((tok, wide), lambda c, s: (0, lax.rem(c, 2)))
    whole = pl.BlockSpec((tok, tok), lambda c, s: (0, 0))
    return pl.pallas_call(
        combine_kernel,
        grid_spec=pltpu.PrefetchScalarGridSpec(
            num_scalar_prefetch=1,
            grid=(4,),
            in_specs=[cols(tok), half, half, cols(cap), cols(cap), whole, whole],
            out_specs=cols(tok),
        ),
        out_shape=jax.ShapeDtypeStruct((tok, d), hidden.dtype),
        compiler_params=pltpu.CompilerParams(vmem_limit_bytes=24 << 20),
        name="combine",
    )(info, hidden, mine, other, keep, back, hot, factors)


def shift(value, axis, size, steps):
    return lax.ppermute(value, axis, [(i, (i + steps) % size) for i in range(size)])


def swap(value, axis):
    return shift(value, axis, 2, 1)


def ring_moves(size):
    out = [0]
    for s in range(1, size // 2 + 1):
        out.append(-s)
        if 2 * s < size:
            out.append(s)
    return out


def ring_scatter(parts, signs, size):
    ups = [p[-2 * sign] for p, sign in zip(parts, signs)]
    downs = [shift(p[sign], "z", size, sign) for p, sign in zip(parts, signs)]
    for i, (p, sign) in enumerate(zip(parts, signs)):
        ups[i] = shift(ups[i], "z", size, -sign) + p[-sign]
    ups = [shift(u, "z", size, -sign) for u, sign in zip(ups, signs)]
    return [(ups[i], downs[i], p[0]) for i, p in enumerate(parts)]


def body(sizes, hidden_in, queries, keys_values, doc_ids, route_ids, route_weights, norm_gain, gate_up, down):
    tok, d = queries.shape
    capacity = tok // 4
    n_z, n_core, n_cx = sizes["z"], sizes["core"], sizes["cx"]
    yhi, z, core = lax.axis_index("yhi"), lax.axis_index("z"), lax.axis_index("core")
    half = n_z * tok
    n_ctx = n_cx * n_core
    moves = ring_moves(n_z)
    heads = keys_values.shape[1] // (4 * HD)
    cx, dp = lax.axis_index("cx"), lax.axis_index("dp")
    info = jnp.stack([z, yhi * half, yhi, core, cx, dp]).astype(jnp.int32)

    wide_t = jnp.swapaxes(gate_up, 2, 3)
    far = pack(info, wide_t, down, n_core, n_cx)
    place = lambda y, k, l: (y * n_z + k) * 2 + l
    across = [
        (place(y, k, l), place(y if l == 0 else 1 - y, (k + n_z // 2) % n_z, l)) for y in range(2) for k in range(n_z) for l in range(2)
    ]

    send, kept = prepare(info, keys_values, doc_ids)
    other = swap(send, "yhi")

    out, mine, hot, factors = plan(info, route_ids, route_weights, queries, hidden_in)
    out, other = lax.optimization_barrier((out, other))
    got = swap(out, "yhi")
    unit = join(send, kept, other)
    theirs = pack(info, wide_t, down, n_core, 1)
    ahead = [(i, i + 1) for i in range(n_ctx - 1)]
    onward = lambda x: lax.ppermute(x, ("cx", "core"), ahead)
    own = {0: unit}
    prior = [onward(unit)]
    for s in range(1, n_z // 2 + 1):
        own[-s] = shift(own[1 - s], "z", n_z, 1)
        if 2 * s < n_z:
            own[s] = shift(own[s - 1], "z", n_z, -1)
        if s == 1:
            own[-s], theirs = lax.optimization_barrier((own[-s], theirs))
            got_1 = swap(theirs, "yhi")
        if s == 2:
            own[-s], prior[0], got = lax.optimization_barrier((own[-s], prior[0], got))
        if s == 4:
            own[-s], far = lax.optimization_barrier((own[-s], far))
            far = lax.ppermute(far, ("yhi", "z", "dp"), across)
    own = [own[m] for m in moves]
    groups = [range(0, 1), range(1, n_z // 2 + 1), range(n_z // 2 + 1, n_z - 1), range(n_z - 1, n_z)]
    layout = []
    for n, group in enumerate(groups):
        if n > 0:
            prior.append(onward(jnp.concatenate([own[i] for i in group], 0) if len(group) > 1 else own[group[0]]))
        layout += [(n, k * unit.shape[0]) for k in range(len(group))]
    layout += [(len(groups) + i, 0) for i in range(n_z)]
    pieces = prior + own

    gain = norm_gain[None]
    first = yhi == 0
    atts, rows = [], []
    for part in range(2):
        if part == 1:
            mine, got_1, far, _ = lax.optimization_barrier((mine, got_1, far, atts[0]))
            far_2 = swap(far, "dp")
        att, keep, away = attend(info, mine, got, pieces, layout, moves, part, heads, tok)
        if part == 1:
            away, far, far_2 = lax.optimization_barrier((away, far, far_2))
            share = jnp.concatenate([far, far_2], 0)
            left, right = shift(share, "cx", n_cx, 1), shift(share, "cx", n_cx, -1)
        atts.append(att)
        rows.append(norm_rows(info, mine, got, part, keep, swap(away, "yhi"), gain))
    got_2 = swap(got_1, "core")
    own_att = jnp.where(first, atts[0], atts[1])
    away_att, rows[1] = lax.optimization_barrier((jnp.where(first, atts[1], atts[0]), rows[1]))
    other_att = swap(away_att, "yhi")

    signs = [1, -1]
    rows = [{0: x, -sign: shift(x, "z", n_z, sign), sign: shift(x, "z", n_z, -sign)} for x, sign in zip(rows, signs)]
    rows[0][-1], left, right = lax.optimization_barrier((rows[0][-1], left, right))
    cut = share.shape[0] // 2
    blocks = [share, left, right, shift(right[:cut], "cx", n_cx, -1), shift(left[cut:], "cx", n_cx, 1)]
    steps = [(0, 0), (-1, 0), (1, 0), (2, 0), (2, 1)]
    for g, sign in zip(rows, signs):
        g[-2 * sign] = shift(g[-sign], "z", n_z, sign)
    blocks = blocks + [swap(x, "core") for x in blocks]
    layout = [(c,) + step for c in range(n_core) for step in steps]
    weights = assemble(info, wide_t, down, got_1, got_2, blocks, layout, n_cx, rows[1][0])
    keys = [(i, m) for i, sign in enumerate(signs) for m in (0, -1, 1, -2 * sign)]
    outs = [{}, {}]
    for (i, m), y in zip(keys, experts([rows[i][m] for i, m in keys], weights, after=[other_att])):
        outs[i][m] = y
    sums = [ups.astype(jnp.float32) + downs + here for ups, downs, here in ring_scatter(outs, signs, n_z)]
    back = swap(jnp.where(first, sums[1], sums[0]).astype(jnp.bfloat16), "yhi")
    keep = jnp.where(first, sums[0], sums[1]).astype(jnp.bfloat16)
    return combine(info, hidden_in, own_att, other_att, keep, back, hot, factors)


def solution(mesh):
    sizes = {"cx": mesh.shape["ctx"] // 2, "core": 2, "yhi": 2, "z": mesh.shape["exp"] // 2, "dp": mesh.shape["dp"]}
    fine = Mesh(mesh.devices.reshape(tuple(sizes.values())), tuple(sizes))
    tokens = ("dp", "cx", "core", "yhi", "z")
    rows = P(tokens, None)
    hidden = ("yhi", "z")
    in_specs = (rows, rows, rows, P(tokens), rows, rows, P(), P(None, None, None, hidden), P(None, hidden, None))
    return jax.shard_map(
        functools.partial(body, sizes), mesh=fine, in_specs=in_specs, out_specs=rows, check_vma=False
    )
```
